32 devices in a mesh: dp: 8 (over z, y), tensor: 4 (over x, core).
Axes of the slice: x: 2, y: 2, z: 4, core: 2. Of those that a mesh axis runs over, the one named last changes fastest.
Arguments:
- tokens_in: bfloat16 [8192, 1024], P(('dp', 'tensor')), may hold values from -6 to 6
- grad_out: bfloat16 [8192, 1024], P(('dp', 'tensor')), may hold values from -6 to 6
- scene_offsets: int32 [4], replicated, may hold values from 0 to 8064, as said below
- input_gain: float32 [1024], replicated, may hold values from 0.25 to 1.75
- weight_zx: bfloat16 [2, 1024, 2048], P(None, None, 'tensor'), may hold values from -0.1875 to 0.1875
- weight_bc: bfloat16 [2, 1024, 128], replicated, may hold values from -0.1875 to 0.1875
- weight_step: bfloat16 [1024, 32], P(None, 'tensor'), may hold values from -0.1875 to 0.1875
- conv_inner: float32 [4, 2048], P(None, 'tensor'), may hold values from -0.5 to 0.5
- conv_inner_bias: float32 [2048], P('tensor'), may hold values from -0.5 to 0.5
- conv_bc: float32 [2, 4, 128], replicated, may hold values from -0.5 to 0.5
- conv_bc_bias: float32 [2, 128], replicated, may hold values from -0.5 to 0.5
- step_bias: float32 [32], P('tensor'), may hold values from -6 to -2
- decay_log: float32 [32], P('tensor'), may hold values from -4 to 2.75
- skip_weight: float32 [32], P('tensor'), may hold values from 0.5 to 2
- norm_gain: float32 [2048], P('tensor'), may hold values from 0.25 to 1.75
- weight_out: bfloat16 [2048, 1024], P('tensor'), may hold values from -0.125 to 0.125
Outputs:
- layer_out: bfloat16 [8192, 1024], P(('dp', 'tensor'))
- grad_tokens: float32 [8192, 1024], P(('dp', 'tensor'))
- grad_input_gain: float32 [1024], replicated
- grad_weight_zx: float32 [2, 1024, 2048], P(None, None, 'tensor')
- grad_weight_bc: float32 [2, 1024, 128], replicated
- grad_weight_step: float32 [1024, 32], P(None, 'tensor')
- grad_conv_inner: float32 [4, 2048], P(None, 'tensor')
- grad_conv_inner_bias: float32 [2048], P('tensor')
- grad_conv_bc: float32 [2, 4, 128], replicated
- grad_conv_bc_bias: float32 [2, 128], replicated
- grad_step_bias: float32 [32], P('tensor')
- grad_decay_log: float32 [32], P('tensor')
- grad_skip_weight: float32 [32], P('tensor')
- grad_norm_gain: float32 [2048], P('tensor')
- grad_weight_out: float32 [2048, 1024], P('tensor')
The draws below stay inside these ranges and needn't reach their ends.
Inputs may be any that keep to these rules, and one draw needn't show every extreme that they name: `scene_offsets`: scene starts in rising order; the first is 0, each is a multiple of 128, and every scene has 128 positions or more.
All inputs are finite; a program needn't handle non-finite values.
Results may differ from the reference program's by a relative error of at most 0.014.
Values may be sent and summed in bfloat16 or wider, within the bound.
No kernel may reach another device: no remote copies, remote signals or barrier semaphores. Data moves between devices by JAX's collectives and lax.ppermute only.
A program may use at most 128 MiB of HBM per device.

```python
import jax
import jax.numpy as jnp
from jax import lax

D = 1024
HEADS = 32
HDIM = 64
STATE = 128
KERNEL = 4
STRETCH = 128
TOK_DEV = 1024
DI = 2048
TOKENS = 8192
N_DP = 8


def draw_scene_offsets(key, part):
    key = jax.random.fold_in(key, 7)
    first_key, second_key, third_key = jax.random.split(key, 3)
    per_group = TOK_DEV // STRETCH
    every = TOKENS // STRETCH
    opening = jax.random.randint(first_key, (), 1, per_group)
    middle = jax.random.randint(second_key, (), every - per_group + 1, every - 1)
    closing = jax.random.randint(third_key, (), middle + 1, every)
    return (jnp.stack([jnp.zeros((), jnp.int32), opening, middle, closing]) * STRETCH).astype(jnp.int32)


def shard_levels(key, dims, cuts, smallest, top_value):
    factor_of, own = 1.0, jax.random.fold_in(key, 6)
    for dim, shards_of in cuts:
        draws = jnp.exp(jax.random.uniform(jax.random.fold_in(own, dim), (shards_of,), jnp.float32, smallest / len(cuts), top_value / len(cuts)))
        factor_of = factor_of * jnp.repeat(draws, dims[dim] // shards_of).reshape([-1 if axis == dim else 1 for axis in range(len(dims))])
    return factor_of


def normal_values(stream_key, dims, spread, limit, cuts=(), held_as=jnp.bfloat16):
    gain = shard_levels(stream_key, dims, cuts, -0.22, 0.18) if cuts else 1.0
    drawn = jax.random.normal(stream_key, dims, jnp.float32) * spread * gain
    return jnp.minimum(jnp.maximum(drawn, -limit), limit).astype(held_as)


def setup_inputs(seed: int = 0) -> dict:
    key_of = jax.random.split(jax.random.key(seed), 17)
    tokens_in = normal_values(key_of[0], (TOKENS, D), 1.0, 6.0, ((0, 32),))
    grad_out = normal_values(key_of[1], (TOKENS, D), 1.0, 6.0, ((0, 32),))
    scene_offsets = draw_scene_offsets(jax.random.fold_in(key_of[16], 71), 0)
    input_gain = jnp.clip(1.0 + 0.15 * jax.random.normal(key_of[3], (D,), jnp.float32), 0.25, 1.75)
    weight_zx = normal_values(key_of[4], (2, D, DI), D ** -0.5, 0.1875, ((2, 4),))
    weight_bc = normal_values(key_of[5], (2, D, STATE), D ** -0.5, 0.1875)
    weight_step = normal_values(key_of[6], (D, HEADS), D ** -0.5, 0.1875, ((1, 4),))
    conv_inner = jnp.clip(jax.random.uniform(key_of[7], (KERNEL, DI), jnp.float32, -0.5, 0.5) * shard_levels(key_of[7], (KERNEL, DI), ((1, 4),), -0.4, 0.0), -0.5, 0.5)
    conv_inner_bias = jnp.clip(jax.random.uniform(key_of[8], (DI,), jnp.float32, -0.5, 0.5) * shard_levels(key_of[8], (DI,), ((0, 4),), -0.4, 0.0), -0.5, 0.5)
    conv_bc = jnp.clip(jax.random.uniform(key_of[9], (2, KERNEL, STATE), jnp.float32, -0.5, 0.5), -0.5, 0.5)
    conv_bc_bias = jnp.clip(jax.random.uniform(key_of[10], (2, STATE), jnp.float32, -0.5, 0.5), -0.5, 0.5)
    step_bias = jnp.clip(-6.0 + 4.0 * jax.random.uniform(key_of[11], (HEADS,), jnp.float32) ** shard_levels(key_of[11], (HEADS,), ((0, 4),), -0.2, 0.2), -6.0, -2.0)
    decay_log = jnp.clip(-4.0 + 6.75 * jax.random.uniform(key_of[12], (HEADS,), jnp.float32) ** shard_levels(key_of[12], (HEADS,), ((0, 4),), -0.2, 0.2), -4.0, 2.75)
    skip_weight = jnp.clip(0.5 + 1.5 * jax.random.uniform(key_of[13], (HEADS,), jnp.float32) ** shard_levels(key_of[13], (HEADS,), ((0, 4),), -0.2, 0.2), 0.5, 2.0)
    norm_gain = jnp.clip(1.0 + 0.15 * jax.random.normal(key_of[14], (DI,), jnp.float32), 0.25, 1.75)
    weight_out = normal_values(key_of[15], (DI, D), DI ** -0.5, 0.125, ((0, 4),))
    return {"tokens_in": tokens_in, "grad_out": grad_out, "scene_offsets": scene_offsets, "input_gain": input_gain, "weight_zx": weight_zx, "weight_bc": weight_bc, "weight_step": weight_step, "conv_inner": conv_inner, "conv_inner_bias": conv_inner_bias, "conv_bc": conv_bc, "conv_bc_bias": conv_bc_bias, "step_bias": step_bias, "decay_log": decay_log, "skip_weight": skip_weight, "norm_gain": norm_gain, "weight_out": weight_out}


EPS = 1e-05
HIGH = lax.Precision.HIGHEST

@jax.custom_vjp
def low(v):
    return lax.optimization_barrier(v.astype(jnp.bfloat16)).astype(jnp.float32)

@jax.custom_vjp
def low_back(v):
    return v

def low_keep(v):
    return (low(v), None)

def low_pass(kept, grad):
    return (grad,)

def back_keep(v):
    return (v, None)

def back_low(kept, grad):
    return (low(grad),)
low.defvjp(low_keep, low_pass)
low_back.defvjp(back_keep, back_low)

def rounded(values):
    return low_back(low(values))

def matmul(left, right):
    return jnp.dot(left, right, precision=HIGH)

def stretch_starts(first_pos, count, offsets):
    heads_pos = first_pos + jnp.arange(count, dtype=jnp.int32) * STRETCH
    return jnp.any(heads_pos[:, None] == offsets[None, :], axis=1)

def tap_masks(first_pos, length, offsets):
    position = first_pos + jnp.arange(length, dtype=jnp.int32)
    opening = jnp.any((position // STRETCH * STRETCH)[:, None] == offsets[None, :], axis=1)
    inside = position % STRETCH
    return [1.0 - (opening & (inside < delay)).astype(jnp.float32) for delay in range(KERNEL)]

def convolve(padded, kernel, bias, masks):
    length = padded.shape[0] - (KERNEL - 1)
    total = jnp.zeros((length, padded.shape[1]), jnp.float32) + bias[None, :]
    for delay in range(KERNEL):
        column = KERNEL - 1 - delay
        total = total + kernel[column][None, :] * padded[column:column + length] * masks[delay][:, None]
    return total

def ssd_block(inner, bvals, cvals, steps, logdec, starts, state):
    length, heads, width = inner.shape
    count = length // STRETCH
    inner_c = inner.reshape(count, STRETCH, heads, width)
    bvals_c = bvals.reshape(count, STRETCH, -1)
    cvals_c = cvals.reshape(count, STRETCH, -1)
    steps_c = steps.reshape(count, STRETCH, heads)
    cumul = jnp.cumsum(logdec.reshape(count, STRETCH, heads), axis=1)
    scores = jnp.einsum('cln,csn->cls', cvals_c, bvals_c, precision=HIGH)
    lower = (jnp.arange(STRETCH)[:, None] >= jnp.arange(STRETCH)[None, :])[None, :, :, None]
    gaps = cumul[:, :, None, :] - cumul[:, None, :, :]
    decay = jnp.exp(jnp.where(lower, gaps, -jnp.inf))
    mixing = scores[:, :, :, None] * decay * steps_c[:, None, :, :]
    within = jnp.einsum('clsh,cshp->clhp', mixing, inner_c, precision=HIGH)
    totals = cumul[:, -1, :]
    weights = jnp.exp(totals[:, None, :] - cumul) * steps_c
    local = jnp.einsum('clh,cln,clhp->chpn', weights, bvals_c, inner_c, precision=HIGH)
    ends = jnp.cumsum(totals, axis=0)
    begins = ends - totals
    marks = jnp.cumsum(starts.astype(jnp.int32))
    order = jnp.arange(count)
    linked = (order[:, None] > order[None, :]) & (marks[:, None] == marks[None, :])
    carried = jnp.exp(jnp.where(linked[:, :, None], begins[:, None, :] - ends[None, :, :], -jnp.inf))
    fresh = (marks == 0).astype(jnp.float32)
    entry = jnp.exp(begins) * fresh[:, None]
    opening = jnp.einsum('cdh,dhpn->chpn', carried, local, precision=HIGH) + entry[:, :, None, None] * state[None]
    across = jnp.exp(cumul)[..., None] * jnp.einsum('cln,chpn->clhp', cvals_c, opening, precision=HIGH)
    outputs = (within + across).reshape(length, heads, width)
    tail = (marks == marks[-1]).astype(jnp.float32)
    keep_end = jnp.exp(ends[-1]) * fresh[-1]
    final = keep_end[:, None, None] * state + jnp.einsum('dh,dhpn->hpn', jnp.exp(ends[-1][None, :] - ends) * tail[:, None], local, precision=HIGH)
    return (outputs, final)

def make_forward(offsets):

    def forward(tokens_f, input_gain, weight_zx, weight_bc, weight_step, conv_inner, conv_inner_bias, conv_bc, conv_bc_bias, step_bias, decay_log, skip_weight, norm_gain, weight_out):
        blocks = tokens_f.reshape(N_DP, TOK_DEV, D)
        kernel = jnp.concatenate([conv_inner, conv_bc[0], conv_bc[1]], axis=1)
        bias = jnp.concatenate([conv_inner_bias, conv_bc_bias[0], conv_bc_bias[1]])
        rates = -jnp.exp(decay_log)

        @jax.checkpoint
        def advance(carry, item):
            state, tail = carry
            block_rows, first_pos = item
            rstd = lax.rsqrt(lax.optimization_barrier(jnp.mean(block_rows * block_rows, axis=1, keepdims=True)) + EPS)
            normed = low(block_rows * rstd * input_gain)
            gate_raw = rounded(matmul(normed, weight_zx[0]))
            inner_raw = rounded(matmul(normed, weight_zx[1]))
            b_raw = rounded(matmul(normed, weight_bc[0]))
            c_raw = rounded(matmul(normed, weight_bc[1]))
            step_raw = rounded(matmul(normed, weight_step))
            conv_cat = jnp.concatenate([inner_raw, b_raw, c_raw], axis=1)
            padded = jnp.concatenate([tail, conv_cat], axis=0)
            masks = tap_masks(first_pos, TOK_DEV, offsets)
            act = jax.nn.silu(convolve(padded, kernel, bias, masks))
            inner = act[:, :DI].reshape(TOK_DEV, HEADS, HDIM)
            bvals = act[:, DI:DI + STATE]
            cvals = act[:, DI + STATE:]
            steps = jax.nn.softplus(step_raw + step_bias)
            logdec = steps * rates
            starts = stretch_starts(first_pos, TOK_DEV // STRETCH, offsets)
            ssd, state = ssd_block(inner, bvals, cvals, steps, logdec, starts, state)
            mixed = (ssd + skip_weight[None, :, None] * inner).reshape(TOK_DEV, DI)
            gated = mixed * jax.nn.silu(gate_raw)
            scale = lax.rsqrt(lax.optimization_barrier(jnp.mean(gated * gated, axis=1, keepdims=True)) + EPS)
            normout = rounded(gated * scale * norm_gain)
            result = block_rows + matmul(normout, weight_out)
            return ((state, padded[TOK_DEV:]), result)
        start_state = (jnp.zeros((HEADS, HDIM, STATE), jnp.float32), jnp.zeros((KERNEL - 1, DI + 2 * STATE), jnp.float32))
        firsts = jnp.arange(N_DP, dtype=jnp.int32) * TOK_DEV
        _, results = lax.scan(advance, start_state, (blocks, firsts))
        return results.reshape(TOKENS, D)
    return forward

def reference(tokens_in, grad_out, scene_offsets, input_gain, weight_zx, weight_bc, weight_step, conv_inner, conv_inner_bias, conv_bc, conv_bc_bias, step_bias, decay_log, skip_weight, norm_gain, weight_out):
    params = [value.astype(jnp.float32) for value in (input_gain, weight_zx, weight_bc, weight_step, conv_inner, conv_inner_bias, conv_bc, conv_bc_bias, step_bias, decay_log, skip_weight, norm_gain, weight_out)]
    forward = make_forward(scene_offsets)
    result, pull = jax.vjp(forward, tokens_in.astype(jnp.float32), *params)
    grads = pull(grad_out.astype(jnp.float32))
    return (result.astype(jnp.bfloat16), grads[0], grads[1], grads[2], grads[3], grads[4], grads[5], grads[6], grads[7], grads[8], grads[9], grads[10], grads[11], grads[12], grads[13])
```

```python
import functools

import jax
import jax.numpy as jnp
from jax import lax
from jax.experimental import pallas as pl
from jax.experimental.pallas import tpu as pltpu
from jax.sharding import PartitionSpec as P

KERNEL = 4
L = 128
HD = 64
DI = 2048
EPS = 1e-05
F32 = jnp.float32
BF = jnp.bfloat16
MIB = 1 << 20


def dot(a, b, ca=1, cb=0):
    return lax.dot_general(a, b, (((ca,), (cb,)), ((), ())), preferred_element_type=F32)


def split(a):
    hi = a.astype(BF)
    return hi, (a - hi.astype(F32)).astype(BF)


def dot_l(a, b, ca=1, cb=0):
    hi, lo = split(a)
    return dot(hi, b, ca, cb) + dot(lo, b, ca, cb)


def dot_r(a, b, ca=1, cb=0):
    hi, lo = split(b)
    return dot(a, hi, ca, cb) + dot(a, lo, ca, cb)


def sigmoid(v):
    return 0.5 * jnp.tanh(0.5 * v) + 0.5


def softplus(v):
    u = jnp.exp(-jnp.abs(v))
    small = u * (1.0 - u * (0.5 - u * (1.0 / 3.0 - u * 0.25)))
    return jnp.maximum(v, 0.0) + jnp.where(u < 0.02, small, jnp.log(1.0 + u))


def per_head(row, heads):
    return jnp.concatenate(
        [jnp.broadcast_to(row[:, h : h + 1], (HD, L)) for h in range(heads)], axis=0
    )


def eights(v):
    return jnp.sum(v.reshape(v.shape[0] // 8, 8, v.shape[1]), axis=0)


def across_lanes(v, width):
    return jnp.concatenate([v] * (width // L), axis=1) if width > L else v


def proj_body(k, aliased, *refs):
    toks = refs[:k]
    gain, wzx, wbc, wst = refs[k : k + 4]
    normed_o, gate_o, cat_o, step_o = refs[k + 4 + (4 if aliased else 0) :]
    width = wzx.shape[2]

    def one(tok):
        x = tok[...].astype(F32)
        rstd = lax.rsqrt(jnp.mean(x * x, axis=1, keepdims=True) + EPS)
        normed = (x * rstd * gain[...]).astype(BF)
        normed_o[...] = normed
        gate_o[...] = dot(normed, wzx[0]).astype(BF)
        cat_o[:, :width] = dot(normed, wzx[1]).astype(BF)
        cat_o[:, width : width + L] = dot(normed, wbc[0]).astype(BF)
        cat_o[:, width + L :] = dot(normed, wbc[1]).astype(BF)
        step_o[...] = dot(normed, wst[...]).astype(BF)

    for j in range(k):
        pl.when(pl.program_id(0) == j)(functools.partial(one, toks[j]))


def project(toks, gain, wzx, wbc, wst, total, first, before):
    k = len(toks)
    share, d = toks[0].shape
    width = wzx.shape[2]

    def whole(a):
        return pl.BlockSpec(a.shape, lambda i: (0,) * a.ndim)

    cols = (d, width, width + 2 * L, L)
    ins = [*toks, gain, wzx, wbc, wst]
    specs = [whole(a) for a in ins]
    alias = {}
    if before is not None:
        alias = {len(ins) + j: j for j in range(4)}
        ins += before
        specs += [pl.BlockSpec(memory_space=pl.ANY)] * 4
    return pl.pallas_call(
        functools.partial(proj_body, k, before is not None),
        grid=(k,),
        in_specs=specs,
        out_specs=[pl.BlockSpec((share, c), lambda i: (i + first, 0)) for c in cols],
        out_shape=[jax.ShapeDtypeStruct((total, c), BF) for c in cols],
        input_output_aliases=alias,
        compiler_params=pltpu.CompilerParams(vmem_limit_bytes=40 * MIB),
        cost_estimate=pl.CostEstimate(
            flops=2 * k * share * d * sum(cols[1:]),
            bytes_accessed=2 * k * share * (d + sum(cols)),
            transcendentals=0,
        ),
        name="project",
    )(*ins)


def cot_body(k, *refs):
    cots = refs[:k]
    wout, all_o, gn_o = refs[k:]

    def one(cot):
        v = cot[...]
        all_o[...] = v
        gn_o[...] = dot(v, wout[...], 1, 1).astype(BF)

    for j in range(k):
        pl.when(pl.program_id(0) == j)(functools.partial(one, cots[j]))


def cotangent(cots, wout):
    k = len(cots)
    share, d = cots[0].shape
    width = wout.shape[0]

    def whole(a):
        return pl.BlockSpec(a.shape, lambda i: (0,) * a.ndim)

    return pl.pallas_call(
        functools.partial(cot_body, k),
        grid=(k,),
        in_specs=[whole(a) for a in (*cots, wout)],
        out_specs=[
            pl.BlockSpec((share, d), lambda i: (i, 0)),
            pl.BlockSpec((share, width), lambda i: (i, 0)),
        ],
        out_shape=[
            jax.ShapeDtypeStruct((k * share, d), BF),
            jax.ShapeDtypeStruct((k * share, width), BF),
        ],
        compiler_params=pltpu.CompilerParams(vmem_limit_bytes=32 * MIB),
        cost_estimate=pl.CostEstimate(
            flops=2 * k * share * d * width,
            bytes_accessed=2 * k * share * (2 * d + width),
            transcendentals=0,
        ),
        name="cotangent",
    )(*cots, wout)


def act_parts(pre, width):
    out = []
    for x0 in range(0, width + 2 * L, L):
        v = pre[:, x0 : x0 + L]
        out.append(v * sigmoid(v))
    return out


def states_body(
    meta, cat, step, rim, kern, bias, sbias, rates, spread, tri,
    pre_o, sin_o, send_o, cum_o, pfx_o, thr_o, buf, state, prod,
):
    c = pl.program_id(0)
    width = spread.shape[1]
    heads = width // HD
    keep = jnp.where(meta[1 + c] == 0, 1.0, 0.0)

    @pl.when(c == 0)
    def _():
        buf[0:8, :] = rim[...].astype(F32)[8:16, :] * keep
        state[...] = jnp.zeros_like(state)
        prod[...] = jnp.ones_like(prod)

    @pl.when(c > 0)
    def _():
        buf[0:8, :] = buf[L : L + 8, :] * keep

    buf[8 : 8 + L, :] = cat[...].astype(F32)
    acts = []
    for x0 in range(0, width + 2 * L, L):
        cols = slice(x0, x0 + L)
        v = bias[:, cols] + kern[3:4, cols] * buf[8 : 8 + L, cols]
        for j in range(1, KERNEL):
            v = v + kern[3 - j : 4 - j, cols] * buf[8 - j : 8 - j + L, cols]
        pre_o[:, cols] = v
        acts.append(v * sigmoid(v))
    steps = softplus(step[...].astype(F32) + sbias[...])
    cum = dot_r(tri[...], steps * rates[...])
    cum_o[...] = cum
    total = cum[L - 1 : L, :]
    weights = dot_l(jnp.exp(total - cum) * steps, spread[...])
    inner = jnp.concatenate(acts[: width // L], axis=1)
    local = dot((inner * weights).astype(BF), acts[-2].astype(BF), 0, 0)
    entering = state[...] * keep
    sin_o[0] = entering.astype(BF)
    dec = jnp.exp(total)
    leaving = per_head(dec, heads) * entering + local
    state[...] = leaving
    send_o[...] = leaving
    here = prod[...] * keep
    pfx_o[0] = here
    prod[...] = here * dec
    thr_o[...] = here * dec


def within_body(meta, pre, step, cum_r, sin, sbias, spread, y_o):
    width = spread.shape[1]
    heads = width // HD
    acts = act_parts(pre, width)
    bb, cb = acts[-2].astype(BF), acts[-1].astype(BF)
    scores = dot(cb, bb, 1, 1)
    steps = softplus(step[...].astype(F32) + sbias[...])
    cum = cum_r[...]
    cum_t, steps_t = cum.T, steps.T
    lower = lax.broadcasted_iota(jnp.int32, (L, L), 0) >= lax.broadcasted_iota(
        jnp.int32, (L, L), 1
    )
    first = lax.broadcasted_iota(jnp.int32, (L, L), 1) < HD
    grown = dot_l(jnp.exp(cum), spread[...])
    far = grown * dot(cb, sin[0], 1, 1)
    for pair in range(heads // 2):
        cols = slice(pair * L, pair * L + L)
        x = acts[pair].astype(BF)
        got = []
        for h in (2 * pair, 2 * pair + 1):
            gap = jnp.where(lower, cum[:, h : h + 1] - cum_t[h : h + 1, :], -1e30)
            mix = scores * jnp.exp(gap) * steps_t[h : h + 1, :]
            got.append(dot(mix.astype(BF), x))
        y_o[:, cols] = jnp.where(first, got[0], got[1]) + far[:, cols]


def gate_body(
    meta, pre, cum, pfx, y, gate, gn, incoming, ngain, skip, spread, ones,
    mixed_o, sums_o,
):
    width = spread.shape[1]
    reach = dot_l(jnp.exp(cum[...]) * pfx[0][0:1, :], spread[...])
    cv = pre[:, width + L :]
    cb = (cv * sigmoid(cv)).astype(BF)
    far = reach * dot(cb, incoming[...], 1, 1)
    squares, crosses = [], []
    for x0 in range(0, width, L):
        cols = slice(x0, x0 + L)
        v = pre[:, cols]
        mixed = y[:, cols] + far[:, cols] + skip[:, cols] * (v * sigmoid(v))
        mixed_o[:, cols] = mixed
        g = gate[:, cols].astype(F32)
        gated = mixed * (g * sigmoid(g))
        squares.append(gated * gated)
        crosses.append(gn[:, cols].astype(F32) * ngain[:, cols] * gated)
    square = dot_r(ones[...], jnp.concatenate(squares, axis=1), 1, 1)
    cross = dot_r(ones[...], jnp.concatenate(crosses, axis=1), 1, 1)
    row = lax.broadcasted_iota(jnp.int32, (8, L), 0)
    sums_o[0] = jnp.where(row == 0, square, cross)


def back_gate_body(
    count, meta, pre, cum_r, mixed_r, gate, gn, sums, ngain, skip, spread,
    normout_o, gm_o, ggr_o, gs_o, toward_o, sfx_o, acc_o, gstate, prod, acc,
):
    i = pl.program_id(0)
    c = count - 1 - i
    width = spread.shape[1]
    heads = width // HD
    keep = jnp.where(meta[1 + c] == 0, 1.0, 0.0)

    @pl.when(i == 0)
    def _():
        gstate[...] = jnp.zeros_like(gstate)
        prod[...] = jnp.ones_like(prod)
        acc[...] = jnp.zeros_like(acc)

    both = sums[0]
    square = jnp.broadcast_to(both[0:1, :], (L, L)).T
    cross = jnp.broadcast_to(both[1:2, :], (L, L)).T
    scale = lax.rsqrt(square * (1.0 / DI) + EPS)
    cubed = scale * scale * scale * cross * (1.0 / DI)
    cum = cum_r[...]
    total = cum[L - 1 : L, :]
    grown = dot_l(jnp.exp(cum), spread[...])
    cv = pre[:, width + L :]
    cb = (cv * sigmoid(cv)).astype(BF)
    moved = []
    for x0 in range(0, width, L):
        cols = slice(x0, x0 + L)
        v = pre[:, cols]
        inner = v * sigmoid(v)
        g = gate[:, cols].astype(F32)
        s = sigmoid(g)
        silu = g * s
        mixed = mixed_r[:, cols]
        gated = mixed * silu
        ng = ngain[:, cols]
        gnv = gn[:, cols].astype(F32)
        scaled = gated * scale
        normout_o[:, cols] = (scaled * ng).astype(BF)
        gg = scale * (gnv * ng) - gated * cubed
        gm = gg * silu
        gm_o[:, cols] = gm.astype(BF)
        ggr_o[:, cols] = (gg * mixed * (s + silu * (1.0 - s))).astype(BF)
        acc[0:8, cols] += eights(gnv * scaled)
        acc[8:16, cols] += eights(gm * inner)
        moved.append((gm * grown[:, cols]).astype(BF))
    leaving = gstate[...]
    gs_o[0] = leaving.astype(BF)
    here = prod[...]
    sfx_o[0] = here
    dec = jnp.exp(total)
    entering = per_head(dec, heads) * leaving + dot(jnp.concatenate(moved, axis=1), cb, 0, 0)
    entering = entering * keep
    gstate[...] = entering
    toward_o[...] = entering
    prod[...] = here * dec * keep

    @pl.when(i == count - 1)
    def _():
        row = lax.broadcasted_iota(jnp.int32, (8, width), 0)
        acc_o[...] = jnp.where(
            row == 0,
            jnp.sum(acc[0:8, :], axis=0, keepdims=True),
            jnp.sum(acc[8:16, :], axis=0, keepdims=True),
        )


def head_product(a, b, spread, ones):
    rows = dot(ones[:, :L], (a * b).astype(BF), 1, 1)
    return dot_l(rows, spread, 1, 1)[0:1, :]


def back_within_body(
    meta, pre, step, cum_r, sin, pfx, gs, gm_r, incoming, sbias, skip, spread, tri, ones,
    ginner_o, gbc_o, glog_o, gst_o,
):
    width = spread.shape[1]
    heads = width // HD
    acts = act_parts(pre, width)
    bb, cb = acts[-2].astype(BF), acts[-1].astype(BF)
    scores = dot(cb, bb, 1, 1)
    steps = softplus(step[...].astype(F32) + sbias[...])
    cum = cum_r[...]
    total = cum[L - 1 : L, :]
    cum_t, steps_t = cum.T, steps.T
    row = lax.broadcasted_iota(jnp.int32, (L, L), 0)
    col = lax.broadcasted_iota(jnp.int32, (L, L), 1)
    lower = row >= col
    first = col < HD
    e = jnp.exp(cum)
    wd = jnp.exp(total - cum)
    grown = dot_l(e, spread[...])
    weights = dot_l(wd * steps, spread[...])
    gsb = gs[0]
    entering = sin[0].astype(F32) + per_head(pfx[0][0:1, :], heads) * incoming[...].astype(F32)
    eb = entering.astype(BF)
    u = dot(bb, gsb, 1, 1)
    v = dot(cb, eb, 1, 1)
    inner = jnp.concatenate(acts[: width // L], axis=1)
    gm = gm_r[...].astype(F32)
    seen = dot((inner * u).astype(BF), spread[...], 1, 1)
    passed = dot((gm * v).astype(BF), spread[...], 1, 1) * e
    gb = dot((inner * weights).astype(BF), gsb)
    gc = dot((gm * grown).astype(BF), eb)
    through = head_product(gsb.astype(F32), entering, spread[...], ones) * jnp.exp(total)
    dscores = jnp.zeros((L, L), F32)
    rowsums = jnp.zeros((L, L), F32)
    colsums = jnp.zeros((L, L), F32)
    for pair in range(heads // 2):
        cols = slice(pair * L, pair * L + L)
        xb = acts[pair].astype(BF)
        gmb = gm_r[:, cols]
        got = []
        for h in (2 * pair, 2 * pair + 1):
            mine = first if h % 2 == 0 else jnp.logical_not(first)
            gmh = jnp.where(mine, gm[:, cols], 0.0).astype(BF)
            dm = dot(gmh, xb, 1, 1)
            gap = jnp.where(lower, cum[:, h : h + 1] - cum_t[h : h + 1, :], -1e30)
            decay = jnp.exp(gap)
            st = steps_t[h : h + 1, :]
            t1 = dm * decay
            dscores = dscores + t1 * st
            gp = t1 * scores
            rowsums = jnp.where(col == h, jnp.sum(gp * st, axis=1, keepdims=True), rowsums)
            colsums = jnp.where(row == h, jnp.sum(gp, axis=0, keepdims=True), colsums)
            mix = (scores * decay * st).astype(BF)
            got.append(dot(mix, gmb, 0, 0))
        ginner_o[:, cols] = (
            jnp.where(first, got[0], got[1])
            + weights[:, cols] * u[:, cols]
            + skip[:, cols] * gm[:, cols]
        )
    db = dscores.astype(BF)
    gbc_o[:, :L] = gb + dot(db, cb, 0, 0)
    gbc_o[:, L:] = gc + dot(db, bb)
    direct = colsums.T
    seen = seen * wd
    gst_o[...] = direct + seen
    later = rowsums - direct * steps + passed
    tr = tri[...]
    glog_o[...] = (
        dot_r(tr, later, 0, 0) + dot_r(tr, steps * seen) - steps * seen + through
    )


def back_conv_body(
    count, meta, cat, rim, pre, step, cum_r, sin, pfx, sfx, ginner_r, gbc_r, glog_r, gst_r,
    incoming, outgoing, kern, sbias, rates, spread, tri, ones,
    gcat_o, gsr_o, head_o, acc_o, hacc_o, buf, acc, hacc,
):
    i = pl.program_id(0)
    c = count - 1 - i
    width = spread.shape[1]
    heads = width // HD
    keep_next = jnp.where(meta[2 + c] == 0, 1.0, 0.0)
    keep = jnp.where(meta[1 + c] == 0, 1.0, 0.0)

    @pl.when(i == 0)
    def _():
        buf[L : L + 8, :] = jnp.zeros_like(buf[L : L + 8, :])
        acc[...] = jnp.zeros_like(acc)
        hacc[...] = jnp.zeros_like(hacc)

    @pl.when(i > 0)
    def _():
        buf[L : L + 8, :] = buf[0:8, :] * keep_next

    step_in = step[...].astype(F32) + sbias[...]
    steps = softplus(step_in)
    cum = cum_r[...]
    total = cum[L - 1 : L, :]
    wd = jnp.exp(total - cum)
    weights = dot_l(wd * steps, spread[...])
    far = outgoing[...].astype(F32) * per_head(sfx[0][0:1, :], heads)
    fb = far.astype(BF)
    entering = sin[0].astype(F32) + per_head(pfx[0][0:1, :], heads) * incoming[...].astype(F32)
    through = head_product(far, entering, spread[...], ones) * jnp.exp(total)
    acts, slopes = [], []
    for x0 in range(0, width + 2 * L, L):
        v = pre[:, x0 : x0 + L]
        s = sigmoid(v)
        a = v * s
        acts.append(a)
        slopes.append(s + a * (1.0 - s))
    bb = acts[-2].astype(BF)
    u = dot(bb, fb, 1, 1)
    inner = jnp.concatenate(acts[: width // L], axis=1)
    seen = dot((inner * u).astype(BF), spread[...], 1, 1) * wd
    gb = dot((inner * weights).astype(BF), fb)
    glog = glog_r[...] + dot_r(tri[...], steps * seen) - steps * seen + through
    gsi = (gst_r[...] + seen + glog * rates[...]) * sigmoid(step_in)
    gsr_o[...] = gsi.astype(BF)
    hacc[0:8, :] += eights(glog * steps * rates[...])
    hacc[8:16, :] += eights(gsi)
    for k, x0 in enumerate(range(0, width + 2 * L, L)):
        cols = slice(x0, x0 + L)
        if x0 < width:
            g = ginner_r[:, cols] + weights[:, cols] * u[:, cols]
        elif x0 == width:
            g = gbc_r[:, :L] + gb
        else:
            g = gbc_r[:, L:]
        g = g * slopes[k]
        buf[0:L, cols] = g
        acc[32:40, cols] += eights(g)
        here = cat[:, cols].astype(F32)
        out = kern[3:4, cols] * g
        acc[24:32, cols] += eights(g * here)
        for j in range(1, KERNEL):
            moved = buf[j : j + L, cols]
            out = out + kern[3 - j : 4 - j, cols] * moved
            acc[24 - 8 * j : 32 - 8 * j, cols] += eights(moved * here)
        gcat_o[:, cols] = out.astype(BF)
    head_o[...] = buf[0:8, :]

    @pl.when(i == count - 1)
    def _():
        past = rim[...].astype(F32)[8:16, :] * keep
        now = buf[0:8, :]
        row = lax.broadcasted_iota(jnp.int32, now.shape, 0)
        result = jnp.zeros_like(now)
        for k in range(5):
            part = jnp.sum(acc[8 * k : 8 * k + 8, :], axis=0, keepdims=True)
            j = 3 - k
            if 1 <= j <= 3:
                for t in range(j):
                    part = part + now[t : t + 1, :] * past[8 + t - j : 9 + t - j, :]
            result = jnp.where(row == k, part, result)
        acc_o[...] = result
        hrow = lax.broadcasted_iota(jnp.int32, (8, L), 0)
        hacc_o[...] = jnp.where(
            hrow == 0,
            jnp.sum(hacc[0:8, :], axis=0, keepdims=True),
            jnp.sum(hacc[8:16, :], axis=0, keepdims=True),
        )


def dgrad_body(k, ggr, gcat, gsr, wzx, wbc, wst, *outs):
    width = wzx.shape[2]

    def one(out):
        r = dot(ggr[...], wzx[0], 1, 1)
        r = r + dot(gcat[:, :width], wzx[1], 1, 1)
        r = r + dot(gcat[:, width : width + L], wbc[0], 1, 1)
        r = r + dot(gcat[:, width + L :], wbc[1], 1, 1)
        r = r + dot(gsr[...], wst[...], 1, 1)
        out[...] = r.astype(BF)

    for j in range(k):
        pl.when(pl.program_id(0) == j)(functools.partial(one, outs[j]))


def outproj_body(k, normout, wout, *outs):
    def one(out):
        out[...] = dot(normout[...], wout[...]).astype(BF)

    for j in range(k):
        pl.when(pl.program_id(0) == j)(functools.partial(one, outs[j]))


def rows_times(body, first, k, share, d, rows, consts, name):
    def whole(a):
        return pl.BlockSpec(a.shape, lambda i: (0,) * a.ndim)

    return pl.pallas_call(
        functools.partial(body, k),
        grid=(k,),
        in_specs=[
            pl.BlockSpec((share, r.shape[1]), lambda i: (first + k - 1 - i, 0)) for r in rows
        ]
        + [whole(a) for a in consts],
        out_specs=[pl.BlockSpec((share, d), lambda i: (0, 0))] * k,
        out_shape=[jax.ShapeDtypeStruct((share, d), BF)] * k,
        compiler_params=pltpu.CompilerParams(vmem_limit_bytes=40 * MIB),
        cost_estimate=pl.CostEstimate(
            flops=2 * k * share * d * sum(r.shape[1] for r in rows),
            bytes_accessed=2 * k * share * (d + sum(r.shape[1] for r in rows)),
            transcendentals=0,
        ),
        name=name,
    )(*rows, *consts)[::-1]


def swap(x, axis, mask):
    count = lax.axis_size(axis)
    return lax.ppermute(x, axis, [(i, i ^ mask) for i in range(count)])


def frames(x, count):
    got = {0: x}
    mask = count // 2
    while mask:
        for d in sorted(got):
            got[d ^ mask] = swap(got[d], "tensor", mask)
        mask //= 2
    return [got[d] for d in range(count)]


def add(a, b):
    return (a.astype(F32) + b.astype(F32)).astype(BF)


def scatter_frames(make, count):
    half = count // 2
    held = []
    for first in (half, 0):
        part = dict(enumerate(make(first, half)))
        mask = 1
        while mask < half:
            for d in list(part):
                if d & mask:
                    part[d ^ mask] = add(part[d ^ mask], swap(part.pop(d), "tensor", mask))
            mask *= 2
        held.append(part[0])
    return held[1].astype(F32) + swap(held[0], "tensor", half).astype(F32)


def bit_of(axis, mask):
    return (lax.axis_index(axis) // mask) % 2


def halves(x, axis, masks):
    for mask in masks:
        half = x.shape[0] // 2
        bit = bit_of(axis, mask)
        sent = lax.dynamic_slice_in_dim(x, (1 - bit) * half, half, 0)
        kept = lax.dynamic_slice_in_dim(x, bit * half, half, 0)
        x = add(kept, swap(sent, axis, mask))
    return x


def doubles(x, axis, masks):
    for mask in masks[::-1]:
        got = swap(x, axis, mask)
        x = jnp.where(
            bit_of(axis, mask) == 0,
            jnp.concatenate([x, got], axis=0),
            jnp.concatenate([got, x], axis=0),
        )
    return x


def masks_of(axis):
    masks, mask = [], 1
    while mask < lax.axis_size(axis):
        masks.append(mask)
        mask *= 2
    return masks


def everyone(x, axis):
    for mask in masks_of(axis):
        x = x + swap(x, axis, mask)
    return x


def chain(decay, state, levels, reverse):
    heads = state.shape[0] // HD

    def scaled(a, s):
        return (a[:heads, None, None] * s.reshape(heads, HD, L)).reshape(s.shape)

    known = levels is not None
    levels = list(levels) if known else []
    before, through = jnp.zeros_like(state), jnp.ones_like(decay)
    masks = masks_of("dp")
    for step, mask in enumerate(masks):
        if known:
            theirs = swap(state.astype(BF), "dp", mask).astype(F32)
            a = levels[step]
        else:
            hi, lo = split(decay)
            tail = jnp.concatenate([hi[None], lo[None], jnp.zeros((14, L), BF)], axis=0)
            got = swap(jnp.concatenate([state.astype(BF), tail], axis=0), "dp", mask).astype(F32)
            theirs, a = got[: state.shape[0]], got[state.shape[0]] + got[state.shape[0] + 1]
            levels.append(a)
        ahead = bit_of("dp", mask) == (0 if reverse else 1)
        before = before + jnp.where(ahead, scaled(through, theirs), 0.0)
        through = jnp.where(ahead, through * a, through)
        state = jnp.where(ahead, scaled(decay, theirs) + state, scaled(a, state) + theirs)
        decay = decay * a
    return before, levels


def on_device(
    tokens_in,
    grad_out,
    scene_offsets,
    input_gain,
    weight_zx,
    weight_bc,
    weight_step,
    conv_inner,
    conv_inner_bias,
    conv_bc,
    conv_bc_bias,
    step_bias,
    decay_log,
    skip_weight,
    norm_gain,
    weight_out,
):
    share, d = tokens_in.shape
    group = lax.axis_size("tensor")
    tokens = share * group
    heads = step_bias.shape[0]
    width = norm_gain.shape[0]
    wide = width + 2 * L
    count = tokens // L
    per = share // L
    half = group // 2
    me = lax.axis_index("tensor")
    place = lax.axis_index("dp")

    heads_pos = place * tokens + jnp.arange(count + 1, dtype=jnp.int32) * L
    starts = jnp.any(heads_pos[:, None] == scene_offsets[None, :], axis=1).astype(jnp.int32)
    meta = jnp.concatenate([me[None].astype(jnp.int32), starts])

    def pad_heads(v):
        return jnp.pad(v, (0, L - heads))[None]

    wst = jnp.pad(weight_step, ((0, 0), (0, L - heads)))
    sbias = pad_heads(step_bias)
    rates = pad_heads(-jnp.exp(decay_log))
    kernel = jnp.concatenate([conv_inner, conv_bc[0], conv_bc[1]], axis=1)
    bias = jnp.concatenate([conv_inner_bias, conv_bc_bias[0], conv_bc_bias[1]])[None]
    skip = jnp.repeat(skip_weight, HD)[None]
    ngain = norm_gain[None]
    gain = input_gain[None]
    spread = (
        jnp.arange(L, dtype=jnp.int32)[:, None] == jnp.arange(width, dtype=jnp.int32)[None] // HD
    ).astype(BF)
    tri = (
        jnp.arange(L, dtype=jnp.int32)[:, None] >= jnp.arange(L, dtype=jnp.int32)[None]
    ).astype(BF)
    ones = jnp.ones((8, width), BF)

    def place_of(c, meta):
        if per == 1:
            return lax.bitwise_xor(c, meta[0])
        return lax.bitwise_xor(lax.div(c, per), meta[0]) * per + lax.rem(c, per)

    def stretched(body, name, ins, outs, scratch, reverse, vmem, flops):
        def order(i):
            return count - 1 - i if reverse else i

        def spec(kind, shape):
            if kind == "rows":
                return pl.BlockSpec((L, shape[1]), lambda i, m: (place_of(order(i), m), 0))
            if kind == "each":
                return pl.BlockSpec((1, *shape[1:]), lambda i, m: (order(i), 0, 0))
            return pl.BlockSpec(shape, lambda i, m: (0,) * len(shape))

        return pl.pallas_call(
            body,
            grid_spec=pltpu.PrefetchScalarGridSpec(
                num_scalar_prefetch=1,
                grid=(count,),
                in_specs=[spec(k, a.shape) for k, a in ins],
                out_specs=[spec(k, s) for k, s, _ in outs],
                scratch_shapes=scratch,
            ),
            out_shape=[jax.ShapeDtypeStruct(s, t) for _, s, t in outs],
            compiler_params=pltpu.CompilerParams(vmem_limit_bytes=vmem * MIB),
            cost_estimate=pl.CostEstimate(
                flops=flops,
                bytes_accessed=sum(a.size * a.dtype.itemsize for _, a in ins),
                transcendentals=tokens * wide,
            ),
            name=name,
        )(meta, *[a for _, a in ins])

    toks = frames(tokens_in, group)
    before = project(toks[:half], gain, weight_zx, weight_bc, wst, tokens, 0, None)
    normed, gate_raw, cat, step_raw = project(
        toks[half:], gain, weight_zx, weight_bc, wst, tokens, half, before
    )
    held, grad_held = lax.optimization_barrier((toks[half], grad_out))
    del held
    cots = frames(grad_held, group)

    last = (lax.bitwise_xor(me, group - 1) + 1) * share - 16
    rim = lax.ppermute(
        lax.dynamic_slice_in_dim(cat, last, 16, 0),
        "dp",
        [(i, i + 1) for i in range(lax.axis_size("dp") - 1)],
    )
    tall = (tokens, L)
    state_shape = (width, L)
    pre, sin, own_end, cum, pfx, through = stretched(
        states_body,
        "states",
        [("rows", cat), ("rows", step_raw), ("one", rim), ("one", kernel), ("one", bias),
         ("one", sbias), ("one", rates), ("one", spread), ("one", tri)],
        [("rows", (tokens, wide), F32), ("each", (count, *state_shape), BF),
         ("one", state_shape, F32), ("rows", tall, F32), ("each", (count, 8, L), F32),
         ("one", (8, L), F32)],
        [pltpu.VMEM((L + 8, wide), F32), pltpu.VMEM(state_shape, F32), pltpu.VMEM((8, L), F32)],
        False, 32, 2 * tokens * width * L * 3,
    )
    incoming, levels = chain(through[0], own_end, None, False)
    incoming = incoming.astype(BF)

    (y,) = stretched(
        within_body,
        "within",
        [("rows", pre), ("rows", step_raw), ("rows", cum), ("each", sin), ("one", sbias),
         ("one", spread)],
        [("rows", (tokens, width), F32)],
        [], False, 32, 2 * tokens * width * L * 6,
    )
    cot_all, gn = cotangent(cots, weight_out)
    mixed, sums = stretched(
        gate_body,
        "gated",
        [("rows", pre), ("rows", cum), ("each", pfx), ("rows", y), ("rows", gate_raw),
         ("rows", gn), ("one", incoming), ("one", ngain), ("one", skip), ("one", spread),
         ("one", ones)],
        [("rows", (tokens, width), F32), ("each", (count, 8, L), F32)],
        [], False, 32, 2 * tokens * width * L * 4,
    )
    sums = everyone(sums, "tensor")
    normout, gm, ggr, gs, toward, sfx, gate_acc = stretched(
        functools.partial(back_gate_body, count),
        "back_gated",
        [("rows", pre), ("rows", cum), ("rows", mixed), ("rows", gate_raw), ("rows", gn),
         ("each", sums), ("one", ngain), ("one", skip), ("one", spread)],
        [("rows", (tokens, width), BF), ("rows", (tokens, width), BF),
         ("rows", (tokens, width), BF), ("each", (count, *state_shape), BF),
         ("one", state_shape, F32), ("each", (count, 8, L), F32), ("one", (8, width), F32)],
        [pltpu.VMEM(state_shape, F32), pltpu.VMEM((8, L), F32), pltpu.VMEM((16, width), F32)],
        True, 32, 2 * tokens * width * L * 3,
    )
    outgoing, _ = chain(through[0], toward, levels, True)
    outgoing = outgoing.astype(BF)

    branch = scatter_frames(
        lambda first, k: rows_times(
            outproj_body, first, k, share, d, [normout], [weight_out], "outproj"
        ),
        group,
    )
    layer_out = (tokens_in.astype(F32) + branch).astype(BF)

    def wgrad(a, b):
        return jnp.einsum("ta,tb->ab", a, b, preferred_element_type=F32).astype(BF)

    masks = masks_of("dp")

    def summed(x):
        return doubles(halves(x, "dp", masks), "dp", masks)

    grad_weight_out = summed(wgrad(normout, cot_all)).astype(F32)
    grad_gate_w = summed(wgrad(normed, ggr))

    ginner, gbc, glog, gst = stretched(
        back_within_body,
        "back_within",
        [("rows", pre), ("rows", step_raw), ("rows", cum), ("each", sin), ("each", pfx),
         ("each", gs), ("rows", gm), ("one", incoming), ("one", sbias), ("one", skip),
         ("one", spread), ("one", tri), ("one", ones)],
        [("rows", (tokens, width), F32), ("rows", (tokens, 2 * L), F32), ("rows", tall, F32),
         ("rows", tall, F32)],
        [], True, 32, 2 * tokens * width * L * 12,
    )
    gcat, gsr, head, conv_acc, head_acc = stretched(
        functools.partial(back_conv_body, count),
        "back_conv",
        [("rows", cat), ("one", rim), ("rows", pre), ("rows", step_raw), ("rows", cum),
         ("each", sin), ("each", pfx), ("each", sfx), ("rows", ginner), ("rows", gbc),
         ("rows", glog), ("rows", gst), ("one", incoming), ("one", outgoing), ("one", kernel),
         ("one", sbias), ("one", rates), ("one", spread), ("one", tri), ("one", ones)],
        [("rows", (tokens, wide), BF), ("rows", tall, BF), ("one", (8, wide), F32),
         ("one", (8, wide), F32), ("one", (8, L), F32)],
        [pltpu.VMEM((L + 8, wide), F32), pltpu.VMEM((40, wide), F32), pltpu.VMEM((16, L), F32)],
        True, 32, 2 * tokens * width * L * 6,
    )

    ahead = lax.ppermute(
        head, "dp", [(i + 1, i) for i in range(lax.axis_size("dp") - 1)]
    ) * (1 - starts[count]).astype(F32)
    extra = jnp.zeros((16, wide), F32)
    for j in range(1, KERNEL):
        extra = extra.at[16 - j :].add(kernel[3 - j] * ahead[:j])
    rim_rows = lax.dynamic_slice_in_dim(gcat, last, 16, 0)
    gcat = lax.dynamic_update_slice_in_dim(gcat, add(rim_rows, extra), last, 0)

    grad_normed = scatter_frames(
        lambda first, k: rows_times(
            dgrad_body, first, k, share, d, [ggr, gcat, gsr],
            [weight_zx, weight_bc, wst], "dgrad",
        ),
        group,
    )
    grad_main = wgrad(normed, gcat)
    grad_inner_w = summed(grad_main[:, :width])
    tmasks = masks_of("tensor")
    grad_bc_w = halves(grad_main[:, width:], "tensor", tmasks)
    grad_bc_w = doubles(summed(grad_bc_w), "tensor", tmasks).astype(F32)
    grad_step_w = jnp.einsum("th,td->hd", gsr, normed, preferred_element_type=F32)[:heads]

    rows_in = tokens_in.astype(F32)
    rstd = lax.rsqrt(jnp.mean(rows_in * rows_in, axis=1, keepdims=True) + EPS)
    unit = rows_in * rstd
    grad_unit = grad_normed * input_gain
    grad_tokens = grad_out.astype(F32) + rstd * (
        grad_unit - unit * jnp.mean(grad_unit * unit, axis=1, keepdims=True)
    )
    grad_input_gain = jnp.sum(grad_normed * unit, axis=0)

    shared = jnp.concatenate([grad_input_gain, conv_acc[:5, width:].reshape(-1)])
    own = jnp.concatenate(
        [
            grad_step_w.reshape(-1),
            conv_acc[:5, :width].reshape(-1),
            gate_acc[:2].reshape(-1),
            head_acc[:2].reshape(-1),
        ]
    )
    shared = everyone(shared, "tensor")
    small = everyone(jnp.concatenate([shared, own]).reshape(-1, L), "dp").reshape(-1)

    def take(n):
        nonlocal small
        got, small = small[:n], small[n:]
        return got

    grad_input_gain = take(d)
    bc_acc = take(5 * 2 * L).reshape(5, 2, L)
    grad_weight_step = take(heads * d).reshape(heads, d).T
    inner_acc = take(5 * width).reshape(5, width)
    gates = take(2 * width).reshape(2, width)
    per_heads = take(2 * L).reshape(2, L)[:, :heads]
    return (
        layer_out,
        grad_tokens,
        grad_input_gain,
        jnp.stack([grad_gate_w, grad_inner_w]).astype(F32),
        jnp.stack([grad_bc_w[:, :L], grad_bc_w[:, L:]]),
        grad_weight_step,
        inner_acc[:4],
        inner_acc[4],
        jnp.moveaxis(bc_acc[:4], 0, 1),
        bc_acc[4],
        per_heads[1],
        per_heads[0],
        jnp.sum(gates[1].reshape(heads, HD), axis=1),
        gates[0],
        grad_weight_out,
    )


def solution(mesh):
    rows = P(("dp", "tensor"), None)
    cols = P(None, "tensor")
    one = P("tensor")
    in_specs = (
        rows, rows, P(), P(), P(None, None, "tensor"), P(), cols, cols, one, P(), P(),
        one, one, one, one, P("tensor", None),
    )
    out_specs = (
        rows, rows, P(), P(None, None, "tensor"), P(), cols, cols, one, P(), P(),
        one, one, one, one, P("tensor", None),
    )
    return jax.shard_map(
        on_device, mesh=mesh, in_specs=in_specs, out_specs=out_specs, check_vma=False
    )
```

```python
import functools

import jax
import jax.numpy as jnp
from jax import lax
from jax.experimental import pallas as pl
from jax.experimental.pallas import tpu as pltpu
from jax.sharding import PartitionSpec as P

KERNEL = 4
L = 128
HD = 64
DI = 2048
EPS = 1e-05
F32 = jnp.float32
BF = jnp.bfloat16
MIB = 1 << 20


def dot(a, b, ca=1, cb=0):
    return lax.dot_general(a, b, (((ca,), (cb,)), ((), ())), preferred_element_type=F32)


def split(a):
    hi = a.astype(BF)
    return hi, (a - hi.astype(F32)).astype(BF)


def dot_l(a, b, ca=1, cb=0):
    hi, lo = split(a)
    return dot(hi, b, ca, cb) + dot(lo, b, ca, cb)


def dot_r(a, b, ca=1, cb=0):
    hi, lo = split(b)
    return dot(a, hi, ca, cb) + dot(a, lo, ca, cb)


def sigmoid(v):
    return 0.5 * jnp.tanh(0.5 * v) + 0.5


def softplus(v):
    u = jnp.exp(-jnp.abs(v))
    small = u * (1.0 - u * (0.5 - u * (1.0 / 3.0 - u * 0.25)))
    return jnp.maximum(v, 0.0) + jnp.where(u < 0.02, small, jnp.log(1.0 + u))


def per_head(row, heads):
    return jnp.concatenate(
        [jnp.broadcast_to(row[:, h : h + 1], (HD, L)) for h in range(heads)], axis=0
    )


def eights(v):
    return jnp.sum(v.reshape(v.shape[0] // 8, 8, v.shape[1]), axis=0)


def across_lanes(v, width):
    return jnp.concatenate([v] * (width // L), axis=1) if width > L else v


def whole(a):
    return pl.BlockSpec(a.shape, lambda *_: (0,) * a.ndim)


def params(vmem):
    return pltpu.CompilerParams(vmem_limit_bytes=vmem * MIB)


def cost(flops, ins):
    return pl.CostEstimate(
        flops=flops, bytes_accessed=2 * sum(a.size * a.dtype.itemsize for a in ins), transcendentals=0
    )


def unit_rows(x, gain):
    x = x.astype(F32)
    rstd = lax.rsqrt(jnp.mean(x * x, axis=1, keepdims=True) + EPS)
    return (x * rstd * gain).astype(BF)


def proj_body(k, rims, deps, meta, *refs):
    toks, past = refs[:k], refs[k : k + rims]
    gain, wzx, wbc, wst = refs[k + rims : k + rims + 4]
    outs = refs[k + rims + 4 + (4 if rims else deps) :]
    normed_o, gate_o, cat_o, step_o = outs[:4]
    width = wzx.shape[2]

    def conv_inputs(normed, out):
        out[:, :width] = dot(normed, wzx[1]).astype(BF)
        out[:, width : width + L] = dot(normed, wbc[0]).astype(BF)
        out[:, width + L :] = dot(normed, wbc[1]).astype(BF)

    def one(j):
        normed = unit_rows(toks[j][...], gain[...])
        normed_o[...] = normed
        conv_inputs(normed, cat_o)
        gate_o[...] = dot(normed, wzx[0]).astype(BF)
        step_o[...] = dot(normed, wst[...]).astype(BF)
        if rims and j == 0:
            rim = past[0][...].astype(F32)
            for p in past[1:]:
                rim = rim + p[...].astype(F32)
            normed = unit_rows(rim, gain[...])
            outs[5][...] = normed
            conv_inputs(normed, outs[4])

    for j in range(k):
        pl.when(pl.program_id(0) == j)(functools.partial(one, j))


def project(meta, toks, past, gain, wzx, wbc, wst, total, first, before):
    k = len(toks)
    share, d = toks[0].shape
    width = wzx.shape[2]
    wide = width + 2 * L
    cols = (d, width, wide, L)
    ins = [*toks, *past, gain, wzx, wbc, wst]
    specs = [whole(a) for a in ins]
    alias = {}
    out_specs = [pl.BlockSpec((share, c), lambda i, m: (i + first, 0)) for c in cols]
    out_shape = [jax.ShapeDtypeStruct((total, c), BF) for c in cols]
    if past:
        alias = {1 + len(ins) + j: j for j in range(4)}
        for c in (wide, d):
            out_specs.append(pl.BlockSpec((16, c), lambda i, m: (0, 0)))
            out_shape.append(jax.ShapeDtypeStruct((16, c), BF))
    ins += before
    specs += [pl.BlockSpec(memory_space=pl.ANY)] * len(before)
    return pl.pallas_call(
        functools.partial(proj_body, k, len(past), len(before)),
        grid_spec=pltpu.PrefetchScalarGridSpec(
            num_scalar_prefetch=1, grid=(k,), in_specs=specs, out_specs=out_specs
        ),
        out_shape=out_shape,
        input_output_aliases=alias,
        compiler_params=params(16),
        cost_estimate=cost(2 * k * share * d * sum(cols[1:]), ins),
        name="project",
    )(meta, *ins)


def prep_body(taps, tbias, btaps, bbias, sbias, decay, skip, ngain, tok, vecs, hv, mats, rows):
    width = taps.shape[1]
    heads = width // HD
    rows[...] = tok[...]
    head = lax.broadcasted_iota(jnp.int32, (L, width), 0)
    lane = lax.broadcasted_iota(jnp.int32, (L, width), 1)
    spread = jnp.where(lax.div(lane, HD) == head, 1.0, 0.0).astype(BF)
    mats[:, :width] = spread
    r = lax.broadcasted_iota(jnp.int32, (L, L), 0)
    c = lax.broadcasted_iota(jnp.int32, (L, L), 1)
    mats[:, width:] = jnp.where(r >= c, 1.0, 0.0).astype(BF)
    hv[...] = jnp.zeros_like(hv)
    hv[0:1, :heads] = sbias[...]
    hv[1:2, :heads] = -jnp.exp(decay[...])
    hv[2:3, :heads] = skip[...]
    vecs[...] = jnp.zeros_like(vecs)
    vecs[0:4, :width] = taps[...]
    vecs[4:5, :width] = tbias[...]
    for k in range(2):
        cols = slice(width + k * L, width + k * L + L)
        vecs[0:4, cols] = btaps[k]
        vecs[4:5, cols] = bbias[k : k + 1, :]
    vecs[5:6, :width] = dot_l(hv[...], spread)[2:3, :]
    vecs[6:7, :width] = ngain[...]


def cot_body(k, *refs):
    cots = refs[:k]
    wout, all_o, gn_o = refs[k:]

    def one(cot):
        v = cot[...]
        all_o[...] = v
        gn_o[...] = dot(v, wout[...], 1, 1).astype(BF)

    for j in range(k):
        pl.when(pl.program_id(0) == j)(functools.partial(one, cots[j]))


def cotangent(cots, wout):
    k = len(cots)
    share, d = cots[0].shape
    width = wout.shape[0]
    return pl.pallas_call(
        functools.partial(cot_body, k),
        grid=(k,),
        in_specs=[whole(a) for a in (*cots, wout)],
        out_specs=[
            pl.BlockSpec((share, d), lambda i: (i, 0)),
            pl.BlockSpec((share, width), lambda i: (i, 0)),
        ],
        out_shape=[
            jax.ShapeDtypeStruct((k * share, d), BF),
            jax.ShapeDtypeStruct((k * share, width), BF),
        ],
        compiler_params=params(12),
        cost_estimate=cost(2 * k * share * d * width, [*cots, wout]),
        name="cotangent",
    )(*cots, wout)


def act_parts(pre, width):
    out = []
    for x0 in range(0, width + 2 * L, L):
        v = pre[:, x0 : x0 + L]
        out.append(v * sigmoid(v))
    return out


def pack(out, state, decay):
    rows = state.shape[0]
    hi, lo = split(jnp.broadcast_to(decay[0:1, :], (16, L)))
    row = lax.broadcasted_iota(jnp.int32, (16, L), 0)
    out[:rows, :] = state.astype(BF)
    tail = jnp.where(row == 0, hi.astype(F32), jnp.where(row == 1, lo.astype(F32), 0.0))
    out[rows:, :] = tail.astype(BF)


def unpack(load):
    v = load[...].astype(F32)
    rows = v.shape[0] - 16
    return v[:rows], v[rows : rows + 1] + v[rows + 1 : rows + 2]


def bit_at(meta, level):
    return jnp.bitwise_and(jnp.right_shift(meta[1], level), 1)


def is_ahead(meta, level, reverse):
    bit = bit_at(meta, level)
    return jnp.where(bit == (0 if reverse else 1), 1.0, 0.0)


def link_body(level, reverse, meta, state, decay, before, through, load,
              load_o, state_o, decay_o, before_o, through_o):
    theirs, a = unpack(load)
    heads = theirs.shape[0] // HD
    ahead = is_ahead(meta, level, reverse)
    mine = decay[0:1, :]
    t = through[0:1, :]
    before_o[...] = before[...] + per_head(t * ahead, heads) * theirs
    through_o[...] = jnp.broadcast_to(t * (ahead * a + (1.0 - ahead)), (8, L))
    joined = (
        per_head(mine * ahead + (1.0 - ahead), heads) * theirs
        + per_head(a * (1.0 - ahead) + ahead, heads) * state[...]
    )
    state_o[...] = joined
    decay_o[...] = jnp.broadcast_to(mine * a, (8, L))
    pack(load_o, joined, mine * a)


def final_link(meta, level, reverse, before, through, load):
    theirs, _ = unpack(load)
    t = through[0:1, :] * is_ahead(meta, level, reverse)
    return before[...] + per_head(t, theirs.shape[0] // HD) * theirs


def states_body(
    meta, cat, step, rim, vecs, hv, mats,
    pre_o, sin_o, end_o, load_o, cum_o, pfx_o, thr_o, buf, state, prod,
):
    c = pl.program_id(0)
    width = vecs.shape[1] - 2 * L
    heads = width // HD
    keep = jnp.where(meta[2 + c] == 0, 1.0, 0.0)

    @pl.when(c == 0)
    def _():
        buf[0:8, :] = rim[...].astype(F32)[8:16, :] * keep
        state[...] = jnp.zeros_like(state)
        prod[...] = jnp.ones_like(prod)

    @pl.when(c > 0)
    def _():
        buf[0:8, :] = buf[L : L + 8, :] * keep

    buf[8 : 8 + L, :] = cat[...].astype(F32)
    acts = []
    for x0 in range(0, width + 2 * L, L):
        cols = slice(x0, x0 + L)
        v = vecs[4:5, cols] + vecs[3:4, cols] * buf[8 : 8 + L, cols]
        for j in range(1, KERNEL):
            v = v + vecs[3 - j : 4 - j, cols] * buf[8 - j : 8 - j + L, cols]
        pre_o[:, cols] = v
        acts.append(v * sigmoid(v))
    steps = softplus(step[...].astype(F32) + hv[0:1, :])
    cum = dot_r(mats[:, width:], steps * hv[1:2, :])
    cum_o[...] = cum
    total = cum[L - 1 : L, :]
    weights = dot_l(jnp.exp(total - cum) * steps, mats[:, :width])
    inner = jnp.concatenate(acts[: width // L], axis=1)
    local = dot((inner * weights).astype(BF), acts[-2].astype(BF), 0, 0)
    entering = state[...] * keep
    sin_o[0] = entering.astype(BF)
    dec = jnp.exp(total)
    leaving = per_head(dec, heads) * entering + local
    state[...] = leaving
    here = prod[...] * keep
    pfx_o[0] = here
    prod[...] = here * dec

    @pl.when(c == pl.num_programs(0) - 1)
    def _():
        end_o[...] = leaving
        thr_o[...] = here * dec
        pack(load_o, leaving, here * dec)


def within_body(meta, pre, step, cum_r, sin, vecs, hv, mats, y_o):
    width = vecs.shape[1] - 2 * L
    heads = width // HD
    acts = act_parts(pre, width)
    bb, cb = acts[-2].astype(BF), acts[-1].astype(BF)
    scores = dot(cb, bb, 1, 1)
    steps = softplus(step[...].astype(F32) + hv[0:1, :])
    cum = cum_r[...]
    cum_t, steps_t = cum.T, steps.T
    lower = lax.broadcasted_iota(jnp.int32, (L, L), 0) >= lax.broadcasted_iota(
        jnp.int32, (L, L), 1
    )
    first = lax.broadcasted_iota(jnp.int32, (L, L), 1) < HD
    grown = dot_l(jnp.exp(cum), mats[:, :width])
    far = grown * dot(cb, sin[0], 1, 1)
    for pair in range(heads // 2):
        cols = slice(pair * L, pair * L + L)
        x = acts[pair].astype(BF)
        got = []
        for h in (2 * pair, 2 * pair + 1):
            gap = jnp.where(lower, cum[:, h : h + 1] - cum_t[h : h + 1, :], -1e30)
            mix = scores * jnp.exp(gap) * steps_t[h : h + 1, :]
            got.append(dot(mix.astype(BF), x))
        y_o[:, cols] = jnp.where(first, got[0], got[1]) + far[:, cols]


def gate_body(
    level, meta, pre, cum, pfx, y, gate, gn, before, through, load, vecs, mats,
    mixed_o, sums_o, incoming,
):
    width = vecs.shape[1] - 2 * L
    ones = jnp.ones((8, width), BF)

    @pl.when(pl.program_id(0) == 0)
    def _():
        incoming[...] = final_link(meta, level, False, before, through, load).astype(BF)

    reach = dot_l(jnp.exp(cum[...]) * pfx[0][0:1, :], mats[:, :width])
    cv = pre[:, width + L :]
    cb = (cv * sigmoid(cv)).astype(BF)
    far = reach * dot(cb, incoming[...], 1, 1)
    squares, crosses = [], []
    for x0 in range(0, width, L):
        cols = slice(x0, x0 + L)
        v = pre[:, cols]
        mixed = y[:, cols] + far[:, cols] + vecs[5:6, cols] * (v * sigmoid(v))
        mixed_o[:, cols] = mixed
        g = gate[:, cols].astype(F32)
        gated = mixed * (g * sigmoid(g))
        squares.append(gated * gated)
        crosses.append(gn[:, cols].astype(F32) * vecs[6:7, cols] * gated)
    square = dot_r(ones, jnp.concatenate(squares, axis=1), 1, 1)
    cross = dot_r(ones, jnp.concatenate(crosses, axis=1), 1, 1)
    row = lax.broadcasted_iota(jnp.int32, (8, L), 0)
    sums_o[0] = jnp.where(row == 0, square, cross)


def back_gate_body(
    count, meta, pre, cum_r, mixed_r, gate, gn, sums, sums2, thr, vecs, mats,
    normout_o, gm_o, ggr_o, gs_o, toward_o, load_o, sfx_o, acc_o, gstate, prod, acc,
):
    i = pl.program_id(0)
    c = count - 1 - i
    width = vecs.shape[1] - 2 * L
    heads = width // HD
    keep = jnp.where(meta[2 + c] == 0, 1.0, 0.0)

    @pl.when(i == 0)
    def _():
        gstate[...] = jnp.zeros_like(gstate)
        prod[...] = jnp.ones_like(prod)
        acc[...] = jnp.zeros_like(acc)

    both = sums[0] + sums2[0]
    square = jnp.broadcast_to(both[0:1, :], (L, L)).T
    cross = jnp.broadcast_to(both[1:2, :], (L, L)).T
    scale = lax.rsqrt(square * (1.0 / DI) + EPS)
    cubed = scale * scale * scale * cross * (1.0 / DI)
    cum = cum_r[...]
    total = cum[L - 1 : L, :]
    grown = dot_l(jnp.exp(cum), mats[:, :width])
    cv = pre[:, width + L :]
    cb = (cv * sigmoid(cv)).astype(BF)
    moved = []
    for x0 in range(0, width, L):
        cols = slice(x0, x0 + L)
        v = pre[:, cols]
        inner = v * sigmoid(v)
        g = gate[:, cols].astype(F32)
        s = sigmoid(g)
        silu = g * s
        mixed = mixed_r[:, cols]
        gated = mixed * silu
        ng = vecs[6:7, cols]
        gnv = gn[:, cols].astype(F32)
        scaled = gated * scale
        normout_o[:, cols] = (scaled * ng).astype(BF)
        gg = scale * (gnv * ng) - gated * cubed
        gm = gg * silu
        gm_o[:, cols] = gm.astype(BF)
        ggr_o[:, cols] = (gg * mixed * (s + silu * (1.0 - s))).astype(BF)
        acc[0:8, cols] += eights(gnv * scaled)
        acc[8:16, cols] += eights(gm * inner)
        moved.append((gm * grown[:, cols]).astype(BF))
    leaving = gstate[...]
    gs_o[0] = leaving.astype(BF)
    here = prod[...]
    sfx_o[0] = here
    dec = jnp.exp(total)
    entering = per_head(dec, heads) * leaving + dot(jnp.concatenate(moved, axis=1), cb, 0, 0)
    entering = entering * keep
    gstate[...] = entering
    prod[...] = here * dec * keep

    @pl.when(i == count - 1)
    def _():
        toward_o[...] = entering
        pack(load_o, entering, thr[...])
        row = lax.broadcasted_iota(jnp.int32, (8, width), 0)
        acc_o[...] = jnp.where(
            row == 0,
            jnp.sum(acc[0:8, :], axis=0, keepdims=True),
            jnp.sum(acc[8:16, :], axis=0, keepdims=True),
        )


def head_product(a, b, spread):
    rows = dot(jnp.ones((8, L), BF), (a * b).astype(BF), 1, 1)
    return dot_l(rows, spread, 1, 1)[0:1, :]


def back_within_body(
    meta, pre, step, cum_r, sin, pfx, gs, gm_r, incoming, vecs, hv, mats,
    ginner_o, gbc_o, glog_o, gst_o,
):
    width = vecs.shape[1] - 2 * L
    heads = width // HD
    acts = act_parts(pre, width)
    bb, cb = acts[-2].astype(BF), acts[-1].astype(BF)
    scores = dot(cb, bb, 1, 1)
    steps = softplus(step[...].astype(F32) + hv[0:1, :])
    cum = cum_r[...]
    total = cum[L - 1 : L, :]
    cum_t, steps_t = cum.T, steps.T
    row = lax.broadcasted_iota(jnp.int32, (L, L), 0)
    col = lax.broadcasted_iota(jnp.int32, (L, L), 1)
    lower = row >= col
    first = col < HD
    e = jnp.exp(cum)
    wd = jnp.exp(total - cum)
    grown = dot_l(e, mats[:, :width])
    weights = dot_l(wd * steps, mats[:, :width])
    gsb = gs[0]
    entering = sin[0].astype(F32) + per_head(pfx[0][0:1, :], heads) * incoming[...].astype(F32)
    eb = entering.astype(BF)
    u = dot(bb, gsb, 1, 1)
    v = dot(cb, eb, 1, 1)
    inner = jnp.concatenate(acts[: width // L], axis=1)
    gm = gm_r[...].astype(F32)
    seen = dot((inner * u).astype(BF), mats[:, :width], 1, 1)
    passed = dot((gm * v).astype(BF), mats[:, :width], 1, 1) * e
    gb = dot((inner * weights).astype(BF), gsb)
    gc = dot((gm * grown).astype(BF), eb)
    through = head_product(gsb.astype(F32), entering, mats[:, :width]) * jnp.exp(total)
    dscores = jnp.zeros((L, L), F32)
    rowsums = jnp.zeros((L, L), F32)
    colsums = jnp.zeros((L, L), F32)
    for pair in range(heads // 2):
        cols = slice(pair * L, pair * L + L)
        xb = acts[pair].astype(BF)
        gmb = gm_r[:, cols]
        got = []
        for h in (2 * pair, 2 * pair + 1):
            mine = first if h % 2 == 0 else jnp.logical_not(first)
            gmh = jnp.where(mine, gm[:, cols], 0.0).astype(BF)
            dm = dot(gmh, xb, 1, 1)
            gap = jnp.where(lower, cum[:, h : h + 1] - cum_t[h : h + 1, :], -1e30)
            decay = jnp.exp(gap)
            st = steps_t[h : h + 1, :]
            t1 = dm * decay
            dscores = dscores + t1 * st
            gp = t1 * scores
            rowsums = jnp.where(col == h, jnp.sum(gp * st, axis=1, keepdims=True), rowsums)
            colsums = jnp.where(row == h, jnp.sum(gp, axis=0, keepdims=True), colsums)
            mix = (scores * decay * st).astype(BF)
            got.append(dot(mix, gmb, 0, 0))
        ginner_o[:, cols] = (
            jnp.where(first, got[0], got[1])
            + weights[:, cols] * u[:, cols]
            + vecs[5:6, cols] * gm[:, cols]
        )
    db = dscores.astype(BF)
    gbc_o[:, :L] = gb + dot(db, cb, 0, 0)
    gbc_o[:, L:] = gc + dot(db, bb)
    direct = colsums.T
    seen = seen * wd
    gst_o[...] = direct + seen
    later = rowsums - direct * steps + passed
    tr = mats[:, width:]
    glog_o[...] = (
        dot_r(tr, later, 0, 0) + dot_r(tr, steps * seen) - steps * seen + through
    )


def crossing(vecs, later):
    row = lax.broadcasted_iota(jnp.int32, (16, later.shape[1]), 0)
    extra = jnp.zeros((16, later.shape[1]), F32)
    for j in range(1, KERNEL):
        for t in range(j):
            part = vecs[3 - j : 4 - j, :] * later[t : t + 1, :]
            extra = extra + jnp.where(row == 16 - j + t, part, 0.0)
    return extra


def back_conv_body(
    count, level, meta, cat, rim, pre, step, cum_r, sin, pfx, sfx, ginner_r, gbc_r, glog_r, gst_r,
    incoming, before, through, load, vecs, hv, mats,
    gcat_o, gsr_o, head_o, extra_o, acc_o, hacc_o, buf, acc, hacc, outgoing,
):
    i = pl.program_id(0)
    c = count - 1 - i
    width = vecs.shape[1] - 2 * L
    heads = width // HD
    keep_next = jnp.where(meta[3 + c] == 0, 1.0, 0.0)
    keep = jnp.where(meta[2 + c] == 0, 1.0, 0.0)

    @pl.when(i == 0)
    def _():
        buf[L : L + 8, :] = jnp.zeros_like(buf[L : L + 8, :])
        acc[...] = jnp.zeros_like(acc)
        hacc[...] = jnp.zeros_like(hacc)
        outgoing[...] = final_link(meta, level, True, before, through, load)

    @pl.when(i > 0)
    def _():
        buf[L : L + 8, :] = buf[0:8, :] * keep_next

    step_in = step[...].astype(F32) + hv[0:1, :]
    steps = softplus(step_in)
    cum = cum_r[...]
    total = cum[L - 1 : L, :]
    wd = jnp.exp(total - cum)
    weights = dot_l(wd * steps, mats[:, :width])
    far = outgoing[...] * per_head(sfx[0][0:1, :], heads)
    fb = far.astype(BF)
    entering = sin[0].astype(F32) + per_head(pfx[0][0:1, :], heads) * incoming[...].astype(F32)
    through = head_product(far, entering, mats[:, :width]) * jnp.exp(total)
    acts, slopes = [], []
    for x0 in range(0, width + 2 * L, L):
        v = pre[:, x0 : x0 + L]
        s = sigmoid(v)
        a = v * s
        acts.append(a)
        slopes.append(s + a * (1.0 - s))
    bb = acts[-2].astype(BF)
    u = dot(bb, fb, 1, 1)
    inner = jnp.concatenate(acts[: width // L], axis=1)
    seen = dot((inner * u).astype(BF), mats[:, :width], 1, 1) * wd
    gb = dot((inner * weights).astype(BF), fb)
    glog = glog_r[...] + dot_r(mats[:, width:], steps * seen) - steps * seen + through
    gsi = (gst_r[...] + seen + glog * hv[1:2, :]) * sigmoid(step_in)
    gsr_o[...] = gsi.astype(BF)
    hacc[0:8, :] += eights(glog * steps * hv[1:2, :])
    hacc[8:16, :] += eights(gsi)
    for k, x0 in enumerate(range(0, width + 2 * L, L)):
        cols = slice(x0, x0 + L)
        if x0 < width:
            g = ginner_r[:, cols] + weights[:, cols] * u[:, cols]
        elif x0 == width:
            g = gbc_r[:, :L] + gb
        else:
            g = gbc_r[:, L:]
        g = g * slopes[k]
        buf[0:L, cols] = g
        acc[32:40, cols] += eights(g)
        here = cat[:, cols].astype(F32)
        out = vecs[3:4, cols] * g
        acc[24:32, cols] += eights(g * here)
        for j in range(1, KERNEL):
            moved = buf[j : j + L, cols]
            out = out + vecs[3 - j : 4 - j, cols] * moved
            acc[24 - 8 * j : 32 - 8 * j, cols] += eights(moved * here)
        gcat_o[:, cols] = out.astype(BF)
    @pl.when(i == count - 1)
    def _():
        head_o[...] = buf[0:8, :]
        past = rim[...].astype(F32)[8:16, :] * keep
        now = buf[0:8, :]
        extra_o[...] = crossing(vecs, now * keep).astype(BF)
        row = lax.broadcasted_iota(jnp.int32, now.shape, 0)
        result = jnp.zeros_like(now)
        for k in range(5):
            part = jnp.sum(acc[8 * k : 8 * k + 8, :], axis=0, keepdims=True)
            j = 3 - k
            if 1 <= j <= 3:
                for t in range(j):
                    part = part + now[t : t + 1, :] * past[8 + t - j : 9 + t - j, :]
            result = jnp.where(row == k, part, result)
        acc_o[...] = result
        hrow = lax.broadcasted_iota(jnp.int32, (8, L), 0)
        hacc_o[...] = jnp.where(
            hrow == 0,
            jnp.sum(hacc[0:8, :], axis=0, keepdims=True),
            jnp.sum(hacc[8:16, :], axis=0, keepdims=True),
        )


def dgrad_body(k, ggr, gcat, gsr, wzx, wbc, wst, *outs):
    width = wzx.shape[2]

    def one(out):
        r = dot(ggr[...], wzx[0], 1, 1)
        r = r + dot(gcat[:, :width], wzx[1], 1, 1)
        r = r + dot(gcat[:, width : width + L], wbc[0], 1, 1)
        r = r + dot(gcat[:, width + L :], wbc[1], 1, 1)
        r = r + dot(gsr[...], wst[...], 1, 1)
        out[...] = r.astype(BF)

    for j in range(k):
        pl.when(pl.program_id(0) == j)(functools.partial(one, outs[j]))


def outproj_body(k, normout, wout, *outs):
    def one(out):
        out[...] = dot(normout[...], wout[...]).astype(BF)

    for j in range(k):
        pl.when(pl.program_id(0) == j)(functools.partial(one, outs[j]))


def rows_times(body, frames_n, share, d, rows, consts, name):
    k = frames_n
    outs = pl.pallas_call(
        functools.partial(body, k),
        grid=(k,),
        in_specs=[pl.BlockSpec((share, r.shape[1]), lambda i: (k - 1 - i, 0)) for r in rows]
        + [whole(a) for a in consts],
        out_specs=[pl.BlockSpec((share, d), lambda i: (0, 0))] * k,
        out_shape=[jax.ShapeDtypeStruct((share, d), BF)] * k,
        compiler_params=params(20),
        cost_estimate=cost(2 * k * share * d * sum(r.shape[1] for r in rows), [*rows, *consts]),
        name=name,
    )(*rows, *consts)
    return list(outs)[::-1]


def after_body(*refs):
    pass


def after(x, *deps):
    return pl.pallas_call(
        after_body,
        in_specs=[pl.BlockSpec(memory_space=pl.ANY)] * (1 + len(deps)),
        out_specs=pl.BlockSpec(memory_space=pl.ANY),
        out_shape=jax.ShapeDtypeStruct(x.shape, x.dtype),
        input_output_aliases={0: 0},
        compiler_params=params(1),
        name="after",
    )(x, *deps)


def hold_body(x, *refs):
    refs[-1][...] = x[...]


def hold(x, *deps):
    return pl.pallas_call(
        hold_body,
        grid=(1,),
        in_specs=[whole(x)] + [pl.BlockSpec(memory_space=pl.ANY)] * len(deps),
        out_specs=whole(x),
        out_shape=jax.ShapeDtypeStruct(x.shape, x.dtype),
        compiler_params=params(4),
        name="hold",
    )(x, *deps)


def add_body(a, b, o):
    o[...] = (a[...].astype(F32) + b[...].astype(F32)).astype(o.dtype)


def add(a, b):
    return pl.pallas_call(
        add_body,
        in_specs=[whole(a), whole(b)],
        out_specs=whole(a),
        out_shape=jax.ShapeDtypeStruct(a.shape, a.dtype),
        grid=(1,),
        compiler_params=params(8),
        cost_estimate=cost(a.size, [a, b]),
        name="add",
    )(a, b)


def swap(x, axis, mask):
    count = lax.axis_size(axis)
    return lax.ppermute(x, axis, [(i, i ^ mask) for i in range(count)])


def frames(x, count):
    got = {0: x}
    mask = count // 2
    while mask:
        for d in sorted(got):
            got[d ^ mask] = swap(got[d], "tensor", mask)
        mask //= 2
    return [got[d] for d in range(count)]


def scatter_frames(parts, count):
    half = count // 2
    held = []
    for first in (half, 0):
        part = dict(enumerate(parts[first : first + half]))
        mask = 1
        while mask < half:
            for d in list(part):
                if d & mask:
                    part[d ^ mask] = add(part[d ^ mask], swap(part.pop(d), "tensor", mask))
            mask *= 2
        held.append(part[0])
    return held[1], swap(held[0], "tensor", half)


def masks_of(axis):
    masks, mask = [], 1
    while mask < lax.axis_size(axis):
        masks.append(mask)
        mask *= 2
    return masks


def halve_body(slot, level, meta, kept, got, send_o, keep_o):
    bit = jnp.bitwise_and(jnp.right_shift(meta[slot], level), 1)
    half = send_o.shape[0]
    for o, b in ((send_o, 1 - bit), (keep_o, bit)):
        rows = pl.ds(pl.multiple_of(b * half, half), half)
        o[...] = (kept[rows, :].astype(F32) + got[rows, :].astype(F32)).astype(BF)


def metaed(body, meta, ins, outs, name, vmem=8):
    return pl.pallas_call(
        body,
        grid_spec=pltpu.PrefetchScalarGridSpec(
            num_scalar_prefetch=1,
            grid=(1,),
            in_specs=[whole(a) for a in ins],
            out_specs=[whole(o) for o in outs],
        ),
        out_shape=outs,
        compiler_params=params(vmem),
        cost_estimate=cost(0, ins),
        name=name,
    )(meta, *ins)


def halve(meta, slot, level, kept, got):
    shape = jax.ShapeDtypeStruct((kept.shape[0] // 2, kept.shape[1]), BF)
    return metaed(
        functools.partial(halve_body, slot, level), meta, [kept, got], [shape, shape], "halve"
    )


def join_body(slot, level, meta, own, got, o):
    bit = jnp.bitwise_and(jnp.right_shift(meta[slot], level), 1)
    half = own.shape[0]
    o[pl.ds(pl.multiple_of(bit * half, half), half), :] = own[...].astype(o.dtype)
    o[pl.ds(pl.multiple_of((1 - bit) * half, half), half), :] = got[...].astype(o.dtype)


def join(meta, slot, level, own, got, dtype=BF):
    shape = jax.ShapeDtypeStruct((own.shape[0] * 2, own.shape[1]), dtype)
    (out,) = metaed(functools.partial(join_body, slot, level), meta, [own, got], [shape], "join")
    return out


def reduced(meta, slot, axis, masks, send, keep, first=0):
    for level in range(first, len(masks)):
        got = swap(send, axis, masks[level])
        if level == len(masks) - 1:
            return add(keep, got)
        send, keep = halve(meta, slot, level + 1, keep, got)


def gathered(meta, slot, axis, masks, x, last):
    for level in range(len(masks) - 1, last, -1):
        x = join(meta, slot, level, x, swap(x, axis, masks[level]))
    return x, swap(x, axis, masks[last])


def wgrad_body(blocks, half, tails, meta, *refs):
    ins, (send_o, keep_o) = refs[:-2], refs[-2:]
    bit = bit_at(meta, 0)
    i = pl.program_id(0)
    g = jnp.where(i < half, (1 - bit) * half + i, bit * half + i - half)
    for p, tail in enumerate(tails):
        (a, b), ins = ins[:2], ins[2:]
        ta = tb = None
        if tail:
            (ta, tb), ins = ins[:2], ins[2:]
        inside = jnp.logical_and(g >= p * blocks, g < (p + 1) * blocks)

        def into(o, a=a, b=b, ta=ta, tb=tb):
            v = dot(a[...], b[...], 0, 0)
            if ta is not None:
                v = v + dot(ta[...], tb[...], 0, 0)
            o[...] = v.astype(BF)

        pl.when(jnp.logical_and(inside, i < half))(functools.partial(into, send_o))
        pl.when(jnp.logical_and(inside, i >= half))(functools.partial(into, keep_o))


def wgrads(meta, pairs, width, blocks, name):
    half = blocks * len(pairs) // 2
    tokens = pairs[0][0].shape[0]

    def cut(i, m):
        bit = jnp.bitwise_and(m[1], 1)
        g = jnp.where(i < half, (1 - bit) * half + i, bit * half + i - half)
        return (0, lax.rem(g, blocks))

    specs, ins = [], []
    for a, b, which, *more in pairs:
        for pair in [(a, b), tuple(more)]:
            for j, v in enumerate(pair):
                ins.append(v)
                specs.append(
                    pl.BlockSpec((v.shape[0], width), cut if j == which else lambda i, m: (0, 0))
                )
    shape = jax.ShapeDtypeStruct((half * width, width), BF)
    return pl.pallas_call(
        functools.partial(wgrad_body, blocks, half, [len(p) > 3 for p in pairs]),
        grid_spec=pltpu.PrefetchScalarGridSpec(
            num_scalar_prefetch=1,
            grid=(2 * half,),
            in_specs=specs,
            out_specs=[
                pl.BlockSpec((width, width), lambda i, m: (jnp.minimum(i, half - 1), 0)),
                pl.BlockSpec((width, width), lambda i, m: (jnp.maximum(i - half, 0), 0)),
            ],
        ),
        out_shape=[shape, shape],
        compiler_params=params(20),
        cost_estimate=cost(4 * half * tokens * width * width, ins),
        name=name,
    )(meta, *ins)


def bc_body(meta, normed, gcat, gsr, rim, extra, send_o, keep_o, step_o):
    bit = jnp.bitwise_and(meta[0], 1)
    half = send_o.shape[0]
    for o, b in ((send_o, 1 - bit), (keep_o, bit)):
        cols = pl.ds(pl.multiple_of(b * half, half), half)
        v = dot(normed[:, cols], gcat[...], 0, 0) + dot(rim[:, cols], extra[...], 0, 0)
        o[...] = v.astype(BF)
    step_o[...] = dot(gsr[...], normed[...], 0, 0)[:8]


def bc_wgrad(meta, normed, gcat, gsr, rim, extra, width):
    tokens, d = normed.shape
    shape = jax.ShapeDtypeStruct((d // 2, 2 * L), BF)
    step = jax.ShapeDtypeStruct((8, d), F32)
    return pl.pallas_call(
        bc_body,
        grid_spec=pltpu.PrefetchScalarGridSpec(
            num_scalar_prefetch=1,
            grid=(1,),
            in_specs=[
                whole(normed),
                pl.BlockSpec((tokens, 2 * L), lambda i, m: (0, width // (2 * L))),
                whole(gsr),
                whole(rim),
                pl.BlockSpec((16, 2 * L), lambda i, m: (0, width // (2 * L))),
            ],
            out_specs=[whole(shape), whole(shape), whole(step)],
        ),
        out_shape=[shape, shape, step],
        compiler_params=params(12),
        cost_estimate=cost(2 * tokens * d * 3 * L, [normed, gsr]),
        name="bc_wgrad",
    )(meta, normed, gcat, gsr, rim, extra)


def wg_out_body(level, blocks, meta, own, got, wout_o, zx_o):
    bit = jnp.bitwise_and(jnp.right_shift(meta[1], level), 1)
    width = wout_o.shape[0]
    for g, src in ((0, own), (1, got)):
        mine = bit if g == 0 else 1 - bit

        @pl.when(mine == 0)
        def _():
            for k in range(blocks):
                wout_o[:, k * width : (k + 1) * width] = src[
                    k * width : (k + 1) * width, :
                ].astype(F32)

        @pl.when(mine == 1)
        def _():
            zx_o[0] = src[...].astype(F32)


def wg_out(meta, own, got, d, width):
    return pl.pallas_call(
        functools.partial(wg_out_body, 0, d // width),
        grid_spec=pltpu.PrefetchScalarGridSpec(
            num_scalar_prefetch=1,
            grid=(1,),
            in_specs=[whole(own), whole(got)],
            out_specs=[
                pl.BlockSpec((width, d), lambda i, m: (0, 0)),
                pl.BlockSpec((1, d, width), lambda i, m: (0, 0, 0)),
            ],
        ),
        out_shape=[
            jax.ShapeDtypeStruct((width, d), F32),
            jax.ShapeDtypeStruct((2, d, width), F32),
        ],
        compiler_params=params(16),
        cost_estimate=cost(0, [own, got]),
        name="out_and_gate_weights",
    )(meta, own, got)


def inner_out_body(meta, own, got, old, zx_o):
    del old
    bit = bit_at(meta, 0)
    half = own.shape[0]
    zx_o[0, pl.ds(pl.multiple_of(bit * half, half), half), :] = own[...].astype(F32)
    zx_o[0, pl.ds(pl.multiple_of((1 - bit) * half, half), half), :] = got[...].astype(F32)


def inner_out(meta, own, got, old):
    _, d, width = old.shape
    return pl.pallas_call(
        inner_out_body,
        grid_spec=pltpu.PrefetchScalarGridSpec(
            num_scalar_prefetch=1,
            grid=(1,),
            in_specs=[whole(own), whole(got), pl.BlockSpec(memory_space=pl.ANY)],
            out_specs=pl.BlockSpec((1, d, width), lambda i, m: (1, 0, 0)),
        ),
        out_shape=jax.ShapeDtypeStruct(old.shape, F32),
        input_output_aliases={3: 0},
        compiler_params=params(12),
        cost_estimate=cost(0, [own, got]),
        name="inner_weights",
    )(meta, own, got, old)


def bc_out_body(meta, own, got, o):
    bit = jnp.bitwise_and(meta[0], 1)
    half = own.shape[0]
    for v, b in ((own, bit), (got, 1 - bit)):
        rows = pl.ds(pl.multiple_of(b * half, half), half)
        o[0, rows, :] = v[:, :L].astype(F32)
        o[1, rows, :] = v[:, L:].astype(F32)


def patch_body(meta, gcat, ahead, vecs, o):
    count = meta.shape[0] - 3
    keep = jnp.where(meta[2 + count] == 0, 1.0, 0.0)
    o[...] = (gcat[...].astype(F32) + crossing(vecs, ahead[...] * keep)).astype(BF)


def patched(meta, gcat, ahead, kernel, share, group):
    wide = gcat.shape[1]

    def spot(i, m):
        return ((jnp.bitwise_xor(m[0], group - 1) + 1) * (share // 16) - 1, 0)

    return pl.pallas_call(
        patch_body,
        grid_spec=pltpu.PrefetchScalarGridSpec(
            num_scalar_prefetch=1,
            grid=(1,),
            in_specs=[pl.BlockSpec((16, wide), spot), whole(ahead), whole(kernel)],
            out_specs=pl.BlockSpec((16, wide), spot),
        ),
        out_shape=jax.ShapeDtypeStruct(gcat.shape, BF),
        input_output_aliases={1: 0},
        compiler_params=params(4),
        cost_estimate=cost(0, [ahead]),
        name="patch",
    )(meta, gcat, ahead, kernel)


def layer_body(tok, a, b, o):
    o[...] = (tok[...].astype(F32) + (a[...].astype(F32) + b[...].astype(F32))).astype(BF)


def tokens_body(tok, cot, a, b, gain, conv, gt_o, acc_o):
    x = tok[...].astype(F32)
    rstd = lax.rsqrt(jnp.mean(x * x, axis=1, keepdims=True) + EPS)
    unit = x * rstd
    gnormed = a[...].astype(F32) + b[...].astype(F32)
    gunit = gnormed * gain[...]
    gt_o[...] = cot[...].astype(F32) + rstd * (
        gunit - unit * jnp.mean(gunit * unit, axis=1, keepdims=True)
    )
    d = x.shape[1]
    acc_o[:, d:] = conv[:, conv.shape[1] - 2 * L :]
    row = lax.broadcasted_iota(jnp.int32, (8, d), 0)
    acc_o[:, :d] = jnp.where(row == 0, jnp.sum(gnormed * unit, axis=0, keepdims=True), 0.0)


def plain(body, ins, outs, name, vmem=12):
    return pl.pallas_call(
        body,
        grid=(1,),
        in_specs=[whole(a) for a in ins],
        out_specs=[whole(o) for o in outs],
        out_shape=outs,
        compiler_params=params(vmem),
        cost_estimate=cost(0, ins),
        name=name,
    )(*ins)


def on_device(
    tokens_in,
    grad_out,
    scene_offsets,
    input_gain,
    weight_zx,
    weight_bc,
    weight_step,
    conv_inner,
    conv_inner_bias,
    conv_bc,
    conv_bc_bias,
    step_bias,
    decay_log,
    skip_weight,
    norm_gain,
    weight_out,
):
    share, d = tokens_in.shape
    group = lax.axis_size("tensor")
    tokens = share * group
    heads = step_bias.shape[0]
    width = norm_gain.shape[0]
    wide = width + 2 * L
    count = tokens // L
    per = share // L
    half = group // 2
    me = lax.axis_index("tensor")
    place = lax.axis_index("dp")

    heads_pos = place * tokens + jnp.arange(count + 1, dtype=jnp.int32) * L
    starts = jnp.any(heads_pos[:, None] == scene_offsets[None, :], axis=1).astype(jnp.int32)
    meta = jnp.concatenate([me[None].astype(jnp.int32), place[None].astype(jnp.int32), starts])
    masks, tmasks = masks_of("dp"), masks_of("tensor")
    levels = len(masks)

    wst = jnp.pad(weight_step, ((0, 0), (0, L - heads)))
    gain = input_gain[None]
    prep_ins = [conv_inner, conv_inner_bias[None], conv_bc, conv_bc_bias, step_bias[None],
                decay_log[None], skip_weight[None], norm_gain[None]]
    prep_outs = [
        jax.ShapeDtypeStruct((8, wide), F32),
        jax.ShapeDtypeStruct((8, L), F32),
        jax.ShapeDtypeStruct((L, width + L), BF),
        jax.ShapeDtypeStruct((16, d), BF),
    ]
    vecs, hv, mats, last_rows = pl.pallas_call(
        prep_body,
        grid=(1,),
        in_specs=[whole(a) for a in prep_ins]
        + [pl.BlockSpec((16, d), lambda i: (share // 16 - 1, 0))],
        out_specs=[whole(o) for o in prep_outs],
        out_shape=prep_outs,
        compiler_params=params(4),
        name="prep",
    )(*prep_ins, tokens_in)

    def place_of(c, meta):
        if per == 1:
            return lax.bitwise_xor(c, meta[0])
        return lax.bitwise_xor(lax.div(c, per), meta[0]) * per + lax.rem(c, per)

    def stretched(body, name, ins, outs, scratch, reverse, vmem, flops):
        def order(i):
            return count - 1 - i if reverse else i

        def spec(kind, shape):
            if kind == "rows":
                return pl.BlockSpec((L, shape[1]), lambda i, m: (place_of(order(i), m), 0))
            if kind == "each":
                return pl.BlockSpec((1, *shape[1:]), lambda i, m: (order(i), 0, 0))
            return pl.BlockSpec(shape, lambda i, m: (0,) * len(shape))

        return pl.pallas_call(
            body,
            grid_spec=pltpu.PrefetchScalarGridSpec(
                num_scalar_prefetch=1,
                grid=(count,),
                in_specs=[spec(k, a.shape) for k, a in ins],
                out_specs=[spec(k, s) for k, s, _ in outs],
                scratch_shapes=scratch,
            ),
            out_shape=[jax.ShapeDtypeStruct(s, t) for _, s, t in outs],
            compiler_params=params(vmem),
            cost_estimate=cost(flops, [a for _, a in ins]),
            name=name,
        )(meta, *[a for _, a in ins])

    held = {0: tokens_in}
    held[half] = swap(tokens_in, "tensor", half)
    mask = half // 2
    while mask:
        for f in [f for f in held if f < half]:
            held[f ^ mask] = swap(held[f], "tensor", mask)
        mask //= 2
    dps = lax.axis_size("dp")
    past = [
        lax.ppermute(
            last_rows,
            ("dp", "tensor"),
            [(i * group + group - 1, (i + 1) * group + t) for i in range(dps - 1)],
        )
        for t in range(group)
    ]
    before = project(
        meta, [held[f] for f in range(half)], [], gain, weight_zx, weight_bc, wst, tokens, 0,
        [vecs, hv, mats],
    )
    mask = half // 2
    while mask:
        for f in [f for f in held if f >= half]:
            held[f ^ mask] = swap(held[f], "tensor", mask)
        mask //= 2
    normed, gate_raw, cat, step_raw, rim, normed_rim = project(
        meta, [held[f] for f in range(half, group)], past, gain, weight_zx, weight_bc, wst,
        tokens, half, before,
    )

    tall = (tokens, L)
    state_shape = (width, L)
    load_shape = (width + 16, L)
    small = (8, L)
    pre, sin, state, load, cum, pfx, decay = stretched(
        states_body,
        "states",
        [("rows", cat), ("rows", step_raw), ("one", rim), ("one", vecs), ("one", hv),
         ("one", mats)],
        [("rows", (tokens, wide), F32), ("each", (count, *state_shape), BF),
         ("one", state_shape, F32), ("one", load_shape, BF), ("rows", tall, F32),
         ("each", (count, 8, L), F32), ("one", small, F32)],
        [pltpu.VMEM((L + 8, wide), F32), pltpu.VMEM(state_shape, F32), pltpu.VMEM(small, F32)],
        False, 10, 2 * tokens * width * L * 3,
    )

    cots = {0: grad_out}
    cots[half] = swap(hold(grad_out, step_raw), "tensor", half)
    late = hold(cots[half], load)
    mask = half // 2
    while mask:
        for f in sorted(cots):
            cots[f ^ mask] = swap(late if f == half else cots[f], "tensor", mask)
        mask //= 2
    cots = [cots[f] for f in range(group)]

    def link(level, reverse, held, load):
        got = swap(load, "dp", masks[level])
        if level == levels - 1:
            return held[2:], got
        shapes = [load_shape, state_shape, small, state_shape, small]
        out = metaed(
            functools.partial(link_body, level, reverse), meta, [*held, got],
            [jax.ShapeDtypeStruct(s, BF if j == 0 else F32) for j, s in enumerate(shapes)],
            "link",
        )
        return out[1:], out[0]

    thr = decay
    fresh = [jnp.zeros(state_shape, F32), jnp.ones(small, F32)]
    own = [state, decay, *fresh]
    for level in range(levels):
        if level == 1 or levels == 1:
            (y,) = stretched(
                within_body,
                "within",
                [("rows", pre), ("rows", step_raw), ("rows", cum), ("each", sin), ("one", vecs),
                 ("one", hv), ("one", mats)],
                [("rows", (tokens, width), F32)],
                [], False, 10, 2 * tokens * width * L * 6,
            )
            load = after(load, y)
        if level == 2:
            cot_all, gn = cotangent(cots, weight_out)
        own, load = link(level, False, own, load)
    if levels < 3:
        cot_all, gn = cotangent(cots, weight_out)
    befores, throughs = own
    mixed, sums, incoming = stretched(
        functools.partial(gate_body, levels - 1),
        "gated",
        [("rows", pre), ("rows", cum), ("each", pfx), ("rows", y), ("rows", gate_raw),
         ("rows", gn), ("one", befores), ("one", throughs), ("one", load), ("one", vecs),
         ("one", mats)],
        [("rows", (tokens, width), F32), ("each", (count, 8, L), F32), ("one", state_shape, BF)],
        [], False, 10, 2 * tokens * width * L * 4,
    )
    for mask in tmasks[::-1][:-1]:
        sums = add(sums, swap(sums, "tensor", mask))
    sums2 = swap(sums, "tensor", 1)
    normout, gm, ggr, gs, toward, load, sfx, gate_acc = stretched(
        functools.partial(back_gate_body, count),
        "back_gated",
        [("rows", pre), ("rows", cum), ("rows", mixed), ("rows", gate_raw), ("rows", gn),
         ("each", sums), ("each", sums2), ("one", thr), ("one", vecs), ("one", mats)],
        [("rows", (tokens, width), BF), ("rows", (tokens, width), BF),
         ("rows", (tokens, width), BF), ("each", (count, *state_shape), BF),
         ("one", state_shape, F32), ("one", load_shape, BF), ("each", (count, 8, L), F32),
         ("one", (8, width), F32)],
        [pltpu.VMEM(state_shape, F32), pltpu.VMEM(small, F32), pltpu.VMEM((16, width), F32)],
        True, 10, 2 * tokens * width * L * 3,
    )

    blocks = d // width
    own, load = link(0, True, [toward, thr, *fresh], load)
    wg_send, wg_keep = wgrads(
        meta, [(normout, cot_all, 1), (normed, ggr, 0)], width, blocks, "out_gate_wgrad"
    )
    load = after(load, wg_keep)
    if levels > 1:
        own, load = link(1, True, own, load)
    wg_got = swap(after(wg_send, load), "dp", 1)
    ginner, gbc, glog, gst = stretched(
        back_within_body,
        "back_within",
        [("rows", pre), ("rows", step_raw), ("rows", cum), ("each", sin), ("each", pfx),
         ("each", gs), ("rows", gm), ("one", incoming), ("one", vecs), ("one", hv),
         ("one", mats)],
        [("rows", (tokens, width), F32), ("rows", (tokens, 2 * L), F32), ("rows", tall, F32),
         ("rows", tall, F32)],
        [], True, 12, 2 * tokens * width * L * 12,
    )
    for level in range(2, levels):
        own, load = link(level, True, own, load)
    befores, throughs = own
    gcat, gsr, head, extra, conv_acc, head_acc = stretched(
        functools.partial(back_conv_body, count, levels - 1),
        "back_conv",
        [("rows", cat), ("one", rim), ("rows", pre), ("rows", step_raw), ("rows", cum),
         ("each", sin), ("each", pfx), ("each", sfx), ("rows", ginner), ("rows", gbc),
         ("rows", glog), ("rows", gst), ("one", incoming), ("one", befores), ("one", throughs),
         ("one", load), ("one", vecs), ("one", hv), ("one", mats)],
        [("rows", (tokens, wide), BF), ("rows", tall, BF), ("one", (8, wide), F32),
         ("one", (16, wide), BF), ("one", (8, wide), F32), ("one", small, F32)],
        [pltpu.VMEM((L + 8, wide), F32), pltpu.VMEM((40, wide), F32), pltpu.VMEM((16, L), F32),
         pltpu.VMEM(state_shape, F32)],
        True, 12, 2 * tokens * width * L * 6,
    )

    in_send, in_keep = wgrads(
        meta, [(normed, gcat, 0, normed_rim, extra)], width, blocks, "inner_wgrad"
    )
    ahead = lax.ppermute(after(head, in_keep), "dp", [(i + 1, i) for i in range(dps - 1)])
    wg_send, wg_keep = halve(meta, 1, 1, after(wg_keep, in_keep), wg_got)
    bc_send, bc_keep, step_acc = bc_wgrad(meta, normed, gcat, gsr, normed_rim, extra, width)
    branch = rows_times(
        outproj_body, group, share, d, [after(normout, wg_keep)], [weight_out], "outproj"
    )
    gcat = patched(meta, gcat, ahead, vecs, share, group)
    grads = rows_times(
        dgrad_body, group, share, d, [ggr, gcat, gsr], [weight_zx, weight_bc, wst], "dgrad"
    )

    inner_sum = reduced(meta, 1, "dp", masks, in_send, in_keep)
    grad_a, grad_b = scatter_frames(grads, group)
    wg_sum = reduced(meta, 1, "dp", masks, wg_send, wg_keep, 1)
    out_a, out_b = scatter_frames(branch, group)
    bc_sum = reduced(meta, 0, "tensor", tmasks, bc_send, bc_keep)
    for mask in masks:
        bc_sum = add(bc_sum, swap(bc_sum, "dp", mask))

    own_shape = jax.ShapeDtypeStruct((share, d), F32)
    grad_tokens, shared = plain(
        tokens_body,
        [tokens_in, grad_out, grad_a, grad_b, gain, conv_acc],
        [own_shape, jax.ShapeDtypeStruct((8, d + 2 * L), F32)],
        "tokens",
    )
    (layer_out,) = plain(
        layer_body, [tokens_in, out_a, out_b], [jax.ShapeDtypeStruct((share, d), BF)], "layer"
    )
    for mask in tmasks:
        shared = add(shared, swap(shared, "tensor", mask))
    sums_all = jnp.concatenate(
        [shared, step_acc, conv_acc[:, :width], gate_acc, head_acc], axis=1
    )
    for mask in masks:
        sums_all = add(sums_all, swap(sums_all, "dp", mask))

    grad_weight_out, grad_zx = wg_out(
        meta, *gathered(meta, 1, "dp", masks, wg_sum, 0), d, width
    )
    grad_zx = inner_out(meta, *gathered(meta, 1, "dp", masks, inner_sum, 0), grad_zx)
    (grad_bc,) = metaed(
        bc_out_body, meta, list(gathered(meta, 0, "tensor", tmasks, bc_sum, 0)),
        [jax.ShapeDtypeStruct((2, d, L), F32)], "bc_weights",
    )

    at = 0

    def take(n):
        nonlocal at
        at += n
        return sums_all[:, at - n : at]

    grad_input_gain = take(d)[0]
    bc_acc = take(2 * L).reshape(8, 2, L)
    grad_weight_step = take(d)[:heads].T
    inner_acc = take(width)
    gates = take(width)
    per_heads = take(L)[:, :heads]
    return (
        layer_out,
        grad_tokens,
        grad_input_gain,
        grad_zx,
        grad_bc,
        grad_weight_step,
        inner_acc[:4],
        inner_acc[4],
        jnp.moveaxis(bc_acc[:4], 0, 1),
        bc_acc[4],
        per_heads[1],
        per_heads[0],
        jnp.sum(gates[1].reshape(heads, HD), axis=1),
        gates[0],
        grad_weight_out,
    )


def solution(mesh):
    rows = P(("dp", "tensor"), None)
    cols = P(None, "tensor")
    one = P("tensor")
    in_specs = (
        rows, rows, P(), P(), P(None, None, "tensor"), P(), cols, cols, one, P(), P(),
        one, one, one, one, P("tensor", None),
    )
    out_specs = (
        rows, rows, P(), P(None, None, "tensor"), P(), cols, cols, one, P(), P(),
        one, one, one, one, P("tensor", None),
    )
    return jax.shard_map(
        on_device, mesh=mesh, in_specs=in_specs, out_specs=out_specs, check_vma=False
    )
```

```python
import functools

import jax
import jax.numpy as jnp
from jax import lax
from jax.experimental import pallas as pl
from jax.experimental.pallas import tpu as pltpu
from jax.sharding import PartitionSpec as P

KERNEL = 4
L = 128
HD = 64
DI = 2048
EPS = 1e-05
F32 = jnp.float32
BF = jnp.bfloat16
MIB = 1 << 20


def dot(a, b, ca=1, cb=0):
    return lax.dot_general(a, b, (((ca,), (cb,)), ((), ())), preferred_element_type=F32)


def split(a):
    hi = a.astype(BF)
    return hi, (a - hi.astype(F32)).astype(BF)


def dot_l(a, b, ca=1, cb=0):
    hi, lo = split(a)
    return dot(hi, b, ca, cb) + dot(lo, b, ca, cb)


def dot_r(a, b, ca=1, cb=0):
    hi, lo = split(b)
    return dot(a, hi, ca, cb) + dot(a, lo, ca, cb)


def sigmoid(v):
    return 0.5 * jnp.tanh(0.5 * v) + 0.5


def softplus(v):
    u = jnp.exp(-jnp.abs(v))
    small = u * (1.0 - u * (0.5 - u * (1.0 / 3.0 - u * 0.25)))
    return jnp.maximum(v, 0.0) + jnp.where(u < 0.02, small, jnp.log(1.0 + u))


def per_head(row, heads):
    return jnp.concatenate(
        [jnp.broadcast_to(row[:, h : h + 1], (HD, L)) for h in range(heads)], axis=0
    )


def eights(v):
    return jnp.sum(v.reshape(v.shape[0] // 8, 8, v.shape[1]), axis=0)


def across_lanes(v, width):
    return jnp.concatenate([v] * (width // L), axis=1) if width > L else v


def whole(a):
    return pl.BlockSpec(a.shape, lambda *_: (0,) * a.ndim)


LAST = []

LONG, SHORT = 10**10, 0


def launch(body, ins, in_specs, outs, out_specs, name, grid=(1,), meta=None, scratch=(),
           aliases=None, vmem=8, flops=0, token=True):
    ins, in_specs = list(ins), list(in_specs)
    lead = 0 if meta is None else 1
    at = lead + len(ins)
    given = LAST[-1] if LAST and not any(LAST[-1] is a for a in ins) else None
    if given is not None:
        ins.append(given)
        in_specs.append(pl.BlockSpec(memory_space=pl.ANY))

    def run(*refs):
        body(*(refs if given is None else refs[:at] + refs[at + 1 :]))

    results = pl.pallas_call(
        run,
        grid_spec=pltpu.PrefetchScalarGridSpec(
            num_scalar_prefetch=lead,
            grid=grid,
            in_specs=in_specs,
            out_specs=list(out_specs),
            scratch_shapes=list(scratch),
        ),
        out_shape=list(outs),
        input_output_aliases={lead + k: v for k, v in (aliases or {}).items()},
        compiler_params=pltpu.CompilerParams(vmem_limit_bytes=vmem * MIB),
        cost_estimate=pl.CostEstimate(
            flops=SHORT if name in ("prep", "last_rows", "project") else LONG,
            bytes_accessed=0,
            transcendentals=0,
        ),
        name=name,
    )(*([] if meta is None else [meta]), *ins)
    if token:
        LAST[:] = [min(results, key=lambda a: a.size)]
    return results


def shaped(shape, dtype=F32):
    return jax.ShapeDtypeStruct(shape, dtype)


def simple(body, ins, outs, name, meta=None, vmem=8, deps=()):
    n = len(ins)

    def run(*refs):
        lead = 0 if meta is None else 1
        body(*refs[: lead + n], *refs[lead + n + len(deps) :])

    return launch(
        run, [*ins, *deps],
        [whole(a) for a in ins] + [pl.BlockSpec(memory_space=pl.ANY)] * len(deps),
        outs, [whole(o) for o in outs], name, meta=meta, vmem=vmem,
    )


def unit_rows(x, gain):
    x = x.astype(F32)
    rstd = lax.rsqrt(jnp.mean(x * x, axis=1, keepdims=True) + EPS)
    return (x * rstd * gain).astype(BF)


def proj_body(k, rims, deps, meta, *refs):
    toks, past = refs[:k], refs[k : k + rims]
    gain, wzx, wbc, wst = refs[k + rims : k + rims + 4]
    outs = refs[k + rims + 4 + deps :]
    normed_o, gate_o, cat_o, step_o = outs[:4]
    width = wzx.shape[2]

    def conv_inputs(normed, out):
        out[:, :width] = dot(normed, wzx[1]).astype(BF)
        out[:, width : width + L] = dot(normed, wbc[0]).astype(BF)
        out[:, width + L :] = dot(normed, wbc[1]).astype(BF)

    def one(j):
        normed = unit_rows(toks[j][...], gain[...])
        normed_o[...] = normed
        conv_inputs(normed, cat_o)
        gate_o[...] = dot(normed, wzx[0]).astype(BF)
        step_o[...] = dot(normed, wst[...], 1, 1).astype(BF)
        if rims and j == 0:
            rim = past[0][...].astype(F32)
            for p in past[1:]:
                rim = rim + p[...].astype(F32)
            normed = unit_rows(rim, gain[...])
            outs[5][...] = normed
            conv_inputs(normed, outs[4])

    for j in range(k):
        pl.when(pl.program_id(0) == j)(functools.partial(one, j))


def project(meta, toks, past, gain, wzx, wbc, wst, total, first, before):
    k = len(toks)
    share, d = toks[0].shape
    width = wzx.shape[2]
    wide = width + 2 * L
    cols = (d, width, wide, L)
    ins = [*toks, *past, gain, wzx, wbc, wst]
    specs = [whole(a) for a in ins]
    out_specs = [pl.BlockSpec((share, c), lambda i, m: (i + first, 0)) for c in cols]
    out_shape = [shaped((total, c), BF) for c in cols]
    if past:
        for c in (wide, d):
            out_specs.append(pl.BlockSpec((16, c), lambda i, m: (0, 0)))
            out_shape.append(shaped((16, c), BF))
    aliases = {len(ins) + j: j for j in range(4)} if before else {}
    return launch(
        functools.partial(proj_body, k, len(past), len(before)),
        ins + before,
        specs + [pl.BlockSpec(memory_space=pl.ANY)] * len(before),
        out_shape,
        out_specs,
        "project",
        grid=(k,),
        meta=meta,
        aliases=aliases,
        vmem=16,
        flops=2 * k * share * d * sum(cols[1:]),
        token=False,
    )


def prep_body(taps, tbias, btaps, bbias, sbias, decay, skip, ngain, wst, vecs, hv, mats, wst_o):
    width = taps.shape[1]
    heads = width // HD
    wst_o[...] = jnp.zeros_like(wst_o)
    wst_o[0:heads, :] = wst[...]
    head = lax.broadcasted_iota(jnp.int32, (L, width), 0)
    lane = lax.broadcasted_iota(jnp.int32, (L, width), 1)
    spread = jnp.where(lax.div(lane, HD) == head, 1.0, 0.0).astype(BF)
    mats[:, :width] = spread
    r = lax.broadcasted_iota(jnp.int32, (L, L), 0)
    c = lax.broadcasted_iota(jnp.int32, (L, L), 1)
    mats[:, width:] = jnp.where(r >= c, 1.0, 0.0).astype(BF)
    hv[...] = jnp.zeros_like(hv)
    hv[0:1, :heads] = sbias[...]
    hv[1:2, :heads] = -jnp.exp(decay[...])
    hv[2:3, :heads] = skip[...]
    vecs[...] = jnp.zeros_like(vecs)
    vecs[0:4, :width] = taps[...]
    vecs[4:5, :width] = tbias[...]
    for k in range(2):
        cols = slice(width + k * L, width + k * L + L)
        vecs[0:4, cols] = btaps[k]
        vecs[4:5, cols] = bbias[k : k + 1, :]
    vecs[5:6, :width] = dot_l(hv[...], spread)[2:3, :]
    vecs[6:7, :width] = ngain[...]


def cot_body(k, *refs):
    cots = refs[:k]
    wout, all_o, gn_o = refs[k:]

    def one(cot):
        v = cot[...]
        all_o[...] = v
        gn_o[...] = dot(v, wout[...], 1, 1).astype(BF)

    for j in range(k):
        pl.when(pl.program_id(0) == j)(functools.partial(one, cots[j]))


def cotangent(cots, wout):
    k = len(cots)
    share, d = cots[0].shape
    width = wout.shape[0]
    return launch(
        functools.partial(cot_body, k),
        [*cots, wout],
        [whole(a) for a in (*cots, wout)],
        [shaped((k * share, d), BF), shaped((k * share, width), BF)],
        [pl.BlockSpec((share, c), lambda i: (i, 0)) for c in (d, width)],
        "cotangent",
        grid=(k,),
        vmem=12,
        flops=2 * k * share * d * width,
    )


def act_parts(pre, width):
    out = []
    for x0 in range(0, width + 2 * L, L):
        v = pre[:, x0 : x0 + L]
        out.append(v * sigmoid(v))
    return out


def pack(out, state, decay):
    rows = state.shape[0]
    hi, lo = split(jnp.broadcast_to(decay[0:1, :], (16, L)))
    row = lax.broadcasted_iota(jnp.int32, (16, L), 0)
    out[:rows, :] = state.astype(BF)
    tail = jnp.where(row == 0, hi.astype(F32), jnp.where(row == 1, lo.astype(F32), 0.0))
    out[rows:, :] = tail.astype(BF)


def unpack(load):
    v = load[...].astype(F32)
    rows = v.shape[0] - 16
    return v[:rows], v[rows : rows + 1] + v[rows + 1 : rows + 2]


def bit_at(meta, level):
    return jnp.bitwise_and(jnp.right_shift(meta[1], level), 1)


def is_ahead(meta, level, reverse):
    bit = bit_at(meta, level)
    return jnp.where(bit == (0 if reverse else 1), 1.0, 0.0)


def link_body(level, reverse, meta, state, decay, before, through, load,
              load_o, state_o, decay_o, before_o, through_o):
    theirs, a = unpack(load)
    heads = theirs.shape[0] // HD
    ahead = is_ahead(meta, level, reverse)
    mine = decay[0:1, :]
    t = through[0:1, :]
    before_o[...] = before[...] + per_head(t * ahead, heads) * theirs
    through_o[...] = jnp.broadcast_to(t * (ahead * a + (1.0 - ahead)), (8, L))
    joined = (
        per_head(mine * ahead + (1.0 - ahead), heads) * theirs
        + per_head(a * (1.0 - ahead) + ahead, heads) * state[...]
    )
    state_o[...] = joined
    decay_o[...] = jnp.broadcast_to(mine * a, (8, L))
    pack(load_o, joined, mine * a)


def final_link(meta, level, reverse, before, through, load):
    theirs, _ = unpack(load)
    t = through[0:1, :] * is_ahead(meta, level, reverse)
    return before[...] + per_head(t, theirs.shape[0] // HD) * theirs


def states_body(
    meta, cat, step, rim, vecs, hv, mats,
    pre_o, sin_o, end_o, load_o, cum_o, pfx_o, thr_o, buf, state, prod,
):
    c = pl.program_id(0)
    width = vecs.shape[1] - 2 * L
    heads = width // HD
    keep = jnp.where(meta[2 + c] == 0, 1.0, 0.0)

    @pl.when(c == 0)
    def _():
        buf[0:8, :] = rim[...].astype(F32)[8:16, :] * keep
        state[...] = jnp.zeros_like(state)
        prod[...] = jnp.ones_like(prod)

    @pl.when(c > 0)
    def _():
        buf[0:8, :] = buf[L : L + 8, :] * keep

    buf[8 : 8 + L, :] = cat[...].astype(F32)
    acts = []
    for x0 in range(0, width + 2 * L, L):
        cols = slice(x0, x0 + L)
        v = vecs[4:5, cols] + vecs[3:4, cols] * buf[8 : 8 + L, cols]
        for j in range(1, KERNEL):
            v = v + vecs[3 - j : 4 - j, cols] * buf[8 - j : 8 - j + L, cols]
        pre_o[:, cols] = v
        acts.append(v * sigmoid(v))
    steps = softplus(step[...].astype(F32) + hv[0:1, :])
    cum = dot_r(mats[:, width:], steps * hv[1:2, :])
    cum_o[...] = cum
    total = cum[L - 1 : L, :]
    weights = dot_l(jnp.exp(total - cum) * steps, mats[:, :width])
    inner = jnp.concatenate(acts[: width // L], axis=1)
    local = dot((inner * weights).astype(BF), acts[-2].astype(BF), 0, 0)
    entering = state[...] * keep
    sin_o[0] = entering.astype(BF)
    dec = jnp.exp(total)
    leaving = per_head(dec, heads) * entering + local
    state[...] = leaving
    here = prod[...] * keep
    pfx_o[0] = here
    prod[...] = here * dec

    @pl.when(c == pl.num_programs(0) - 1)
    def _():
        end_o[...] = leaving
        thr_o[...] = here * dec
        pack(load_o, leaving, here * dec)


def within_body(meta, pre, step, cum_r, sin, vecs, hv, mats, y_o):
    width = vecs.shape[1] - 2 * L
    heads = width // HD
    acts = act_parts(pre, width)
    bb, cb = acts[-2].astype(BF), acts[-1].astype(BF)
    scores = dot(cb, bb, 1, 1)
    steps = softplus(step[...].astype(F32) + hv[0:1, :])
    cum = cum_r[...]
    cum_t, steps_t = cum.T, steps.T
    lower = lax.broadcasted_iota(jnp.int32, (L, L), 0) >= lax.broadcasted_iota(
        jnp.int32, (L, L), 1
    )
    first = lax.broadcasted_iota(jnp.int32, (L, L), 1) < HD
    grown = dot_l(jnp.exp(cum), mats[:, :width])
    far = grown * dot(cb, sin[0], 1, 1)
    for pair in range(heads // 2):
        cols = slice(pair * L, pair * L + L)
        x = acts[pair].astype(BF)
        got = []
        for h in (2 * pair, 2 * pair + 1):
            gap = jnp.where(lower, cum[:, h : h + 1] - cum_t[h : h + 1, :], -1e30)
            mix = scores * jnp.exp(gap) * steps_t[h : h + 1, :]
            got.append(dot(mix.astype(BF), x))
        y_o[:, cols] = jnp.where(first, got[0], got[1]) + far[:, cols]


def gate_body(
    level, meta, pre, cum, pfx, y, gate, gn, before, through, load, vecs, mats,
    mixed_o, sums_o, incoming,
):
    width = vecs.shape[1] - 2 * L
    ones = jnp.ones((8, width), BF)

    @pl.when(pl.program_id(0) == 0)
    def _():
        incoming[...] = final_link(meta, level, False, before, through, load).astype(BF)

    reach = dot_l(jnp.exp(cum[...]) * pfx[0][0:1, :], mats[:, :width])
    cv = pre[:, width + L :]
    cb = (cv * sigmoid(cv)).astype(BF)
    far = reach * dot(cb, incoming[...], 1, 1)
    squares, crosses = [], []
    for x0 in range(0, width, L):
        cols = slice(x0, x0 + L)
        v = pre[:, cols]
        mixed = y[:, cols] + far[:, cols] + vecs[5:6, cols] * (v * sigmoid(v))
        mixed_o[:, cols] = mixed
        g = gate[:, cols].astype(F32)
        gated = mixed * (g * sigmoid(g))
        squares.append(gated * gated)
        crosses.append(gn[:, cols].astype(F32) * vecs[6:7, cols] * gated)
    square = dot_r(ones, jnp.concatenate(squares, axis=1), 1, 1)
    cross = dot_r(ones, jnp.concatenate(crosses, axis=1), 1, 1)
    row = lax.broadcasted_iota(jnp.int32, (8, L), 0)
    sums_o[0] = jnp.where(row == 0, square, cross)


def back_gate_body(
    count, meta, pre, cum_r, mixed_r, gate, gn, sums, sums2, thr, vecs, mats,
    normout_o, gm_o, ggr_o, gs_o, toward_o, load_o, sfx_o, acc_o, gstate, prod, acc,
):
    i = pl.program_id(0)
    c = count - 1 - i
    width = vecs.shape[1] - 2 * L
    heads = width // HD
    keep = jnp.where(meta[2 + c] == 0, 1.0, 0.0)

    @pl.when(i == 0)
    def _():
        gstate[...] = jnp.zeros_like(gstate)
        prod[...] = jnp.ones_like(prod)
        acc[...] = jnp.zeros_like(acc)

    both = sums[0] + sums2[0]
    square = jnp.broadcast_to(both[0:1, :], (L, L)).T
    cross = jnp.broadcast_to(both[1:2, :], (L, L)).T
    scale = lax.rsqrt(square * (1.0 / DI) + EPS)
    cubed = scale * scale * scale * cross * (1.0 / DI)
    cum = cum_r[...]
    total = cum[L - 1 : L, :]
    grown = dot_l(jnp.exp(cum), mats[:, :width])
    cv = pre[:, width + L :]
    cb = (cv * sigmoid(cv)).astype(BF)
    moved = []
    for x0 in range(0, width, L):
        cols = slice(x0, x0 + L)
        v = pre[:, cols]
        inner = v * sigmoid(v)
        g = gate[:, cols].astype(F32)
        s = sigmoid(g)
        silu = g * s
        mixed = mixed_r[:, cols]
        gated = mixed * silu
        ng = vecs[6:7, cols]
        gnv = gn[:, cols].astype(F32)
        scaled = gated * scale
        normout_o[:, cols] = (scaled * ng).astype(BF)
        gg = scale * (gnv * ng) - gated * cubed
        gm = gg * silu
        gm_o[:, cols] = gm.astype(BF)
        ggr_o[:, cols] = (gg * mixed * (s + silu * (1.0 - s))).astype(BF)
        acc[0:8, cols] += eights(gnv * scaled)
        acc[8:16, cols] += eights(gm * inner)
        moved.append((gm * grown[:, cols]).astype(BF))
    leaving = gstate[...]
    gs_o[0] = leaving.astype(BF)
    here = prod[...]
    sfx_o[0] = here
    dec = jnp.exp(total)
    entering = per_head(dec, heads) * leaving + dot(jnp.concatenate(moved, axis=1), cb, 0, 0)
    entering = entering * keep
    gstate[...] = entering
    prod[...] = here * dec * keep

    @pl.when(i == count - 1)
    def _():
        toward_o[...] = entering
        pack(load_o, entering, thr[...])
        row = lax.broadcasted_iota(jnp.int32, (8, width), 0)
        acc_o[...] = jnp.where(
            row == 0,
            jnp.sum(acc[0:8, :], axis=0, keepdims=True),
            jnp.sum(acc[8:16, :], axis=0, keepdims=True),
        )


def head_product(a, b, spread):
    rows = dot(jnp.ones((8, L), BF), (a * b).astype(BF), 1, 1)
    return dot_l(rows, spread, 1, 1)[0:1, :]


def back_within_body(
    meta, pre, step, cum_r, sin, pfx, gs, gm_r, incoming, vecs, hv, mats,
    ginner_o, gbc_o, glog_o, gst_o,
):
    width = vecs.shape[1] - 2 * L
    heads = width // HD
    acts = act_parts(pre, width)
    bb, cb = acts[-2].astype(BF), acts[-1].astype(BF)
    scores = dot(cb, bb, 1, 1)
    steps = softplus(step[...].astype(F32) + hv[0:1, :])
    cum = cum_r[...]
    total = cum[L - 1 : L, :]
    cum_t, steps_t = cum.T, steps.T
    row = lax.broadcasted_iota(jnp.int32, (L, L), 0)
    col = lax.broadcasted_iota(jnp.int32, (L, L), 1)
    lower = row >= col
    first = col < HD
    e = jnp.exp(cum)
    wd = jnp.exp(total - cum)
    grown = dot_l(e, mats[:, :width])
    weights = dot_l(wd * steps, mats[:, :width])
    gsb = gs[0]
    entering = sin[0].astype(F32) + per_head(pfx[0][0:1, :], heads) * incoming[...].astype(F32)
    eb = entering.astype(BF)
    u = dot(bb, gsb, 1, 1)
    v = dot(cb, eb, 1, 1)
    inner = jnp.concatenate(acts[: width // L], axis=1)
    gm = gm_r[...].astype(F32)
    seen = dot((inner * u).astype(BF), mats[:, :width], 1, 1)
    passed = dot((gm * v).astype(BF), mats[:, :width], 1, 1) * e
    gb = dot((inner * weights).astype(BF), gsb)
    gc = dot((gm * grown).astype(BF), eb)
    through = head_product(gsb.astype(F32), entering, mats[:, :width]) * jnp.exp(total)
    dscores = jnp.zeros((L, L), F32)
    rowsums = jnp.zeros((L, L), F32)
    colsums = jnp.zeros((L, L), F32)
    for pair in range(heads // 2):
        cols = slice(pair * L, pair * L + L)
        xb = acts[pair].astype(BF)
        gmb = gm_r[:, cols]
        got = []
        for h in (2 * pair, 2 * pair + 1):
            mine = first if h % 2 == 0 else jnp.logical_not(first)
            gmh = jnp.where(mine, gm[:, cols], 0.0).astype(BF)
            dm = dot(gmh, xb, 1, 1)
            gap = jnp.where(lower, cum[:, h : h + 1] - cum_t[h : h + 1, :], -1e30)
            decay = jnp.exp(gap)
            st = steps_t[h : h + 1, :]
            t1 = dm * decay
            dscores = dscores + t1 * st
            gp = t1 * scores
            rowsums = jnp.where(col == h, jnp.sum(gp * st, axis=1, keepdims=True), rowsums)
            colsums = jnp.where(row == h, jnp.sum(gp, axis=0, keepdims=True), colsums)
            mix = (scores * decay * st).astype(BF)
            got.append(dot(mix, gmb, 0, 0))
        ginner_o[:, cols] = (
            jnp.where(first, got[0], got[1])
            + weights[:, cols] * u[:, cols]
            + vecs[5:6, cols] * gm[:, cols]
        )
    db = dscores.astype(BF)
    gbc_o[:, :L] = gb + dot(db, cb, 0, 0)
    gbc_o[:, L:] = gc + dot(db, bb)
    direct = colsums.T
    seen = seen * wd
    gst_o[...] = direct + seen
    later = rowsums - direct * steps + passed
    tr = mats[:, width:]
    glog_o[...] = (
        dot_r(tr, later, 0, 0) + dot_r(tr, steps * seen) - steps * seen + through
    )


def crossing(vecs, later):
    row = lax.broadcasted_iota(jnp.int32, (16, later.shape[1]), 0)
    extra = jnp.zeros((16, later.shape[1]), F32)
    for j in range(1, KERNEL):
        for t in range(j):
            part = vecs[3 - j : 4 - j, :] * later[t : t + 1, :]
            extra = extra + jnp.where(row == 16 - j + t, part, 0.0)
    return extra


def back_conv_body(
    count, level, meta, cat, rim, pre, step, cum_r, sin, pfx, sfx, ginner_r, gbc_r, glog_r, gst_r,
    incoming, before, through, load, vecs, hv, mats,
    gcat_o, gsr_o, head_o, extra_o, acc_o, hacc_o, buf, acc, hacc, outgoing,
):
    i = pl.program_id(0)
    c = count - 1 - i
    width = vecs.shape[1] - 2 * L
    heads = width // HD
    keep_next = jnp.where(meta[3 + c] == 0, 1.0, 0.0)
    keep = jnp.where(meta[2 + c] == 0, 1.0, 0.0)

    @pl.when(i == 0)
    def _():
        buf[L : L + 8, :] = jnp.zeros_like(buf[L : L + 8, :])
        acc[...] = jnp.zeros_like(acc)
        hacc[...] = jnp.zeros_like(hacc)
        outgoing[...] = final_link(meta, level, True, before, through, load)

    @pl.when(i > 0)
    def _():
        buf[L : L + 8, :] = buf[0:8, :] * keep_next

    step_in = step[...].astype(F32) + hv[0:1, :]
    steps = softplus(step_in)
    cum = cum_r[...]
    total = cum[L - 1 : L, :]
    wd = jnp.exp(total - cum)
    weights = dot_l(wd * steps, mats[:, :width])
    far = outgoing[...] * per_head(sfx[0][0:1, :], heads)
    fb = far.astype(BF)
    entering = sin[0].astype(F32) + per_head(pfx[0][0:1, :], heads) * incoming[...].astype(F32)
    through = head_product(far, entering, mats[:, :width]) * jnp.exp(total)
    acts, slopes = [], []
    for x0 in range(0, width + 2 * L, L):
        v = pre[:, x0 : x0 + L]
        s = sigmoid(v)
        a = v * s
        acts.append(a)
        slopes.append(s + a * (1.0 - s))
    bb = acts[-2].astype(BF)
    u = dot(bb, fb, 1, 1)
    inner = jnp.concatenate(acts[: width // L], axis=1)
    seen = dot((inner * u).astype(BF), mats[:, :width], 1, 1) * wd
    gb = dot((inner * weights).astype(BF), fb)
    glog = glog_r[...] + dot_r(mats[:, width:], steps * seen) - steps * seen + through
    gsi = (gst_r[...] + seen + glog * hv[1:2, :]) * sigmoid(step_in)
    gsr_o[...] = gsi.astype(BF)
    hacc[0:8, :] += eights(glog * steps * hv[1:2, :])
    hacc[8:16, :] += eights(gsi)
    for k, x0 in enumerate(range(0, width + 2 * L, L)):
        cols = slice(x0, x0 + L)
        if x0 < width:
            g = ginner_r[:, cols] + weights[:, cols] * u[:, cols]
        elif x0 == width:
            g = gbc_r[:, :L] + gb
        else:
            g = gbc_r[:, L:]
        g = g * slopes[k]
        buf[0:L, cols] = g
        acc[32:40, cols] += eights(g)
        here = cat[:, cols].astype(F32)
        out = vecs[3:4, cols] * g
        acc[24:32, cols] += eights(g * here)
        for j in range(1, KERNEL):
            moved = buf[j : j + L, cols]
            out = out + vecs[3 - j : 4 - j, cols] * moved
            acc[24 - 8 * j : 32 - 8 * j, cols] += eights(moved * here)
        gcat_o[:, cols] = out.astype(BF)
    @pl.when(i == count - 1)
    def _():
        head_o[...] = buf[0:8, :]
        past = rim[...].astype(F32)[8:16, :] * keep
        now = buf[0:8, :]
        extra_o[...] = crossing(vecs, now * keep).astype(BF)
        row = lax.broadcasted_iota(jnp.int32, now.shape, 0)
        result = jnp.zeros_like(now)
        for k in range(5):
            part = jnp.sum(acc[8 * k : 8 * k + 8, :], axis=0, keepdims=True)
            j = 3 - k
            if 1 <= j <= 3:
                for t in range(j):
                    part = part + now[t : t + 1, :] * past[8 + t - j : 9 + t - j, :]
            result = jnp.where(row == k, part, result)
        acc_o[...] = result
        hrow = lax.broadcasted_iota(jnp.int32, (8, L), 0)
        hacc_o[...] = jnp.where(
            hrow == 0,
            jnp.sum(hacc[0:8, :], axis=0, keepdims=True),
            jnp.sum(hacc[8:16, :], axis=0, keepdims=True),
        )


def dgrad_body(k, ggr, gcat, gsr, wzx, wbc, wst, *outs):
    width = wzx.shape[2]

    def one(out):
        r = dot(ggr[...], wzx[0], 1, 1)
        r = r + dot(gcat[:, :width], wzx[1], 1, 1)
        r = r + dot(gcat[:, width : width + L], wbc[0], 1, 1)
        r = r + dot(gcat[:, width + L :], wbc[1], 1, 1)
        r = r + dot(gsr[...], wst[...])
        out[...] = r.astype(BF)

    for j in range(k):
        pl.when(pl.program_id(0) == j)(functools.partial(one, outs[j]))


def outproj_body(k, normout, wout, *outs):
    def one(out):
        out[...] = dot(normout[...], wout[...]).astype(BF)

    for j in range(k):
        pl.when(pl.program_id(0) == j)(functools.partial(one, outs[j]))


def rows_times(body, frames_n, share, d, rows, consts, name):
    k = frames_n
    outs = launch(
        functools.partial(body, k),
        [*rows, *consts],
        [pl.BlockSpec((share, r.shape[1]), lambda i: (k - 1 - i, 0)) for r in rows]
        + [whole(a) for a in consts],
        [shaped((share, d), BF)] * k,
        [pl.BlockSpec((share, d), lambda i: (0, 0))] * k,
        name,
        grid=(k,),
        vmem=20,
        flops=2 * k * share * d * sum(r.shape[1] for r in rows),
    )
    return list(outs)[::-1]


def hold_body(x, o):
    o[...] = x[...]


def hold(x, *deps):
    return simple(hold_body, [x], [shaped(x.shape, x.dtype)], "hold", deps=deps)[0]


def add_body(a, b, o):
    o[...] = (a[...].astype(F32) + b[...].astype(F32)).astype(o.dtype)


def add(a, b):
    return simple(add_body, [a, b], [shaped(a.shape, a.dtype)], "add")[0]


def swap(x, axis, mask):
    count = lax.axis_size(axis)
    return lax.ppermute(x, axis, [(i, i ^ mask) for i in range(count)])


def masks_of(axis):
    masks, mask = [], 1
    while mask < lax.axis_size(axis):
        masks.append(mask)
        mask *= 2
    return masks


def halve_body(slot, level, meta, kept, got, send_o, keep_o):
    bit = jnp.bitwise_and(jnp.right_shift(meta[slot], level), 1)
    half = send_o.shape[0]
    for o, b in ((send_o, 1 - bit), (keep_o, bit)):
        rows = pl.ds(pl.multiple_of(b * half, half), half)
        o[...] = (kept[rows, :].astype(F32) + got[rows, :].astype(F32)).astype(BF)


def halve(meta, slot, level, kept, got):
    shape = shaped((kept.shape[0] // 2, kept.shape[1]), BF)
    return simple(
        functools.partial(halve_body, slot, level), [kept, got], [shape, shape], "halve", meta
    )


def join_body(slot, level, meta, own, got, o):
    bit = jnp.bitwise_and(jnp.right_shift(meta[slot], level), 1)
    half = own.shape[0]
    o[pl.ds(pl.multiple_of(bit * half, half), half), :] = own[...]
    o[pl.ds(pl.multiple_of((1 - bit) * half, half), half), :] = got[...]


def join(meta, slot, level, own, got):
    shape = shaped((own.shape[0] * 2, own.shape[1]), BF)
    return simple(functools.partial(join_body, slot, level), [own, got], [shape], "join", meta)[0]


def wgrad_body(blocks, half, tails, meta, *refs):
    ins, (send_o, keep_o) = refs[:-2], refs[-2:]
    bit = bit_at(meta, 0)
    i = pl.program_id(0)
    g = jnp.where(i < half, (1 - bit) * half + i, bit * half + i - half)
    for p, tail in enumerate(tails):
        (a, b), ins = ins[:2], ins[2:]
        ta = tb = None
        if tail:
            (ta, tb), ins = ins[:2], ins[2:]
        inside = jnp.logical_and(g >= p * blocks, g < (p + 1) * blocks)

        def into(o, a=a, b=b, ta=ta, tb=tb):
            v = dot(a[...], b[...], 0, 0)
            if ta is not None:
                v = v + dot(ta[...], tb[...], 0, 0)
            o[...] = v.astype(BF)

        pl.when(jnp.logical_and(inside, i < half))(functools.partial(into, send_o))
        pl.when(jnp.logical_and(inside, i >= half))(functools.partial(into, keep_o))


def wgrads(meta, pairs, width, blocks, name):
    half = blocks * len(pairs) // 2
    tokens = pairs[0][0].shape[0]

    def cut(i, m):
        bit = jnp.bitwise_and(m[1], 1)
        g = jnp.where(i < half, (1 - bit) * half + i, bit * half + i - half)
        return (0, lax.rem(g, blocks))

    specs, ins = [], []
    for a, b, which, *more in pairs:
        for pair in [(a, b), tuple(more)]:
            for j, v in enumerate(pair):
                ins.append(v)
                specs.append(
                    pl.BlockSpec((v.shape[0], width), cut if j == which else lambda i, m: (0, 0))
                )
    return launch(
        functools.partial(wgrad_body, blocks, half, [len(p) > 3 for p in pairs]),
        ins,
        specs,
        [shaped((half * width, width), BF)] * 2,
        [
            pl.BlockSpec((width, width), lambda i, m: (jnp.minimum(i, half - 1), 0)),
            pl.BlockSpec((width, width), lambda i, m: (jnp.maximum(i - half, 0), 0)),
        ],
        name,
        grid=(2 * half,),
        meta=meta,
        vmem=20,
        flops=4 * half * tokens * width * width,
    )


def bc_body(meta, normed, gcat, gsr, rim, extra, send_o, keep_o, step_o):
    bit = jnp.bitwise_and(meta[0], 1)
    half = send_o.shape[0]
    for o, b in ((send_o, 1 - bit), (keep_o, bit)):
        cols = pl.ds(pl.multiple_of(b * half, half), half)
        v = dot(normed[:, cols], gcat[...], 0, 0) + dot(rim[:, cols], extra[...], 0, 0)
        o[...] = v.astype(BF)
    step_o[...] = dot(gsr[...], normed[...], 0, 0)[:8]


def bc_wgrad(meta, normed, gcat, gsr, rim, extra, width):
    tokens, d = normed.shape

    def tail(rows):
        return pl.BlockSpec((rows, 2 * L), lambda i, m: (0, width // (2 * L)))

    outs = [shaped((d // 2, 2 * L), BF)] * 2 + [shaped((8, d))]
    return launch(
        bc_body,
        [normed, gcat, gsr, rim, extra],
        [whole(normed), tail(tokens), whole(gsr), whole(rim), tail(16)],
        outs,
        [whole(o) for o in outs],
        "bc_wgrad",
        meta=meta,
        vmem=12,
        flops=2 * tokens * d * 3 * L,
    )


def columns_body(blocks, meta, own, got, o):
    width = o.shape[0]
    bit = bit_at(meta, 0)
    half = blocks // 2
    for src, b in ((own, bit), (got, 1 - bit)):
        for side in range(2):

            @pl.when(b == side)
            def _(src=src, side=side):
                for k in range(half):
                    at = (side * half + k) * width
                    o[:, at : at + width] = src[k * width : (k + 1) * width, :].astype(F32)


def columns(meta, own, got, d, width):
    return simple(
        functools.partial(columns_body, d // width), [own, got], [shaped((width, d))],
        "out_weights", meta, 16,
    )[0]


def rows_body(meta, own, got, *rest):
    zx_o = rest[-1]
    bit = bit_at(meta, 0)
    half = own.shape[0]
    zx_o[0, pl.ds(pl.multiple_of(bit * half, half), half), :] = own[...].astype(F32)
    zx_o[0, pl.ds(pl.multiple_of((1 - bit) * half, half), half), :] = got[...].astype(F32)


def rows_of(meta, own, got, which, d, width, old):
    ins, specs, aliases = [own, got], [whole(own), whole(got)], {}
    if old is not None:
        ins.append(old)
        specs.append(pl.BlockSpec(memory_space=pl.ANY))
        aliases = {2: 0}
    return launch(
        rows_body, ins, specs, [shaped((2, d, width))],
        [pl.BlockSpec((1, d, width), lambda i, m: (which, 0, 0))],
        "zx_weights", meta=meta, aliases=aliases, vmem=16, token=False,
    )[0]


def bc_out_body(meta, own, got, o):
    bit = jnp.bitwise_and(meta[0], 1)
    half = own.shape[0]
    for v, b in ((own, bit), (got, 1 - bit)):
        rows = pl.ds(pl.multiple_of(b * half, half), half)
        o[0, rows, :] = v[:, :L].astype(F32)
        o[1, rows, :] = v[:, L:].astype(F32)


def patch_body(meta, gcat, ahead, vecs, o):
    count = meta.shape[0] - 3
    keep = jnp.where(meta[2 + count] == 0, 1.0, 0.0)
    o[...] = (gcat[...].astype(F32) + crossing(vecs, ahead[...] * keep)).astype(BF)


def patched(meta, gcat, ahead, vecs, share, group):
    wide = gcat.shape[1]

    def spot(i, m):
        return ((jnp.bitwise_xor(m[0], group - 1) + 1) * (share // 16) - 1, 0)

    return launch(
        patch_body,
        [gcat, ahead, vecs],
        [pl.BlockSpec((16, wide), spot), whole(ahead), whole(vecs)],
        [shaped(gcat.shape, BF)],
        [pl.BlockSpec((16, wide), spot)],
        "patch",
        meta=meta,
        aliases={0: 0},
        token=False,
    )[0]


def layer_body(tok, a, b, o):
    o[...] = (tok[...].astype(F32) + (a[...].astype(F32) + b[...].astype(F32))).astype(BF)


def tokens_body(tok, cot, a, b, gain, conv, gt_o, acc_o):
    x = tok[...].astype(F32)
    rstd = lax.rsqrt(jnp.mean(x * x, axis=1, keepdims=True) + EPS)
    unit = x * rstd
    gnormed = a[...].astype(F32) + b[...].astype(F32)
    gunit = gnormed * gain[...]
    gt_o[...] = cot[...].astype(F32) + rstd * (
        gunit - unit * jnp.mean(gunit * unit, axis=1, keepdims=True)
    )
    d = x.shape[1]
    acc_o[:, d:] = conv[:, conv.shape[1] - 2 * L :]
    row = lax.broadcasted_iota(jnp.int32, (8, d), 0)
    acc_o[:, :d] = jnp.where(row == 0, jnp.sum(gnormed * unit, axis=0, keepdims=True), 0.0)


def finish_body(a, b, mats, gain_o, bc_o, bcb_o, step_o, taps_o, bias_o, sb_o, dl_o, sk_o, ng_o):
    d, width, heads = gain_o.shape[1], taps_o.shape[1], sb_o.shape[1]
    at = [0]

    def take(n):
        at[0] += n
        cols = slice(at[0] - n, at[0])
        return a[:, cols] + b[:, cols]

    gain_o[...] = take(d)[0:1]
    for k in range(2):
        v = take(L)
        bc_o[k] = v[0:4]
        bcb_o[k : k + 1, :] = v[4:5]
    step_o[...] = take(d)[:heads]
    v = take(width)
    taps_o[...] = v[0:4]
    bias_o[...] = v[4:5]
    v = take(width)
    ng_o[...] = v[0:1]
    sk_o[...] = dot_l(v, mats[:, :width], 1, 1)[1:2, :heads]
    v = take(L)
    dl_o[...] = v[0:1, :heads]
    sb_o[...] = v[1:2, :heads]


def pack_body(shared, step, conv, gate, head, o):
    at = 0
    for ref in (shared, step, conv, gate, head):
        n = ref.shape[1] if ref is not conv else ref.shape[1] - 2 * L
        o[:, at : at + n] = ref[:, :n]
        at += n


class Plan:
    def __init__(self):
        self.now, self.links, self.chains, self.done = 0.0, {}, [], set()

    def add(self, name, priority, chain):
        self.chains.append([name, priority, chain, None])
        self.step(self.chains[-1])

    def step(self, entry):
        try:
            link, us, latency, spend = next(entry[2])
        except StopIteration:
            self.chains.remove(entry)
            self.done.add(entry[0])
            return
        if link is None:
            entry[3] = (us, 0.0, spend)
            return
        start = max(self.now, self.links.get(link, 0.0))
        self.links[link] = start + us
        entry[3] = (None, start + us + latency, spend)
        self.now += 1.0

    def ready(self, entry):
        name, at, _ = entry[3]
        if name is not None:
            return 0.0 if name in self.done else 1e9
        return at

    def run(self, until=None):
        while self.chains and (until is None or until not in self.done):
            able = [e for e in self.chains if self.ready(e) <= self.now]
            if able:
                entry = min(able, key=lambda e: e[1])
            else:
                entry = min(self.chains, key=self.ready)
                self.now = self.ready(entry)
            self.now += entry[3][2]
            self.step(entry)


def on_device(
    tokens_in,
    grad_out,
    scene_offsets,
    input_gain,
    weight_zx,
    weight_bc,
    weight_step,
    conv_inner,
    conv_inner_bias,
    conv_bc,
    conv_bc_bias,
    step_bias,
    decay_log,
    skip_weight,
    norm_gain,
    weight_out,
):
    share, d = tokens_in.shape
    group = lax.axis_size("tensor")
    tokens = share * group
    heads = step_bias.shape[0]
    width = norm_gain.shape[0]
    wide = width + 2 * L
    count = tokens // L
    per = share // L
    half = group // 2
    me = lax.axis_index("tensor")
    place = lax.axis_index("dp")

    heads_pos = place * tokens + jnp.arange(count + 1, dtype=jnp.int32) * L
    starts = jnp.any(heads_pos[:, None] == scene_offsets[None, :], axis=1).astype(jnp.int32)
    meta = jnp.concatenate([me[None].astype(jnp.int32), place[None].astype(jnp.int32), starts])
    masks, tmasks = masks_of("dp"), masks_of("tensor")
    levels = len(masks)

    LAST.clear()
    gain = input_gain[None]
    prep_ins = [conv_inner, conv_inner_bias[None], conv_bc, conv_bc_bias, step_bias[None],
                decay_log[None], skip_weight[None], norm_gain[None], weight_step.T]
    prep_outs = [shaped((8, wide)), shaped((8, L)), shaped((L, width + L), BF),
                 shaped((L, d), BF)]
    (last_rows,) = launch(
        hold_body, [tokens_in], [pl.BlockSpec((16, d), lambda i: (share // 16 - 1, 0))],
        [shaped((16, d), BF)], [pl.BlockSpec((16, d), lambda i: (0, 0))], "last_rows",
    )
    vecs, hv, mats, wst = launch(
        prep_body,
        [pltpu.with_memory_space_constraint(a, pltpu.HBM) for a in prep_ins],
        [whole(a) for a in prep_ins],
        prep_outs, [whole(o) for o in prep_outs], "prep", vmem=4,
    )

    def place_of(c, meta):
        if per == 1:
            return lax.bitwise_xor(c, meta[0])
        return lax.bitwise_xor(lax.div(c, per), meta[0]) * per + lax.rem(c, per)

    def stretched(body, name, ins, outs, scratch, reverse, vmem, flops, span=None, old=()):
        begin, length = span or (0, count)

        def order(i):
            return count - 1 - i - begin if reverse else i + begin

        def spec(kind, shape):
            if kind == "rows":
                return pl.BlockSpec((L, shape[1]), lambda i, m: (place_of(order(i), m), 0))
            if kind == "each":
                return pl.BlockSpec((1, *shape[1:]), lambda i, m: (order(i), 0, 0))
            return pl.BlockSpec(shape, lambda i, m: (0,) * len(shape))

        n = len(ins)

        def run(*refs):
            body(*refs[: 1 + n], *refs[1 + n + len(old) :])

        return launch(
            run,
            [a for _, a in ins] + list(old),
            [spec(k, a.shape) for k, a in ins] + [pl.BlockSpec(memory_space=pl.ANY)] * len(old),
            [shaped(s, t) for _, s, t in outs],
            [spec(k, s) for k, s, _ in outs],
            name,
            grid=(length,),
            meta=meta,
            scratch=scratch,
            aliases={n + j: j for j in range(len(old))},
            vmem=vmem,
            flops=flops,
        )

    def spread_out(held, keys):
        mask = half // 2
        while mask:
            for f in [f for f in held if f in keys]:
                held[f ^ mask] = swap(held[f], "tensor", mask)
            mask //= 2

    near, far = range(half), range(half, group)
    held = {0: tokens_in}
    arrived = swap(tokens_in, "tensor", half)
    spread_out(held, near)
    dps = lax.axis_size("dp")
    past = [
        lax.ppermute(
            last_rows,
            ("dp", "tensor"),
            [(i * group + group - 1, (i + 1) * group + t) for i in range(dps - 1)],
        )
        for t in range(group)
    ]
    weights = (gain, weight_zx, weight_bc, wst)
    *before, rim, normed_rim = project(meta, [held[f] for f in near], past, *weights, tokens, 0, [])
    held[half] = hold(arrived, before[3])
    spread_out(held, far)
    cots = {0: grad_out}
    cots[half] = swap(hold(grad_out), "tensor", half)
    before = project(meta, [held[half]], [], *weights, tokens, half, list(before))
    normed, gate_raw, cat, step_raw = project(
        meta, [held[f] for f in far[1:]], [], *weights, tokens, half + 1, list(before)
    )

    tall = (tokens, L)
    state_shape = (width, L)
    load_shape = (width + 16, L)
    small = (8, L)
    pre, sin, state, load, cum, pfx, decay = stretched(
        states_body,
        "states",
        [("rows", cat), ("rows", step_raw), ("one", rim), ("one", vecs), ("one", hv),
         ("one", mats)],
        [("rows", (tokens, wide), F32), ("each", (count, *state_shape), BF),
         ("one", state_shape, F32), ("one", load_shape, BF), ("rows", tall, F32),
         ("each", (count, 8, L), F32), ("one", small, F32)],
        [pltpu.VMEM((L + 8, wide), F32), pltpu.VMEM(state_shape, F32), pltpu.VMEM(small, F32)],
        False, 10, 2 * tokens * width * L * 3,
    )

    def link(level, reverse, held, load):
        shapes = [load_shape, state_shape, small, state_shape, small]
        out = simple(
            functools.partial(link_body, level, reverse), [*held, load],
            [shaped(s, BF if j == 0 else F32) for j, s in enumerate(shapes)], "link", meta,
        )
        return out[1:], out[0]

    thr = decay
    fresh = [jnp.zeros(state_shape, F32), jnp.ones(small, F32)]
    own = [state, decay, *fresh]
    load = swap(load, "dp", 1)
    late = {half: hold(cots[half])}
    spread_out(late, far)
    spread_out(cots, near)
    cots.update({f: late[f] for f in far[1:]})
    (y,) = stretched(
        within_body,
        "within",
        [("rows", pre), ("rows", step_raw), ("rows", cum), ("each", sin), ("one", vecs),
         ("one", hv), ("one", mats)],
        [("rows", (tokens, width), F32)],
        [], False, 10, 2 * tokens * width * L * 6,
    )
    for level in range(levels - 1):
        own, load = link(level, False, own, load)
        load = swap(load, "dp", masks[level + 1])
        if level == levels - 2:
            cot_all, gn = cotangent([cots[f] for f in range(group)], weight_out)
    befores, throughs = own[2:]
    mixed, sums, incoming = stretched(
        functools.partial(gate_body, levels - 1),
        "gated",
        [("rows", pre), ("rows", cum), ("each", pfx), ("rows", y), ("rows", gate_raw),
         ("rows", gn), ("one", befores), ("one", throughs), ("one", load), ("one", vecs),
         ("one", mats)],
        [("rows", (tokens, width), F32), ("each", (count, 8, L), F32), ("one", state_shape, BF)],
        [], False, 10, 2 * tokens * width * L * 4,
    )
    for mask in tmasks[::-1][:-1]:
        sums = add(sums, swap(sums, "tensor", mask))
    sums2 = swap(sums, "tensor", 1)
    normout, gm, ggr, gs, toward, load, sfx, gate_acc = stretched(
        functools.partial(back_gate_body, count),
        "back_gated",
        [("rows", pre), ("rows", cum), ("rows", mixed), ("rows", gate_raw), ("rows", gn),
         ("each", sums), ("each", sums2), ("one", thr), ("one", vecs), ("one", mats)],
        [("rows", (tokens, width), BF), ("rows", (tokens, width), BF),
         ("rows", (tokens, width), BF), ("each", (count, *state_shape), BF),
         ("one", state_shape, F32), ("one", load_shape, BF), ("each", (count, 8, L), F32),
         ("one", (8, width), F32)],
        [pltpu.VMEM(state_shape, F32), pltpu.VMEM(small, F32), pltpu.VMEM((16, width), F32)],
        True, 10, 2 * tokens * width * L * 3,
    )

    plan = Plan()
    kept = {}
    blocks = d // width
    axes = {"dp": ["y", "z", "z"] + ["z"] * levels, "tensor": ["core", "x"] + ["x"] * levels}
    spans = {"dp": [1, 1, 2] + [2] * levels, "tensor": [1, 1] + [2] * levels}
    hops = {"core": 1.0, "x": 4.0, "y": 4.0, "z": 4.5}
    rates = {"core": 600.0, "x": 90.0, "y": 90.0, "z": 90.0}

    def moved(x, axis, level):
        link_name = axes[axis][level]
        size = 2 * x.size * x.dtype.itemsize * spans[axis][level] / 1e3
        got = swap(x, axis, 1 << level)
        return got, link_name, size / rates[link_name], hops[link_name]

    def halving(key, axis, send, keep, first=0):
        top = len(masks_of(axis))
        slot = 1 if axis == "dp" else 0
        for level in range(first, top):
            got, *way = moved(send, axis, level)
            yield (*way, 0.8)
            if level == top - 1:
                kept[key] = add(keep, got)
            else:
                send, keep = halve(meta, slot, level + 1, keep, got)

    def doubling(key, axis, x, finish):
        slot = 1 if axis == "dp" else 0
        for level in range(len(masks_of(axis)) - 1, -1, -1):
            got, *way = moved(x, axis, level)
            yield (*way, 2.0 if level == 0 else 0.7)
            if level == 0:
                finish(x, got)
            else:
                x = join(meta, slot, level, x, got)

    def weights_chain(key, pairs, name, spend, finish):
        send, keep = wgrads(meta, pairs, width, blocks, name)
        yield from halving(key, "dp", send, keep)
        yield from doubling(key, "dp", kept[key], finish)

    def zx(which):
        def finish(own, got):
            kept["zx"] = rows_of(meta, own, got, which, d, width, kept.get("zx"))

        return finish

    def out_weights(own, got):
        kept["wout"] = columns(meta, own, got, d, width)

    def first_links():
        own = [toward, thr, *fresh]
        load = first_load
        for level in range(levels):
            got, *way = moved(load, "dp", level)
            if level == levels - 1:
                kept["links"] = (*own[2:], got)
                yield (*way, 0.0)
            else:
                yield (*way, 1.0)
                own, load = link(level, True, own, got)

    def within_part(begin, length):
        kept["within"] = stretched(
            back_within_body,
            "back_within",
            [("rows", pre), ("rows", step_raw), ("rows", cum), ("each", sin), ("each", pfx),
             ("each", gs), ("rows", gm), ("one", incoming), ("one", vecs), ("one", hv),
             ("one", mats)],
            [("rows", (tokens, width), F32), ("rows", (tokens, 2 * L), F32), ("rows", tall, F32),
             ("rows", tall, F32)],
            [], True, 12, 2 * tokens * width * L * 12, (begin, length), kept.get("within", ()),
        )

    def within_chain():
        part = count // 2
        for begin in range(0, count, part):
            yield (None, "begin", 0.0, 6.0)
            within_part(begin, part)

    def scattered(key, frames_in):
        sums_in = []
        for first in (half, 0):
            part = dict(enumerate(frames_in[first : first + half]))
            mask, level = 1, 0
            while mask < half:
                sent = [(f, moved(part.pop(f), "tensor", level)) for f in list(part) if f & mask]
                for f, (got, *way) in sent:
                    yield (*way, 0.7)
                    part[f ^ mask] = add(part[f ^ mask], got)
                mask, level = 2 * mask, level + 1
            sums_in.append(part[0])
            if first:
                got, *way = moved(part[0], "tensor", level)
                crossing_way = way
                sums_in[0] = got
        kept[key] = (sums_in[1], sums_in[0])
        yield (*crossing_way, 1.6)

    def branch_chain():
        yield (None, "begin", 0.0, 2.0)
        branch = rows_times(
            outproj_body, group, share, d, [normout], [weight_out], "outproj"
        )
        yield from scattered("branch", branch)
        (kept["layer"],) = simple(
            layer_body, [tokens_in, *kept["branch"]], [shaped((share, d), BF)], "layer"
        )

    def tokens_chain():
        ahead = lax.ppermute(kept["head"], "dp", [(i + 1, i) for i in range(dps - 1)])
        yield ("z", 0.5, 5.0, 5.4)
        gcat = patched(meta, kept["gcat"], ahead, vecs, share, group)
        grads = rows_times(
            dgrad_body, group, share, d, [ggr, gcat, kept["gsr"]], [weight_zx, weight_bc, wst],
            "dgrad",
        )
        yield from scattered("grad", grads)
        kept["tokens"], shared = simple(
            tokens_body, [tokens_in, grad_out, *kept["grad"], gain, kept["conv_acc"]],
            [shaped((share, d)), shaped((8, d + 2 * L))], "tokens", None, 12,
        )
        for level in range(len(tmasks)):
            got, *way = moved(shared, "tensor", level)
            yield (*way, 0.6)
            shared = add(shared, got)
        parts = [shared, kept["step_acc"], kept["conv_acc"], gate_acc, kept["head_acc"]]
        size = sum(a.shape[1] for a in parts) - 2 * L
        (total,) = simple(pack_body, parts, [shaped((8, size))], "pack")
        for level in range(levels):
            got, *way = moved(total, "dp", level)
            yield (*way, 0.6)
            if level < levels - 1:
                total = add(total, got)
        outs = [(1, d), (2, 4, L), (2, L), (heads, d), (4, width), (1, width), (1, heads),
                (1, heads), (1, heads), (1, width)]
        kept["small"] = simple(
            finish_body, [total, got, mats], [shaped(s) for s in outs], "finish"
        )

    def bc_chain():
        yield (None, "begin", 0.0, 1.7)
        send, keep, kept["step_acc"] = bc_wgrad(
            meta, normed, kept["gcat"], kept["gsr"], normed_rim, kept["extra"], width
        )
        yield from halving("bc", "tensor", send, keep)
        total = kept["bc"]
        for level in range(levels):
            got, *way = moved(total, "dp", level)
            yield (*way, 0.6)
            total = add(total, got)

        def finish(own, got):
            (kept["bc_out"],) = simple(
                bc_out_body, [own, got], [shaped((2, d, L))], "bc_weights", meta
            )

        yield from doubling("bc", "tensor", total, finish)

    plan.done.add("begin")
    first_load = load
    plan.add("links", 0, first_links())
    plan.add("W", 5, weights_chain("W", [(normout, cot_all, 1)], "out_wgrad", 2.0, out_weights))
    plan.add("G", 6, weights_chain("G", [(normed, ggr, 0)], "gate_wgrad", 2.0, zx(0)))
    plan.add("within", 8, within_chain())
    plan.add("branch", 9, branch_chain())
    plan.run("links")
    plan.run("within")
    befores, throughs, load = kept["links"]
    ginner, gbc, glog, gst = kept["within"]
    gcat, gsr, head, extra, conv_acc, head_acc = stretched(
        functools.partial(back_conv_body, count, levels - 1),
        "back_conv",
        [("rows", cat), ("one", rim), ("rows", pre), ("rows", step_raw), ("rows", cum),
         ("each", sin), ("each", pfx), ("each", sfx), ("rows", ginner), ("rows", gbc),
         ("rows", glog), ("rows", gst), ("one", incoming), ("one", befores), ("one", throughs),
         ("one", load), ("one", vecs), ("one", hv), ("one", mats)],
        [("rows", (tokens, wide), BF), ("rows", tall, BF), ("one", (8, wide), F32),
         ("one", (16, wide), BF), ("one", (8, wide), F32), ("one", small, F32)],
        [pltpu.VMEM((L + 8, wide), F32), pltpu.VMEM((40, wide), F32), pltpu.VMEM((16, L), F32),
         pltpu.VMEM(state_shape, F32)],
        True, 12, 2 * tokens * width * L * 6,
    )
    plan.now += 10.0

    kept.update(head=head, gcat=gcat, gsr=gsr, extra=extra, conv_acc=conv_acc, head_acc=head_acc)
    plan.add(
        "I", 1,
        weights_chain("I", [(normed, gcat, 0, normed_rim, extra)], "inner_wgrad", 2.7, zx(1)),
    )
    plan.add("tokens", 2, tokens_chain())
    plan.add("bc", 3, bc_chain())
    plan.run()

    gain_g, bc_g, bcb_g, step_g, taps_g, bias_g, sb_g, dl_g, sk_g, ng_g = kept["small"]
    return (
        kept["layer"],
        kept["tokens"],
        gain_g[0],
        kept["zx"],
        kept["bc_out"],
        step_g.T,
        taps_g,
        bias_g[0],
        bc_g,
        bcb_g,
        sb_g[0],
        dl_g[0],
        sk_g[0],
        ng_g[0],
        kept["wout"],
    )


def solution(mesh):
    rows = P(("dp", "tensor"), None)
    cols = P(None, "tensor")
    one = P("tensor")
    in_specs = (
        rows, rows, P(), P(), P(None, None, "tensor"), P(), cols, cols, one, P(), P(),
        one, one, one, one, P("tensor", None),
    )
    out_specs = (
        rows, rows, P(), P(None, None, "tensor"), P(), cols, cols, one, P(), P(),
        one, one, one, one, P("tensor", None),
    )
    return jax.shard_map(
        on_device, mesh=mesh, in_specs=in_specs, out_specs=out_specs, check_vma=False
    )
```

```python
import functools

import jax
import jax.numpy as jnp
from jax import lax
from jax.experimental import pallas as pl
from jax.experimental.pallas import tpu as pltpu
from jax.sharding import PartitionSpec as P

KERNEL = 4
L = 128
HD = 64
DI = 2048
EPS = 1e-05
F32 = jnp.float32
BF = jnp.bfloat16
MIB = 1 << 20
ROW = 256


def dot(a, b, ca=1, cb=0):
    return lax.dot_general(a, b, (((ca,), (cb,)), ((), ())), preferred_element_type=F32)


def split(a):
    hi = a.astype(BF)
    return hi, (a - hi.astype(F32)).astype(BF)


def dot_l(a, b, ca=1, cb=0):
    hi, lo = split(a)
    return dot(hi, b, ca, cb) + dot(lo, b, ca, cb)


def dot_r(a, b, ca=1, cb=0):
    hi, lo = split(b)
    return dot(a, hi, ca, cb) + dot(a, lo, ca, cb)


def sigmoid(v):
    return 0.5 * jnp.tanh(0.5 * v) + 0.5


def softplus(v):
    u = jnp.exp(-jnp.abs(v))
    small = u * (1.0 - u * (0.5 - u * (1.0 / 3.0 - u * 0.25)))
    return jnp.maximum(v, 0.0) + jnp.where(u < 0.02, small, jnp.log(1.0 + u))


def per_head(row, heads):
    return jnp.concatenate(
        [jnp.broadcast_to(row[:, h : h + 1], (HD, L)) for h in range(heads)], axis=0
    )


def eights(v):
    return jnp.sum(v.reshape(v.shape[0] // 8, 8, v.shape[1]), axis=0)


def across_lanes(v, width):
    return jnp.concatenate([v] * (width // L), axis=1) if width > L else v


def whole(a):
    return pl.BlockSpec(a.shape, lambda *_: (0,) * a.ndim)


LAST = []

def launch(body, ins, in_specs, outs, out_specs, name, grid=(1,), meta=None, scratch=(),
           aliases=None, vmem=8, flops=0, token=True):
    ins, in_specs = list(ins), list(in_specs)
    lead = 0 if meta is None else 1
    at = lead + len(ins)
    given = LAST[-1] if LAST and not any(LAST[-1] is a for a in ins) else None
    if given is not None:
        ins.append(given)
        in_specs.append(pl.BlockSpec(memory_space=pl.ANY))

    def run(*refs):
        body(*(refs if given is None else refs[:at] + refs[at + 1 :]))

    results = pl.pallas_call(
        run,
        grid_spec=pltpu.PrefetchScalarGridSpec(
            num_scalar_prefetch=lead,
            grid=grid,
            in_specs=in_specs,
            out_specs=list(out_specs),
            scratch_shapes=list(scratch),
        ),
        out_shape=list(outs),
        input_output_aliases={lead + k: v for k, v in (aliases or {}).items()},
        compiler_params=pltpu.CompilerParams(vmem_limit_bytes=vmem * MIB),
        cost_estimate=pl.CostEstimate(
            flops=flops,
            bytes_accessed=0,
            transcendentals=0,
        ),
        name=name,
    )(*([] if meta is None else [meta]), *ins)
    if token:
        LAST[:] = [min(results, key=lambda a: a.size)]
    return results


def space_body(o):
    o[...] = jnp.zeros_like(o)


def space():
    o = shaped((8, L))
    launch(space_body, [], [], [o], [whole(o)], "space", vmem=1, flops=10**10)


def shaped(shape, dtype=F32):
    return jax.ShapeDtypeStruct(shape, dtype)


def simple(body, ins, outs, name, meta=None, vmem=8, deps=()):
    n = len(ins)

    def run(*refs):
        lead = 0 if meta is None else 1
        body(*refs[: lead + n], *refs[lead + n + len(deps) :])

    return launch(
        run, [*ins, *deps],
        [whole(a) for a in ins] + [pl.BlockSpec(memory_space=pl.ANY)] * len(deps),
        outs, [whole(o) for o in outs], name, meta=meta, vmem=vmem,
    )


def unit_rows(x, gain):
    x = x.astype(F32)
    rstd = lax.rsqrt(jnp.mean(x * x, axis=1, keepdims=True) + EPS)
    return (x * rstd * gain).astype(BF)


def proj_body(k, rims, deps, meta, *refs):
    toks, past = refs[:k], refs[k : k + rims]
    gain, wzx, wbc, wst = refs[k + rims : k + rims + 4]
    outs = refs[k + rims + 4 + deps :]
    normed_o, gate_o, cat_o, step_o = outs[:4]
    width = wzx.shape[2]

    def conv_inputs(normed, out):
        out[:, :width] = dot(normed, wzx[1]).astype(BF)
        out[:, width : width + L] = dot(normed, wbc[0]).astype(BF)
        out[:, width + L :] = dot(normed, wbc[1]).astype(BF)

    def one(j):
        normed = unit_rows(toks[j][...], gain[...])
        normed_o[...] = normed
        conv_inputs(normed, cat_o)
        gate_o[...] = dot(normed, wzx[0]).astype(BF)
        step_o[...] = dot(normed, wst[...], 1, 1).astype(BF)
        if rims and j == 0:
            rim = past[0][...].astype(F32)
            for p in past[1:]:
                rim = rim + p[...].astype(F32)
            normed = unit_rows(rim, gain[...])
            outs[5][...] = normed
            conv_inputs(normed, outs[4])

    for j in range(k):
        pl.when(pl.program_id(0) == j)(functools.partial(one, j))


def project(meta, toks, past, gain, wzx, wbc, wst, total, first, before):
    k = len(toks)
    share, d = toks[0].shape
    width = wzx.shape[2]
    wide = width + 2 * L
    cols = (d, width, wide, L)
    ins = [*toks, *past, gain, wzx, wbc, wst]
    specs = [whole(a) for a in ins]
    out_specs = [pl.BlockSpec((share, c), lambda i, m: (i + first, 0)) for c in cols]
    out_shape = [shaped((total, c), BF) for c in cols]
    if past:
        for c in (wide, d):
            out_specs.append(pl.BlockSpec((16, c), lambda i, m: (0, 0)))
            out_shape.append(shaped((16, c), BF))
    aliases = {len(ins) + j: j for j in range(4)} if before else {}
    return launch(
        functools.partial(proj_body, k, len(past), len(before)),
        ins + before,
        specs + [pl.BlockSpec(memory_space=pl.ANY)] * len(before),
        out_shape,
        out_specs,
        "project",
        grid=(k,),
        meta=meta,
        aliases=aliases,
        vmem=16,
        token=False,
    )


def prep_body(taps, tbias, btaps, bbias, sbias, decay, skip, ngain, wst, vecs, hv, mats, wst_o):
    width = taps.shape[1]
    heads = width // HD
    wst_o[...] = jnp.zeros_like(wst_o)
    wst_o[0:heads, :] = wst[...]
    head = lax.broadcasted_iota(jnp.int32, (L, width), 0)
    lane = lax.broadcasted_iota(jnp.int32, (L, width), 1)
    spread = jnp.where(lax.div(lane, HD) == head, 1.0, 0.0).astype(BF)
    mats[:, :width] = spread
    r = lax.broadcasted_iota(jnp.int32, (L, L), 0)
    c = lax.broadcasted_iota(jnp.int32, (L, L), 1)
    mats[:, width:] = jnp.where(r >= c, 1.0, 0.0).astype(BF)
    hv[...] = jnp.zeros_like(hv)
    hv[0:1, :heads] = sbias[...]
    hv[1:2, :heads] = -jnp.exp(decay[...])
    hv[2:3, :heads] = skip[...]
    vecs[...] = jnp.zeros_like(vecs)
    vecs[0:4, :width] = taps[...]
    vecs[4:5, :width] = tbias[...]
    for k in range(2):
        cols = slice(width + k * L, width + k * L + L)
        vecs[0:4, cols] = btaps[k]
        vecs[4:5, cols] = bbias[k : k + 1, :]
    vecs[5:6, :width] = dot_l(hv[...], spread)[2:3, :]
    vecs[6:7, :width] = ngain[...]


def cot_body(k, *refs):
    cots = refs[:k]
    wout, all_o, gn_o = refs[k:]

    def one(cot):
        v = cot[...]
        all_o[...] = v
        gn_o[...] = dot(v, wout[...], 1, 1).astype(BF)

    for j in range(k):
        pl.when(pl.program_id(0) == j)(functools.partial(one, cots[j]))


def cotangent(cots, wout):
    k = len(cots)
    share, d = cots[0].shape
    width = wout.shape[0]
    return launch(
        functools.partial(cot_body, k),
        [*cots, wout],
        [whole(a) for a in (*cots, wout)],
        [shaped((k * share, d), BF), shaped((k * share, width), BF)],
        [pl.BlockSpec((share, c), lambda i: (i, 0)) for c in (d, width)],
        "cotangent",
        grid=(k,),
        vmem=12,
    )


def act_parts(pre, width):
    out = []
    for x0 in range(0, width + 2 * L, L):
        v = pre[:, x0 : x0 + L]
        out.append(v * sigmoid(v))
    return out


def pack(out, state, decay):
    rows = state.shape[0]
    hi, lo = split(jnp.broadcast_to(decay[0:1, :], (16, L)))
    row = lax.broadcasted_iota(jnp.int32, (16, L), 0)
    out[:rows, :] = state.astype(BF)
    tail = jnp.where(row == 0, hi.astype(F32), jnp.where(row == 1, lo.astype(F32), 0.0))
    out[rows:, :] = tail.astype(BF)


def unpack(load):
    v = load[...].astype(F32)
    rows = v.shape[0] - 16
    return v[:rows], v[rows : rows + 1] + v[rows + 1 : rows + 2]


def bit_at(meta, level):
    return jnp.bitwise_and(jnp.right_shift(meta[1], level), 1)


def is_ahead(meta, level, reverse):
    bit = bit_at(meta, level)
    return jnp.where(bit == (0 if reverse else 1), 1.0, 0.0)


def link_body(level, reverse, meta, state, decay, before, through, load,
              load_o, state_o, decay_o, before_o, through_o):
    theirs, a = unpack(load)
    heads = theirs.shape[0] // HD
    ahead = is_ahead(meta, level, reverse)
    mine = decay[0:1, :]
    t = through[0:1, :]
    before_o[...] = before[...] + per_head(t * ahead, heads) * theirs
    through_o[...] = jnp.broadcast_to(t * (ahead * a + (1.0 - ahead)), (8, L))
    joined = (
        per_head(mine * ahead + (1.0 - ahead), heads) * theirs
        + per_head(a * (1.0 - ahead) + ahead, heads) * state[...]
    )
    state_o[...] = joined
    decay_o[...] = jnp.broadcast_to(mine * a, (8, L))
    pack(load_o, joined, mine * a)


def final_link(meta, level, reverse, before, through, load):
    theirs, _ = unpack(load)
    t = through[0:1, :] * is_ahead(meta, level, reverse)
    return before[...] + per_head(t, theirs.shape[0] // HD) * theirs


def states_body(
    meta, cat, step, rim, vecs, hv, mats,
    pre_o, sin_o, end_o, load_o, cum_o, pfx_o, thr_o, buf, state, prod,
):
    c = pl.program_id(0)
    width = vecs.shape[1] - 2 * L
    heads = width // HD
    keep = jnp.where(meta[2 + c] == 0, 1.0, 0.0)

    @pl.when(c == 0)
    def _():
        buf[0:8, :] = rim[...].astype(F32)[8:16, :] * keep
        state[...] = jnp.zeros_like(state)
        prod[...] = jnp.ones_like(prod)

    @pl.when(c > 0)
    def _():
        buf[0:8, :] = buf[L : L + 8, :] * keep

    buf[8 : 8 + L, :] = cat[...].astype(F32)
    acts = []
    for x0 in range(0, width + 2 * L, L):
        cols = slice(x0, x0 + L)
        v = vecs[4:5, cols] + vecs[3:4, cols] * buf[8 : 8 + L, cols]
        for j in range(1, KERNEL):
            v = v + vecs[3 - j : 4 - j, cols] * buf[8 - j : 8 - j + L, cols]
        pre_o[:, cols] = v
        acts.append(v * sigmoid(v))
    steps = softplus(step[...].astype(F32) + hv[0:1, :])
    cum = dot_r(mats[:, width:], steps * hv[1:2, :])
    cum_o[...] = cum
    total = cum[L - 1 : L, :]
    weights = dot_l(jnp.exp(total - cum) * steps, mats[:, :width])
    inner = jnp.concatenate(acts[: width // L], axis=1)
    local = dot((inner * weights).astype(BF), acts[-2].astype(BF), 0, 0)
    entering = state[...] * keep
    sin_o[0] = entering.astype(BF)
    dec = jnp.exp(total)
    leaving = per_head(dec, heads) * entering + local
    state[...] = leaving
    here = prod[...] * keep
    pfx_o[0] = here
    prod[...] = here * dec

    @pl.when(c == pl.num_programs(0) - 1)
    def _():
        end_o[...] = leaving
        thr_o[...] = here * dec
        pack(load_o, leaving, here * dec)


def within_body(meta, pre, step, cum_r, sin, vecs, hv, mats, y_o):
    width = vecs.shape[1] - 2 * L
    heads = width // HD
    acts = act_parts(pre, width)
    bb, cb = acts[-2].astype(BF), acts[-1].astype(BF)
    scores = dot(cb, bb, 1, 1)
    steps = softplus(step[...].astype(F32) + hv[0:1, :])
    cum = cum_r[...]
    cum_t, steps_t = cum.T, steps.T
    lower = lax.broadcasted_iota(jnp.int32, (L, L), 0) >= lax.broadcasted_iota(
        jnp.int32, (L, L), 1
    )
    first = lax.broadcasted_iota(jnp.int32, (L, L), 1) < HD
    grown = dot_l(jnp.exp(cum), mats[:, :width])
    far = grown * dot(cb, sin[0], 1, 1)
    for pair in range(heads // 2):
        cols = slice(pair * L, pair * L + L)
        x = acts[pair].astype(BF)
        got = []
        for h in (2 * pair, 2 * pair + 1):
            gap = jnp.where(lower, cum[:, h : h + 1] - cum_t[h : h + 1, :], -1e30)
            mix = scores * jnp.exp(gap) * steps_t[h : h + 1, :]
            got.append(dot(mix.astype(BF), x))
        y_o[:, cols] = jnp.where(first, got[0], got[1]) + far[:, cols]


def gate_body(
    level, meta, pre, cum, pfx, y, gate, gn, before, through, load, vecs, mats,
    mixed_o, sums_o, incoming,
):
    width = vecs.shape[1] - 2 * L
    ones = jnp.ones((8, width), BF)

    @pl.when(pl.program_id(0) == 0)
    def _():
        incoming[...] = final_link(meta, level, False, before, through, load).astype(BF)

    reach = dot_l(jnp.exp(cum[...]) * pfx[0][0:1, :], mats[:, :width])
    cv = pre[:, width + L :]
    cb = (cv * sigmoid(cv)).astype(BF)
    far = reach * dot(cb, incoming[...], 1, 1)
    squares, crosses = [], []
    for x0 in range(0, width, L):
        cols = slice(x0, x0 + L)
        v = pre[:, cols]
        mixed = y[:, cols] + far[:, cols] + vecs[5:6, cols] * (v * sigmoid(v))
        mixed_o[:, cols] = mixed
        g = gate[:, cols].astype(F32)
        gated = mixed * (g * sigmoid(g))
        squares.append(gated * gated)
        crosses.append(gn[:, cols].astype(F32) * vecs[6:7, cols] * gated)
    square = dot_r(ones, jnp.concatenate(squares, axis=1), 1, 1)
    cross = dot_r(ones, jnp.concatenate(crosses, axis=1), 1, 1)
    row = lax.broadcasted_iota(jnp.int32, (8, L), 0)
    sums_o[0] = jnp.where(row == 0, square, cross)


def back_gate_body(
    count, meta, pre, cum_r, mixed_r, gate, gn, sums, sums2, thr, vecs, mats,
    normout_o, gm_o, ggr_o, gs_o, toward_o, load_o, sfx_o, acc_o, gstate, prod, acc,
):
    i = pl.program_id(0)
    c = count - 1 - i
    width = vecs.shape[1] - 2 * L
    heads = width // HD
    keep = jnp.where(meta[2 + c] == 0, 1.0, 0.0)

    @pl.when(i == 0)
    def _():
        gstate[...] = jnp.zeros_like(gstate)
        prod[...] = jnp.ones_like(prod)
        acc[...] = jnp.zeros_like(acc)

    both = sums[0] + sums2[0]
    square = jnp.broadcast_to(both[0:1, :], (L, L)).T
    cross = jnp.broadcast_to(both[1:2, :], (L, L)).T
    scale = lax.rsqrt(square * (1.0 / DI) + EPS)
    cubed = scale * scale * scale * cross * (1.0 / DI)
    cum = cum_r[...]
    total = cum[L - 1 : L, :]
    grown = dot_l(jnp.exp(cum), mats[:, :width])
    cv = pre[:, width + L :]
    cb = (cv * sigmoid(cv)).astype(BF)
    moved = []
    for x0 in range(0, width, L):
        cols = slice(x0, x0 + L)
        v = pre[:, cols]
        inner = v * sigmoid(v)
        g = gate[:, cols].astype(F32)
        s = sigmoid(g)
        silu = g * s
        mixed = mixed_r[:, cols]
        gated = mixed * silu
        ng = vecs[6:7, cols]
        gnv = gn[:, cols].astype(F32)
        scaled = gated * scale
        normout_o[:, cols] = (scaled * ng).astype(BF)
        gg = scale * (gnv * ng) - gated * cubed
        gm = gg * silu
        gm_o[:, cols] = gm.astype(BF)
        ggr_o[:, cols] = (gg * mixed * (s + silu * (1.0 - s))).astype(BF)
        acc[0:8, cols] += eights(gnv * scaled)
        acc[8:16, cols] += eights(gm * inner)
        moved.append((gm * grown[:, cols]).astype(BF))
    leaving = gstate[...]
    gs_o[0] = leaving.astype(BF)
    here = prod[...]
    sfx_o[0] = here
    dec = jnp.exp(total)
    entering = per_head(dec, heads) * leaving + dot(jnp.concatenate(moved, axis=1), cb, 0, 0)
    entering = entering * keep
    gstate[...] = entering
    prod[...] = here * dec * keep

    @pl.when(i == count - 1)
    def _():
        toward_o[...] = entering
        pack(load_o, entering, thr[...])
        row = lax.broadcasted_iota(jnp.int32, (8, width), 0)
        acc_o[...] = jnp.where(
            row == 0,
            jnp.sum(acc[0:8, :], axis=0, keepdims=True),
            jnp.sum(acc[8:16, :], axis=0, keepdims=True),
        )


def head_product(a, b, spread):
    rows = dot(jnp.ones((8, L), BF), (a * b).astype(BF), 1, 1)
    return dot_l(rows, spread, 1, 1)[0:1, :]


def back_within_body(
    meta, pre, step, cum_r, sin, pfx, gs, gm_r, incoming, vecs, hv, mats,
    ginner_o, gbc_o, glog_o, gst_o,
):
    width = vecs.shape[1] - 2 * L
    heads = width // HD
    acts = act_parts(pre, width)
    bb, cb = acts[-2].astype(BF), acts[-1].astype(BF)
    scores = dot(cb, bb, 1, 1)
    steps = softplus(step[...].astype(F32) + hv[0:1, :])
    cum = cum_r[...]
    total = cum[L - 1 : L, :]
    cum_t, steps_t = cum.T, steps.T
    row = lax.broadcasted_iota(jnp.int32, (L, L), 0)
    col = lax.broadcasted_iota(jnp.int32, (L, L), 1)
    lower = row >= col
    first = col < HD
    e = jnp.exp(cum)
    wd = jnp.exp(total - cum)
    grown = dot_l(e, mats[:, :width])
    weights = dot_l(wd * steps, mats[:, :width])
    gsb = gs[0]
    entering = sin[0].astype(F32) + per_head(pfx[0][0:1, :], heads) * incoming[...].astype(F32)
    eb = entering.astype(BF)
    u = dot(bb, gsb, 1, 1)
    v = dot(cb, eb, 1, 1)
    inner = jnp.concatenate(acts[: width // L], axis=1)
    gm = gm_r[...].astype(F32)
    seen = dot((inner * u).astype(BF), mats[:, :width], 1, 1)
    passed = dot((gm * v).astype(BF), mats[:, :width], 1, 1) * e
    gb = dot((inner * weights).astype(BF), gsb)
    gc = dot((gm * grown).astype(BF), eb)
    through = head_product(gsb.astype(F32), entering, mats[:, :width]) * jnp.exp(total)
    dscores = jnp.zeros((L, L), F32)
    rowsums = jnp.zeros((L, L), F32)
    colsums = jnp.zeros((L, L), F32)
    for pair in range(heads // 2):
        cols = slice(pair * L, pair * L + L)
        xb = acts[pair].astype(BF)
        gmb = gm_r[:, cols]
        got = []
        for h in (2 * pair, 2 * pair + 1):
            mine = first if h % 2 == 0 else jnp.logical_not(first)
            gmh = jnp.where(mine, gm[:, cols], 0.0).astype(BF)
            dm = dot(gmh, xb, 1, 1)
            gap = jnp.where(lower, cum[:, h : h + 1] - cum_t[h : h + 1, :], -1e30)
            decay = jnp.exp(gap)
            st = steps_t[h : h + 1, :]
            t1 = dm * decay
            dscores = dscores + t1 * st
            gp = t1 * scores
            rowsums = jnp.where(col == h, jnp.sum(gp * st, axis=1, keepdims=True), rowsums)
            colsums = jnp.where(row == h, jnp.sum(gp, axis=0, keepdims=True), colsums)
            mix = (scores * decay * st).astype(BF)
            got.append(dot(mix, gmb, 0, 0))
        ginner_o[:, cols] = (
            jnp.where(first, got[0], got[1])
            + weights[:, cols] * u[:, cols]
            + vecs[5:6, cols] * gm[:, cols]
        )
    db = dscores.astype(BF)
    gbc_o[:, :L] = gb + dot(db, cb, 0, 0)
    gbc_o[:, L:] = gc + dot(db, bb)
    direct = colsums.T
    seen = seen * wd
    gst_o[...] = direct + seen
    later = rowsums - direct * steps + passed
    tr = mats[:, width:]
    glog_o[...] = (
        dot_r(tr, later, 0, 0) + dot_r(tr, steps * seen) - steps * seen + through
    )


def crossing(vecs, later):
    row = lax.broadcasted_iota(jnp.int32, (16, later.shape[1]), 0)
    extra = jnp.zeros((16, later.shape[1]), F32)
    for j in range(1, KERNEL):
        for t in range(j):
            part = vecs[3 - j : 4 - j, :] * later[t : t + 1, :]
            extra = extra + jnp.where(row == 16 - j + t, part, 0.0)
    return extra


def back_conv_body(
    count, level, meta, cat, rim, pre, step, cum_r, sin, pfx, sfx, ginner_r, gbc_r, glog_r, gst_r,
    incoming, before, through, load, vecs, hv, mats,
    gcat_o, gsr_o, head_o, extra_o, acc_o, hacc_o, buf, acc, hacc, outgoing,
):
    i = pl.program_id(0)
    c = count - 1 - i
    width = vecs.shape[1] - 2 * L
    heads = width // HD
    keep_next = jnp.where(meta[3 + c] == 0, 1.0, 0.0)
    keep = jnp.where(meta[2 + c] == 0, 1.0, 0.0)

    @pl.when(i == 0)
    def _():
        buf[L : L + 8, :] = jnp.zeros_like(buf[L : L + 8, :])
        acc[...] = jnp.zeros_like(acc)
        hacc[...] = jnp.zeros_like(hacc)
        outgoing[...] = final_link(meta, level, True, before, through, load)

    @pl.when(i > 0)
    def _():
        buf[L : L + 8, :] = buf[0:8, :] * keep_next

    step_in = step[...].astype(F32) + hv[0:1, :]
    steps = softplus(step_in)
    cum = cum_r[...]
    total = cum[L - 1 : L, :]
    wd = jnp.exp(total - cum)
    weights = dot_l(wd * steps, mats[:, :width])
    far = outgoing[...] * per_head(sfx[0][0:1, :], heads)
    fb = far.astype(BF)
    entering = sin[0].astype(F32) + per_head(pfx[0][0:1, :], heads) * incoming[...].astype(F32)
    through = head_product(far, entering, mats[:, :width]) * jnp.exp(total)
    acts, slopes = [], []
    for x0 in range(0, width + 2 * L, L):
        v = pre[:, x0 : x0 + L]
        s = sigmoid(v)
        a = v * s
        acts.append(a)
        slopes.append(s + a * (1.0 - s))
    bb = acts[-2].astype(BF)
    u = dot(bb, fb, 1, 1)
    inner = jnp.concatenate(acts[: width // L], axis=1)
    seen = dot((inner * u).astype(BF), mats[:, :width], 1, 1) * wd
    gb = dot((inner * weights).astype(BF), fb)
    glog = glog_r[...] + dot_r(mats[:, width:], steps * seen) - steps * seen + through
    gsi = (gst_r[...] + seen + glog * hv[1:2, :]) * sigmoid(step_in)
    gsr_o[...] = gsi.astype(BF)
    hacc[0:8, :] += eights(glog * steps * hv[1:2, :])
    hacc[8:16, :] += eights(gsi)
    for k, x0 in enumerate(range(0, width + 2 * L, L)):
        cols = slice(x0, x0 + L)
        if x0 < width:
            g = ginner_r[:, cols] + weights[:, cols] * u[:, cols]
        elif x0 == width:
            g = gbc_r[:, :L] + gb
        else:
            g = gbc_r[:, L:]
        g = g * slopes[k]
        buf[0:L, cols] = g
        acc[32:40, cols] += eights(g)
        here = cat[:, cols].astype(F32)
        out = vecs[3:4, cols] * g
        acc[24:32, cols] += eights(g * here)
        for j in range(1, KERNEL):
            moved = buf[j : j + L, cols]
            out = out + vecs[3 - j : 4 - j, cols] * moved
            acc[24 - 8 * j : 32 - 8 * j, cols] += eights(moved * here)
        gcat_o[:, cols] = out.astype(BF)
    @pl.when(i == count - 1)
    def _():
        head_o[...] = buf[0:8, :]
        past = rim[...].astype(F32)[8:16, :] * keep
        now = buf[0:8, :]
        extra_o[...] = crossing(vecs, now * keep).astype(BF)
        row = lax.broadcasted_iota(jnp.int32, now.shape, 0)
        result = jnp.zeros_like(now)
        for k in range(5):
            part = jnp.sum(acc[8 * k : 8 * k + 8, :], axis=0, keepdims=True)
            j = 3 - k
            if 1 <= j <= 3:
                for t in range(j):
                    part = part + now[t : t + 1, :] * past[8 + t - j : 9 + t - j, :]
            result = jnp.where(row == k, part, result)
        acc_o[...] = result
        hrow = lax.broadcasted_iota(jnp.int32, (8, L), 0)
        hacc_o[...] = jnp.where(
            hrow == 0,
            jnp.sum(hacc[0:8, :], axis=0, keepdims=True),
            jnp.sum(hacc[8:16, :], axis=0, keepdims=True),
        )


def dgrad_body(k, ggr, gcat, gsr, wzx, wbc, wst, *outs):
    width = wzx.shape[2]

    def one(out):
        r = dot(ggr[...], wzx[0], 1, 1)
        r = r + dot(gcat[:, :width], wzx[1], 1, 1)
        r = r + dot(gcat[:, width : width + L], wbc[0], 1, 1)
        r = r + dot(gcat[:, width + L :], wbc[1], 1, 1)
        r = r + dot(gsr[...], wst[...])
        out[...] = r.astype(BF)

    for j in range(k):
        pl.when(pl.program_id(0) == j)(functools.partial(one, outs[j]))


def outproj_body(k, normout, wout, *outs):
    def one(out):
        out[...] = dot(normout[...], wout[...]).astype(BF)

    for j in range(k):
        pl.when(pl.program_id(0) == j)(functools.partial(one, outs[j]))


def rows_times(body, frames_n, share, d, rows, consts, name):
    k = frames_n
    outs = launch(
        functools.partial(body, k),
        [*rows, *consts],
        [pl.BlockSpec((share, r.shape[1]), lambda i: (k - 1 - i, 0)) for r in rows]
        + [whole(a) for a in consts],
        [shaped((share, d), BF)] * k,
        [pl.BlockSpec((share, d), lambda i: (0, 0))] * k,
        name,
        grid=(k,),
        vmem=20,
    )
    return list(outs)[::-1]


def hold_body(x, o):
    o[...] = x[...]


def hold(x, *deps):
    return simple(hold_body, [x], [shaped(x.shape, x.dtype)], "hold", deps=deps)[0]


def add_body(a, b, o):
    o[...] = (a[...].astype(F32) + b[...].astype(F32)).astype(o.dtype)


def add(a, b):
    return simple(add_body, [a, b], [shaped(a.shape, a.dtype)], "add")[0]


def swap(x, axis, mask):
    count = lax.axis_size(axis)
    return lax.ppermute(x, axis, [(i, i ^ mask) for i in range(count)])


def masks_of(axis):
    masks, mask = [], 1
    while mask < lax.axis_size(axis):
        masks.append(mask)
        mask *= 2
    return masks


def halve_body(slot, level, meta, kept, got, send_o, keep_o):
    bit = jnp.bitwise_and(jnp.right_shift(meta[slot], level), 1)
    half = send_o.shape[0]
    for o, b in ((send_o, 1 - bit), (keep_o, bit)):
        rows = pl.ds(pl.multiple_of(b * half, half), half)
        o[...] = (kept[rows, :].astype(F32) + got[rows, :].astype(F32)).astype(BF)


def halve(meta, slot, level, kept, got):
    shape = shaped((kept.shape[0] // 2, kept.shape[1]), BF)
    return simple(
        functools.partial(halve_body, slot, level), [kept, got], [shape, shape], "halve", meta
    )


def join_body(slot, level, meta, own, got, o):
    bit = jnp.bitwise_and(jnp.right_shift(meta[slot], level), 1)
    half = own.shape[0]
    o[pl.ds(pl.multiple_of(bit * half, half), half), :] = own[...]
    o[pl.ds(pl.multiple_of((1 - bit) * half, half), half), :] = got[...]


def join(meta, slot, level, own, got):
    shape = shaped((own.shape[0] * 2, own.shape[1]), BF)
    return simple(functools.partial(join_body, slot, level), [own, got], [shape], "join", meta)[0]


def wgrad_body(blocks, half, tails, meta, *refs):
    ins, (send_o, keep_o) = refs[:-2], refs[-2:]
    bit = bit_at(meta, 0)
    i = pl.program_id(0)
    g = jnp.where(i < half, (1 - bit) * half + i, bit * half + i - half)
    for p, tail in enumerate(tails):
        (a, b), ins = ins[:2], ins[2:]
        ta = tb = None
        if tail:
            (ta, tb), ins = ins[:2], ins[2:]
        inside = jnp.logical_and(g >= p * blocks, g < (p + 1) * blocks)

        def into(o, a=a, b=b, ta=ta, tb=tb):
            v = dot(a[...], b[...], 0, 0)
            if ta is not None:
                v = v + dot(ta[...], tb[...], 0, 0)
            o[...] = v.astype(BF)

        pl.when(jnp.logical_and(inside, i < half))(functools.partial(into, send_o))
        pl.when(jnp.logical_and(inside, i >= half))(functools.partial(into, keep_o))


def wgrads(meta, pairs, width, blocks, name):
    half = blocks * len(pairs) // 2
    tokens = pairs[0][0].shape[0]

    def cut(i, m):
        bit = jnp.bitwise_and(m[1], 1)
        g = jnp.where(i < half, (1 - bit) * half + i, bit * half + i - half)
        return (0, lax.rem(g, blocks))

    specs, ins = [], []
    for a, b, which, *more in pairs:
        for pair in [(a, b), tuple(more)]:
            for j, v in enumerate(pair):
                ins.append(v)
                specs.append(
                    pl.BlockSpec((v.shape[0], width), cut if j == which else lambda i, m: (0, 0))
                )
    return launch(
        functools.partial(wgrad_body, blocks, half, [len(p) > 3 for p in pairs]),
        ins,
        specs,
        [shaped((half * width, width), BF)] * 2,
        [
            pl.BlockSpec((width, width), lambda i, m: (jnp.minimum(i, half - 1), 0)),
            pl.BlockSpec((width, width), lambda i, m: (jnp.maximum(i - half, 0), 0)),
        ],
        name,
        grid=(2 * half,),
        meta=meta,
        vmem=20,
    )


def bc_body(meta, normed, gcat, gsr, rim, extra, send_o, keep_o, step_o):
    bit = jnp.bitwise_and(meta[0], 1)
    half = send_o.shape[0]
    for o, b in ((send_o, 1 - bit), (keep_o, bit)):
        cols = pl.ds(pl.multiple_of(b * half, half), half)
        v = dot(normed[:, cols], gcat[...], 0, 0) + dot(rim[:, cols], extra[...], 0, 0)
        o[...] = v.astype(BF)
    step_o[...] = dot(gsr[...], normed[...], 0, 0)[:8]


def bc_wgrad(meta, normed, gcat, gsr, rim, extra, width):
    tokens, d = normed.shape

    def tail(rows):
        return pl.BlockSpec((rows, 2 * L), lambda i, m: (0, width // (2 * L)))

    outs = [shaped((d // 2, 2 * L), BF)] * 2 + [shaped((8, d))]
    return launch(
        bc_body,
        [normed, gcat, gsr, rim, extra],
        [whole(normed), tail(tokens), whole(gsr), whole(rim), tail(16)],
        outs,
        [whole(o) for o in outs],
        "bc_wgrad",
        meta=meta,
        vmem=12,
    )


def wg_out_body(blocks, meta, own, got, wout_o, zx_o):
    bit = bit_at(meta, 0)
    width = wout_o.shape[0]
    for src, side in ((own, bit), (got, 1 - bit)):

        @pl.when(side == 0)
        def _(src=src):
            for k in range(blocks):
                rows = slice(k * width, (k + 1) * width)
                wout_o[:, rows] = src[rows, :].astype(F32)

        @pl.when(side == 1)
        def _(src=src):
            zx_o[0] = src[...].astype(F32)


def wg_out(meta, own, got, d, width):
    return launch(
        functools.partial(wg_out_body, d // width), [own, got], [whole(own), whole(got)],
        [shaped((width, d)), shaped((2, d, width))],
        [pl.BlockSpec((width, d), lambda i, m: (0, 0)),
         pl.BlockSpec((1, d, width), lambda i, m: (0, 0, 0))],
        "out_weights", meta=meta, vmem=20, token=False,
    )


def rows_body(meta, own, got, *rest):
    zx_o = rest[-1]
    bit = bit_at(meta, 0)
    half = own.shape[0]
    zx_o[0, pl.ds(pl.multiple_of(bit * half, half), half), :] = own[...].astype(F32)
    zx_o[0, pl.ds(pl.multiple_of((1 - bit) * half, half), half), :] = got[...].astype(F32)


def rows_of(meta, own, got, which, d, width, old):
    ins, specs, aliases = [own, got], [whole(own), whole(got)], {}
    if old is not None:
        ins.append(old)
        specs.append(pl.BlockSpec(memory_space=pl.ANY))
        aliases = {2: 0}
    return launch(
        rows_body, ins, specs, [shaped((2, d, width))],
        [pl.BlockSpec((1, d, width), lambda i, m: (which, 0, 0))],
        "zx_weights", meta=meta, aliases=aliases, vmem=16, token=False,
    )[0]


def bc_out_body(meta, own, got, o):
    bit = jnp.bitwise_and(meta[0], 1)
    half = own.shape[0]
    for v, b in ((own, bit), (got, 1 - bit)):
        rows = pl.ds(pl.multiple_of(b * half, half), half)
        o[0, rows, :] = v[:, :L].astype(F32)
        o[1, rows, :] = v[:, L:].astype(F32)


def patch_body(meta, gcat, ahead, vecs, o):
    count = meta.shape[0] - 3
    keep = jnp.where(meta[2 + count] == 0, 1.0, 0.0)
    o[...] = (gcat[...].astype(F32) + crossing(vecs, ahead[...] * keep)).astype(BF)


def patched(meta, gcat, ahead, vecs, share, group):
    wide = gcat.shape[1]

    def spot(i, m):
        return ((jnp.bitwise_xor(m[0], group - 1) + 1) * (share // 16) - 1, 0)

    return launch(
        patch_body,
        [gcat, ahead, vecs],
        [pl.BlockSpec((16, wide), spot), whole(ahead), whole(vecs)],
        [shaped(gcat.shape, BF)],
        [pl.BlockSpec((16, wide), spot)],
        "patch",
        meta=meta,
        aliases={0: 0},
        token=False,
    )[0]


def layer_body(tok, a, b, o):
    o[...] = (tok[...].astype(F32) + (a[...].astype(F32) + b[...].astype(F32))).astype(BF)


def tokens_body(tok, cot, a, b, gain, conv, gt_o, acc_o):
    x = tok[...].astype(F32)
    rstd = lax.rsqrt(jnp.mean(x * x, axis=1, keepdims=True) + EPS)
    unit = x * rstd
    gnormed = a[...].astype(F32) + b[...].astype(F32)
    gunit = gnormed * gain[...]
    gt_o[...] = cot[...].astype(F32) + rstd * (
        gunit - unit * jnp.mean(gunit * unit, axis=1, keepdims=True)
    )
    d = x.shape[1]
    acc_o[...] = jnp.zeros_like(acc_o)
    sums = jnp.sum(gnormed * unit, axis=0, keepdims=True)
    for k in range(d // ROW):
        acc_o[k : k + 1, :] = sums[:, k * ROW : (k + 1) * ROW]
    acc_o[d // ROW : d // ROW + 5, :] = conv[0:5, conv.shape[1] - ROW :]


def halves_of(v):
    hi, lo = split(v)
    return jnp.concatenate([hi, lo], axis=0)


def whole_of(v):
    n = v.shape[0] // 2
    v = v.astype(F32)
    return v[:n] + v[n:]


def lead_body(bc, shared, o):
    rows = bc.shape[0]
    o[:rows, :] = bc[...]
    o[rows:, :] = halves_of(shared[...])


def misc_halve_body(level, meta, kept, shared, got, send_o, keep_o, shared_o):
    bit = jnp.bitwise_and(jnp.right_shift(meta[0], level), 1)
    half = keep_o.shape[0]
    total = shared[...] + whole_of(got[2 * half :, :])
    shared_o[...] = total
    for o, b in ((send_o, 1 - bit), (keep_o, bit)):
        rows = pl.ds(pl.multiple_of(b * half, half), half)
        o[0:half, :] = (kept[rows, :].astype(F32) + got[rows, :].astype(F32)).astype(BF)
    send_o[half:, :] = halves_of(total)


def misc_pack_body(kept, shared, got, step, conv, gate, head, o):
    rows = kept.shape[0]
    o[0:rows, :] = (kept[...].astype(F32) + got[0:rows, :].astype(F32)).astype(BF)
    d = step.shape[1]
    at = rows
    for k in range(d // ROW):
        o[at : at + 8, :] = step[:, k * ROW : (k + 1) * ROW].astype(BF)
        at += 8
    total = shared[...] + whole_of(got[rows:, :])
    width = gate.shape[1]
    parts = [total]
    for ref, first, n in ((conv, 0, 5), (gate, 0, 2)):
        for k in range(width // ROW):
            parts.append(ref[first : first + n, k * ROW : (k + 1) * ROW])
    used = 7 * (width // ROW)
    parts.append(jnp.concatenate([head[0:1, :], head[1:2, :]], axis=1))
    parts.append(jnp.zeros((31 - used, ROW), F32))
    o[at:, :] = halves_of(jnp.concatenate(parts, axis=0))


def misc_sum(a, b, plain_rows):
    first = a[0:plain_rows, :].astype(F32) + b[0:plain_rows, :].astype(F32)
    return first, whole_of(a[plain_rows:, :]) + whole_of(b[plain_rows:, :])


def misc_add_body(plain_rows, a, b, o):
    first, rest = misc_sum(a, b, plain_rows)
    o[0:plain_rows, :] = first.astype(BF)
    o[plain_rows:, :] = halves_of(rest)


def misc_finish_body(bc_rows, a, b, mats, bcw_o, gain_o, bc_o, bcb_o, step_o, taps_o, bias_o,
                     sb_o, dl_o, sk_o, ng_o):
    d, width, heads = gain_o.shape[1], taps_o.shape[1], sb_o.shape[1]
    n = d // ROW
    first, rest = misc_sum(a, b, bc_rows + 8 * n)
    bcw_o[...] = first[0:bc_rows].astype(BF)
    for k in range(n):
        cols = slice(k * ROW, (k + 1) * ROW)
        at = bc_rows + 8 * k
        step_o[:, cols] = first[at : at + heads]
        gain_o[:, cols] = rest[k : k + 1]
    for k in range(2):
        v = rest[n : n + 5, k * L : (k + 1) * L]
        bc_o[k] = v[0:4]
        bcb_o[k : k + 1, :] = v[4:5]
    at = 16
    m = width // ROW
    gates = []
    for k in range(m):
        cols = slice(k * ROW, (k + 1) * ROW)
        taps_o[:, cols] = rest[at : at + 4]
        bias_o[:, cols] = rest[at + 4 : at + 5]
        at += 5
    for k in range(m):
        cols = slice(k * ROW, (k + 1) * ROW)
        ng_o[:, cols] = rest[at : at + 1]
        gates.append(jnp.broadcast_to(rest[at + 1 : at + 2], (8, ROW)))
        at += 2
    sk = dot_l(jnp.concatenate(gates, axis=1), mats[:, :width], 1, 1)
    sk_o[...] = sk[0:1, :heads]
    dl_o[...] = rest[at : at + 1, :heads]
    sb_o[...] = rest[at : at + 1, L : L + heads]


class Plan:
    def __init__(self):
        self.now, self.links, self.chains, self.done = 0.0, {}, [], set()

    def add(self, name, priority, chain, spend=0.0):
        self.chains.append([name, priority, chain, None])
        self.now += spend
        self.step(self.chains[-1])

    def step(self, entry):
        if entry[3] and entry[3][0] is None:
            space()
        try:
            link, us, latency, spend = next(entry[2])
        except StopIteration:
            self.chains.remove(entry)
            self.done.add(entry[0])
            return
        if link is None:
            entry[3] = (us, 0.0, spend)
            return
        start = max(self.now, self.links.get(link, 0.0))
        self.links[link] = start + us
        entry[3] = (None, start + us + latency, spend)
        self.now += 1.0

    def ready(self, entry):
        name, at, _ = entry[3]
        if name is not None:
            return 0.0 if name in self.done else 1e9
        return at

    def run(self, until=None):
        while self.chains and (until is None or until not in self.done):
            able = [e for e in self.chains if self.ready(e) <= self.now]
            if able:
                entry = min(able, key=lambda e: e[1])
            else:
                entry = min(self.chains, key=self.ready)
                self.now = self.ready(entry)
            self.now += entry[3][2]
            self.step(entry)


def on_device(
    tokens_in,
    grad_out,
    scene_offsets,
    input_gain,
    weight_zx,
    weight_bc,
    weight_step,
    conv_inner,
    conv_inner_bias,
    conv_bc,
    conv_bc_bias,
    step_bias,
    decay_log,
    skip_weight,
    norm_gain,
    weight_out,
):
    share, d = tokens_in.shape
    group = lax.axis_size("tensor")
    tokens = share * group
    heads = step_bias.shape[0]
    width = norm_gain.shape[0]
    wide = width + 2 * L
    count = tokens // L
    per = share // L
    half = group // 2
    me = lax.axis_index("tensor")
    place = lax.axis_index("dp")

    heads_pos = place * tokens + jnp.arange(count + 1, dtype=jnp.int32) * L
    starts = jnp.any(heads_pos[:, None] == scene_offsets[None, :], axis=1).astype(jnp.int32)
    meta = jnp.concatenate([me[None].astype(jnp.int32), place[None].astype(jnp.int32), starts])
    masks, tmasks = masks_of("dp"), masks_of("tensor")
    levels = len(masks)

    LAST.clear()
    gain = input_gain[None]
    prep_ins = [conv_inner, conv_inner_bias[None], conv_bc, conv_bc_bias, step_bias[None],
                decay_log[None], skip_weight[None], norm_gain[None], weight_step.T]
    prep_outs = [shaped((8, wide)), shaped((8, L)), shaped((L, width + L), BF),
                 shaped((L, d), BF)]
    vecs, hv, mats, wst = launch(
        prep_body,
        [pltpu.with_memory_space_constraint(a, pltpu.HBM) for a in prep_ins],
        [whole(a) for a in prep_ins],
        prep_outs, [whole(o) for o in prep_outs], "prep", vmem=4,
    )
    def place_of(c, meta):
        if per == 1:
            return lax.bitwise_xor(c, meta[0])
        return lax.bitwise_xor(lax.div(c, per), meta[0]) * per + lax.rem(c, per)

    def stretched(body, name, ins, outs, scratch, reverse, vmem, flops, span=None, old=()):
        begin, length = span or (0, count)

        def order(i):
            return count - 1 - i - begin if reverse else i + begin

        def spec(kind, shape):
            if kind == "rows":
                return pl.BlockSpec((L, shape[1]), lambda i, m: (place_of(order(i), m), 0))
            if kind == "each":
                return pl.BlockSpec((1, *shape[1:]), lambda i, m: (order(i), 0, 0))
            return pl.BlockSpec(shape, lambda i, m: (0,) * len(shape))

        n = len(ins)

        def run(*refs):
            body(*refs[: 1 + n], *refs[1 + n + len(old) :])

        return launch(
            run,
            [a for _, a in ins] + list(old),
            [spec(k, a.shape) for k, a in ins] + [pl.BlockSpec(memory_space=pl.ANY)] * len(old),
            [shaped(s, t) for _, s, t in outs],
            [spec(k, s) for k, s, _ in outs],
            name,
            grid=(length,),
            meta=meta,
            scratch=scratch,
            aliases={n + j: j for j in range(len(old))},
            vmem=vmem,
            flops=0,
        )

    def spread_out(held, keys):
        mask = half // 2
        while mask:
            for f in [f for f in held if f in keys]:
                held[f ^ mask] = swap(held[f], "tensor", mask)
            mask //= 2

    near, far = range(half), range(half, group)
    held = {0: tokens_in}
    arrived = swap(tokens_in, "tensor", half)
    spread_out(held, near)
    dps = lax.axis_size("dp")
    weights = (gain, weight_zx, weight_bc, wst)
    before = project(meta, [held[f] for f in near], [], *weights, tokens, 0, [])
    (last_rows,) = launch(
        lambda tok, _, o: hold_body(tok, o), [tokens_in, before[3]],
        [pl.BlockSpec((16, d), lambda i: (share // 16 - 1, 0)), pl.BlockSpec(memory_space=pl.ANY)],
        [shaped((16, d), BF)], [pl.BlockSpec((16, d), lambda i: (0, 0))], "last_rows",
    )
    past = [
        lax.ppermute(
            last_rows,
            ("dp", "tensor"),
            [(i * group + group - 1, (i + 1) * group + t) for i in range(dps - 1)],
        )
        for t in range(group)
    ]
    space()
    held[half] = hold(arrived, before[3])
    spread_out(held, far)
    before = project(meta, [held[half]], [], *weights, tokens, half, list(before))
    space()
    normed, gate_raw, cat, step_raw, rim, normed_rim = project(
        meta, [held[f] for f in far[1:]], past, *weights, tokens, half + 1, list(before)
    )
    cots = {0: grad_out}
    cots[half] = swap(hold(grad_out, rim), "tensor", half)

    tall = (tokens, L)
    state_shape = (width, L)
    load_shape = (width + 16, L)
    small = (8, L)
    pre, sin, state, load, cum, pfx, decay = stretched(
        states_body,
        "states",
        [("rows", cat), ("rows", step_raw), ("one", rim), ("one", vecs), ("one", hv),
         ("one", mats)],
        [("rows", (tokens, wide), F32), ("each", (count, *state_shape), BF),
         ("one", state_shape, F32), ("one", load_shape, BF), ("rows", tall, F32),
         ("each", (count, 8, L), F32), ("one", small, F32)],
        [pltpu.VMEM((L + 8, wide), F32), pltpu.VMEM(state_shape, F32), pltpu.VMEM(small, F32)],
        False, 10, 2 * tokens * width * L * 3,
    )

    def link(level, reverse, held, load):
        shapes = [load_shape, state_shape, small, state_shape, small]
        out = simple(
            functools.partial(link_body, level, reverse), [*held, load],
            [shaped(s, BF if j == 0 else F32) for j, s in enumerate(shapes)], "link", meta,
        )
        return out[1:], out[0]

    thr = decay
    fresh = [jnp.zeros(state_shape, F32), jnp.ones(small, F32)]
    own = [state, decay, *fresh]
    load = swap(load, "dp", 1)
    (y,) = stretched(
        within_body,
        "within",
        [("rows", pre), ("rows", step_raw), ("rows", cum), ("each", sin), ("one", vecs),
         ("one", hv), ("one", mats)],
        [("rows", (tokens, width), F32)],
        [], False, 10, 2 * tokens * width * L * 6,
    )
    for level in range(levels - 1):
        space()
        own, load = link(level, False, own, load)
        load = swap(load, "dp", masks[level + 1])
        if level == 0:
            space()
            late = {half: hold(cots[half])}
            spread_out(late, far)
            spread_out(cots, near)
            cots.update({f: late[f] for f in far[1:]})
        if level == levels - 2:
            space()
            cot_all, gn = cotangent([cots[f] for f in range(group)], weight_out)
    befores, throughs = own[2:]
    space()
    mixed, sums, incoming = stretched(
        functools.partial(gate_body, levels - 1),
        "gated",
        [("rows", pre), ("rows", cum), ("each", pfx), ("rows", y), ("rows", gate_raw),
         ("rows", gn), ("one", befores), ("one", throughs), ("one", load), ("one", vecs),
         ("one", mats)],
        [("rows", (tokens, width), F32), ("each", (count, 8, L), F32), ("one", state_shape, BF)],
        [], False, 10, 2 * tokens * width * L * 4,
    )
    for mask in tmasks[::-1][:-1]:
        got = swap(sums, "tensor", mask)
        space()
        sums = add(sums, got)
    sums2 = swap(sums, "tensor", 1)
    space()
    normout, gm, ggr, gs, toward, load, sfx, gate_acc = stretched(
        functools.partial(back_gate_body, count),
        "back_gated",
        [("rows", pre), ("rows", cum), ("rows", mixed), ("rows", gate_raw), ("rows", gn),
         ("each", sums), ("each", sums2), ("one", thr), ("one", vecs), ("one", mats)],
        [("rows", (tokens, width), BF), ("rows", (tokens, width), BF),
         ("rows", (tokens, width), BF), ("each", (count, *state_shape), BF),
         ("one", state_shape, F32), ("one", load_shape, BF), ("each", (count, 8, L), F32),
         ("one", (8, width), F32)],
        [pltpu.VMEM(state_shape, F32), pltpu.VMEM(small, F32), pltpu.VMEM((16, width), F32)],
        True, 10, 2 * tokens * width * L * 3,
    )

    plan = Plan()
    kept = {}
    blocks = d // width
    axes = {"dp": ["y", "z", "z"] + ["z"] * levels, "tensor": ["core", "x"] + ["x"] * levels}
    spans = {"dp": [1, 1, 2] + [2] * levels, "tensor": [1, 1] + [2] * levels}
    hops = {"core": 1.0, "x": 4.0, "y": 4.0, "z": 4.5}
    rates = {"core": 600.0, "x": 90.0, "y": 90.0, "z": 90.0}

    def moved(x, axis, level):
        link_name = axes[axis][level]
        size = 2 * x.size * x.dtype.itemsize * spans[axis][level] / 1e3
        got = swap(x, axis, 1 << level)
        return got, link_name, size / rates[link_name], hops[link_name]

    def halving(key, axis, send, keep, first=0):
        top = len(masks_of(axis))
        slot = 1 if axis == "dp" else 0
        for level in range(first, top):
            got, *way = moved(send, axis, level)
            yield (*way, 0.8)
            if level == top - 1:
                kept[key] = add(keep, got)
            else:
                send, keep = halve(meta, slot, level + 1, keep, got)

    def doubling(key, axis, x, finish):
        slot = 1 if axis == "dp" else 0
        for level in range(len(masks_of(axis)) - 1, -1, -1):
            got, *way = moved(x, axis, level)
            yield (*way, 2.0 if level == 0 else 0.7)
            if level == 0:
                if key == "I":
                    yield (None, "WG", 0.0, 2.0)
                finish(x, got)
            else:
                x = join(meta, slot, level, x, got)

    def weights_chain(key, pairs, name, finish):
        send, keep = wgrads(meta, pairs, width, blocks, name)
        yield from halving(key, "dp", send, keep)
        yield from doubling(key, "dp", kept[key], finish)

    def inner_out(own, got):
        kept["zx"] = rows_of(meta, own, got, 1, d, width, kept["zx"])

    def out_gate(own, got):
        kept["wout"], kept["zx"] = wg_out(meta, own, got, d, width)

    def first_links():
        own = [toward, thr, *fresh]
        load = first_load
        for level in range(levels):
            got, *way = moved(load, "dp", level)
            if level == levels - 1:
                kept["links"] = (*own[2:], got)
                yield (*way, 0.0)
            else:
                yield (*way, 1.0)
                own, load = link(level, True, own, got)

    def within_part(begin, length):
        kept["within"] = stretched(
            back_within_body,
            "back_within",
            [("rows", pre), ("rows", step_raw), ("rows", cum), ("each", sin), ("each", pfx),
             ("each", gs), ("rows", gm), ("one", incoming), ("one", vecs), ("one", hv),
             ("one", mats)],
            [("rows", (tokens, width), F32), ("rows", (tokens, 2 * L), F32), ("rows", tall, F32),
             ("rows", tall, F32)],
            [], True, 12, 2 * tokens * width * L * 12, (begin, length), kept.get("within", ()),
        )

    def within_chain():
        part = count // 2
        for begin in range(0, count, part):
            yield (None, "begin", 0.0, 6.0)
            within_part(begin, part)

    def scattered(key, frames_in):
        sums_in = []
        for first in (half, 0):
            part = dict(enumerate(frames_in[first : first + half]))
            mask, level = 1, 0
            while mask < half:
                sent = [(f, moved(part.pop(f), "tensor", level)) for f in list(part) if f & mask]
                for f, (got, *way) in sent:
                    yield (*way, 0.7)
                    part[f ^ mask] = add(part[f ^ mask], got)
                mask, level = 2 * mask, level + 1
            sums_in.append(part[0])
            if first:
                got, *way = moved(part[0], "tensor", level)
                crossing_way = way
                sums_in[0] = got
        kept[key] = (sums_in[1], sums_in[0])
        yield (*crossing_way, 1.6)

    def branch_chain():
        yield (None, "begin", 0.0, 2.0)
        branch = rows_times(
            outproj_body, group, share, d, [normout], [weight_out], "outproj"
        )
        yield from scattered("branch", branch)
        (kept["layer"],) = simple(
            layer_body, [tokens_in, *kept["branch"]], [shaped((share, d), BF)], "layer"
        )

    def tokens_chain():
        ahead = lax.ppermute(kept["head"], "dp", [(i + 1, i) for i in range(dps - 1)])
        yield ("z", 0.5, 5.0, 5.4)
        gcat = patched(meta, kept["gcat"], ahead, vecs, share, group)
        grads = rows_times(
            dgrad_body, group, share, d, [ggr, gcat, kept["gsr"]], [weight_zx, weight_bc, wst],
            "dgrad",
        )
        yield from scattered("grad", grads)
        kept["tokens"], shared = simple(
            tokens_body, [tokens_in, grad_out, *kept["grad"], gain, kept["conv_acc"]],
            [shaped((share, d)), shaped((16, ROW))], "tokens", None, 12,
        )
        yield (None, "bc", 0.0, 0.5)
        send, keep = kept["bc"]
        (load,) = simple(lead_body, [send, shared], [shaped((send.shape[0] + 32, ROW), BF)], "lead")
        for level in range(len(tmasks)):
            got, *way = moved(load, "tensor", level)
            yield (*way, 0.6)
            if level < len(tmasks) - 1:
                rows = keep.shape[0] // 2
                load, keep, shared = simple(
                    functools.partial(misc_halve_body, level + 1), [keep, shared, got],
                    [shaped((rows + 32, ROW), BF), shaped((rows, ROW), BF), shaped((16, ROW))],
                    "misc_halve", meta,
                )
        rows = keep.shape[0]
        flat = rows + 8 * (d // ROW)
        (load,) = simple(
            misc_pack_body,
            [keep, shared, got, kept["step_acc"], kept["conv_acc"], gate_acc, kept["head_acc"]],
            [shaped((flat + 96, ROW), BF)], "misc_pack",
        )
        for level in range(levels):
            got, *way = moved(load, "dp", level)
            yield (*way, 0.6)
            if level < levels - 1:
                (load,) = simple(
                    functools.partial(misc_add_body, flat), [load, got],
                    [shaped(load.shape, BF)], "misc_add",
                )
        outs = [(1, d), (2, 4, L), (2, L), (heads, d), (4, width), (1, width), (1, heads),
                (1, heads), (1, heads), (1, width)]
        total, *kept["small"] = simple(
            functools.partial(misc_finish_body, rows), [load, got, mats],
            [shaped((rows, ROW), BF)] + [shaped(s) for s in outs], "misc_finish",
        )

        def finish(own, got):
            (kept["bc_out"],) = simple(
                bc_out_body, [own, got], [shaped((2, d, L))], "bc_weights", meta
            )

        yield from doubling("bc", "tensor", total, finish)

    def bc_chain():
        yield (None, "begin", 0.0, 1.7)
        send, keep, kept["step_acc"] = bc_wgrad(
            meta, normed, kept["gcat"], kept["gsr"], normed_rim, kept["extra"], width
        )
        kept["bc"] = (send, keep)

    plan.done.add("begin")
    first_load = load
    plan.add("links", 0, first_links())
    plan.add(
        "WG", 5,
        weights_chain("WG", [(normout, cot_all, 1), (normed, ggr, 0)], "out_wgrad", out_gate),
        4.3,
    )
    plan.add("within", 8, within_chain())
    plan.add("branch", 9, branch_chain())
    plan.run("links")
    plan.run("within")
    space()
    befores, throughs, load = kept["links"]
    ginner, gbc, glog, gst = kept["within"]
    gcat, gsr, head, extra, conv_acc, head_acc = stretched(
        functools.partial(back_conv_body, count, levels - 1),
        "back_conv",
        [("rows", cat), ("one", rim), ("rows", pre), ("rows", step_raw), ("rows", cum),
         ("each", sin), ("each", pfx), ("each", sfx), ("rows", ginner), ("rows", gbc),
         ("rows", glog), ("rows", gst), ("one", incoming), ("one", befores), ("one", throughs),
         ("one", load), ("one", vecs), ("one", hv), ("one", mats)],
        [("rows", (tokens, wide), BF), ("rows", tall, BF), ("one", (8, wide), F32),
         ("one", (16, wide), BF), ("one", (8, wide), F32), ("one", small, F32)],
        [pltpu.VMEM((L + 8, wide), F32), pltpu.VMEM((40, wide), F32), pltpu.VMEM((16, L), F32),
         pltpu.VMEM(state_shape, F32)],
        True, 12, 2 * tokens * width * L * 6,
    )
    plan.now += 10.0

    kept.update(head=head, gcat=gcat, gsr=gsr, extra=extra, conv_acc=conv_acc, head_acc=head_acc)
    plan.add(
        "I", 1,
        weights_chain("I", [(normed, gcat, 0, normed_rim, extra)], "inner_wgrad", inner_out),
        2.7,
    )
    plan.add("tokens", 2, tokens_chain())
    plan.add("bc", 3, bc_chain())
    plan.run()

    gain_g, bc_g, bcb_g, step_g, taps_g, bias_g, sb_g, dl_g, sk_g, ng_g = kept["small"]
    return (
        kept["layer"],
        kept["tokens"],
        gain_g[0],
        kept["zx"],
        kept["bc_out"],
        step_g.T,
        taps_g,
        bias_g[0],
        bc_g,
        bcb_g,
        sb_g[0],
        dl_g[0],
        sk_g[0],
        ng_g[0],
        kept["wout"],
    )


def solution(mesh):
    rows = P(("dp", "tensor"), None)
    cols = P(None, "tensor")
    one = P("tensor")
    in_specs = (
        rows, rows, P(), P(), P(None, None, "tensor"), P(), cols, cols, one, P(), P(),
        one, one, one, one, P("tensor", None),
    )
    out_specs = (
        rows, rows, P(), P(None, None, "tensor"), P(), cols, cols, one, P(), P(),
        one, one, one, one, P("tensor", None),
    )
    return jax.shard_map(
        on_device, mesh=mesh, in_specs=in_specs, out_specs=out_specs, check_vma=False
    )
```

```python
import functools
from typing import Any, NamedTuple

import jax
import jax.numpy as jnp
from jax import lax
from jax.experimental import pallas as pl
from jax.experimental.pallas import tpu as pltpu
from jax.sharding import PartitionSpec as P

KERNEL = 4
L = 128
HD = 64
DI = 2048
EPS = 1e-05
F32 = jnp.float32
BF = jnp.bfloat16
MIB = 1 << 20
ROW = 256


def dot(a, b, ca=1, cb=0):
    return lax.dot_general(a, b, (((ca,), (cb,)), ((), ())), preferred_element_type=F32)


def split(a):
    hi = a.astype(BF)
    return hi, (a - hi.astype(F32)).astype(BF)


def dot_l(a, b, ca=1, cb=0):
    hi, lo = split(a)
    return dot(hi, b, ca, cb) + dot(lo, b, ca, cb)


def dot_r(a, b, ca=1, cb=0):
    hi, lo = split(b)
    return dot(a, hi, ca, cb) + dot(a, lo, ca, cb)


def sigmoid(v):
    return 0.5 * jnp.tanh(0.5 * v) + 0.5


def softplus(v):
    u = jnp.exp(-jnp.abs(v))
    small = u * (1.0 - u * (0.5 - u * (1.0 / 3.0 - u * 0.25)))
    return jnp.maximum(v, 0.0) + jnp.where(u < 0.02, small, jnp.log(1.0 + u))


def per_head(row, heads):
    return jnp.concatenate(
        [jnp.broadcast_to(row[:, h : h + 1], (HD, L)) for h in range(heads)], axis=0
    )


def eights(v):
    return jnp.sum(v.reshape(v.shape[0] // 8, 8, v.shape[1]), axis=0)


def across_lanes(v, width):
    return jnp.concatenate([v] * (width // L), axis=1) if width > L else v


def whole(a):
    return pl.BlockSpec(a.shape, lambda *_: (0,) * a.ndim)


LAST = []

def launch(body, ins, in_specs, outs, out_specs, name, grid=(1,), meta=None, scratch=(),
           aliases=None, vmem=8, flops=0, token=True):
    ins, in_specs = list(ins), list(in_specs)
    lead = 0 if meta is None else 1
    at = lead + len(ins)
    given = LAST[-1] if LAST and not any(LAST[-1] is a for a in ins) else None
    if given is not None:
        ins.append(given)
        in_specs.append(pl.BlockSpec(memory_space=pl.ANY))

    def run(*refs):
        body(*(refs if given is None else refs[:at] + refs[at + 1 :]))

    results = pl.pallas_call(
        run,
        grid_spec=pltpu.PrefetchScalarGridSpec(
            num_scalar_prefetch=lead,
            grid=grid,
            in_specs=in_specs,
            out_specs=list(out_specs),
            scratch_shapes=list(scratch),
        ),
        out_shape=list(outs),
        input_output_aliases={lead + k: v for k, v in (aliases or {}).items()},
        compiler_params=pltpu.CompilerParams(vmem_limit_bytes=vmem * MIB),
        cost_estimate=pl.CostEstimate(
            flops=flops,
            bytes_accessed=0,
            transcendentals=0,
        ),
        name=name,
    )(*([] if meta is None else [meta]), *ins)
    if token:
        LAST[:] = [min(results, key=lambda a: a.size)]
    return results


def space_body(o):
    o[...] = jnp.zeros_like(o)


def space():
    o = shaped((8, L))
    launch(space_body, [], [], [o], [whole(o)], "space", vmem=1, flops=10**10)


def shaped(shape, dtype=F32):
    return jax.ShapeDtypeStruct(shape, dtype)


def simple(body, ins, outs, name, meta=None, vmem=8, deps=()):
    n = len(ins)

    def run(*refs):
        lead = 0 if meta is None else 1
        body(*refs[: lead + n], *refs[lead + n + len(deps) :])

    return launch(
        run, [*ins, *deps],
        [whole(a) for a in ins] + [pl.BlockSpec(memory_space=pl.ANY)] * len(deps),
        outs, [whole(o) for o in outs], name, meta=meta, vmem=vmem,
    )


def unit_rows(x, gain):
    x = x.astype(F32)
    rstd = lax.rsqrt(jnp.mean(x * x, axis=1, keepdims=True) + EPS)
    return (x * rstd * gain).astype(BF)


def proj_body(k, rims, deps, meta, *refs):
    toks, past = refs[:k], refs[k : k + rims]
    gain, wzx, wbc, wst = refs[k + rims : k + rims + 4]
    outs = refs[k + rims + 4 + deps :]
    normed_o, gate_o, cat_o, step_o = outs[:4]
    width = wzx.shape[2]

    def conv_inputs(normed, out):
        out[:, :width] = dot(normed, wzx[1]).astype(BF)
        out[:, width : width + L] = dot(normed, wbc[0]).astype(BF)
        out[:, width + L :] = dot(normed, wbc[1]).astype(BF)

    def one(j):
        normed = unit_rows(toks[j][...], gain[...])
        normed_o[...] = normed
        conv_inputs(normed, cat_o)
        gate_o[...] = dot(normed, wzx[0]).astype(BF)
        step_o[...] = dot(normed, wst[...], 1, 1).astype(BF)
        if rims and j == 0:
            rim = past[0][...].astype(F32)
            for p in past[1:]:
                rim = rim + p[...].astype(F32)
            normed = unit_rows(rim, gain[...])
            outs[5][...] = normed
            conv_inputs(normed, outs[4])

    for j in range(k):
        pl.when(pl.program_id(0) == j)(functools.partial(one, j))


def project(meta, toks, past, gain, wzx, wbc, wst, total, first, before):
    k = len(toks)
    share, d = toks[0].shape
    width = wzx.shape[2]
    wide = width + 2 * L
    cols = (d, width, wide, L)
    ins = [*toks, *past, gain, wzx, wbc, wst]
    specs = [whole(a) for a in ins]
    out_specs = [pl.BlockSpec((share, c), lambda i, m: (i + first, 0)) for c in cols]
    out_shape = [shaped((total, c), BF) for c in cols]
    if past:
        for c in (wide, d):
            out_specs.append(pl.BlockSpec((16, c), lambda i, m: (0, 0)))
            out_shape.append(shaped((16, c), BF))
    aliases = {len(ins) + j: j for j in range(4)} if before else {}
    return launch(
        functools.partial(proj_body, k, len(past), len(before)),
        ins + before,
        specs + [pl.BlockSpec(memory_space=pl.ANY)] * len(before),
        out_shape,
        out_specs,
        "project",
        grid=(k,),
        meta=meta,
        aliases=aliases,
        vmem=16,
        token=False,
    )


def prep_body(taps, tbias, btaps, bbias, sbias, decay, skip, ngain, wst, vecs, hv, mats, wst_o):
    width = taps.shape[1]
    heads = width // HD
    wst_o[...] = jnp.zeros_like(wst_o)
    wst_o[0:heads, :] = wst[...]
    head = lax.broadcasted_iota(jnp.int32, (L, width), 0)
    lane = lax.broadcasted_iota(jnp.int32, (L, width), 1)
    spread = jnp.where(lax.div(lane, HD) == head, 1.0, 0.0).astype(BF)
    mats[:, :width] = spread
    r = lax.broadcasted_iota(jnp.int32, (L, L), 0)
    c = lax.broadcasted_iota(jnp.int32, (L, L), 1)
    mats[:, width:] = jnp.where(r >= c, 1.0, 0.0).astype(BF)
    hv[...] = jnp.zeros_like(hv)
    hv[0:1, :heads] = sbias[...]
    hv[1:2, :heads] = -jnp.exp(decay[...])
    hv[2:3, :heads] = skip[...]
    vecs[...] = jnp.zeros_like(vecs)
    vecs[0:4, :width] = taps[...]
    vecs[4:5, :width] = tbias[...]
    for k in range(2):
        cols = slice(width + k * L, width + k * L + L)
        vecs[0:4, cols] = btaps[k]
        vecs[4:5, cols] = bbias[k : k + 1, :]
    vecs[5:6, :width] = dot_l(hv[...], spread)[2:3, :]
    vecs[6:7, :width] = ngain[...]


def cot_body(k, *refs):
    cots = refs[:k]
    wout, all_o, gn_o = refs[k:]

    def one(cot):
        v = cot[...]
        all_o[...] = v
        gn_o[...] = dot(v, wout[...], 1, 1).astype(BF)

    for j in range(k):
        pl.when(pl.program_id(0) == j)(functools.partial(one, cots[j]))


def cotangent(cots, wout):
    k = len(cots)
    share, d = cots[0].shape
    width = wout.shape[0]
    return launch(
        functools.partial(cot_body, k),
        [*cots, wout],
        [whole(a) for a in (*cots, wout)],
        [shaped((k * share, d), BF), shaped((k * share, width), BF)],
        [pl.BlockSpec((share, c), lambda i: (i, 0)) for c in (d, width)],
        "cotangent",
        grid=(k,),
        vmem=12,
    )


def act_parts(pre, width):
    out = []
    for x0 in range(0, width + 2 * L, L):
        v = pre[:, x0 : x0 + L]
        out.append(v * sigmoid(v))
    return out


def pack(out, state, decay):
    rows = state.shape[0]
    hi, lo = split(jnp.broadcast_to(decay[0:1, :], (16, L)))
    row = lax.broadcasted_iota(jnp.int32, (16, L), 0)
    out[:rows, :] = state.astype(BF)
    tail = jnp.where(row == 0, hi.astype(F32), jnp.where(row == 1, lo.astype(F32), 0.0))
    out[rows:, :] = tail.astype(BF)


def unpack(load):
    v = load[...].astype(F32)
    rows = v.shape[0] - 16
    return v[:rows], v[rows : rows + 1] + v[rows + 1 : rows + 2]


def bit_at(meta, level):
    return jnp.bitwise_and(jnp.right_shift(meta[1], level), 1)


def is_ahead(meta, level, reverse):
    bit = bit_at(meta, level)
    return jnp.where(bit == (0 if reverse else 1), 1.0, 0.0)


def link_body(level, reverse, meta, state, decay, before, through, load,
              load_o, state_o, decay_o, before_o, through_o):
    theirs, a = unpack(load)
    heads = theirs.shape[0] // HD
    ahead = is_ahead(meta, level, reverse)
    mine = decay[0:1, :]
    t = through[0:1, :]
    before_o[...] = before[...] + per_head(t * ahead, heads) * theirs
    through_o[...] = jnp.broadcast_to(t * (ahead * a + (1.0 - ahead)), (8, L))
    joined = (
        per_head(mine * ahead + (1.0 - ahead), heads) * theirs
        + per_head(a * (1.0 - ahead) + ahead, heads) * state[...]
    )
    state_o[...] = joined
    decay_o[...] = jnp.broadcast_to(mine * a, (8, L))
    pack(load_o, joined, mine * a)


def final_link(meta, level, reverse, before, through, load):
    theirs, _ = unpack(load)
    t = through[0:1, :] * is_ahead(meta, level, reverse)
    return before[...] + per_head(t, theirs.shape[0] // HD) * theirs


def states_body(
    at, meta, cat, step, rim, vecs, hv, mats,
    pre_o, sin_o, end_o, load_o, cum_o, pfx_o, thr_o, buf, state, prod,
):
    width = vecs.shape[1] - 2 * L
    heads = width // HD
    keep = jnp.where(meta[2 + at.c] == 0, 1.0, 0.0)
    before, buf = buf.at[at.other], buf.at[at.sub]

    def follow():
        buf[0:8, :] = before[L : L + 8, :] * keep

    if at.first is None:
        follow()
    else:

        @pl.when(at.first)
        def _():
            buf[0:8, :] = rim[...].astype(F32)[8:16, :] * keep
            state[...] = jnp.zeros_like(state)
            prod[...] = jnp.ones_like(prod)

        pl.when(jnp.logical_not(at.first))(follow)

    buf[8 : 8 + L, :] = cat[...].astype(F32)
    acts = []
    for x0 in range(0, width + 2 * L, L):
        cols = slice(x0, x0 + L)
        v = vecs[4:5, cols] + vecs[3:4, cols] * buf[8 : 8 + L, cols]
        for j in range(1, KERNEL):
            v = v + vecs[3 - j : 4 - j, cols] * buf[8 - j : 8 - j + L, cols]
        pre_o[:, cols] = v
        acts.append(v * sigmoid(v))
    steps = softplus(step[...].astype(F32) + hv[0:1, :])
    cum = dot_r(mats[:, width:], steps * hv[1:2, :])
    cum_o[...] = cum
    total = cum[L - 1 : L, :]
    weights = dot_l(jnp.exp(total - cum) * steps, mats[:, :width])
    inner = jnp.concatenate(acts[: width // L], axis=1)
    local = dot((inner * weights).astype(BF), acts[-2].astype(BF), 0, 0)
    entering = state[...] * keep
    sin_o[0] = entering.astype(BF)
    dec = jnp.exp(total)
    leaving = per_head(dec, heads) * entering + local
    state[...] = leaving
    here = prod[...] * keep
    pfx_o[0] = here
    prod[...] = here * dec

    if at.last is not None:

        @pl.when(at.last)
        def _():
            end_o[...] = leaving
            thr_o[...] = here * dec
            pack(load_o, leaving, here * dec)


def within_body(at, meta, pre, step, cum_r, sin, vecs, hv, mats, y_o):
    width = vecs.shape[1] - 2 * L
    heads = width // HD
    acts = act_parts(pre, width)
    bb, cb = acts[-2].astype(BF), acts[-1].astype(BF)
    scores = dot(cb, bb, 1, 1)
    steps = softplus(step[...].astype(F32) + hv[0:1, :])
    cum = cum_r[...]
    cum_t, steps_t = cum.T, steps.T
    lower = lax.broadcasted_iota(jnp.int32, (L, L), 0) >= lax.broadcasted_iota(
        jnp.int32, (L, L), 1
    )
    first = lax.broadcasted_iota(jnp.int32, (L, L), 1) < HD
    grown = dot_l(jnp.exp(cum), mats[:, :width])
    far = grown * dot(cb, sin[0], 1, 1)
    for pair in range(heads // 2):
        cols = slice(pair * L, pair * L + L)
        x = acts[pair].astype(BF)
        got = []
        for h in (2 * pair, 2 * pair + 1):
            gap = jnp.where(lower, cum[:, h : h + 1] - cum_t[h : h + 1, :], -1e30)
            mix = scores * jnp.exp(gap) * steps_t[h : h + 1, :]
            got.append(dot(mix.astype(BF), x))
        y_o[:, cols] = jnp.where(first, got[0], got[1]) + far[:, cols]


def gate_body(
    level, at, meta, pre, cum, pfx, y, gate, gn, before, through, load, vecs, mats,
    mixed_o, sums_o, incoming,
):
    width = vecs.shape[1] - 2 * L
    ones = jnp.ones((8, width), BF)

    if at.first is not None:

        @pl.when(at.first)
        def _():
            incoming[...] = final_link(meta, level, False, before, through, load).astype(BF)

    reach = dot_l(jnp.exp(cum[...]) * pfx[0][0:1, :], mats[:, :width])
    cv = pre[:, width + L :]
    cb = (cv * sigmoid(cv)).astype(BF)
    far = reach * dot(cb, incoming[...], 1, 1)
    squares, crosses = [], []
    for x0 in range(0, width, L):
        cols = slice(x0, x0 + L)
        v = pre[:, cols]
        mixed = y[:, cols] + far[:, cols] + vecs[5:6, cols] * (v * sigmoid(v))
        mixed_o[:, cols] = mixed
        g = gate[:, cols].astype(F32)
        gated = mixed * (g * sigmoid(g))
        squares.append(gated * gated)
        crosses.append(gn[:, cols].astype(F32) * vecs[6:7, cols] * gated)
    square = dot_r(ones, jnp.concatenate(squares, axis=1), 1, 1)
    cross = dot_r(ones, jnp.concatenate(crosses, axis=1), 1, 1)
    row = lax.broadcasted_iota(jnp.int32, (8, L), 0)
    sums_o[0] = jnp.where(row == 0, square, cross)


def back_gate_body(
    at, meta, pre, cum_r, mixed_r, gate, gn, sums, sums2, thr, vecs, mats,
    normout_o, gm_o, ggr_o, gs_o, toward_o, load_o, sfx_o, acc_o, gstate, prod, acc,
):
    width = vecs.shape[1] - 2 * L
    heads = width // HD
    keep = jnp.where(meta[2 + at.c] == 0, 1.0, 0.0)

    if at.first is not None:

        @pl.when(at.first)
        def _():
            gstate[...] = jnp.zeros_like(gstate)
            prod[...] = jnp.ones_like(prod)
            acc[...] = jnp.zeros_like(acc)

    both = sums[0] + sums2[0]
    square = jnp.broadcast_to(both[0:1, :], (L, L)).T
    cross = jnp.broadcast_to(both[1:2, :], (L, L)).T
    scale = lax.rsqrt(square * (1.0 / DI) + EPS)
    cubed = scale * scale * scale * cross * (1.0 / DI)
    cum = cum_r[...]
    total = cum[L - 1 : L, :]
    grown = dot_l(jnp.exp(cum), mats[:, :width])
    cv = pre[:, width + L :]
    cb = (cv * sigmoid(cv)).astype(BF)
    moved = []
    for x0 in range(0, width, L):
        cols = slice(x0, x0 + L)
        v = pre[:, cols]
        inner = v * sigmoid(v)
        g = gate[:, cols].astype(F32)
        s = sigmoid(g)
        silu = g * s
        mixed = mixed_r[:, cols]
        gated = mixed * silu
        ng = vecs[6:7, cols]
        gnv = gn[:, cols].astype(F32)
        scaled = gated * scale
        normout_o[:, cols] = (scaled * ng).astype(BF)
        gg = scale * (gnv * ng) - gated * cubed
        gm = gg * silu
        gm_o[:, cols] = gm.astype(BF)
        ggr_o[:, cols] = (gg * mixed * (s + silu * (1.0 - s))).astype(BF)
        acc[0:8, cols] += eights(gnv * scaled)
        acc[8:16, cols] += eights(gm * inner)
        moved.append((gm * grown[:, cols]).astype(BF))
    leaving = gstate[...]
    gs_o[0] = leaving.astype(BF)
    here = prod[...]
    sfx_o[0] = here
    dec = jnp.exp(total)
    entering = per_head(dec, heads) * leaving + dot(jnp.concatenate(moved, axis=1), cb, 0, 0)
    entering = entering * keep
    gstate[...] = entering
    prod[...] = here * dec * keep

    if at.last is not None:

        @pl.when(at.last)
        def _():
            toward_o[...] = entering
            pack(load_o, entering, thr[...])
            row = lax.broadcasted_iota(jnp.int32, (8, width), 0)
            acc_o[...] = jnp.where(
                row == 0,
                jnp.sum(acc[0:8, :], axis=0, keepdims=True),
                jnp.sum(acc[8:16, :], axis=0, keepdims=True),
            )


def head_product(a, b, spread):
    rows = dot(jnp.ones((8, L), BF), (a * b).astype(BF), 1, 1)
    return dot_l(rows, spread, 1, 1)[0:1, :]


def back_within_body(
    at, meta, pre, step, cum_r, sin, pfx, gs, gm_r, incoming, vecs, hv, mats,
    ginner_o, gbc_o, glog_o, gst_o,
):
    width = vecs.shape[1] - 2 * L
    heads = width // HD
    acts = act_parts(pre, width)
    bb, cb = acts[-2].astype(BF), acts[-1].astype(BF)
    scores = dot(cb, bb, 1, 1)
    steps = softplus(step[...].astype(F32) + hv[0:1, :])
    cum = cum_r[...]
    total = cum[L - 1 : L, :]
    cum_t, steps_t = cum.T, steps.T
    row = lax.broadcasted_iota(jnp.int32, (L, L), 0)
    col = lax.broadcasted_iota(jnp.int32, (L, L), 1)
    lower = row >= col
    first = col < HD
    e = jnp.exp(cum)
    wd = jnp.exp(total - cum)
    grown = dot_l(e, mats[:, :width])
    weights = dot_l(wd * steps, mats[:, :width])
    gsb = gs[0]
    entering = sin[0].astype(F32) + per_head(pfx[0][0:1, :], heads) * incoming[...].astype(F32)
    eb = entering.astype(BF)
    u = dot(bb, gsb, 1, 1)
    v = dot(cb, eb, 1, 1)
    inner = jnp.concatenate(acts[: width // L], axis=1)
    gm = gm_r[...].astype(F32)
    seen = dot((inner * u).astype(BF), mats[:, :width], 1, 1)
    passed = dot((gm * v).astype(BF), mats[:, :width], 1, 1) * e
    gb = dot((inner * weights).astype(BF), gsb)
    gc = dot((gm * grown).astype(BF), eb)
    through = head_product(gsb.astype(F32), entering, mats[:, :width]) * jnp.exp(total)
    dscores = jnp.zeros((L, L), F32)
    rowsums = jnp.zeros((L, L), F32)
    colsums = jnp.zeros((L, L), F32)
    for pair in range(heads // 2):
        cols = slice(pair * L, pair * L + L)
        xb = acts[pair].astype(BF)
        gmb = gm_r[:, cols]
        got = []
        for h in (2 * pair, 2 * pair + 1):
            mine = first if h % 2 == 0 else jnp.logical_not(first)
            gmh = jnp.where(mine, gm[:, cols], 0.0).astype(BF)
            dm = dot(gmh, xb, 1, 1)
            gap = jnp.where(lower, cum[:, h : h + 1] - cum_t[h : h + 1, :], -1e30)
            decay = jnp.exp(gap)
            st = steps_t[h : h + 1, :]
            t1 = dm * decay
            dscores = dscores + t1 * st
            gp = t1 * scores
            rowsums = jnp.where(col == h, jnp.sum(gp * st, axis=1, keepdims=True), rowsums)
            colsums = jnp.where(row == h, jnp.sum(gp, axis=0, keepdims=True), colsums)
            mix = (scores * decay * st).astype(BF)
            got.append(dot(mix, gmb, 0, 0))
        ginner_o[:, cols] = (
            jnp.where(first, got[0], got[1])
            + weights[:, cols] * u[:, cols]
            + vecs[5:6, cols] * gm[:, cols]
        )
    db = dscores.astype(BF)
    gbc_o[:, :L] = gb + dot(db, cb, 0, 0)
    gbc_o[:, L:] = gc + dot(db, bb)
    direct = colsums.T
    seen = seen * wd
    gst_o[...] = direct + seen
    later = rowsums - direct * steps + passed
    tr = mats[:, width:]
    glog_o[...] = (
        dot_r(tr, later, 0, 0) + dot_r(tr, steps * seen) - steps * seen + through
    )


def crossing(vecs, later):
    row = lax.broadcasted_iota(jnp.int32, (16, later.shape[1]), 0)
    extra = jnp.zeros((16, later.shape[1]), F32)
    for j in range(1, KERNEL):
        for t in range(j):
            part = vecs[3 - j : 4 - j, :] * later[t : t + 1, :]
            extra = extra + jnp.where(row == 16 - j + t, part, 0.0)
    return extra


def back_conv_body(
    level, at, meta, cat, rim, pre, step, cum_r, sin, pfx, sfx, ginner_r, gbc_r, glog_r, gst_r,
    incoming, before, through, load, vecs, hv, mats,
    gcat_o, gsr_o, head_o, extra_o, acc_o, hacc_o, buf, acc, hacc, outgoing,
):
    width = vecs.shape[1] - 2 * L
    heads = width // HD
    keep_next = jnp.where(meta[3 + at.c] == 0, 1.0, 0.0)
    keep = jnp.where(meta[2 + at.c] == 0, 1.0, 0.0)
    later, buf = buf.at[at.other], buf.at[at.sub]

    def follow():
        buf[L : L + 8, :] = later[0:8, :] * keep_next

    if at.first is None:
        follow()
    else:

        @pl.when(at.first)
        def _():
            buf[L : L + 8, :] = jnp.zeros((8, width + 2 * L), F32)
            acc[...] = jnp.zeros_like(acc)
            hacc[...] = jnp.zeros_like(hacc)
            outgoing[...] = final_link(meta, level, True, before, through, load)

        pl.when(jnp.logical_not(at.first))(follow)

    step_in = step[...].astype(F32) + hv[0:1, :]
    steps = softplus(step_in)
    cum = cum_r[...]
    total = cum[L - 1 : L, :]
    wd = jnp.exp(total - cum)
    weights = dot_l(wd * steps, mats[:, :width])
    far = outgoing[...] * per_head(sfx[0][0:1, :], heads)
    fb = far.astype(BF)
    entering = sin[0].astype(F32) + per_head(pfx[0][0:1, :], heads) * incoming[...].astype(F32)
    through = head_product(far, entering, mats[:, :width]) * jnp.exp(total)
    acts, slopes = [], []
    for x0 in range(0, width + 2 * L, L):
        v = pre[:, x0 : x0 + L]
        s = sigmoid(v)
        a = v * s
        acts.append(a)
        slopes.append(s + a * (1.0 - s))
    bb = acts[-2].astype(BF)
    u = dot(bb, fb, 1, 1)
    inner = jnp.concatenate(acts[: width // L], axis=1)
    seen = dot((inner * u).astype(BF), mats[:, :width], 1, 1) * wd
    gb = dot((inner * weights).astype(BF), fb)
    glog = glog_r[...] + dot_r(mats[:, width:], steps * seen) - steps * seen + through
    gsi = (gst_r[...] + seen + glog * hv[1:2, :]) * sigmoid(step_in)
    gsr_o[...] = gsi.astype(BF)
    hacc[0:8, :] += eights(glog * steps * hv[1:2, :])
    hacc[8:16, :] += eights(gsi)
    for k, x0 in enumerate(range(0, width + 2 * L, L)):
        cols = slice(x0, x0 + L)
        if x0 < width:
            g = ginner_r[:, cols] + weights[:, cols] * u[:, cols]
        elif x0 == width:
            g = gbc_r[:, :L] + gb
        else:
            g = gbc_r[:, L:]
        g = g * slopes[k]
        buf[0:L, cols] = g
        acc[32:40, cols] += eights(g)
        here = cat[:, cols].astype(F32)
        out = vecs[3:4, cols] * g
        acc[24:32, cols] += eights(g * here)
        for j in range(1, KERNEL):
            moved = buf[j : j + L, cols]
            out = out + vecs[3 - j : 4 - j, cols] * moved
            acc[24 - 8 * j : 32 - 8 * j, cols] += eights(moved * here)
        gcat_o[:, cols] = out.astype(BF)
    if at.last is not None:

        @pl.when(at.last)
        def _():
            head_o[...] = buf[0:8, :]
            past = rim[...].astype(F32)[8:16, :] * keep
            now = buf[0:8, :]
            extra_o[...] = crossing(vecs, now * keep).astype(BF)
            row = lax.broadcasted_iota(jnp.int32, now.shape, 0)
            result = jnp.zeros_like(now)
            for k in range(5):
                part = jnp.sum(acc[8 * k : 8 * k + 8, :], axis=0, keepdims=True)
                j = 3 - k
                if 1 <= j <= 3:
                    for t in range(j):
                        part = part + now[t : t + 1, :] * past[8 + t - j : 9 + t - j, :]
                result = jnp.where(row == k, part, result)
            acc_o[...] = result
            hrow = lax.broadcasted_iota(jnp.int32, (8, L), 0)
            hacc_o[...] = jnp.where(
                hrow == 0,
                jnp.sum(hacc[0:8, :], axis=0, keepdims=True),
                jnp.sum(hacc[8:16, :], axis=0, keepdims=True),
            )


def dgrad_body(k, ggr, gcat, gsr, wzx, wbc, wst, *outs):
    width = wzx.shape[2]

    def one(out):
        r = dot(ggr[...], wzx[0], 1, 1)
        r = r + dot(gcat[:, :width], wzx[1], 1, 1)
        r = r + dot(gcat[:, width : width + L], wbc[0], 1, 1)
        r = r + dot(gcat[:, width + L :], wbc[1], 1, 1)
        r = r + dot(gsr[...], wst[...])
        out[...] = r.astype(BF)

    for j in range(k):
        pl.when(pl.program_id(0) == j)(functools.partial(one, outs[j]))


def outproj_body(k, normout, wout, *outs):
    def one(out):
        out[...] = dot(normout[...], wout[...]).astype(BF)

    for j in range(k):
        pl.when(pl.program_id(0) == j)(functools.partial(one, outs[j]))


def rows_times(body, frames_n, share, d, rows, consts, name):
    k = frames_n
    outs = launch(
        functools.partial(body, k),
        [*rows, *consts],
        [pl.BlockSpec((share, r.shape[1]), lambda i: (k - 1 - i, 0)) for r in rows]
        + [whole(a) for a in consts],
        [shaped((share, d), BF)] * k,
        [pl.BlockSpec((share, d), lambda i: (0, 0))] * k,
        name,
        grid=(k,),
        vmem=20,
    )
    return list(outs)[::-1]


def total_body(*refs):
    total = refs[0][...].astype(F32)
    for ref in refs[1:-1]:
        total = total + ref[...].astype(F32)
    refs[-1][...] = total.astype(BF)


def hold_body(x, o):
    o[...] = x[...]


def hold(x, *deps):
    return simple(hold_body, [x], [shaped(x.shape, x.dtype)], "hold", deps=deps)[0]


def add_body(a, b, o):
    o[...] = (a[...].astype(F32) + b[...].astype(F32)).astype(o.dtype)


def add(a, b):
    return simple(add_body, [a, b], [shaped(a.shape, a.dtype)], "add")[0]


def swap(x, axis, mask):
    count = lax.axis_size(axis)
    return lax.ppermute(x, axis, [(i, i ^ mask) for i in range(count)])


def masks_of(axis):
    masks, mask = [], 1
    while mask < lax.axis_size(axis):
        masks.append(mask)
        mask *= 2
    return masks


def halve_body(slot, level, meta, kept, got, send_o, keep_o):
    bit = jnp.bitwise_and(jnp.right_shift(meta[slot], level), 1)
    half = send_o.shape[0]
    for o, b in ((send_o, 1 - bit), (keep_o, bit)):
        rows = pl.ds(pl.multiple_of(b * half, half), half)
        o[...] = (kept[rows, :].astype(F32) + got[rows, :].astype(F32)).astype(BF)


def halve(meta, slot, level, kept, got):
    shape = shaped((kept.shape[0] // 2, kept.shape[1]), BF)
    return simple(
        functools.partial(halve_body, slot, level), [kept, got], [shape, shape], "halve", meta
    )


def join_body(slot, level, meta, own, got, o):
    bit = jnp.bitwise_and(jnp.right_shift(meta[slot], level), 1)
    half = own.shape[0]
    o[pl.ds(pl.multiple_of(bit * half, half), half), :] = own[...]
    o[pl.ds(pl.multiple_of((1 - bit) * half, half), half), :] = got[...]


def join(meta, slot, level, own, got):
    shape = shaped((own.shape[0] * 2, own.shape[1]), BF)
    return simple(functools.partial(join_body, slot, level), [own, got], [shape], "join", meta)[0]


def wgrad_body(blocks, half, tails, meta, *refs):
    ins, (send_o, keep_o) = refs[:-2], refs[-2:]
    bit = bit_at(meta, 0)
    i = pl.program_id(0)
    g = jnp.where(i < half, (1 - bit) * half + i, bit * half + i - half)
    for p, tail in enumerate(tails):
        (a, b), ins = ins[:2], ins[2:]
        ta = tb = None
        if tail:
            (ta, tb), ins = ins[:2], ins[2:]
        inside = jnp.logical_and(g >= p * blocks, g < (p + 1) * blocks)

        def into(o, a=a, b=b, ta=ta, tb=tb):
            v = dot(a[...], b[...], 0, 0)
            if ta is not None:
                v = v + dot(ta[...], tb[...], 0, 0)
            o[...] = v.astype(BF)

        pl.when(jnp.logical_and(inside, i < half))(functools.partial(into, send_o))
        pl.when(jnp.logical_and(inside, i >= half))(functools.partial(into, keep_o))


def wgrads(meta, pairs, width, blocks, name):
    half = blocks * len(pairs) // 2
    tokens = pairs[0][0].shape[0]

    def cut(i, m):
        bit = jnp.bitwise_and(m[1], 1)
        g = jnp.where(i < half, (1 - bit) * half + i, bit * half + i - half)
        return (0, lax.rem(g, blocks))

    specs, ins = [], []
    for a, b, which, *more in pairs:
        for pair in [(a, b), tuple(more)]:
            for j, v in enumerate(pair):
                ins.append(v)
                specs.append(
                    pl.BlockSpec((v.shape[0], width), cut if j == which else lambda i, m: (0, 0))
                )
    return launch(
        functools.partial(wgrad_body, blocks, half, [len(p) > 3 for p in pairs]),
        ins,
        specs,
        [shaped((half * width, width), BF)] * 2,
        [
            pl.BlockSpec((width, width), lambda i, m: (jnp.minimum(i, half - 1), 0)),
            pl.BlockSpec((width, width), lambda i, m: (jnp.maximum(i - half, 0), 0)),
        ],
        name,
        grid=(2 * half,),
        meta=meta,
        vmem=20,
    )


def bc_body(meta, normed, gcat, gsr, rim, extra, send_o, keep_o, step_o):
    bit = jnp.bitwise_and(meta[0], 1)
    half = send_o.shape[0]
    for o, b in ((send_o, 1 - bit), (keep_o, bit)):
        cols = pl.ds(pl.multiple_of(b * half, half), half)
        v = dot(normed[:, cols], gcat[...], 0, 0) + dot(rim[:, cols], extra[...], 0, 0)
        o[...] = v.astype(BF)
    step_o[...] = dot(gsr[...], normed[...], 0, 0)[:8]


def bc_wgrad(meta, normed, gcat, gsr, rim, extra, width):
    tokens, d = normed.shape

    def tail(rows):
        return pl.BlockSpec((rows, 2 * L), lambda i, m: (0, width // (2 * L)))

    outs = [shaped((d // 2, 2 * L), BF)] * 2 + [shaped((8, d))]
    return launch(
        bc_body,
        [normed, gcat, gsr, rim, extra],
        [whole(normed), tail(tokens), whole(gsr), whole(rim), tail(16)],
        outs,
        [whole(o) for o in outs],
        "bc_wgrad",
        meta=meta,
        vmem=12,
    )


def wg_out_body(blocks, meta, own, got, wout_o, zx_o):
    bit = bit_at(meta, 0)
    width = wout_o.shape[0]
    for src, side in ((own, bit), (got, 1 - bit)):

        @pl.when(side == 0)
        def _(src=src):
            for k in range(blocks):
                rows = slice(k * width, (k + 1) * width)
                wout_o[:, rows] = src[rows, :].astype(F32)

        @pl.when(side == 1)
        def _(src=src):
            zx_o[0] = src[...].astype(F32)


def wg_out(meta, own, got, d, width):
    return launch(
        functools.partial(wg_out_body, d // width), [own, got], [whole(own), whole(got)],
        [shaped((width, d)), shaped((2, d, width))],
        [pl.BlockSpec((width, d), lambda i, m: (0, 0)),
         pl.BlockSpec((1, d, width), lambda i, m: (0, 0, 0))],
        "out_weights", meta=meta, vmem=20, token=False,
    )


def rows_body(meta, own, got, *rest):
    zx_o = rest[-1]
    bit = bit_at(meta, 0)
    half = own.shape[0]
    zx_o[0, pl.ds(pl.multiple_of(bit * half, half), half), :] = own[...].astype(F32)
    zx_o[0, pl.ds(pl.multiple_of((1 - bit) * half, half), half), :] = got[...].astype(F32)


def rows_of(meta, own, got, which, d, width, old):
    ins, specs, aliases = [own, got], [whole(own), whole(got)], {}
    if old is not None:
        ins.append(old)
        specs.append(pl.BlockSpec(memory_space=pl.ANY))
        aliases = {2: 0}
    return launch(
        rows_body, ins, specs, [shaped((2, d, width))],
        [pl.BlockSpec((1, d, width), lambda i, m: (which, 0, 0))],
        "zx_weights", meta=meta, aliases=aliases, vmem=16, token=False,
    )[0]


def bc_out_body(meta, own, got, o):
    bit = jnp.bitwise_and(meta[0], 1)
    half = own.shape[0]
    for v, b in ((own, bit), (got, 1 - bit)):
        rows = pl.ds(pl.multiple_of(b * half, half), half)
        o[0, rows, :] = v[:, :L].astype(F32)
        o[1, rows, :] = v[:, L:].astype(F32)


def patch_body(meta, gcat, ahead, vecs, o):
    count = meta.shape[0] - 3
    keep = jnp.where(meta[2 + count] == 0, 1.0, 0.0)
    o[...] = (gcat[...].astype(F32) + crossing(vecs, ahead[...] * keep)).astype(BF)


def patched(meta, gcat, ahead, vecs, share, group):
    wide = gcat.shape[1]

    def spot(i, m):
        return ((jnp.bitwise_xor(m[0], group - 1) + 1) * (share // 16) - 1, 0)

    return launch(
        patch_body,
        [gcat, ahead, vecs],
        [pl.BlockSpec((16, wide), spot), whole(ahead), whole(vecs)],
        [shaped(gcat.shape, BF)],
        [pl.BlockSpec((16, wide), spot)],
        "patch",
        meta=meta,
        aliases={0: 0},
        token=False,
    )[0]


def layer_body(tok, a, b, o):
    o[...] = (tok[...].astype(F32) + (a[...].astype(F32) + b[...].astype(F32))).astype(BF)


def tokens_body(tok, cot, a, b, gain, conv, gt_o, acc_o):
    x = tok[...].astype(F32)
    rstd = lax.rsqrt(jnp.mean(x * x, axis=1, keepdims=True) + EPS)
    unit = x * rstd
    gnormed = a[...].astype(F32) + b[...].astype(F32)
    gunit = gnormed * gain[...]
    gt_o[...] = cot[...].astype(F32) + rstd * (
        gunit - unit * jnp.mean(gunit * unit, axis=1, keepdims=True)
    )
    d = x.shape[1]
    acc_o[...] = jnp.zeros_like(acc_o)
    sums = jnp.sum(gnormed * unit, axis=0, keepdims=True)
    for k in range(d // ROW):
        acc_o[k : k + 1, :] = sums[:, k * ROW : (k + 1) * ROW]
    acc_o[d // ROW : d // ROW + 5, :] = conv[0:5, conv.shape[1] - ROW :]


def halves_of(v):
    hi, lo = split(v)
    return jnp.concatenate([hi, lo], axis=0)


def whole_of(v):
    n = v.shape[0] // 2
    v = v.astype(F32)
    return v[:n] + v[n:]


def lead_body(bc, shared, o):
    rows = bc.shape[0]
    o[:rows, :] = bc[...]
    o[rows:, :] = halves_of(shared[...])


def misc_halve_body(level, meta, kept, shared, got, send_o, keep_o, shared_o):
    bit = jnp.bitwise_and(jnp.right_shift(meta[0], level), 1)
    half = keep_o.shape[0]
    total = shared[...] + whole_of(got[2 * half :, :])
    shared_o[...] = total
    for o, b in ((send_o, 1 - bit), (keep_o, bit)):
        rows = pl.ds(pl.multiple_of(b * half, half), half)
        o[0:half, :] = (kept[rows, :].astype(F32) + got[rows, :].astype(F32)).astype(BF)
    send_o[half:, :] = halves_of(total)


def misc_pack_body(kept, shared, got, step, conv, gate, head, o):
    rows = kept.shape[0]
    o[0:rows, :] = (kept[...].astype(F32) + got[0:rows, :].astype(F32)).astype(BF)
    d = step.shape[1]
    at = rows
    for k in range(d // ROW):
        o[at : at + 8, :] = step[:, k * ROW : (k + 1) * ROW].astype(BF)
        at += 8
    total = shared[...] + whole_of(got[rows:, :])
    width = gate.shape[1]
    parts = [total]
    for ref, first, n in ((conv, 0, 5), (gate, 0, 2)):
        for k in range(width // ROW):
            parts.append(ref[first : first + n, k * ROW : (k + 1) * ROW])
    used = 7 * (width // ROW)
    parts.append(jnp.concatenate([head[0:1, :], head[1:2, :]], axis=1))
    parts.append(jnp.zeros((31 - used, ROW), F32))
    o[at:, :] = halves_of(jnp.concatenate(parts, axis=0))


def misc_sum(a, b, plain_rows):
    first = a[0:plain_rows, :].astype(F32) + b[0:plain_rows, :].astype(F32)
    return first, whole_of(a[plain_rows:, :]) + whole_of(b[plain_rows:, :])


def misc_add_body(plain_rows, a, b, o):
    first, rest = misc_sum(a, b, plain_rows)
    o[0:plain_rows, :] = first.astype(BF)
    o[plain_rows:, :] = halves_of(rest)


def misc_finish_body(bc_rows, a, b, mats, bcw_o, gain_o, bc_o, bcb_o, step_o, taps_o, bias_o,
                     sb_o, dl_o, sk_o, ng_o):
    d, width, heads = gain_o.shape[1], taps_o.shape[1], sb_o.shape[1]
    n = d // ROW
    first, rest = misc_sum(a, b, bc_rows + 8 * n)
    bcw_o[...] = first[0:bc_rows].astype(BF)
    for k in range(n):
        cols = slice(k * ROW, (k + 1) * ROW)
        at = bc_rows + 8 * k
        step_o[:, cols] = first[at : at + heads]
        gain_o[:, cols] = rest[k : k + 1]
    for k in range(2):
        v = rest[n : n + 5, k * L : (k + 1) * L]
        bc_o[k] = v[0:4]
        bcb_o[k : k + 1, :] = v[4:5]
    at = 16
    m = width // ROW
    gates = []
    for k in range(m):
        cols = slice(k * ROW, (k + 1) * ROW)
        taps_o[:, cols] = rest[at : at + 4]
        bias_o[:, cols] = rest[at + 4 : at + 5]
        at += 5
    for k in range(m):
        cols = slice(k * ROW, (k + 1) * ROW)
        ng_o[:, cols] = rest[at : at + 1]
        gates.append(jnp.broadcast_to(rest[at + 1 : at + 2], (8, ROW)))
        at += 2
    sk = dot_l(jnp.concatenate(gates, axis=1), mats[:, :width], 1, 1)
    sk_o[...] = sk[0:1, :heads]
    dl_o[...] = rest[at : at + 1, :heads]
    sb_o[...] = rest[at : at + 1, L : L + heads]


class Spot(NamedTuple):
    c: Any
    sub: int
    other: int
    first: Any
    last: Any


class Plan:
    def __init__(self):
        self.now, self.links, self.chains, self.done = 0.0, {}, [], set()

    def add(self, name, priority, chain, spend=0.0):
        self.chains.append([name, priority, chain, None])
        self.now += spend
        self.step(self.chains[-1])

    def step(self, entry):
        if entry[3] and entry[3][0] is None:
            space()
        try:
            link, us, latency, spend = next(entry[2])
        except StopIteration:
            self.chains.remove(entry)
            self.done.add(entry[0])
            return
        if link is None:
            entry[3] = (us, 0.0, spend)
            return
        start = max(self.now, self.links.get(link, 0.0))
        self.links[link] = start + us
        entry[3] = (None, start + us + latency, spend)
        self.now += 1.0

    def ready(self, entry):
        name, at, _ = entry[3]
        if name is not None:
            return 0.0 if name in self.done else 1e9
        return at

    def run(self, until=None):
        while self.chains and (until is None or until not in self.done):
            able = [e for e in self.chains if self.ready(e) <= self.now]
            if able:
                entry = min(able, key=lambda e: e[1])
            else:
                entry = min(self.chains, key=self.ready)
                self.now = self.ready(entry)
            self.now += entry[3][2]
            self.step(entry)


def on_device(
    tokens_in,
    grad_out,
    scene_offsets,
    input_gain,
    weight_zx,
    weight_bc,
    weight_step,
    conv_inner,
    conv_inner_bias,
    conv_bc,
    conv_bc_bias,
    step_bias,
    decay_log,
    skip_weight,
    norm_gain,
    weight_out,
):
    share, d = tokens_in.shape
    group = lax.axis_size("tensor")
    tokens = share * group
    heads = step_bias.shape[0]
    width = norm_gain.shape[0]
    wide = width + 2 * L
    count = tokens // L
    per = share // L
    half = group // 2
    me = lax.axis_index("tensor")
    place = lax.axis_index("dp")

    heads_pos = place * tokens + jnp.arange(count + 1, dtype=jnp.int32) * L
    starts = jnp.any(heads_pos[:, None] == scene_offsets[None, :], axis=1).astype(jnp.int32)
    meta = jnp.concatenate([me[None].astype(jnp.int32), place[None].astype(jnp.int32), starts])
    masks, tmasks = masks_of("dp"), masks_of("tensor")
    levels = len(masks)

    LAST.clear()
    def spread_out(held, keys):
        mask = half // 2
        while mask:
            for f in [f for f in held if f in keys]:
                held[f ^ mask] = swap(held[f], "tensor", mask)
            mask //= 2

    near, far = range(half), range(half, group)
    held = {0: tokens_in}
    arrived = swap(tokens_in, "tensor", half)
    spread_out(held, near)
    dps = lax.axis_size("dp")
    (last_rows,) = launch(
        lambda tok, _, o: hold_body(tok, o), [tokens_in, held[1]],
        [pl.BlockSpec((16, d), lambda i: (share // 16 - 1, 0)), pl.BlockSpec(memory_space=pl.ANY)],
        [shaped((16, d), BF)], [pl.BlockSpec((16, d), lambda i: (0, 0))], "last_rows",
    )
    past = [
        lax.ppermute(
            last_rows,
            ("dp", "tensor"),
            [(i * group + group - 1, (i + 1) * group + t) for i in range(dps - 1)],
        )
        for t in range(1, group, 2)
    ]
    gain = input_gain[None]
    prep_ins = [conv_inner, conv_inner_bias[None], conv_bc, conv_bc_bias, step_bias[None],
                decay_log[None], skip_weight[None], norm_gain[None], weight_step.T]
    prep_outs = [shaped((8, wide)), shaped((8, L)), shaped((L, width + L), BF),
                 shaped((L, d), BF)]
    vecs, hv, mats, wst = launch(
        prep_body,
        [pltpu.with_memory_space_constraint(a, pltpu.HBM) for a in prep_ins],
        [whole(a) for a in prep_ins],
        prep_outs, [whole(o) for o in prep_outs], "prep", vmem=4,
    )
    def stretched(body, name, ins, outs, scratch, reverse, vmem, flops, span=None, old=()):
        del flops
        begin, length = span or (0, count // per)

        def order(i):
            return count // per - 1 - i - begin if reverse else i + begin

        def spec(kind, shape):
            if kind == "rows":
                return pl.BlockSpec(
                    (share, shape[1]), lambda i, m: (lax.bitwise_xor(order(i), m[0]), 0)
                )
            if kind == "each":
                return pl.BlockSpec((per, *shape[1:]), lambda i, m: (order(i), 0, 0))
            return pl.BlockSpec(shape, lambda i, m: (0,) * len(shape))

        kinds = [k for k, _ in ins] + [k for k, _, _ in outs]
        n = len(ins)

        def run(meta, *refs):
            refs = refs[:n] + refs[n + len(old) :]
            step = pl.program_id(0)
            for sub in range(per):
                pos = per - 1 - sub if reverse else sub

                def view(kind, ref, pos=pos):
                    if kind == "rows":
                        return ref.at[pl.ds(pos * L, L)]
                    return ref.at[pl.ds(pos, 1)] if kind == "each" else ref

                views = [view(k, r) for k, r in zip(kinds, refs)]
                at = Spot(
                    order(step) * per + pos,
                    sub,
                    (sub - 1) % per,
                    step == 0 if sub == 0 else None,
                    step == length - 1 if sub == per - 1 else None,
                )
                body(at, meta, *views, *refs[len(kinds) :])

        return launch(
            run,
            [a for _, a in ins] + list(old),
            [spec(k, a.shape) for k, a in ins] + [pl.BlockSpec(memory_space=pl.ANY)] * len(old),
            [shaped(s, t) for _, s, t in outs],
            [spec(k, s) for k, s, _ in outs],
            name,
            grid=(length,),
            meta=meta,
            scratch=scratch,
            aliases={n + j: j for j in range(len(old))},
            vmem=vmem,
        )

    weights = (gain, weight_zx, weight_bc, wst)
    before = project(meta, [held[f] for f in near], [], *weights, tokens, 0, [])
    space()
    held[half] = hold(arrived, before[3])
    (own_past,) = simple(total_body, past, [shaped((16, d), BF)], "past")
    past = [own_past, swap(own_past, "tensor", 1)]
    spread_out(held, far)
    before = project(meta, [held[half]], [], *weights, tokens, half, list(before))
    space()
    normed, gate_raw, cat, step_raw, rim, normed_rim = project(
        meta, [held[f] for f in far[1:]], past, *weights, tokens, half + 1, list(before)
    )
    cots = {0: grad_out}
    cots[half] = swap(hold(grad_out, rim), "tensor", half)

    tall = (tokens, L)
    state_shape = (width, L)
    load_shape = (width + 16, L)
    small = (8, L)
    pre, sin, state, load, cum, pfx, decay = stretched(
        states_body,
        "states",
        [("rows", cat), ("rows", step_raw), ("one", rim), ("one", vecs), ("one", hv),
         ("one", mats)],
        [("rows", (tokens, wide), F32), ("each", (count, *state_shape), BF),
         ("one", state_shape, F32), ("one", load_shape, BF), ("rows", tall, F32),
         ("each", (count, 8, L), F32), ("one", small, F32)],
        [pltpu.VMEM((per, L + 8, wide), F32), pltpu.VMEM(state_shape, F32),
         pltpu.VMEM(small, F32)],
        False, 14, 2 * tokens * width * L * 3,
    )

    def link(level, reverse, held, load):
        shapes = [load_shape, state_shape, small, state_shape, small]
        out = simple(
            functools.partial(link_body, level, reverse), [*held, load],
            [shaped(s, BF if j == 0 else F32) for j, s in enumerate(shapes)], "link", meta,
        )
        return out[1:], out[0]

    thr = decay
    fresh = [jnp.zeros(state_shape, F32), jnp.ones(small, F32)]
    own = [state, decay, *fresh]
    load = swap(load, "dp", 1)
    (y,) = stretched(
        within_body,
        "within",
        [("rows", pre), ("rows", step_raw), ("rows", cum), ("each", sin), ("one", vecs),
         ("one", hv), ("one", mats)],
        [("rows", (tokens, width), F32)],
        [], False, 14, 2 * tokens * width * L * 6,
    )
    for level in range(levels - 1):
        space()
        own, load = link(level, False, own, load)
        load = swap(load, "dp", masks[level + 1])
        if level == 0:
            space()
            late = {half: hold(cots[half])}
            spread_out(late, far)
            spread_out(cots, near)
            cots.update({f: late[f] for f in far[1:]})
        if level == levels - 2:
            space()
            cot_all, gn = cotangent([cots[f] for f in range(group)], weight_out)
    befores, throughs = own[2:]
    space()
    mixed, sums, incoming = stretched(
        functools.partial(gate_body, levels - 1),
        "gated",
        [("rows", pre), ("rows", cum), ("each", pfx), ("rows", y), ("rows", gate_raw),
         ("rows", gn), ("one", befores), ("one", throughs), ("one", load), ("one", vecs),
         ("one", mats)],
        [("rows", (tokens, width), F32), ("each", (count, 8, L), F32), ("one", state_shape, BF)],
        [], False, 14, 2 * tokens * width * L * 4,
    )
    for mask in tmasks[::-1][:-1]:
        got = swap(sums, "tensor", mask)
        space()
        sums = add(sums, got)
    sums2 = swap(sums, "tensor", 1)
    space()
    normout, gm, ggr, gs, toward, load, sfx, gate_acc = stretched(
        back_gate_body,
        "back_gated",
        [("rows", pre), ("rows", cum), ("rows", mixed), ("rows", gate_raw), ("rows", gn),
         ("each", sums), ("each", sums2), ("one", thr), ("one", vecs), ("one", mats)],
        [("rows", (tokens, width), BF), ("rows", (tokens, width), BF),
         ("rows", (tokens, width), BF), ("each", (count, *state_shape), BF),
         ("one", state_shape, F32), ("one", load_shape, BF), ("each", (count, 8, L), F32),
         ("one", (8, width), F32)],
        [pltpu.VMEM(state_shape, F32), pltpu.VMEM(small, F32), pltpu.VMEM((16, width), F32)],
        True, 14, 2 * tokens * width * L * 3,
    )

    plan = Plan()
    kept = {}
    blocks = d // width
    axes = {"dp": ["y", "z", "z"] + ["z"] * levels, "tensor": ["core", "x"] + ["x"] * levels}
    spans = {"dp": [1, 1, 2] + [2] * levels, "tensor": [1, 1] + [2] * levels}
    hops = {"core": 2.5, "x": 5.0, "y": 5.0, "z": 6.0}
    rates = {"core": 600.0, "x": 90.0, "y": 90.0, "z": 90.0}

    def moved(x, axis, level):
        link_name = axes[axis][level]
        size = 2 * x.size * x.dtype.itemsize * spans[axis][level] / 1e3
        got = swap(x, axis, 1 << level)
        return got, link_name, size / rates[link_name], hops[link_name]

    def halving(key, axis, send, keep, first=0):
        top = len(masks_of(axis))
        slot = 1 if axis == "dp" else 0
        for level in range(first, top):
            got, *way = moved(send, axis, level)
            yield (*way, 0.8)
            if level == top - 1:
                kept[key] = add(keep, got)
            else:
                send, keep = halve(meta, slot, level + 1, keep, got)

    def doubling(key, axis, x, finish):
        slot = 1 if axis == "dp" else 0
        for level in range(len(masks_of(axis)) - 1, -1, -1):
            got, *way = moved(x, axis, level)
            yield (*way, 2.0 if level == 0 else 0.7)
            if level == 0:
                if key == "I":
                    yield (None, "WG", 0.0, 2.0)
                finish(x, got)
            else:
                x = join(meta, slot, level, x, got)

    def weights_chain(key, pairs, name, finish):
        send, keep = wgrads(meta, pairs, width, blocks, name)
        yield from halving(key, "dp", send, keep)
        yield from doubling(key, "dp", kept[key], finish)

    def inner_out(own, got):
        kept["zx"] = rows_of(meta, own, got, 1, d, width, kept["zx"])

    def out_gate(own, got):
        kept["wout"], kept["zx"] = wg_out(meta, own, got, d, width)

    def first_links():
        own = [toward, thr, *fresh]
        load = first_load
        for level in range(levels):
            got, *way = moved(load, "dp", level)
            if level == levels - 1:
                kept["links"] = (*own[2:], got)
                yield (*way, 0.0)
            else:
                yield (*way, 1.0)
                own, load = link(level, True, own, got)

    def within_part(begin, length):
        kept["within"] = stretched(
            back_within_body,
            "back_within",
            [("rows", pre), ("rows", step_raw), ("rows", cum), ("each", sin), ("each", pfx),
             ("each", gs), ("rows", gm), ("one", incoming), ("one", vecs), ("one", hv),
             ("one", mats)],
            [("rows", (tokens, width), F32), ("rows", (tokens, 2 * L), F32), ("rows", tall, F32),
             ("rows", tall, F32)],
            [], True, 16, 2 * tokens * width * L * 12, (begin, length), kept.get("within", ()),
        )

    def within_chain():
        part = group // 2
        for begin in range(0, group, part):
            yield (None, "begin", 0.0, 6.0)
            within_part(begin, part)

    def scattered(key, frames_in):
        sums_in = []
        for first in (half, 0):
            part = dict(enumerate(frames_in[first : first + half]))
            mask, level = 1, 0
            while mask < half:
                sent = [(f, moved(part.pop(f), "tensor", level)) for f in list(part) if f & mask]
                for f, (got, *way) in sent:
                    yield (*way, 0.7)
                    part[f ^ mask] = add(part[f ^ mask], got)
                mask, level = 2 * mask, level + 1
            sums_in.append(part[0])
            if first:
                got, *way = moved(part[0], "tensor", level)
                crossing_way = way
                sums_in[0] = got
        kept[key] = (sums_in[1], sums_in[0])
        yield (*crossing_way, 1.6)

    def branch_chain():
        yield (None, "begin", 0.0, 2.0)
        branch = rows_times(
            outproj_body, group, share, d, [normout], [weight_out], "outproj"
        )
        yield from scattered("branch", branch)
        (kept["layer"],) = simple(
            layer_body, [tokens_in, *kept["branch"]], [shaped((share, d), BF)], "layer"
        )

    def tokens_chain():
        ahead = lax.ppermute(kept["head"], "dp", [(i + 1, i) for i in range(dps - 1)])
        yield ("halo", 0.5, 9.0, 5.4)
        space()
        space()
        gcat = patched(meta, kept["gcat"], ahead, vecs, share, group)
        grads = rows_times(
            dgrad_body, group, share, d, [ggr, gcat, kept["gsr"]], [weight_zx, weight_bc, wst],
            "dgrad",
        )
        yield from scattered("grad", grads)
        kept["tokens"], shared = simple(
            tokens_body, [tokens_in, grad_out, *kept["grad"], gain, kept["conv_acc"]],
            [shaped((share, d)), shaped((16, ROW))], "tokens", None, 12,
        )
        yield (None, "bc", 0.0, 0.5)
        send, keep = kept["bc"]
        (load,) = simple(lead_body, [send, shared], [shaped((send.shape[0] + 32, ROW), BF)], "lead")
        for level in range(len(tmasks)):
            got, *way = moved(load, "tensor", level)
            yield (*way, 0.6)
            if level < len(tmasks) - 1:
                rows = keep.shape[0] // 2
                load, keep, shared = simple(
                    functools.partial(misc_halve_body, level + 1), [keep, shared, got],
                    [shaped((rows + 32, ROW), BF), shaped((rows, ROW), BF), shaped((16, ROW))],
                    "misc_halve", meta,
                )
        rows = keep.shape[0]
        flat = rows + 8 * (d // ROW)
        (load,) = simple(
            misc_pack_body,
            [keep, shared, got, kept["step_acc"], kept["conv_acc"], gate_acc, kept["head_acc"]],
            [shaped((flat + 96, ROW), BF)], "misc_pack",
        )
        for level in range(levels):
            got, *way = moved(load, "dp", level)
            yield (*way, 0.6)
            if level < levels - 1:
                (load,) = simple(
                    functools.partial(misc_add_body, flat), [load, got],
                    [shaped(load.shape, BF)], "misc_add",
                )
        outs = [(1, d), (2, 4, L), (2, L), (heads, d), (4, width), (1, width), (1, heads),
                (1, heads), (1, heads), (1, width)]
        total, *kept["small"] = simple(
            functools.partial(misc_finish_body, rows), [load, got, mats],
            [shaped((rows, ROW), BF)] + [shaped(s) for s in outs], "misc_finish",
        )

        def finish(own, got):
            (kept["bc_out"],) = simple(
                bc_out_body, [own, got], [shaped((2, d, L))], "bc_weights", meta
            )

        yield from doubling("bc", "tensor", total, finish)

    def bc_chain():
        yield (None, "begin", 0.0, 1.7)
        send, keep, kept["step_acc"] = bc_wgrad(
            meta, normed, kept["gcat"], kept["gsr"], normed_rim, kept["extra"], width
        )
        kept["bc"] = (send, keep)

    plan.done.add("begin")
    first_load = load
    plan.add("links", 0, first_links())
    plan.add(
        "WG", 5,
        weights_chain("WG", [(normout, cot_all, 1), (normed, ggr, 0)], "out_wgrad", out_gate),
        4.3,
    )
    plan.add("within", 8, within_chain())
    plan.add("branch", 9, branch_chain())
    plan.run("links")
    plan.run("within")
    space()
    befores, throughs, load = kept["links"]
    ginner, gbc, glog, gst = kept["within"]
    gcat, gsr, head, extra, conv_acc, head_acc = stretched(
        functools.partial(back_conv_body, levels - 1),
        "back_conv",
        [("rows", cat), ("one", rim), ("rows", pre), ("rows", step_raw), ("rows", cum),
         ("each", sin), ("each", pfx), ("each", sfx), ("rows", ginner), ("rows", gbc),
         ("rows", glog), ("rows", gst), ("one", incoming), ("one", befores), ("one", throughs),
         ("one", load), ("one", vecs), ("one", hv), ("one", mats)],
        [("rows", (tokens, wide), BF), ("rows", tall, BF), ("one", (8, wide), F32),
         ("one", (16, wide), BF), ("one", (8, wide), F32), ("one", small, F32)],
        [pltpu.VMEM((per, L + 8, wide), F32), pltpu.VMEM((40, wide), F32), pltpu.VMEM((16, L), F32),
         pltpu.VMEM(state_shape, F32)],
        True, 16, 2 * tokens * width * L * 6,
    )
    plan.now += 10.0

    kept.update(head=head, gcat=gcat, gsr=gsr, extra=extra, conv_acc=conv_acc, head_acc=head_acc)
    plan.add("tokens", 2, tokens_chain())
    plan.add(
        "I", 1,
        weights_chain("I", [(normed, gcat, 0, normed_rim, extra)], "inner_wgrad", inner_out),
        2.7,
    )
    plan.add("bc", 3, bc_chain())
    plan.run()

    gain_g, bc_g, bcb_g, step_g, taps_g, bias_g, sb_g, dl_g, sk_g, ng_g = kept["small"]
    return (
        kept["layer"],
        kept["tokens"],
        gain_g[0],
        kept["zx"],
        kept["bc_out"],
        step_g.T,
        taps_g,
        bias_g[0],
        bc_g,
        bcb_g,
        sb_g[0],
        dl_g[0],
        sk_g[0],
        ng_g[0],
        kept["wout"],
    )


def solution(mesh):
    rows = P(("dp", "tensor"), None)
    cols = P(None, "tensor")
    one = P("tensor")
    in_specs = (
        rows, rows, P(), P(), P(None, None, "tensor"), P(), cols, cols, one, P(), P(),
        one, one, one, one, P("tensor", None),
    )
    out_specs = (
        rows, rows, P(), P(None, None, "tensor"), P(), cols, cols, one, P(), P(),
        one, one, one, one, P("tensor", None),
    )
    return jax.shard_map(
        on_device, mesh=mesh, in_specs=in_specs, out_specs=out_specs, check_vma=False
    )
```

```python
import functools
from types import SimpleNamespace
from typing import Any, NamedTuple

import jax
import jax.numpy as jnp
from jax import lax
from jax.experimental import pallas as pl
from jax.experimental.pallas import tpu as pltpu
from jax.sharding import PartitionSpec as P

KERNEL = 4
L = 128
HD = 64
DI = 2048
EPS = 1e-05
F32 = jnp.float32
BF = jnp.bfloat16
MIB = 1 << 20
ROW = 256
DP, TP = "dp", "tensor"
ROWS, EACH, ONE = range(3)


def dot(a, b, ca=1, cb=0):
    return lax.dot_general(a, b, (((ca,), (cb,)), ((), ())), preferred_element_type=F32)


def split(a):
    hi = a.astype(BF)
    return hi, (a - hi.astype(F32)).astype(BF)


def dot_l(a, b, ca=1, cb=0):
    hi, lo = split(a)
    return dot(hi, b, ca, cb) + dot(lo, b, ca, cb)


def dot_r(a, b, ca=1, cb=0):
    hi, lo = split(b)
    return dot(a, hi, ca, cb) + dot(a, lo, ca, cb)


def sigmoid(v):
    return 0.5 * jnp.tanh(0.5 * v) + 0.5


def softplus(v):
    u = jnp.exp(-jnp.abs(v))
    small = u * (1.0 - u * (0.5 - u * (1.0 / 3.0 - u * 0.25)))
    return jnp.maximum(v, 0.0) + jnp.where(u < 0.02, small, jnp.log(1.0 + u))


def per_head(row, heads):
    return jnp.concatenate(
        [jnp.broadcast_to(row[:, h : h + 1], (HD, L)) for h in range(heads)], axis=0
    )


def eights(v):
    return jnp.sum(v.reshape(v.shape[0] // 8, 8, v.shape[1]), axis=0)


def across_lanes(v, width):
    return jnp.concatenate([v] * (width // L), axis=1) if width > L else v


def whole(a):
    return pl.BlockSpec(a.shape, lambda *_: (0,) * a.ndim)


LAST = []

def launch(body, ins, in_specs, outs, out_specs, name, grid=(1,), meta=None, scratch=(),
           aliases=None, vmem=8, flops=0, token=True):
    ins, in_specs = list(ins), list(in_specs)
    lead = 0 if meta is None else 1
    at = lead + len(ins)
    given = LAST[-1] if LAST and not any(LAST[-1] is a for a in ins) else None
    if given is not None:
        ins.append(given)
        in_specs.append(pl.BlockSpec(memory_space=pl.ANY))

    def run(*refs):
        body(*(refs if given is None else refs[:at] + refs[at + 1 :]))

    results = pl.pallas_call(
        run,
        grid_spec=pltpu.PrefetchScalarGridSpec(
            num_scalar_prefetch=lead,
            grid=grid,
            in_specs=in_specs,
            out_specs=list(out_specs),
            scratch_shapes=list(scratch),
        ),
        out_shape=list(outs),
        input_output_aliases={lead + k: v for k, v in (aliases or {}).items()},
        compiler_params=pltpu.CompilerParams(vmem_limit_bytes=vmem * MIB),
        cost_estimate=pl.CostEstimate(
            flops=flops,
            bytes_accessed=0,
            transcendentals=0,
        ),
        name=name,
    )(*([] if meta is None else [meta]), *ins)
    if token:
        LAST[:] = [min(results, key=lambda a: a.size)]
    return results


def space_body(o):
    o[...] = jnp.zeros_like(o)


def space(flops=10 * 10**9):
    o = shaped((8, L))
    launch(space_body, [], [], [o], [whole(o)], "space", vmem=1, flops=flops)


def shaped(shape, dtype=F32):
    return jax.ShapeDtypeStruct(shape, dtype)


def simple(body, ins, outs, name, meta=None, vmem=8, deps=()):
    n = len(ins)

    def run(*refs):
        lead = 0 if meta is None else 1
        body(*refs[: lead + n], *refs[lead + n + len(deps) :])

    return launch(
        run, [*ins, *deps],
        [whole(a) for a in ins] + [pl.BlockSpec(memory_space=pl.ANY)] * len(deps),
        outs, [whole(o) for o in outs], name, meta=meta, vmem=vmem,
    )


def unit_rows(x, gain):
    x = x.astype(F32)
    rstd = lax.rsqrt(jnp.mean(x * x, axis=1, keepdims=True) + EPS)
    return (x * rstd * gain).astype(BF)


def proj_body(k, rims, deps, meta, *refs):
    toks, past = refs[:k], refs[k : k + rims]
    gain, wzx, wbc, wst = refs[k + rims : k + rims + 4]
    outs = refs[k + rims + 4 + deps :]
    normed_o, gate_o, cat_o, step_o = outs[:4]
    width = wzx.shape[2]

    def conv_inputs(normed, out):
        out[:, :width] = dot(normed, wzx[1]).astype(BF)
        out[:, width : width + L] = dot(normed, wbc[0]).astype(BF)
        out[:, width + L :] = dot(normed, wbc[1]).astype(BF)

    def one(j):
        normed = unit_rows(toks[j][...], gain[...])
        normed_o[...] = normed
        conv_inputs(normed, cat_o)
        gate_o[...] = dot(normed, wzx[0]).astype(BF)
        step_o[...] = dot(normed, wst[...], 1, 1).astype(BF)
        if rims and j == 0:
            rim = past[0][...].astype(F32)
            for p in past[1:]:
                rim = rim + p[...].astype(F32)
            normed = unit_rows(rim, gain[...])
            outs[5][...] = normed
            conv_inputs(normed, outs[4])

    for j in range(k):
        pl.when(pl.program_id(0) == j)(functools.partial(one, j))


def project(meta, toks, past, gain, wzx, wbc, wst, total, first, before):
    k = len(toks)
    share, d = toks[0].shape
    width = wzx.shape[2]
    wide = width + 2 * L
    cols = (d, width, wide, L)
    ins = [*toks, *past, gain, wzx, wbc, wst]
    specs = [whole(a) for a in ins]
    out_specs = [pl.BlockSpec((share, c), lambda i, m: (i + first, 0)) for c in cols]
    out_shape = [shaped((total, c), BF) for c in cols]
    if past:
        for c in (wide, d):
            out_specs.append(pl.BlockSpec((16, c), lambda i, m: (0, 0)))
            out_shape.append(shaped((16, c), BF))
    aliases = {len(ins) + j: j for j in range(4)} if before else {}
    return launch(
        functools.partial(proj_body, k, len(past), len(before)),
        ins + before,
        specs + [pl.BlockSpec(memory_space=pl.ANY)] * len(before),
        out_shape,
        out_specs,
        "project",
        grid=(k,),
        meta=meta,
        aliases=aliases,
        vmem=16,
        token=False,
    )


def prep_body(taps, tbias, btaps, bbias, sbias, decay, skip, ngain, wst, vecs, hv, mats, wst_o):
    width = taps.shape[1]
    heads = width // HD
    wst_o[...] = jnp.zeros_like(wst_o)
    wst_o[0:heads, :] = wst[...]
    head = lax.broadcasted_iota(jnp.int32, (L, width), 0)
    lane = lax.broadcasted_iota(jnp.int32, (L, width), 1)
    spread = jnp.where(lax.div(lane, HD) == head, 1.0, 0.0).astype(BF)
    mats[:, :width] = spread
    r = lax.broadcasted_iota(jnp.int32, (L, L), 0)
    c = lax.broadcasted_iota(jnp.int32, (L, L), 1)
    mats[:, width:] = jnp.where(r >= c, 1.0, 0.0).astype(BF)
    hv[...] = jnp.zeros_like(hv)
    hv[0:1, :heads] = sbias[...]
    hv[1:2, :heads] = -jnp.exp(decay[...])
    hv[2:3, :heads] = skip[...]
    vecs[...] = jnp.zeros_like(vecs)
    vecs[0:4, :width] = taps[...]
    vecs[4:5, :width] = tbias[...]
    for k in range(2):
        cols = slice(width + k * L, width + k * L + L)
        vecs[0:4, cols] = btaps[k]
        vecs[4:5, cols] = bbias[k : k + 1, :]
    vecs[5:6, :width] = dot_l(hv[...], spread)[2:3, :]
    vecs[6:7, :width] = ngain[...]


def cot_body(k, *refs):
    cots = refs[:k]
    wout, all_o, gn_o = refs[k:]

    def one(cot):
        v = cot[...]
        all_o[...] = v
        gn_o[...] = dot(v, wout[...], 1, 1).astype(BF)

    for j in range(k):
        pl.when(pl.program_id(0) == j)(functools.partial(one, cots[j]))


def cotangent(cots, wout):
    k = len(cots)
    share, d = cots[0].shape
    width = wout.shape[0]
    return launch(
        functools.partial(cot_body, k),
        [*cots, wout],
        [whole(a) for a in (*cots, wout)],
        [shaped((k * share, d), BF), shaped((k * share, width), BF)],
        [pl.BlockSpec((share, c), lambda i: (i, 0)) for c in (d, width)],
        "cotangent",
        grid=(k,),
        vmem=12,
    )


def act_parts(pre, width):
    out = []
    for x0 in range(0, width + 2 * L, L):
        v = pre[:, x0 : x0 + L]
        out.append(v * sigmoid(v))
    return out


def pack(out, state, decay):
    rows = state.shape[0]
    hi, lo = split(jnp.broadcast_to(decay[0:1, :], (16, L)))
    row = lax.broadcasted_iota(jnp.int32, (16, L), 0)
    out[:rows, :] = state.astype(BF)
    tail = jnp.where(row == 0, hi.astype(F32), jnp.where(row == 1, lo.astype(F32), 0.0))
    out[rows:, :] = tail.astype(BF)


def unpack(load):
    v = load[...].astype(F32)
    rows = v.shape[0] - 16
    return v[:rows], v[rows : rows + 1] + v[rows + 1 : rows + 2]


def bit_at(meta, level):
    return jnp.bitwise_and(jnp.right_shift(meta[1], level), 1)


def is_ahead(meta, level, reverse):
    bit = bit_at(meta, level)
    return jnp.where(bit == (0 if reverse else 1), 1.0, 0.0)


def link_body(level, reverse, meta, state, decay, before, through, load,
              load_o, state_o, decay_o, before_o, through_o):
    theirs, a = unpack(load)
    heads = theirs.shape[0] // HD
    ahead = is_ahead(meta, level, reverse)
    mine = decay[0:1, :]
    t = through[0:1, :]
    before_o[...] = before[...] + per_head(t * ahead, heads) * theirs
    through_o[...] = jnp.broadcast_to(t * (ahead * a + (1.0 - ahead)), (8, L))
    joined = (
        per_head(mine * ahead + (1.0 - ahead), heads) * theirs
        + per_head(a * (1.0 - ahead) + ahead, heads) * state[...]
    )
    state_o[...] = joined
    decay_o[...] = jnp.broadcast_to(mine * a, (8, L))
    pack(load_o, joined, mine * a)


def final_link(meta, level, reverse, before, through, load):
    theirs, _ = unpack(load)
    t = through[0:1, :] * is_ahead(meta, level, reverse)
    return before[...] + per_head(t, theirs.shape[0] // HD) * theirs


def states_body(
    at, meta, cat, step, rim, vecs, hv, mats,
    pre_o, sin_o, end_o, load_o, cum_o, pfx_o, thr_o, buf, state, prod,
):
    width = vecs.shape[1] - 2 * L
    heads = width // HD
    keep = jnp.where(meta[2 + at.c] == 0, 1.0, 0.0)
    before, buf = buf.at[at.other], buf.at[at.sub]

    def follow():
        buf[0:8, :] = before[L : L + 8, :] * keep

    if at.first is None:
        follow()
    else:

        @pl.when(at.first)
        def _():
            buf[0:8, :] = rim[...].astype(F32)[8:16, :] * keep
            state[...] = jnp.zeros_like(state)
            prod[...] = jnp.ones_like(prod)

        pl.when(jnp.logical_not(at.first))(follow)

    buf[8 : 8 + L, :] = cat[...].astype(F32)
    acts = []
    for x0 in range(0, width + 2 * L, L):
        cols = slice(x0, x0 + L)
        v = vecs[4:5, cols] + vecs[3:4, cols] * buf[8 : 8 + L, cols]
        for j in range(1, KERNEL):
            v = v + vecs[3 - j : 4 - j, cols] * buf[8 - j : 8 - j + L, cols]
        pre_o[:, cols] = v
        acts.append(v * sigmoid(v))
    steps = softplus(step[...].astype(F32) + hv[0:1, :])
    cum = dot_r(mats[:, width:], steps * hv[1:2, :])
    cum_o[...] = cum
    total = cum[L - 1 : L, :]
    weights = dot_l(jnp.exp(total - cum) * steps, mats[:, :width])
    inner = jnp.concatenate(acts[: width // L], axis=1)
    local = dot((inner * weights).astype(BF), acts[-2].astype(BF), 0, 0)
    entering = state[...] * keep
    sin_o[0] = entering.astype(BF)
    dec = jnp.exp(total)
    leaving = per_head(dec, heads) * entering + local
    state[...] = leaving
    here = prod[...] * keep
    pfx_o[0] = here
    prod[...] = here * dec

    if at.last is not None:

        @pl.when(at.last)
        def _():
            end_o[...] = leaving
            thr_o[...] = here * dec
            pack(load_o, leaving, here * dec)


def within_body(at, meta, pre, step, cum_r, sin, vecs, hv, mats, y_o):
    width = vecs.shape[1] - 2 * L
    heads = width // HD
    acts = act_parts(pre, width)
    bb, cb = acts[-2].astype(BF), acts[-1].astype(BF)
    scores = dot(cb, bb, 1, 1)
    steps = softplus(step[...].astype(F32) + hv[0:1, :])
    cum = cum_r[...]
    cum_t, steps_t = cum.T, steps.T
    lower = lax.broadcasted_iota(jnp.int32, (L, L), 0) >= lax.broadcasted_iota(
        jnp.int32, (L, L), 1
    )
    first = lax.broadcasted_iota(jnp.int32, (L, L), 1) < HD
    grown = dot_l(jnp.exp(cum), mats[:, :width])
    far = grown * dot(cb, sin[0], 1, 1)
    for pair in range(heads // 2):
        cols = slice(pair * L, pair * L + L)
        x = acts[pair].astype(BF)
        got = []
        for h in (2 * pair, 2 * pair + 1):
            gap = jnp.where(lower, cum[:, h : h + 1] - cum_t[h : h + 1, :], -1e30)
            mix = scores * jnp.exp(gap) * steps_t[h : h + 1, :]
            got.append(dot(mix.astype(BF), x))
        y_o[:, cols] = jnp.where(first, got[0], got[1]) + far[:, cols]


def gate_body(
    level, at, meta, pre, cum, pfx, y, gate, gn, before, through, load, vecs, mats,
    mixed_o, sums_o, incoming,
):
    width = vecs.shape[1] - 2 * L
    ones = jnp.ones((8, width), BF)

    if at.first is not None:

        @pl.when(at.first)
        def _():
            incoming[...] = final_link(meta, level, False, before, through, load).astype(BF)

    reach = dot_l(jnp.exp(cum[...]) * pfx[0][0:1, :], mats[:, :width])
    cv = pre[:, width + L :]
    cb = (cv * sigmoid(cv)).astype(BF)
    far = reach * dot(cb, incoming[...], 1, 1)
    squares, crosses = [], []
    for x0 in range(0, width, L):
        cols = slice(x0, x0 + L)
        v = pre[:, cols]
        mixed = y[:, cols] + far[:, cols] + vecs[5:6, cols] * (v * sigmoid(v))
        mixed_o[:, cols] = mixed
        g = gate[:, cols].astype(F32)
        gated = mixed * (g * sigmoid(g))
        squares.append(gated * gated)
        crosses.append(gn[:, cols].astype(F32) * vecs[6:7, cols] * gated)
    square = dot_r(ones, jnp.concatenate(squares, axis=1), 1, 1)
    cross = dot_r(ones, jnp.concatenate(crosses, axis=1), 1, 1)
    row = lax.broadcasted_iota(jnp.int32, (8, L), 0)
    sums_o[0] = jnp.where(row == 0, square, cross)


def back_gate_body(
    at, meta, pre, cum_r, mixed_r, gate, gn, sums, sums2, thr, vecs, mats,
    normout_o, gm_o, ggr_o, gs_o, toward_o, load_o, sfx_o, acc_o, gstate, prod, acc,
):
    width = vecs.shape[1] - 2 * L
    heads = width // HD
    keep = jnp.where(meta[2 + at.c] == 0, 1.0, 0.0)

    if at.first is not None:

        @pl.when(at.first)
        def _():
            gstate[...] = jnp.zeros_like(gstate)
            prod[...] = jnp.ones_like(prod)
            acc[...] = jnp.zeros_like(acc)

    both = sums[0] + sums2[0]
    square = jnp.broadcast_to(both[0:1, :], (L, L)).T
    cross = jnp.broadcast_to(both[1:2, :], (L, L)).T
    scale = lax.rsqrt(square * (1.0 / DI) + EPS)
    cubed = scale * scale * scale * cross * (1.0 / DI)
    cum = cum_r[...]
    total = cum[L - 1 : L, :]
    grown = dot_l(jnp.exp(cum), mats[:, :width])
    cv = pre[:, width + L :]
    cb = (cv * sigmoid(cv)).astype(BF)
    moved = []
    for x0 in range(0, width, L):
        cols = slice(x0, x0 + L)
        v = pre[:, cols]
        inner = v * sigmoid(v)
        g = gate[:, cols].astype(F32)
        s = sigmoid(g)
        silu = g * s
        mixed = mixed_r[:, cols]
        gated = mixed * silu
        ng = vecs[6:7, cols]
        gnv = gn[:, cols].astype(F32)
        scaled = gated * scale
        normout_o[:, cols] = (scaled * ng).astype(BF)
        gg = scale * (gnv * ng) - gated * cubed
        gm = gg * silu
        gm_o[:, cols] = gm.astype(BF)
        ggr_o[:, cols] = (gg * mixed * (s + silu * (1.0 - s))).astype(BF)
        acc[0:8, cols] += eights(gnv * scaled)
        acc[8:16, cols] += eights(gm * inner)
        moved.append((gm * grown[:, cols]).astype(BF))
    leaving = gstate[...]
    gs_o[0] = leaving.astype(BF)
    here = prod[...]
    sfx_o[0] = here
    dec = jnp.exp(total)
    entering = per_head(dec, heads) * leaving + dot(jnp.concatenate(moved, axis=1), cb, 0, 0)
    entering = entering * keep
    gstate[...] = entering
    prod[...] = here * dec * keep

    if at.last is not None:

        @pl.when(at.last)
        def _():
            toward_o[...] = entering
            pack(load_o, entering, thr[...])
            row = lax.broadcasted_iota(jnp.int32, (8, width), 0)
            acc_o[...] = jnp.where(
                row == 0,
                jnp.sum(acc[0:8, :], axis=0, keepdims=True),
                jnp.sum(acc[8:16, :], axis=0, keepdims=True),
            )


def head_product(a, b, spread):
    rows = dot(jnp.ones((8, L), BF), (a * b).astype(BF), 1, 1)
    return dot_l(rows, spread, 1, 1)[0:1, :]


def back_within_body(
    at, meta, pre, step, cum_r, sin, pfx, gs, gm_r, incoming, vecs, hv, mats,
    ginner_o, gbc_o, glog_o, gst_o,
):
    width = vecs.shape[1] - 2 * L
    heads = width // HD
    acts = act_parts(pre, width)
    bb, cb = acts[-2].astype(BF), acts[-1].astype(BF)
    scores = dot(cb, bb, 1, 1)
    steps = softplus(step[...].astype(F32) + hv[0:1, :])
    cum = cum_r[...]
    total = cum[L - 1 : L, :]
    cum_t, steps_t = cum.T, steps.T
    row = lax.broadcasted_iota(jnp.int32, (L, L), 0)
    col = lax.broadcasted_iota(jnp.int32, (L, L), 1)
    lower = row >= col
    first = col < HD
    e = jnp.exp(cum)
    wd = jnp.exp(total - cum)
    grown = dot_l(e, mats[:, :width])
    weights = dot_l(wd * steps, mats[:, :width])
    gsb = gs[0]
    entering = sin[0].astype(F32) + per_head(pfx[0][0:1, :], heads) * incoming[...].astype(F32)
    eb = entering.astype(BF)
    u = dot(bb, gsb, 1, 1)
    v = dot(cb, eb, 1, 1)
    inner = jnp.concatenate(acts[: width // L], axis=1)
    gm = gm_r[...].astype(F32)
    seen = dot((inner * u).astype(BF), mats[:, :width], 1, 1)
    passed = dot((gm * v).astype(BF), mats[:, :width], 1, 1) * e
    gb = dot((inner * weights).astype(BF), gsb)
    gc = dot((gm * grown).astype(BF), eb)
    through = head_product(gsb.astype(F32), entering, mats[:, :width]) * jnp.exp(total)
    dscores = jnp.zeros((L, L), F32)
    rowsums = jnp.zeros((L, L), F32)
    colsums = jnp.zeros((L, L), F32)
    for pair in range(heads // 2):
        cols = slice(pair * L, pair * L + L)
        xb = acts[pair].astype(BF)
        gmb = gm_r[:, cols]
        got = []
        for h in (2 * pair, 2 * pair + 1):
            mine = first if h % 2 == 0 else jnp.logical_not(first)
            gmh = jnp.where(mine, gm[:, cols], 0.0).astype(BF)
            dm = dot(gmh, xb, 1, 1)
            gap = jnp.where(lower, cum[:, h : h + 1] - cum_t[h : h + 1, :], -1e30)
            decay = jnp.exp(gap)
            st = steps_t[h : h + 1, :]
            t1 = dm * decay
            dscores = dscores + t1 * st
            gp = t1 * scores
            rowsums = jnp.where(col == h, jnp.sum(gp * st, axis=1, keepdims=True), rowsums)
            colsums = jnp.where(row == h, jnp.sum(gp, axis=0, keepdims=True), colsums)
            mix = (scores * decay * st).astype(BF)
            got.append(dot(mix, gmb, 0, 0))
        ginner_o[:, cols] = (
            jnp.where(first, got[0], got[1])
            + weights[:, cols] * u[:, cols]
            + vecs[5:6, cols] * gm[:, cols]
        )
    db = dscores.astype(BF)
    gbc_o[:, :L] = gb + dot(db, cb, 0, 0)
    gbc_o[:, L:] = gc + dot(db, bb)
    direct = colsums.T
    seen = seen * wd
    gst_o[...] = direct + seen
    later = rowsums - direct * steps + passed
    tr = mats[:, width:]
    glog_o[...] = (
        dot_r(tr, later, 0, 0) + dot_r(tr, steps * seen) - steps * seen + through
    )


def crossing(vecs, later):
    row = lax.broadcasted_iota(jnp.int32, (16, later.shape[1]), 0)
    extra = jnp.zeros((16, later.shape[1]), F32)
    for j in range(1, KERNEL):
        for t in range(j):
            part = vecs[3 - j : 4 - j, :] * later[t : t + 1, :]
            extra = extra + jnp.where(row == 16 - j + t, part, 0.0)
    return extra


def back_conv_body(
    level, at, meta, cat, rim, pre, step, cum_r, sin, pfx, sfx, ginner_r, gbc_r, glog_r, gst_r,
    incoming, before, through, load, vecs, hv, mats,
    gcat_o, gsr_o, head_o, extra_o, acc_o, hacc_o, buf, acc, hacc, outgoing,
):
    width = vecs.shape[1] - 2 * L
    heads = width // HD
    keep_next = jnp.where(meta[3 + at.c] == 0, 1.0, 0.0)
    keep = jnp.where(meta[2 + at.c] == 0, 1.0, 0.0)
    later, buf = buf.at[at.other], buf.at[at.sub]

    def follow():
        buf[L : L + 8, :] = later[0:8, :] * keep_next

    if at.first is None:
        follow()
    else:

        @pl.when(at.first)
        def _():
            buf[L : L + 8, :] = jnp.zeros((8, width + 2 * L), F32)
            acc[...] = jnp.zeros_like(acc)
            hacc[...] = jnp.zeros_like(hacc)
            outgoing[...] = final_link(meta, level, True, before, through, load)

        pl.when(jnp.logical_not(at.first))(follow)

    step_in = step[...].astype(F32) + hv[0:1, :]
    steps = softplus(step_in)
    cum = cum_r[...]
    total = cum[L - 1 : L, :]
    wd = jnp.exp(total - cum)
    weights = dot_l(wd * steps, mats[:, :width])
    far = outgoing[...] * per_head(sfx[0][0:1, :], heads)
    fb = far.astype(BF)
    entering = sin[0].astype(F32) + per_head(pfx[0][0:1, :], heads) * incoming[...].astype(F32)
    through = head_product(far, entering, mats[:, :width]) * jnp.exp(total)
    acts, slopes = [], []
    for x0 in range(0, width + 2 * L, L):
        v = pre[:, x0 : x0 + L]
        s = sigmoid(v)
        a = v * s
        acts.append(a)
        slopes.append(s + a * (1.0 - s))
    bb = acts[-2].astype(BF)
    u = dot(bb, fb, 1, 1)
    inner = jnp.concatenate(acts[: width // L], axis=1)
    seen = dot((inner * u).astype(BF), mats[:, :width], 1, 1) * wd
    gb = dot((inner * weights).astype(BF), fb)
    glog = glog_r[...] + dot_r(mats[:, width:], steps * seen) - steps * seen + through
    gsi = (gst_r[...] + seen + glog * hv[1:2, :]) * sigmoid(step_in)
    gsr_o[...] = gsi.astype(BF)
    hacc[0:8, :] += eights(glog * steps * hv[1:2, :])
    hacc[8:16, :] += eights(gsi)
    for k, x0 in enumerate(range(0, width + 2 * L, L)):
        cols = slice(x0, x0 + L)
        if x0 < width:
            g = ginner_r[:, cols] + weights[:, cols] * u[:, cols]
        elif x0 == width:
            g = gbc_r[:, :L] + gb
        else:
            g = gbc_r[:, L:]
        g = g * slopes[k]
        buf[0:L, cols] = g
        acc[32:40, cols] += eights(g)
        here = cat[:, cols].astype(F32)
        out = vecs[3:4, cols] * g
        acc[24:32, cols] += eights(g * here)
        for j in range(1, KERNEL):
            moved = buf[j : j + L, cols]
            out = out + vecs[3 - j : 4 - j, cols] * moved
            acc[24 - 8 * j : 32 - 8 * j, cols] += eights(moved * here)
        gcat_o[:, cols] = out.astype(BF)
    if at.last is not None:

        @pl.when(at.last)
        def _():
            head_o[...] = buf[0:8, :]
            past = rim[...].astype(F32)[8:16, :] * keep
            now = buf[0:8, :]
            extra_o[...] = crossing(vecs, now * keep).astype(BF)
            row = lax.broadcasted_iota(jnp.int32, now.shape, 0)
            result = jnp.zeros_like(now)
            for k in range(5):
                part = jnp.sum(acc[8 * k : 8 * k + 8, :], axis=0, keepdims=True)
                j = 3 - k
                if 1 <= j <= 3:
                    for t in range(j):
                        part = part + now[t : t + 1, :] * past[8 + t - j : 9 + t - j, :]
                result = jnp.where(row == k, part, result)
            acc_o[...] = result
            hrow = lax.broadcasted_iota(jnp.int32, (8, L), 0)
            hacc_o[...] = jnp.where(
                hrow == 0,
                jnp.sum(hacc[0:8, :], axis=0, keepdims=True),
                jnp.sum(hacc[8:16, :], axis=0, keepdims=True),
            )


def dgrad_body(k, ggr, gcat, gsr, normed, wzx, wbc, wst, gain, conv, *refs):
    outs, shared_o, acc = refs[:k], refs[k], refs[k + 1]
    width, d = wzx.shape[2], gain.shape[1]
    i = pl.program_id(0)

    @pl.when(i == 0)
    def _():
        acc[...] = jnp.zeros_like(acc)

    r = dot(ggr[...], wzx[0], 1, 1)
    r = r + dot(gcat[:, :width], wzx[1], 1, 1)
    r = r + dot(gcat[:, width : width + L], wbc[0], 1, 1)
    r = r + dot(gcat[:, width + L :], wbc[1], 1, 1)
    r = r + dot(gsr[...], wst[...])
    acc[...] += eights(r * normed[...].astype(F32))
    rounded = r.astype(BF)

    def into(out):
        out[...] = rounded

    for j in range(k):
        pl.when(i == j)(functools.partial(into, outs[j]))

    @pl.when(i == k - 1)
    def _():
        shared_o[...] = jnp.zeros_like(shared_o)
        sums = jnp.sum(acc[...], axis=0, keepdims=True) / gain[...]
        for c in range(d // ROW):
            shared_o[c : c + 1, :] = sums[:, c * ROW : (c + 1) * ROW]
        shared_o[d // ROW : d // ROW + 5, :] = conv[0:5, conv.shape[1] - ROW :]


def outproj_body(k, normout, wout, *outs):
    def one(out):
        out[...] = dot(normout[...], wout[...]).astype(BF)

    for j in range(k):
        pl.when(pl.program_id(0) == j)(functools.partial(one, outs[j]))


def rows_times(body, frames_n, share, d, rows, consts, name, more=(), scratch=()):
    k = frames_n
    outs = launch(
        functools.partial(body, k),
        [*rows, *consts],
        [pl.BlockSpec((share, r.shape[1]), lambda i: (k - 1 - i, 0)) for r in rows]
        + [whole(a) for a in consts],
        [shaped((share, d), BF)] * k + list(more),
        [pl.BlockSpec((share, d), lambda i: (0, 0))] * k + [whole(o) for o in more],
        name,
        grid=(k,),
        scratch=scratch,
        vmem=20,
    )
    return [*outs[:k][::-1], *outs[k:]]


def total_body(*refs):
    total = refs[0][...].astype(F32)
    for ref in refs[1:-1]:
        total = total + ref[...].astype(F32)
    refs[-1][...] = total.astype(BF)


def hold_body(x, o):
    o[...] = x[...]


def hold(x, *deps):
    return simple(hold_body, [x], [shaped(x.shape, x.dtype)], "hold", deps=deps)[0]


def add_body(a, b, o):
    o[...] = (a[...].astype(F32) + b[...].astype(F32)).astype(o.dtype)


def add(a, b):
    return simple(add_body, [a, b], [shaped(a.shape, a.dtype)], "add")[0]


def swap(x, axis, mask):
    count = lax.axis_size(axis)
    return lax.ppermute(x, axis, [(i, i ^ mask) for i in range(count)])


def masks_of(axis):
    masks, mask = [], 1
    while mask < lax.axis_size(axis):
        masks.append(mask)
        mask *= 2
    return masks


def halve_body(slot, level, meta, kept, got, send_o, keep_o):
    bit = jnp.bitwise_and(jnp.right_shift(meta[slot], level), 1)
    half = send_o.shape[0]
    for o, b in ((send_o, 1 - bit), (keep_o, bit)):
        rows = pl.ds(pl.multiple_of(b * half, half), half)
        o[...] = (kept[rows, :].astype(F32) + got[rows, :].astype(F32)).astype(BF)


def halve(meta, slot, level, kept, got):
    shape = shaped((kept.shape[0] // 2, kept.shape[1]), BF)
    return simple(
        functools.partial(halve_body, slot, level), [kept, got], [shape, shape], "halve", meta
    )


def join_body(slot, level, meta, own, got, o):
    bit = jnp.bitwise_and(jnp.right_shift(meta[slot], level), 1)
    half = own.shape[0]
    o[pl.ds(pl.multiple_of(bit * half, half), half), :] = own[...]
    o[pl.ds(pl.multiple_of((1 - bit) * half, half), half), :] = got[...]


def join(meta, slot, level, own, got):
    shape = shaped((own.shape[0] * 2, own.shape[1]), BF)
    return simple(functools.partial(join_body, slot, level), [own, got], [shape], "join", meta)[0]


def wgrad_body(blocks, half, tails, meta, *refs):
    ins, (send_o, keep_o) = refs[:-2], refs[-2:]
    bit = bit_at(meta, 0)
    i = pl.program_id(0)
    g = jnp.where(i < half, (1 - bit) * half + i, bit * half + i - half)
    for p, tail in enumerate(tails):
        (a, b), ins = ins[:2], ins[2:]
        ta = tb = None
        if tail:
            (ta, tb), ins = ins[:2], ins[2:]
        inside = jnp.logical_and(g >= p * blocks, g < (p + 1) * blocks)

        def into(o, a=a, b=b, ta=ta, tb=tb):
            v = dot(a[...], b[...], 0, 0)
            if ta is not None:
                v = v + dot(ta[...], tb[...], 0, 0)
            o[...] = v.astype(BF)

        pl.when(jnp.logical_and(inside, i < half))(functools.partial(into, send_o))
        pl.when(jnp.logical_and(inside, i >= half))(functools.partial(into, keep_o))


def wgrads(meta, pairs, width, blocks):
    half = blocks * len(pairs) // 2
    tokens = pairs[0][0].shape[0]

    def cut(i, m):
        bit = jnp.bitwise_and(m[1], 1)
        g = jnp.where(i < half, (1 - bit) * half + i, bit * half + i - half)
        return (0, lax.rem(g, blocks))

    specs, ins = [], []
    for a, b, which, *more in pairs:
        for pair in [(a, b), tuple(more)]:
            for j, v in enumerate(pair):
                ins.append(v)
                specs.append(
                    pl.BlockSpec((v.shape[0], width), cut if j == which else lambda i, m: (0, 0))
                )
    return launch(
        functools.partial(wgrad_body, blocks, half, [len(p) > 3 for p in pairs]),
        ins,
        specs,
        [shaped((half * width, width), BF)] * 2,
        [
            pl.BlockSpec((width, width), lambda i, m: (jnp.minimum(i, half - 1), 0)),
            pl.BlockSpec((width, width), lambda i, m: (jnp.maximum(i - half, 0), 0)),
        ],
        "wgrad",
        grid=(2 * half,),
        meta=meta,
        vmem=20,
    )


def bc_body(meta, normed, gcat, gsr, rim, extra, send_o, keep_o, step_o):
    bit = jnp.bitwise_and(meta[0], 1)
    half = send_o.shape[0]
    for o, b in ((send_o, 1 - bit), (keep_o, bit)):
        cols = pl.ds(pl.multiple_of(b * half, half), half)
        v = dot(normed[:, cols], gcat[...], 0, 0) + dot(rim[:, cols], extra[...], 0, 0)
        o[...] = v.astype(BF)
    step_o[...] = dot(gsr[...], normed[...], 0, 0)[:8]


def bc_wgrad(meta, normed, gcat, gsr, rim, extra, width):
    tokens, d = normed.shape

    def tail(rows):
        return pl.BlockSpec((rows, 2 * L), lambda i, m: (0, width // (2 * L)))

    outs = [shaped((d // 2, 2 * L), BF)] * 2 + [shaped((8, d))]
    return launch(
        bc_body,
        [normed, gcat, gsr, rim, extra],
        [whole(normed), tail(tokens), whole(gsr), whole(rim), tail(16)],
        outs,
        [whole(o) for o in outs],
        "bc_wgrad",
        meta=meta,
        vmem=12,
    )


def columns_body(blocks, meta, own, got, o):
    width = o.shape[0]
    bit = bit_at(meta, 0)
    half = blocks // 2
    for src, b in ((own, bit), (got, 1 - bit)):
        for side in range(2):

            @pl.when(b == side)
            def _(src=src, side=side):
                for k in range(half):
                    at = (side * half + k) * width
                    o[:, at : at + width] = src[k * width : (k + 1) * width, :].astype(F32)


def columns(meta, own, got, d, width):
    return simple(
        functools.partial(columns_body, d // width), [own, got], [shaped((width, d))],
        "out_weights", meta, 16,
    )[0]


def rows_body(meta, own, got, *rest):
    zx_o = rest[-1]
    bit = bit_at(meta, 0)
    half = own.shape[0]
    zx_o[0, pl.ds(pl.multiple_of(bit * half, half), half), :] = own[...].astype(F32)
    zx_o[0, pl.ds(pl.multiple_of((1 - bit) * half, half), half), :] = got[...].astype(F32)


def rows_of(meta, own, got, which, d, width, old):
    ins, specs, aliases = [own, got], [whole(own), whole(got)], {}
    if old is not None:
        ins.append(old)
        specs.append(pl.BlockSpec(memory_space=pl.ANY))
        aliases = {2: 0}
    return launch(
        rows_body, ins, specs, [shaped((2, d, width))],
        [pl.BlockSpec((1, d, width), lambda i, m: (which, 0, 0))],
        "zx_weights", meta=meta, aliases=aliases, vmem=16, token=False,
    )[0]


def bc_out_body(meta, own, got, o):
    bit = jnp.bitwise_and(meta[0], 1)
    half = own.shape[0]
    for v, b in ((own, bit), (got, 1 - bit)):
        rows = pl.ds(pl.multiple_of(b * half, half), half)
        o[0, rows, :] = v[:, :L].astype(F32)
        o[1, rows, :] = v[:, L:].astype(F32)


def patch_body(meta, gcat, ahead, vecs, o):
    count = meta.shape[0] - 3
    keep = jnp.where(meta[2 + count] == 0, 1.0, 0.0)
    o[...] = (gcat[...].astype(F32) + crossing(vecs, ahead[...] * keep)).astype(BF)


def patched(meta, gcat, ahead, vecs, share, group):
    wide = gcat.shape[1]

    def spot(i, m):
        return ((jnp.bitwise_xor(m[0], group - 1) + 1) * (share // 16) - 1, 0)

    return launch(
        patch_body,
        [gcat, ahead, vecs],
        [pl.BlockSpec((16, wide), spot), whole(ahead), whole(vecs)],
        [shaped(gcat.shape, BF)],
        [pl.BlockSpec((16, wide), spot)],
        "patch",
        meta=meta,
        aliases={0: 0},
        token=False,
    )[0]


def layer_body(tok, a, b, o):
    o[...] = (tok[...].astype(F32) + (a[...].astype(F32) + b[...].astype(F32))).astype(BF)


def tokens_body(tok, cot, a, b, gain, gt_o):
    x = tok[...].astype(F32)
    rstd = lax.rsqrt(jnp.mean(x * x, axis=1, keepdims=True) + EPS)
    unit = x * rstd
    gunit = (a[...].astype(F32) + b[...].astype(F32)) * gain[...]
    gt_o[...] = cot[...].astype(F32) + rstd * (
        gunit - unit * jnp.mean(gunit * unit, axis=1, keepdims=True)
    )


def halves_of(v):
    hi, lo = split(v)
    return jnp.concatenate([hi, lo], axis=0)


def whole_of(v):
    n = v.shape[0] // 2
    v = v.astype(F32)
    return v[:n] + v[n:]


def lead_body(bc, shared, o):
    rows = bc.shape[0]
    o[:rows, :] = bc[...]
    o[rows:, :] = halves_of(shared[...])


def misc_halve_body(level, meta, kept, shared, got, send_o, keep_o, shared_o):
    bit = jnp.bitwise_and(jnp.right_shift(meta[0], level), 1)
    half = keep_o.shape[0]
    total = shared[...] + whole_of(got[2 * half :, :])
    shared_o[...] = total
    for o, b in ((send_o, 1 - bit), (keep_o, bit)):
        rows = pl.ds(pl.multiple_of(b * half, half), half)
        o[0:half, :] = (kept[rows, :].astype(F32) + got[rows, :].astype(F32)).astype(BF)
    send_o[half:, :] = halves_of(total)


def misc_pack_body(kept, shared, got, step, conv, gate, head, o):
    rows = kept.shape[0]
    o[0:rows, :] = (kept[...].astype(F32) + got[0:rows, :].astype(F32)).astype(BF)
    d = step.shape[1]
    at = rows
    for k in range(d // ROW):
        o[at : at + 8, :] = step[:, k * ROW : (k + 1) * ROW].astype(BF)
        at += 8
    total = shared[...] + whole_of(got[rows:, :])
    width = gate.shape[1]
    parts = [total]
    for ref, first, n in ((conv, 0, 5), (gate, 0, 2)):
        for k in range(width // ROW):
            parts.append(ref[first : first + n, k * ROW : (k + 1) * ROW])
    used = 7 * (width // ROW)
    parts.append(jnp.concatenate([head[0:1, :], head[1:2, :]], axis=1))
    parts.append(jnp.zeros((31 - used, ROW), F32))
    o[at:, :] = halves_of(jnp.concatenate(parts, axis=0))


def misc_sum(a, b, plain_rows):
    first = a[0:plain_rows, :].astype(F32) + b[0:plain_rows, :].astype(F32)
    return first, whole_of(a[plain_rows:, :]) + whole_of(b[plain_rows:, :])


def misc_add_body(plain_rows, a, b, o):
    first, rest = misc_sum(a, b, plain_rows)
    o[0:plain_rows, :] = first.astype(BF)
    o[plain_rows:, :] = halves_of(rest)


def misc_finish_body(bc_rows, a, b, mats, bcw_o, gain_o, bc_o, bcb_o, step_o, taps_o, bias_o,
                     sb_o, dl_o, sk_o, ng_o):
    d, width, heads = gain_o.shape[1], taps_o.shape[1], sb_o.shape[1]
    n = d // ROW
    first, rest = misc_sum(a, b, bc_rows + 8 * n)
    bcw_o[...] = first[0:bc_rows].astype(BF)
    for k in range(n):
        cols = slice(k * ROW, (k + 1) * ROW)
        at = bc_rows + 8 * k
        step_o[:, cols] = first[at : at + heads]
        gain_o[:, cols] = rest[k : k + 1]
    for k in range(2):
        v = rest[n : n + 5, k * L : (k + 1) * L]
        bc_o[k] = v[0:4]
        bcb_o[k : k + 1, :] = v[4:5]
    at = 16
    m = width // ROW
    gates = []
    for k in range(m):
        cols = slice(k * ROW, (k + 1) * ROW)
        taps_o[:, cols] = rest[at : at + 4]
        bias_o[:, cols] = rest[at + 4 : at + 5]
        at += 5
    for k in range(m):
        cols = slice(k * ROW, (k + 1) * ROW)
        ng_o[:, cols] = rest[at : at + 1]
        gates.append(jnp.broadcast_to(rest[at + 1 : at + 2], (8, ROW)))
        at += 2
    sk = dot_l(jnp.concatenate(gates, axis=1), mats[:, :width], 1, 1)
    sk_o[...] = sk[0:1, :heads]
    dl_o[...] = rest[at : at + 1, :heads]
    sb_o[...] = rest[at : at + 1, L : L + heads]


class Spot(NamedTuple):
    c: Any
    sub: int
    other: int
    first: Any
    last: Any


ORDER = "LWGLFLWFLTGIWGTWIMMTGMTWMIGMWITBGBMBIWIMGMBMI"


def run_chains(chains, done, order):
    needs = {name: next(chain) for name, chain in chains.items()}

    def step(name):
        need, waits = needs[name]
        if need is not None and need not in done:
            return False
        if waits:
            space()
        try:
            needs[name] = next(chains[name])
        except StopIteration:
            del needs[name]
            done.add(name)
        return True

    for name in order:
        if not step(name):
            raise ValueError(name)
    while needs:
        for name in list(needs):
            step(name)


def on_device(
    tokens_in,
    grad_out,
    scene_offsets,
    input_gain,
    weight_zx,
    weight_bc,
    weight_step,
    conv_inner,
    conv_inner_bias,
    conv_bc,
    conv_bc_bias,
    step_bias,
    decay_log,
    skip_weight,
    norm_gain,
    weight_out,
):
    share, d = tokens_in.shape
    group = lax.axis_size(TP)
    tokens = share * group
    heads = step_bias.shape[0]
    width = norm_gain.shape[0]
    wide = width + 2 * L
    count = tokens // L
    per = share // L
    half = group // 2
    me = lax.axis_index(TP)
    place = lax.axis_index(DP)

    heads_pos = place * tokens + jnp.arange(count + 1, dtype=jnp.int32) * L
    starts = jnp.any(heads_pos[:, None] == scene_offsets[None, :], axis=1).astype(jnp.int32)
    meta = jnp.concatenate([me[None].astype(jnp.int32), place[None].astype(jnp.int32), starts])
    masks, tmasks = masks_of(DP), masks_of(TP)
    levels = len(masks)

    LAST.clear()
    def spread_out(held, keys):
        mask = half // 2
        while mask:
            for f in [f for f in held if f in keys]:
                held[f ^ mask] = swap(held[f], TP, mask)
            mask //= 2

    near, far = range(half), range(half, group)
    held = {0: tokens_in}
    arrived = swap(tokens_in, TP, half)
    spread_out(held, near)
    dps = lax.axis_size(DP)
    (last_rows,) = launch(
        lambda tok, _, o: hold_body(tok, o), [tokens_in, held[1]],
        [pl.BlockSpec((16, d), lambda i: (share // 16 - 1, 0)), pl.BlockSpec(memory_space=pl.ANY)],
        [shaped((16, d), BF)], [pl.BlockSpec((16, d), lambda i: (0, 0))], "last_rows",
    )
    past = [
        lax.ppermute(
            last_rows,
            (DP, TP),
            [(i * group + group - 1, (i + 1) * group + t) for i in range(dps - 1)],
        )
        for t in range(1, group, 2)
    ]
    gain = input_gain[None]
    prep_ins = [conv_inner, conv_inner_bias[None], conv_bc, conv_bc_bias, step_bias[None],
                decay_log[None], skip_weight[None], norm_gain[None], weight_step.T]
    prep_outs = [shaped((8, wide)), shaped((8, L)), shaped((L, width + L), BF),
                 shaped((L, d), BF)]
    vecs, hv, mats, wst = launch(
        prep_body,
        [pltpu.with_memory_space_constraint(a, pltpu.HBM) for a in prep_ins],
        [whole(a) for a in prep_ins],
        prep_outs, [whole(o) for o in prep_outs], "prep", vmem=4,
    )
    def stretched(body, name, ins, outs, scratch, reverse, vmem, span=None, old=()):
        begin, length = span or (0, count // per)

        def order(i):
            return count // per - 1 - i - begin if reverse else i + begin

        def spec(kind, shape):
            if kind == ROWS:
                return pl.BlockSpec(
                    (share, shape[1]), lambda i, m: (lax.bitwise_xor(order(i), m[0]), 0)
                )
            if kind == EACH:
                return pl.BlockSpec((per, *shape[1:]), lambda i, m: (order(i), 0, 0))
            return pl.BlockSpec(shape, lambda i, m: (0,) * len(shape))

        kinds = [k for k, _ in ins] + [k for k, _, _ in outs]
        n = len(ins)

        def run(meta, *refs):
            refs = refs[:n] + refs[n + len(old) :]
            step = pl.program_id(0)
            for sub in range(per):
                pos = per - 1 - sub if reverse else sub

                def view(kind, ref, pos=pos):
                    if kind == ROWS:
                        return ref.at[pl.ds(pos * L, L)]
                    return ref.at[pl.ds(pos, 1)] if kind == EACH else ref

                views = [view(k, r) for k, r in zip(kinds, refs)]
                at = Spot(
                    order(step) * per + pos,
                    sub,
                    (sub - 1) % per,
                    step == 0 if sub == 0 else None,
                    step == length - 1 if sub == per - 1 else None,
                )
                body(at, meta, *views, *refs[len(kinds) :])

        return launch(
            run,
            [a for _, a in ins] + list(old),
            [spec(k, a.shape) for k, a in ins] + [pl.BlockSpec(memory_space=pl.ANY)] * len(old),
            [shaped(s, t) for _, s, t in outs],
            [spec(k, s) for k, s, _ in outs],
            name,
            grid=(length,),
            meta=meta,
            scratch=scratch,
            aliases={n + j: j for j in range(len(old))},
            vmem=vmem,
        )

    weights = (gain, weight_zx, weight_bc, wst)
    before = project(meta, [held[f] for f in near], [], *weights, tokens, 0, [])
    space()
    held[half] = hold(arrived, before[3])
    (own_past,) = simple(total_body, past, [shaped((16, d), BF)], "past")
    past = [own_past, swap(own_past, TP, 1)]
    spread_out(held, far)
    before = project(meta, [held[half]], [], *weights, tokens, half, list(before))
    space()
    normed, gate_raw, cat, step_raw, rim, normed_rim = project(
        meta, [held[f] for f in far[1:]], past, *weights, tokens, half + 1, list(before)
    )
    cots = {0: grad_out}
    cots[half] = swap(hold(grad_out, rim), TP, half)

    tall = (tokens, L)
    state_shape = (width, L)
    load_shape = (width + 16, L)
    small = (8, L)
    pre, sin, state, load, cum, pfx, decay = stretched(
        states_body,
        "states",
        [(ROWS, cat), (ROWS, step_raw), (ONE, rim), (ONE, vecs), (ONE, hv),
         (ONE, mats)],
        [(ROWS, (tokens, wide), F32), (EACH, (count, *state_shape), BF),
         (ONE, state_shape, F32), (ONE, load_shape, BF), (ROWS, tall, F32),
         (EACH, (count, 8, L), F32), (ONE, small, F32)],
        [pltpu.VMEM((per, L + 8, wide), F32), pltpu.VMEM(state_shape, F32),
         pltpu.VMEM(small, F32)],
        False, 14,
    )

    def link(level, reverse, held, load):
        shapes = [load_shape, state_shape, small, state_shape, small]
        out = simple(
            functools.partial(link_body, level, reverse), [*held, load],
            [shaped(s, BF if j == 0 else F32) for j, s in enumerate(shapes)], "link", meta,
        )
        return out[1:], out[0]

    thr = decay
    fresh = [jnp.zeros(state_shape, F32), jnp.ones(small, F32)]
    own = [state, decay, *fresh]
    load = swap(load, DP, 1)
    (y,) = stretched(
        within_body,
        "within",
        [(ROWS, pre), (ROWS, step_raw), (ROWS, cum), (EACH, sin), (ONE, vecs),
         (ONE, hv), (ONE, mats)],
        [(ROWS, (tokens, width), F32)],
        [], False, 14,
    )
    for level in range(levels - 1):
        space()
        own, load = link(level, False, own, load)
        load = swap(load, DP, masks[level + 1])
        if level == 0:
            space()
            late = {half: hold(cots[half])}
            spread_out(late, far)
            spread_out(cots, near)
            cots.update({f: late[f] for f in far[1:]})
        if level == levels - 2:
            space()
            cot_all, gn = cotangent([cots[f] for f in range(group)], weight_out)
    befores, throughs = own[2:]
    space()
    mixed, sums, incoming = stretched(
        functools.partial(gate_body, levels - 1),
        "gated",
        [(ROWS, pre), (ROWS, cum), (EACH, pfx), (ROWS, y), (ROWS, gate_raw),
         (ROWS, gn), (ONE, befores), (ONE, throughs), (ONE, load), (ONE, vecs),
         (ONE, mats)],
        [(ROWS, (tokens, width), F32), (EACH, (count, 8, L), F32), (ONE, state_shape, BF)],
        [], False, 14,
    )
    for mask in tmasks[::-1][:-1]:
        got = swap(sums, TP, mask)
        space()
        sums = add(sums, got)
    sums2 = swap(sums, TP, 1)
    space()
    normout, gm, ggr, gs, toward, first_load, sfx, gate_acc = stretched(
        back_gate_body,
        "back_gated",
        [(ROWS, pre), (ROWS, cum), (ROWS, mixed), (ROWS, gate_raw), (ROWS, gn),
         (EACH, sums), (EACH, sums2), (ONE, thr), (ONE, vecs), (ONE, mats)],
        [(ROWS, (tokens, width), BF), (ROWS, (tokens, width), BF),
         (ROWS, (tokens, width), BF), (EACH, (count, *state_shape), BF),
         (ONE, state_shape, F32), (ONE, load_shape, BF), (EACH, (count, 8, L), F32),
         (ONE, (8, width), F32)],
        [pltpu.VMEM(state_shape, F32), pltpu.VMEM(small, F32), pltpu.VMEM((16, width), F32)],
        True, 14,
    )

    kept = SimpleNamespace(within=())
    done = set()
    blocks = d // width

    def weights_chain(pairs, finish, need=None, last=None):
        yield need, False
        send, keep = wgrads(meta, [pairs()], width, blocks)
        for level in range(levels):
            got = swap(send, DP, masks[level])
            yield None, True
            if level < levels - 1:
                send, keep = halve(meta, 1, level + 1, keep, got)
            else:
                total = add(keep, got)
        for level in range(levels - 1, -1, -1):
            got = swap(total, DP, masks[level])
            yield None if level else last, True
            if level:
                total = join(meta, 1, level, total, got)
        finish(total, got)

    def out_weights(own, got):
        kept.wout = columns(meta, own, got, d, width)

    def gate_weights(own, got):
        kept.zx = rows_of(meta, own, got, 0, d, width, None)

    def inner_weights(own, got):
        kept.zx = rows_of(meta, own, got, 1, d, width, kept.zx)

    def links_chain():
        yield None, False
        own, load = [toward, thr, *fresh], first_load
        for level in range(levels):
            got = swap(load, DP, masks[level])
            yield None if level < levels - 1 else "F", True
            if level < levels - 1:
                own, load = link(level, True, own, got)
        befores, throughs = own[2:]
        ginner, gbc, glog, gst = kept.within
        kept.gcat, kept.gsr, kept.head, kept.extra, kept.conv_acc, kept.head_acc = stretched(
            functools.partial(back_conv_body, levels - 1),
            "back_conv",
            [(ROWS, cat), (ONE, rim), (ROWS, pre), (ROWS, step_raw), (ROWS, cum),
             (EACH, sin), (EACH, pfx), (EACH, sfx), (ROWS, ginner), (ROWS, gbc),
             (ROWS, glog), (ROWS, gst), (ONE, incoming), (ONE, befores), (ONE, throughs),
             (ONE, got), (ONE, vecs), (ONE, hv), (ONE, mats)],
            [(ROWS, (tokens, wide), BF), (ROWS, tall, BF), (ONE, (8, wide), F32),
             (ONE, (16, wide), BF), (ONE, (8, wide), F32), (ONE, small, F32)],
            [pltpu.VMEM((per, L + 8, wide), F32), pltpu.VMEM((40, wide), F32),
             pltpu.VMEM((16, L), F32), pltpu.VMEM(state_shape, F32)],
            True, 16,
        )

    def within_chain():
        for begin in (0, half):
            yield None, False
            kept.within = stretched(
                back_within_body,
                "back_within",
                [(ROWS, pre), (ROWS, step_raw), (ROWS, cum), (EACH, sin), (EACH, pfx),
                 (EACH, gs), (ROWS, gm), (ONE, incoming), (ONE, vecs), (ONE, hv), (ONE, mats)],
                [(ROWS, (tokens, width), F32), (ROWS, (tokens, 2 * L), F32), (ROWS, tall, F32),
                 (ROWS, tall, F32)],
                [], True, 16, (begin, half), kept.within,
            )

    def scattered(frames_in):
        sums_in = []
        for first in (0, half):
            part = dict(enumerate(frames_in[first : first + half]))
            mask = 1
            while mask < half:
                for f in [f for f in part if f & mask]:
                    got = swap(part.pop(f), TP, mask)
                    yield None, True
                    part[f ^ mask] = add(part[f ^ mask], got)
                mask *= 2
            sums_in.append(part[0])
        got = swap(sums_in[1], TP, half)
        yield None, True
        return sums_in[0], got

    def branch_chain():
        yield None, False
        branch = rows_times(outproj_body, group, share, d, [normout], [weight_out], "outproj")
        parts = yield from scattered(branch)
        (kept.layer,) = simple(layer_body, [tokens_in, *parts], [shaped((share, d), BF)], "layer")

    def tokens_chain():
        yield "L", False
        ahead = lax.ppermute(kept.head, DP, [(i + 1, i) for i in range(dps - 1)])
        yield None, True
        gcat = patched(meta, kept.gcat, ahead, vecs, share, group)
        *grads, kept.shared = rows_times(
            dgrad_body, group, share, d, [ggr, gcat, kept.gsr, normed],
            [weight_zx, weight_bc, wst, gain, kept.conv_acc],
            "dgrad", [shaped((16, ROW))], [pltpu.VMEM((8, d), F32)],
        )
        done.add("dgrad")
        parts = yield from scattered(grads)
        (kept.tokens,) = simple(
            tokens_body, [tokens_in, grad_out, *parts, gain], [shaped((share, d))], "tokens",
            None, 12,
        )

    def misc_chain():
        yield "L", False
        send, keep, step_acc = bc_wgrad(
            meta, normed, kept.gcat, kept.gsr, normed_rim, kept.extra, width
        )
        yield "dgrad", False
        shared = kept.shared
        (load,) = simple(lead_body, [send, shared], [shaped((send.shape[0] + 32, ROW), BF)], "lead")
        for level in range(len(tmasks)):
            got = swap(load, TP, tmasks[level])
            yield None, True
            if level < len(tmasks) - 1:
                rows = keep.shape[0] // 2
                load, keep, shared = simple(
                    functools.partial(misc_halve_body, level + 1), [keep, shared, got],
                    [shaped((rows + 32, ROW), BF), shaped((rows, ROW), BF), shaped((16, ROW))],
                    "misc_halve", meta,
                )
        rows = keep.shape[0]
        flat = rows + 8 * (d // ROW)
        (load,) = simple(
            misc_pack_body,
            [keep, shared, got, step_acc, kept.conv_acc, gate_acc, kept.head_acc],
            [shaped((flat + 96, ROW), BF)], "misc_pack",
        )
        for level in range(levels):
            got = swap(load, DP, masks[level])
            yield None, True
            if level < levels - 1:
                (load,) = simple(
                    functools.partial(misc_add_body, flat), [load, got],
                    [shaped(load.shape, BF)], "misc_add",
                )
        outs = [(1, d), (2, 4, L), (2, L), (heads, d), (4, width), (1, width), (1, heads),
                (1, heads), (1, heads), (1, width)]
        total, *kept.small = simple(
            functools.partial(misc_finish_body, rows), [load, got, mats],
            [shaped((rows, ROW), BF)] + [shaped(s) for s in outs], "misc_finish",
        )
        for level in range(len(tmasks) - 1, -1, -1):
            got = swap(total, TP, tmasks[level])
            yield None, True
            if level:
                total = join(meta, 0, level, total, got)
        (kept.bc,) = simple(bc_out_body, [total, got], [shaped((2, d, L))], "bc_weights", meta)

    run_chains(
        {
            "L": links_chain(),
            "W": weights_chain(lambda: (normout, cot_all, 1), out_weights),
            "G": weights_chain(lambda: (normed, ggr, 0), gate_weights),
            "F": within_chain(),
            "B": branch_chain(),
            "T": tokens_chain(),
            "I": weights_chain(
                lambda: (normed, kept.gcat, 0, normed_rim, kept.extra), inner_weights, "L", "G"
            ),
            "M": misc_chain(),
        },
        done,
        ORDER if (dps, group) == (8, 4) else "",
    )

    gain_g, bc_g, bcb_g, step_g, taps_g, bias_g, sb_g, dl_g, sk_g, ng_g = kept.small
    return (
        kept.layer,
        kept.tokens,
        gain_g[0],
        kept.zx,
        kept.bc,
        step_g.T,
        taps_g,
        bias_g[0],
        bc_g,
        bcb_g,
        sb_g[0],
        dl_g[0],
        sk_g[0],
        ng_g[0],
        kept.wout,
    )


def solution(mesh):
    rows = P((DP, TP), None)
    cols = P(None, TP)
    one = P(TP)
    in_specs = (
        rows, rows, P(), P(), P(None, None, TP), P(), cols, cols, one, P(), P(),
        one, one, one, one, P(TP, None),
    )
    out_specs = (
        rows, rows, P(), P(None, None, TP), P(), cols, cols, one, P(), P(),
        one, one, one, one, P(TP, None),
    )
    return jax.shard_map(
        on_device, mesh=mesh, in_specs=in_specs, out_specs=out_specs, check_vma=False
    )
```

```python
import functools
from types import SimpleNamespace
from typing import Any, NamedTuple

import jax
import jax.numpy as jnp
from jax import lax
from jax.experimental import pallas as pl
from jax.experimental.pallas import tpu as pltpu
from jax.sharding import PartitionSpec as P

KERNEL = 4
L = 128
HD = 64
DI = 2048
EPS = 1e-05
F32 = jnp.float32
BF = jnp.bfloat16
MIB = 1 << 20
ROW = 256
DP, TP = "dp", "tensor"
ROWS, EACH, ONE = range(3)


def dot(a, b, ca=1, cb=0):
    return lax.dot_general(a, b, (((ca,), (cb,)), ((), ())), preferred_element_type=F32)


def split(a):
    hi = a.astype(BF)
    return hi, (a - hi.astype(F32)).astype(BF)


def dot_l(a, b, ca=1, cb=0):
    hi, lo = split(a)
    return dot(hi, b, ca, cb) + dot(lo, b, ca, cb)


def dot_r(a, b, ca=1, cb=0):
    hi, lo = split(b)
    return dot(a, hi, ca, cb) + dot(a, lo, ca, cb)


def sigmoid(v):
    return 0.5 * jnp.tanh(0.5 * v) + 0.5


def softplus(v):
    u = jnp.exp(-jnp.abs(v))
    small = u * (1.0 - u * (0.5 - u * (1.0 / 3.0 - u * 0.25)))
    return jnp.maximum(v, 0.0) + jnp.where(u < 0.02, small, jnp.log(1.0 + u))


def per_head(row, heads):
    return jnp.concatenate(
        [jnp.broadcast_to(row[:, h : h + 1], (HD, L)) for h in range(heads)], axis=0
    )


def eights(v):
    return jnp.sum(v.reshape(v.shape[0] // 8, 8, v.shape[1]), axis=0)


def across_lanes(v, width):
    return jnp.concatenate([v] * (width // L), axis=1) if width > L else v


def whole(a):
    return pl.BlockSpec(a.shape, lambda *_: (0,) * a.ndim)


LAST = []

def launch(body, ins, in_specs, outs, out_specs, name, grid=(1,), meta=None, scratch=(),
           aliases=None, vmem=8, flops=0, token=True):
    ins, in_specs = list(ins), list(in_specs)
    lead = 0 if meta is None else 1
    at = lead + len(ins)
    given = LAST[-1] if LAST and not any(LAST[-1] is a for a in ins) else None
    if given is not None:
        ins.append(given)
        in_specs.append(pl.BlockSpec(memory_space=pl.ANY))

    def run(*refs):
        body(*(refs if given is None else refs[:at] + refs[at + 1 :]))

    results = pl.pallas_call(
        run,
        grid_spec=pltpu.PrefetchScalarGridSpec(
            num_scalar_prefetch=lead,
            grid=grid,
            in_specs=in_specs,
            out_specs=list(out_specs),
            scratch_shapes=list(scratch),
        ),
        out_shape=list(outs),
        input_output_aliases={lead + k: v for k, v in (aliases or {}).items()},
        compiler_params=pltpu.CompilerParams(vmem_limit_bytes=vmem * MIB),
        cost_estimate=pl.CostEstimate(
            flops=flops,
            bytes_accessed=0,
            transcendentals=0,
        ),
        name=name,
    )(*([] if meta is None else [meta]), *ins)
    if token:
        LAST[:] = [min(results, key=lambda a: a.size)]
    return results


def space_body(o):
    o[...] = jnp.zeros_like(o)


def space(flops=10 * 10**9):
    o = shaped((8, L))
    launch(space_body, [], [], [o], [whole(o)], "space", vmem=1, flops=flops)


def shaped(shape, dtype=F32):
    return jax.ShapeDtypeStruct(shape, dtype)


def simple(body, ins, outs, name, meta=None, vmem=8, deps=()):
    n = len(ins)

    def run(*refs):
        lead = 0 if meta is None else 1
        body(*refs[: lead + n], *refs[lead + n + len(deps) :])

    return launch(
        run, [*ins, *deps],
        [whole(a) for a in ins] + [pl.BlockSpec(memory_space=pl.ANY)] * len(deps),
        outs, [whole(o) for o in outs], name, meta=meta, vmem=vmem,
    )


def unit_rows(x, gain):
    x = x.astype(F32)
    rstd = lax.rsqrt(jnp.mean(x * x, axis=1, keepdims=True) + EPS)
    return (x * rstd * gain).astype(BF)


def proj_body(k, rims, deps, meta, *refs):
    toks, past = refs[:k], refs[k : k + rims]
    gain, wzx, wbc, wst = refs[k + rims : k + rims + 4]
    outs = refs[k + rims + 4 + deps :]
    normed_o, gate_o, cat_o, step_o = outs[:4]
    width = wzx.shape[2]

    def conv_inputs(normed, out):
        out[:, :width] = dot(normed, wzx[1]).astype(BF)
        out[:, width : width + L] = dot(normed, wbc[0]).astype(BF)
        out[:, width + L :] = dot(normed, wbc[1]).astype(BF)

    def one(j):
        normed = unit_rows(toks[j][...], gain[...])
        normed_o[...] = normed
        conv_inputs(normed, cat_o)
        gate_o[...] = dot(normed, wzx[0]).astype(BF)
        step_o[...] = dot(normed, wst[...], 1, 1).astype(BF)
        if rims and j == 0:
            rim = past[0][...].astype(F32)
            for p in past[1:]:
                rim = rim + p[...].astype(F32)
            normed = unit_rows(rim, gain[...])
            outs[5][...] = normed
            conv_inputs(normed, outs[4])

    for j in range(k):
        pl.when(pl.program_id(0) == j)(functools.partial(one, j))


def project(meta, toks, past, gain, wzx, wbc, wst, total, first, before):
    k = len(toks)
    share, d = toks[0].shape
    width = wzx.shape[2]
    wide = width + 2 * L
    cols = (d, width, wide, L)
    ins = [*toks, *past, gain, wzx, wbc, wst]
    specs = [whole(a) for a in ins]
    out_specs = [pl.BlockSpec((share, c), lambda i, m: (i + first, 0)) for c in cols]
    out_shape = [shaped((total, c), BF) for c in cols]
    if past:
        for c in (wide, d):
            out_specs.append(pl.BlockSpec((16, c), lambda i, m: (0, 0)))
            out_shape.append(shaped((16, c), BF))
    aliases = {len(ins) + j: j for j in range(4)} if before else {}
    return launch(
        functools.partial(proj_body, k, len(past), len(before)),
        ins + before,
        specs + [pl.BlockSpec(memory_space=pl.ANY)] * len(before),
        out_shape,
        out_specs,
        "project",
        grid=(k,),
        meta=meta,
        aliases=aliases,
        vmem=16,
        token=False,
    )


def prep_body(taps, tbias, btaps, bbias, sbias, decay, skip, ngain, wst, vecs, hv, mats, wst_o):
    width = taps.shape[1]
    heads = width // HD
    wst_o[...] = jnp.zeros_like(wst_o)
    wst_o[0:heads, :] = wst[...]
    head = lax.broadcasted_iota(jnp.int32, (L, width), 0)
    lane = lax.broadcasted_iota(jnp.int32, (L, width), 1)
    spread = jnp.where(lax.div(lane, HD) == head, 1.0, 0.0).astype(BF)
    mats[:, :width] = spread
    r = lax.broadcasted_iota(jnp.int32, (L, L), 0)
    c = lax.broadcasted_iota(jnp.int32, (L, L), 1)
    mats[:, width:] = jnp.where(r >= c, 1.0, 0.0).astype(BF)
    hv[...] = jnp.zeros_like(hv)
    hv[0:1, :heads] = sbias[...]
    hv[1:2, :heads] = -jnp.exp(decay[...])
    hv[2:3, :heads] = skip[...]
    vecs[...] = jnp.zeros_like(vecs)
    vecs[0:4, :width] = taps[...]
    vecs[4:5, :width] = tbias[...]
    for k in range(2):
        cols = slice(width + k * L, width + k * L + L)
        vecs[0:4, cols] = btaps[k]
        vecs[4:5, cols] = bbias[k : k + 1, :]
    vecs[5:6, :width] = dot_l(hv[...], spread)[2:3, :]
    vecs[6:7, :width] = ngain[...]


def cot_body(k, *refs):
    cots = refs[:k]
    wout, all_o, gn_o = refs[k:]

    def one(cot):
        v = cot[...]
        all_o[...] = v
        gn_o[...] = dot(v, wout[...], 1, 1).astype(BF)

    for j in range(k):
        pl.when(pl.program_id(0) == j)(functools.partial(one, cots[j]))


def cotangent(cots, wout):
    k = len(cots)
    share, d = cots[0].shape
    width = wout.shape[0]
    return launch(
        functools.partial(cot_body, k),
        [*cots, wout],
        [whole(a) for a in (*cots, wout)],
        [shaped((k * share, d), BF), shaped((k * share, width), BF)],
        [pl.BlockSpec((share, c), lambda i: (i, 0)) for c in (d, width)],
        "cotangent",
        grid=(k,),
        vmem=12,
    )


def act_parts(pre, width):
    out = []
    for x0 in range(0, width + 2 * L, L):
        v = pre[:, x0 : x0 + L]
        out.append(v * sigmoid(v))
    return out


def pack(out, state, decay):
    rows = state.shape[0]
    hi, lo = split(jnp.broadcast_to(decay[0:1, :], (16, L)))
    row = lax.broadcasted_iota(jnp.int32, (16, L), 0)
    out[:rows, :] = state.astype(BF)
    tail = jnp.where(row == 0, hi.astype(F32), jnp.where(row == 1, lo.astype(F32), 0.0))
    out[rows:, :] = tail.astype(BF)


def unpack(load):
    v = load[...].astype(F32)
    rows = v.shape[0] - 16
    return v[:rows], v[rows : rows + 1] + v[rows + 1 : rows + 2]


def bit_at(meta, level):
    return jnp.bitwise_and(jnp.right_shift(meta[1], level), 1)


def is_ahead(meta, level, reverse):
    bit = bit_at(meta, level)
    return jnp.where(bit == (0 if reverse else 1), 1.0, 0.0)


def link_body(level, reverse, final, meta, state, decay, before, through, load,
              load_o, before_o, through_o, *more):
    theirs, a = unpack(load)
    heads = theirs.shape[0] // HD
    ahead = is_ahead(meta, level, reverse)
    mine = decay[0:1, :]
    t = through[0:1, :]
    before_o[...] = before[...] + per_head(t * ahead, heads) * theirs
    through_o[...] = jnp.broadcast_to(t * (ahead * a + (1.0 - ahead)), (8, L))
    joined = (
        per_head(mine * ahead + (1.0 - ahead), heads) * theirs
        + per_head(a * (1.0 - ahead) + ahead, heads) * state[...]
    )
    pack(load_o, joined, mine * a)
    if not final:
        state_o, decay_o = more
        state_o[...] = joined
        decay_o[...] = jnp.broadcast_to(mine * a, (8, L))


def final_link(meta, level, reverse, before, through, load):
    theirs, _ = unpack(load)
    t = through[0:1, :] * is_ahead(meta, level, reverse)
    return before[...] + per_head(t, theirs.shape[0] // HD) * theirs


def states_body(
    at, meta, cat, step, rim, vecs, hv, mats,
    pre_o, sin_o, end_o, load_o, cum_o, pfx_o, thr_o, buf, state, prod,
):
    width = vecs.shape[1] - 2 * L
    heads = width // HD
    keep = jnp.where(meta[2 + at.c] == 0, 1.0, 0.0)
    before, buf = buf.at[at.other], buf.at[at.sub]

    def follow():
        buf[0:8, :] = before[L : L + 8, :] * keep

    if at.first is None:
        follow()
    else:

        @pl.when(at.first)
        def _():
            buf[0:8, :] = rim[...].astype(F32)[8:16, :] * keep
            state[...] = jnp.zeros_like(state)
            prod[...] = jnp.ones_like(prod)

        pl.when(jnp.logical_not(at.first))(follow)

    buf[8 : 8 + L, :] = cat[...].astype(F32)
    acts = []
    for x0 in range(0, width + 2 * L, L):
        cols = slice(x0, x0 + L)
        v = vecs[4:5, cols] + vecs[3:4, cols] * buf[8 : 8 + L, cols]
        for j in range(1, KERNEL):
            v = v + vecs[3 - j : 4 - j, cols] * buf[8 - j : 8 - j + L, cols]
        pre_o[:, cols] = v
        acts.append(v * sigmoid(v))
    steps = softplus(step[...].astype(F32) + hv[0:1, :])
    cum = dot_r(mats[:, width:], steps * hv[1:2, :])
    cum_o[...] = cum
    total = cum[L - 1 : L, :]
    weights = dot((jnp.exp(total - cum) * steps).astype(BF), mats[:, :width])
    inner = jnp.concatenate(acts[: width // L], axis=1)
    local = dot((inner * weights).astype(BF), acts[-2].astype(BF), 0, 0)
    entering = state[...] * keep
    sin_o[0] = entering.astype(BF)
    dec = jnp.exp(total)
    leaving = per_head(dec, heads) * entering + local
    state[...] = leaving
    here = prod[...] * keep
    pfx_o[0] = here
    prod[...] = here * dec

    if at.last is not None:

        @pl.when(at.last)
        def _():
            end_o[...] = leaving
            thr_o[...] = here * dec
            pack(load_o, leaving, here * dec)


def within_body(at, meta, pre, step, cum_r, sin, vecs, hv, mats, y_o):
    width = vecs.shape[1] - 2 * L
    heads = width // HD
    acts = act_parts(pre, width)
    bb, cb = acts[-2].astype(BF), acts[-1].astype(BF)
    scores = dot(cb, bb, 1, 1)
    steps = softplus(step[...].astype(F32) + hv[0:1, :])
    cum = cum_r[...]
    cum_t, steps_t = cum.T, steps.T
    lower = lax.broadcasted_iota(jnp.int32, (L, L), 0) >= lax.broadcasted_iota(
        jnp.int32, (L, L), 1
    )
    first = lax.broadcasted_iota(jnp.int32, (L, L), 1) < HD
    grown = dot(jnp.exp(cum).astype(BF), mats[:, :width])
    far = grown * dot(cb, sin[0], 1, 1)
    for pair in range(heads // 2):
        cols = slice(pair * L, pair * L + L)
        x = acts[pair].astype(BF)
        got = []
        for h in (2 * pair, 2 * pair + 1):
            gap = jnp.where(lower, cum[:, h : h + 1] - cum_t[h : h + 1, :], -1e30)
            mix = scores * jnp.exp(gap) * steps_t[h : h + 1, :]
            got.append(dot(mix.astype(BF), x))
        y_o[:, cols] = jnp.where(first, got[0], got[1]) + far[:, cols]


def gate_body(
    level, at, meta, pre, cum, pfx, y, gate, gn, before, through, load, vecs, mats,
    mixed_o, sums_o, incoming,
):
    width = vecs.shape[1] - 2 * L
    ones = jnp.ones((8, L), BF)

    if at.first is not None:

        @pl.when(at.first)
        def _():
            incoming[...] = final_link(meta, level, False, before, through, load).astype(BF)

    reach = dot((jnp.exp(cum[...]) * pfx[0][0:1, :]).astype(BF), mats[:, :width])
    cv = pre[:, width + L :]
    cb = (cv * sigmoid(cv)).astype(BF)
    far = reach * dot(cb, incoming[...], 1, 1)
    squares, crosses = [], []
    for x0 in range(0, width, L):
        cols = slice(x0, x0 + L)
        v = pre[:, cols]
        mixed = y[:, cols] + far[:, cols] + vecs[5:6, cols] * (v * sigmoid(v))
        mixed_o[:, cols] = mixed
        g = gate[:, cols].astype(F32)
        gated = mixed * (g * sigmoid(g))
        squares.append(gated * gated)
        crosses.append(gn[:, cols].astype(F32) * vecs[6:7, cols] * gated)
    square = dot_r(ones, functools.reduce(jnp.add, squares), 1, 1)
    cross = dot_r(ones, functools.reduce(jnp.add, crosses), 1, 1)
    sums_o[0, 0:1] = square[0:1]
    sums_o[0, 1:2] = cross[0:1]


def back_gate_body(
    at, meta, pre, cum_r, mixed_r, gate, gn, sums, sums2, thr, vecs, mats,
    normout_o, gm_o, ggr_o, gs_o, toward_o, load_o, sfx_o, acc_o, gstate, prod, acc,
):
    width = vecs.shape[1] - 2 * L
    heads = width // HD
    keep = jnp.where(meta[2 + at.c] == 0, 1.0, 0.0)

    if at.first is not None:

        @pl.when(at.first)
        def _():
            gstate[...] = jnp.zeros_like(gstate)
            prod[...] = jnp.ones_like(prod)
            acc[...] = jnp.zeros_like(acc)

    both = sums[0] + sums2[0]
    square = jnp.broadcast_to(both[0:1, :], (L, L)).T
    cross = jnp.broadcast_to(both[1:2, :], (L, L)).T
    scale = lax.rsqrt(square * (1.0 / DI) + EPS)
    cubed = scale * scale * scale * cross * (1.0 / DI)
    cum = cum_r[...]
    total = cum[L - 1 : L, :]
    grown = dot(jnp.exp(cum).astype(BF), mats[:, :width])
    cv = pre[:, width + L :]
    cb = (cv * sigmoid(cv)).astype(BF)
    moved = []
    for x0 in range(0, width, L):
        cols = slice(x0, x0 + L)
        v = pre[:, cols]
        inner = v * sigmoid(v)
        g = gate[:, cols].astype(F32)
        s = sigmoid(g)
        silu = g * s
        mixed = mixed_r[:, cols]
        gated = mixed * silu
        ng = vecs[6:7, cols]
        gnv = gn[:, cols].astype(F32)
        scaled = gated * scale
        normout_o[:, cols] = (scaled * ng).astype(BF)
        gg = scale * (gnv * ng) - gated * cubed
        gm = gg * silu
        gm_o[:, cols] = gm.astype(BF)
        ggr_o[:, cols] = (gg * mixed * (s + silu * (1.0 - s))).astype(BF)
        acc[0:8, cols] += eights(gnv * scaled)
        acc[8:16, cols] += eights(gm * inner)
        moved.append((gm * grown[:, cols]).astype(BF))
    leaving = gstate[...]
    gs_o[0] = leaving.astype(BF)
    here = prod[...]
    sfx_o[0] = here
    dec = jnp.exp(total)
    entering = per_head(dec, heads) * leaving + dot(jnp.concatenate(moved, axis=1), cb, 0, 0)
    entering = entering * keep
    gstate[...] = entering
    prod[...] = here * dec * keep

    if at.last is not None:

        @pl.when(at.last)
        def _():
            toward_o[...] = entering
            pack(load_o, entering, thr[...])
            row = lax.broadcasted_iota(jnp.int32, (8, width), 0)
            acc_o[...] = jnp.where(
                row == 0,
                jnp.sum(acc[0:8, :], axis=0, keepdims=True),
                jnp.sum(acc[8:16, :], axis=0, keepdims=True),
            )


def head_product(a, b, spread):
    rows = dot(jnp.ones((8, L), BF), (a * b).astype(BF), 1, 1)
    return dot_l(rows, spread, 1, 1)[0:1, :]


def back_within_body(
    at, meta, pre, step, cum_r, sin, pfx, gs, gm_r, incoming, vecs, hv, mats,
    ginner_o, gbc_o, glog_o, gst_o,
):
    width = vecs.shape[1] - 2 * L
    heads = width // HD
    acts = act_parts(pre, width)
    bb, cb = acts[-2].astype(BF), acts[-1].astype(BF)
    scores = dot(cb, bb, 1, 1)
    steps = softplus(step[...].astype(F32) + hv[0:1, :])
    cum = cum_r[...]
    total = cum[L - 1 : L, :]
    cum_t, steps_t = cum.T, steps.T
    row = lax.broadcasted_iota(jnp.int32, (L, L), 0)
    col = lax.broadcasted_iota(jnp.int32, (L, L), 1)
    lower = row >= col
    first = col < HD
    e = jnp.exp(cum)
    wd = jnp.exp(total - cum)
    grown = dot(e.astype(BF), mats[:, :width])
    weights = dot((wd * steps).astype(BF), mats[:, :width])
    gsb = gs[0]
    entering = sin[0].astype(F32) + per_head(pfx[0][0:1, :], heads) * incoming[...].astype(F32)
    eb = entering.astype(BF)
    u = dot(bb, gsb, 1, 1)
    v = dot(cb, eb, 1, 1)
    inner = jnp.concatenate(acts[: width // L], axis=1)
    gm = gm_r[...].astype(F32)
    seen = dot((inner * u).astype(BF), mats[:, :width], 1, 1)
    passed = dot((gm * v).astype(BF), mats[:, :width], 1, 1) * e
    gb = dot((inner * weights).astype(BF), gsb)
    gc = dot((gm * grown).astype(BF), eb)
    through = head_product(gsb.astype(F32), entering, mats[:, :width]) * jnp.exp(total)
    dscores = jnp.zeros((L, L), F32)
    rowsums = jnp.zeros((L, L), F32)
    colsums = jnp.zeros((L, L), F32)
    for pair in range(heads // 2):
        cols = slice(pair * L, pair * L + L)
        xb = acts[pair].astype(BF)
        gmb = gm_r[:, cols]
        got = []
        for h in (2 * pair, 2 * pair + 1):
            mine = first if h % 2 == 0 else jnp.logical_not(first)
            gmh = jnp.where(mine, gm[:, cols], 0.0).astype(BF)
            dm = dot(gmh, xb, 1, 1)
            gap = jnp.where(lower, cum[:, h : h + 1] - cum_t[h : h + 1, :], -1e30)
            decay = jnp.exp(gap)
            st = steps_t[h : h + 1, :]
            t1 = dm * decay
            dscores = dscores + t1 * st
            gp = t1 * scores
            rowsums = jnp.where(col == h, jnp.sum(gp * st, axis=1, keepdims=True), rowsums)
            colsums = jnp.where(row == h, jnp.sum(gp, axis=0, keepdims=True), colsums)
            mix = (scores * decay * st).astype(BF)
            got.append(dot(mix, gmb, 0, 0))
        ginner_o[:, cols] = (
            jnp.where(first, got[0], got[1])
            + weights[:, cols] * u[:, cols]
            + vecs[5:6, cols] * gm[:, cols]
        )
    db = dscores.astype(BF)
    gbc_o[:, :L] = gb + dot(db, cb, 0, 0)
    gbc_o[:, L:] = gc + dot(db, bb)
    direct = colsums.T
    seen = seen * wd
    gst_o[...] = direct + seen
    later = rowsums - direct * steps + passed
    tr = mats[:, width:]
    glog_o[...] = (
        dot_r(tr, later, 0, 0) + dot_r(tr, steps * seen) - steps * seen + through
    )


def crossing(vecs, later):
    row = lax.broadcasted_iota(jnp.int32, (16, later.shape[1]), 0)
    extra = jnp.zeros((16, later.shape[1]), F32)
    for j in range(1, KERNEL):
        for t in range(j):
            part = vecs[3 - j : 4 - j, :] * later[t : t + 1, :]
            extra = extra + jnp.where(row == 16 - j + t, part, 0.0)
    return extra


def back_conv_body(
    level, at, meta, cat, rim, pre, step, cum_r, sin, pfx, sfx, ginner_r, gbc_r, glog_r, gst_r,
    incoming, before, through, load, vecs, hv, mats,
    gcat_o, gsr_o, head_o, extra_o, acc_o, hacc_o, buf, acc, hacc, outgoing,
):
    width = vecs.shape[1] - 2 * L
    heads = width // HD
    keep_next = jnp.where(meta[3 + at.c] == 0, 1.0, 0.0)
    keep = jnp.where(meta[2 + at.c] == 0, 1.0, 0.0)
    later, buf = buf.at[at.other], buf.at[at.sub]

    def follow():
        buf[L : L + 8, :] = later[0:8, :] * keep_next

    if at.first is None:
        follow()
    else:

        @pl.when(at.first)
        def _():
            buf[L : L + 8, :] = jnp.zeros((8, width + 2 * L), F32)
            acc[...] = jnp.zeros_like(acc)
            hacc[...] = jnp.zeros_like(hacc)
            outgoing[...] = final_link(meta, level, True, before, through, load)

        pl.when(jnp.logical_not(at.first))(follow)

    step_in = step[...].astype(F32) + hv[0:1, :]
    steps = softplus(step_in)
    cum = cum_r[...]
    total = cum[L - 1 : L, :]
    wd = jnp.exp(total - cum)
    weights = dot((wd * steps).astype(BF), mats[:, :width])
    far = outgoing[...] * per_head(sfx[0][0:1, :], heads)
    fb = far.astype(BF)
    entering = sin[0].astype(F32) + per_head(pfx[0][0:1, :], heads) * incoming[...].astype(F32)
    through = head_product(far, entering, mats[:, :width]) * jnp.exp(total)
    acts, slopes = [], []
    for x0 in range(0, width + 2 * L, L):
        v = pre[:, x0 : x0 + L]
        s = sigmoid(v)
        a = v * s
        acts.append(a)
        slopes.append(s + a * (1.0 - s))
    bb = acts[-2].astype(BF)
    u = dot(bb, fb, 1, 1)
    inner = jnp.concatenate(acts[: width // L], axis=1)
    seen = dot((inner * u).astype(BF), mats[:, :width], 1, 1) * wd
    gb = dot((inner * weights).astype(BF), fb)
    glog = glog_r[...] + dot_r(mats[:, width:], steps * seen) - steps * seen + through
    gsi = (gst_r[...] + seen + glog * hv[1:2, :]) * sigmoid(step_in)
    gsr_o[...] = gsi.astype(BF)
    hacc[0:8, :] += eights(glog * steps * hv[1:2, :])
    hacc[8:16, :] += eights(gsi)
    for k, x0 in enumerate(range(0, width + 2 * L, L)):
        cols = slice(x0, x0 + L)
        if x0 < width:
            g = ginner_r[:, cols] + weights[:, cols] * u[:, cols]
        elif x0 == width:
            g = gbc_r[:, :L] + gb
        else:
            g = gbc_r[:, L:]
        g = g * slopes[k]
        buf[0:L, cols] = g
        acc[32:40, cols] += eights(g)
        here = cat[:, cols].astype(F32)
        out = vecs[3:4, cols] * g
        acc[24:32, cols] += eights(g * here)
        for j in range(1, KERNEL):
            moved = buf[j : j + L, cols]
            out = out + vecs[3 - j : 4 - j, cols] * moved
            acc[24 - 8 * j : 32 - 8 * j, cols] += eights(moved * here)
        gcat_o[:, cols] = out.astype(BF)
    if at.last is not None:

        @pl.when(at.last)
        def _():
            head_o[...] = buf[0:8, :]
            past = rim[...].astype(F32)[8:16, :] * keep
            now = buf[0:8, :]
            extra_o[...] = crossing(vecs, now * keep).astype(BF)
            row = lax.broadcasted_iota(jnp.int32, now.shape, 0)
            result = jnp.zeros_like(now)
            for k in range(5):
                part = jnp.sum(acc[8 * k : 8 * k + 8, :], axis=0, keepdims=True)
                j = 3 - k
                if 1 <= j <= 3:
                    for t in range(j):
                        part = part + now[t : t + 1, :] * past[8 + t - j : 9 + t - j, :]
                result = jnp.where(row == k, part, result)
            acc_o[...] = result
            hrow = lax.broadcasted_iota(jnp.int32, (8, L), 0)
            hacc_o[...] = jnp.where(
                hrow == 0,
                jnp.sum(hacc[0:8, :], axis=0, keepdims=True),
                jnp.sum(hacc[8:16, :], axis=0, keepdims=True),
            )


def dgrad_body(k, ggr, gcat, gsr, normed, wzx, wbc, wst, gain, conv, *refs):
    outs, shared_o, acc = refs[:k], refs[k], refs[k + 1]
    width, d = wzx.shape[2], gain.shape[1]
    i = pl.program_id(0)

    @pl.when(i == 0)
    def _():
        acc[...] = jnp.zeros_like(acc)

    r = dot(ggr[...], wzx[0], 1, 1)
    r = r + dot(gcat[:, :width], wzx[1], 1, 1)
    r = r + dot(gcat[:, width : width + L], wbc[0], 1, 1)
    r = r + dot(gcat[:, width + L :], wbc[1], 1, 1)
    r = r + dot(gsr[...], wst[...])
    acc[...] += eights(r * normed[...].astype(F32))
    rounded = r.astype(BF)

    def into(out):
        out[...] = rounded

    for j in range(k):
        pl.when(i == j)(functools.partial(into, outs[j]))

    @pl.when(i == k - 1)
    def _():
        shared_o[...] = jnp.zeros_like(shared_o)
        sums = jnp.sum(acc[...], axis=0, keepdims=True) / gain[...]
        for c in range(d // ROW):
            shared_o[c : c + 1, :] = sums[:, c * ROW : (c + 1) * ROW]
        shared_o[d // ROW : d // ROW + 5, :] = conv[0:5, conv.shape[1] - ROW :]


def outproj_body(k, normout, wout, *outs):
    def one(out):
        out[...] = dot(normout[...], wout[...]).astype(BF)

    for j in range(k):
        pl.when(pl.program_id(0) == j)(functools.partial(one, outs[j]))


def rows_times(body, frames_n, share, d, rows, consts, name, more=(), scratch=()):
    k = frames_n
    outs = launch(
        functools.partial(body, k),
        [*rows, *consts],
        [pl.BlockSpec((share, r.shape[1]), lambda i: (k - 1 - i, 0)) for r in rows]
        + [whole(a) for a in consts],
        [shaped((share, d), BF)] * k + list(more),
        [pl.BlockSpec((share, d), lambda i: (0, 0))] * k + [whole(o) for o in more],
        name,
        grid=(k,),
        scratch=scratch,
        vmem=20,
    )
    return [*outs[:k][::-1], *outs[k:]]


def total_body(*refs):
    total = refs[0][...].astype(F32)
    for ref in refs[1:-1]:
        total = total + ref[...].astype(F32)
    refs[-1][...] = total.astype(BF)


def hold_body(x, o):
    o[...] = x[...]


def hold(x, *deps):
    return simple(hold_body, [x], [shaped(x.shape, x.dtype)], "hold", deps=deps)[0]


def add_body(a, b, o):
    o[...] = (a[...].astype(F32) + b[...].astype(F32)).astype(o.dtype)


def add(a, b):
    return simple(add_body, [a, b], [shaped(a.shape, a.dtype)], "add")[0]


def swap(x, axis, mask):
    count = lax.axis_size(axis)
    return lax.ppermute(x, axis, [(i, i ^ mask) for i in range(count)])


def masks_of(axis):
    masks, mask = [], 1
    while mask < lax.axis_size(axis):
        masks.append(mask)
        mask *= 2
    return masks


def halve_body(slot, level, meta, kept, got, send_o, keep_o):
    bit = jnp.bitwise_and(jnp.right_shift(meta[slot], level), 1)
    half = send_o.shape[0]
    for o, b in ((send_o, 1 - bit), (keep_o, bit)):
        rows = pl.ds(pl.multiple_of(b * half, half), half)
        o[...] = (kept[rows, :].astype(F32) + got[rows, :].astype(F32)).astype(BF)


def halve(meta, slot, level, kept, got):
    shape = shaped((kept.shape[0] // 2, kept.shape[1]), BF)
    return simple(
        functools.partial(halve_body, slot, level), [kept, got], [shape, shape], "halve", meta
    )


def join_body(slot, level, meta, own, got, o):
    bit = jnp.bitwise_and(jnp.right_shift(meta[slot], level), 1)
    half = own.shape[0]
    o[pl.ds(pl.multiple_of(bit * half, half), half), :] = own[...]
    o[pl.ds(pl.multiple_of((1 - bit) * half, half), half), :] = got[...]


def join(meta, slot, level, own, got):
    shape = shaped((own.shape[0] * 2, own.shape[1]), BF)
    return simple(functools.partial(join_body, slot, level), [own, got], [shape], "join", meta)[0]


def wgrad_body(blocks, half, tails, meta, *refs):
    ins, (send_o, keep_o) = refs[:-2], refs[-2:]
    bit = bit_at(meta, 0)
    i = pl.program_id(0)
    g = jnp.where(i < half, (1 - bit) * half + i, bit * half + i - half)
    for p, tail in enumerate(tails):
        (a, b), ins = ins[:2], ins[2:]
        ta = tb = None
        if tail:
            (ta, tb), ins = ins[:2], ins[2:]
        inside = jnp.logical_and(g >= p * blocks, g < (p + 1) * blocks)

        def into(o, a=a, b=b, ta=ta, tb=tb):
            v = dot(a[...], b[...], 0, 0)
            if ta is not None:
                v = v + dot(ta[...], tb[...], 0, 0)
            o[...] = v.astype(BF)

        pl.when(jnp.logical_and(inside, i < half))(functools.partial(into, send_o))
        pl.when(jnp.logical_and(inside, i >= half))(functools.partial(into, keep_o))


def wgrads(meta, pairs, width, blocks):
    half = blocks * len(pairs) // 2
    tokens = pairs[0][0].shape[0]

    def cut(i, m):
        bit = jnp.bitwise_and(m[1], 1)
        g = jnp.where(i < half, (1 - bit) * half + i, bit * half + i - half)
        return (0, lax.rem(g, blocks))

    specs, ins = [], []
    for a, b, which, *more in pairs:
        for pair in [(a, b), tuple(more)]:
            for j, v in enumerate(pair):
                ins.append(v)
                specs.append(
                    pl.BlockSpec((v.shape[0], width), cut if j == which else lambda i, m: (0, 0))
                )
    return launch(
        functools.partial(wgrad_body, blocks, half, [len(p) > 3 for p in pairs]),
        ins,
        specs,
        [shaped((half * width, width), BF)] * 2,
        [
            pl.BlockSpec((width, width), lambda i, m: (jnp.minimum(i, half - 1), 0)),
            pl.BlockSpec((width, width), lambda i, m: (jnp.maximum(i - half, 0), 0)),
        ],
        "wgrad",
        grid=(2 * half,),
        meta=meta,
        vmem=20,
    )


def bc_body(meta, normed, gcat, gsr, rim, extra, send_o, keep_o, step_o):
    bit = jnp.bitwise_and(meta[0], 1)
    half = send_o.shape[0]
    for o, b in ((send_o, 1 - bit), (keep_o, bit)):
        cols = pl.ds(pl.multiple_of(b * half, half), half)
        v = dot(normed[:, cols], gcat[...], 0, 0) + dot(rim[:, cols], extra[...], 0, 0)
        o[...] = v.astype(BF)
    step_o[...] = dot(gsr[...], normed[...], 0, 0)[:8]


def bc_wgrad(meta, normed, gcat, gsr, rim, extra, width):
    tokens, d = normed.shape

    def tail(rows):
        return pl.BlockSpec((rows, 2 * L), lambda i, m: (0, width // (2 * L)))

    outs = [shaped((d // 2, 2 * L), BF)] * 2 + [shaped((8, d))]
    return launch(
        bc_body,
        [normed, gcat, gsr, rim, extra],
        [whole(normed), tail(tokens), whole(gsr), whole(rim), tail(16)],
        outs,
        [whole(o) for o in outs],
        "bc_wgrad",
        meta=meta,
        vmem=12,
    )


def columns_body(blocks, width, src, *rest):
    o = rest[-1]
    for k in range(blocks):
        o[:, k * width : (k + 1) * width] = src[k * width : (k + 1) * width, :].astype(F32)


def columns(meta, src, mine, d, width, old):
    half = src.shape[0]
    ins, specs, aliases = [src], [whole(src)], {}
    if old is not None:
        ins.append(old)
        specs.append(pl.BlockSpec(memory_space=pl.ANY))
        aliases = {1: 0}
    return launch(
        lambda meta, *refs: columns_body(half // width, width, *refs), ins, specs,
        [shaped((width, d))],
        [pl.BlockSpec((width, half), lambda i, m: (0, bit_at(m, 0) ^ (1 - mine)))],
        "out_weights", meta=meta, aliases=aliases, vmem=16, token=False,
    )[0]


def rows_body(src, *rest):
    rest[-1][0] = src[...].astype(F32)


def rows_of(meta, src, mine, which, d, width, old):
    half = src.shape[0]
    ins, specs, aliases = [src], [whole(src)], {}
    if old is not None:
        ins.append(old)
        specs.append(pl.BlockSpec(memory_space=pl.ANY))
        aliases = {1: 0}
    return launch(
        lambda meta, *refs: rows_body(*refs), ins, specs, [shaped((2, d, width))],
        [pl.BlockSpec((1, half, width), lambda i, m: (which, bit_at(m, 0) ^ (1 - mine), 0))],
        "zx_weights", meta=meta, aliases=aliases, vmem=16, token=False,
    )[0]


def bc_out_body(meta, own, got, o):
    bit = jnp.bitwise_and(meta[0], 1)
    half = own.shape[0]
    for v, b in ((own, bit), (got, 1 - bit)):
        rows = pl.ds(pl.multiple_of(b * half, half), half)
        o[0, rows, :] = v[:, :L].astype(F32)
        o[1, rows, :] = v[:, L:].astype(F32)


def patch_body(meta, gcat, ahead, vecs, o):
    count = meta.shape[0] - 3
    keep = jnp.where(meta[2 + count] == 0, 1.0, 0.0)
    o[...] = (gcat[...].astype(F32) + crossing(vecs, ahead[...] * keep)).astype(BF)


def patched(meta, gcat, ahead, vecs, share, group):
    wide = gcat.shape[1]

    def spot(i, m):
        return ((jnp.bitwise_xor(m[0], group - 1) + 1) * (share // 16) - 1, 0)

    return launch(
        patch_body,
        [gcat, ahead, vecs],
        [pl.BlockSpec((16, wide), spot), whole(ahead), whole(vecs)],
        [shaped(gcat.shape, BF)],
        [pl.BlockSpec((16, wide), spot)],
        "patch",
        meta=meta,
        aliases={0: 0},
        token=False,
    )[0]


def layer_body(tok, a, b, o):
    o[...] = (tok[...].astype(F32) + (a[...].astype(F32) + b[...].astype(F32))).astype(BF)


def tokens_body(tok, cot, a, b, gain, gt_o):
    x = tok[...].astype(F32)
    rstd = lax.rsqrt(jnp.mean(x * x, axis=1, keepdims=True) + EPS)
    unit = x * rstd
    gunit = (a[...].astype(F32) + b[...].astype(F32)) * gain[...]
    gt_o[...] = cot[...].astype(F32) + rstd * (
        gunit - unit * jnp.mean(gunit * unit, axis=1, keepdims=True)
    )


def halves_of(v):
    hi, lo = split(v)
    return jnp.concatenate([hi, lo], axis=0)


def whole_of(v):
    n = v.shape[0] // 2
    v = v.astype(F32)
    return v[:n] + v[n:]


def lead_body(bc, shared, o):
    rows = bc.shape[0]
    o[:rows, :] = bc[...]
    o[rows:, :] = halves_of(shared[...])


def misc_halve_body(level, meta, kept, shared, got, send_o, keep_o, shared_o):
    bit = jnp.bitwise_and(jnp.right_shift(meta[0], level), 1)
    half = keep_o.shape[0]
    total = shared[...] + whole_of(got[2 * half :, :])
    shared_o[...] = total
    for o, b in ((send_o, 1 - bit), (keep_o, bit)):
        rows = pl.ds(pl.multiple_of(b * half, half), half)
        o[0:half, :] = (kept[rows, :].astype(F32) + got[rows, :].astype(F32)).astype(BF)
    send_o[half:, :] = halves_of(total)


def misc_pack_body(kept, shared, got, step, conv, gate, head, o):
    rows = kept.shape[0]
    o[0:rows, :] = (kept[...].astype(F32) + got[0:rows, :].astype(F32)).astype(BF)
    d = step.shape[1]
    at = rows
    for k in range(d // ROW):
        o[at : at + 8, :] = step[:, k * ROW : (k + 1) * ROW].astype(BF)
        at += 8
    total = shared[...] + whole_of(got[rows:, :])
    width = gate.shape[1]
    parts = [total]
    for ref, first, n in ((conv, 0, 5), (gate, 0, 2)):
        for k in range(width // ROW):
            parts.append(ref[first : first + n, k * ROW : (k + 1) * ROW])
    used = 7 * (width // ROW)
    parts.append(jnp.concatenate([head[0:1, :], head[1:2, :]], axis=1))
    parts.append(jnp.zeros((31 - used, ROW), F32))
    o[at:, :] = halves_of(jnp.concatenate(parts, axis=0))


def misc_sum(a, b, plain_rows):
    first = a[0:plain_rows, :].astype(F32) + b[0:plain_rows, :].astype(F32)
    return first, whole_of(a[plain_rows:, :]) + whole_of(b[plain_rows:, :])


def misc_add_body(plain_rows, a, b, o):
    first, rest = misc_sum(a, b, plain_rows)
    o[0:plain_rows, :] = first.astype(BF)
    o[plain_rows:, :] = halves_of(rest)


def misc_finish_body(bc_rows, a, b, mats, bcw_o, gain_o, bc_o, bcb_o, step_o, taps_o, bias_o,
                     sb_o, dl_o, sk_o, ng_o):
    d, width, heads = gain_o.shape[1], taps_o.shape[1], sb_o.shape[1]
    n = d // ROW
    first, rest = misc_sum(a, b, bc_rows + 8 * n)
    bcw_o[...] = first[0:bc_rows].astype(BF)
    for k in range(n):
        cols = slice(k * ROW, (k + 1) * ROW)
        at = bc_rows + 8 * k
        step_o[:, cols] = first[at : at + heads]
        gain_o[:, cols] = rest[k : k + 1]
    for k in range(2):
        v = rest[n : n + 5, k * L : (k + 1) * L]
        bc_o[k] = v[0:4]
        bcb_o[k : k + 1, :] = v[4:5]
    at = 16
    m = width // ROW
    gates = []
    for k in range(m):
        cols = slice(k * ROW, (k + 1) * ROW)
        taps_o[:, cols] = rest[at : at + 4]
        bias_o[:, cols] = rest[at + 4 : at + 5]
        at += 5
    for k in range(m):
        cols = slice(k * ROW, (k + 1) * ROW)
        ng_o[:, cols] = rest[at : at + 1]
        gates.append(jnp.broadcast_to(rest[at + 1 : at + 2], (8, ROW)))
        at += 2
    sk = dot_l(jnp.concatenate(gates, axis=1), mats[:, :width], 1, 1)
    sk_o[...] = sk[0:1, :heads]
    dl_o[...] = rest[at : at + 1, :heads]
    sb_o[...] = rest[at : at + 1, L : L + heads]


class Spot(NamedTuple):
    c: Any
    sub: int
    other: int
    first: Any
    last: Any


ORDER = "LWLFLGFWLGTIWMGTWMIGTMTWMIGMWTIBBMBGIMIMWBGMI"


def run_chains(chains, done, order):
    needs = {name: next(chain) for name, chain in chains.items()}

    def step(name):
        need, waits = needs[name]
        if need is not None and need not in done:
            return False
        if waits:
            space()
        try:
            needs[name] = next(chains[name])
        except StopIteration:
            del needs[name]
            done.add(name)
        return True

    for name in order:
        if not step(name):
            raise ValueError(name)
    while needs:
        for name in list(needs):
            step(name)


def on_device(
    tokens_in,
    grad_out,
    scene_offsets,
    input_gain,
    weight_zx,
    weight_bc,
    weight_step,
    conv_inner,
    conv_inner_bias,
    conv_bc,
    conv_bc_bias,
    step_bias,
    decay_log,
    skip_weight,
    norm_gain,
    weight_out,
):
    share, d = tokens_in.shape
    group = lax.axis_size(TP)
    tokens = share * group
    heads = step_bias.shape[0]
    width = norm_gain.shape[0]
    wide = width + 2 * L
    count = tokens // L
    per = share // L
    half = group // 2
    me = lax.axis_index(TP)
    place = lax.axis_index(DP)

    heads_pos = place * tokens + jnp.arange(count + 1, dtype=jnp.int32) * L
    starts = jnp.any(heads_pos[:, None] == scene_offsets[None, :], axis=1).astype(jnp.int32)
    meta = jnp.concatenate([me[None].astype(jnp.int32), place[None].astype(jnp.int32), starts])
    masks, tmasks = masks_of(DP), masks_of(TP)
    levels = len(masks)

    LAST.clear()
    def spread_out(held, keys):
        mask = half // 2
        while mask:
            for f in [f for f in held if f in keys]:
                held[f ^ mask] = swap(held[f], TP, mask)
            mask //= 2

    near, far = range(half), range(half, group)
    held = {0: tokens_in}
    arrived = swap(tokens_in, TP, half)
    spread_out(held, near)
    dps = lax.axis_size(DP)
    (last_rows,) = launch(
        lambda tok, _, o: hold_body(tok, o), [tokens_in, held[1]],
        [pl.BlockSpec((16, d), lambda i: (share // 16 - 1, 0)), pl.BlockSpec(memory_space=pl.ANY)],
        [shaped((16, d), BF)], [pl.BlockSpec((16, d), lambda i: (0, 0))], "last_rows",
    )
    past = [
        lax.ppermute(
            last_rows,
            (DP, TP),
            [(i * group + group - 1, (i + 1) * group + t) for i in range(dps - 1)],
        )
        for t in range(1, group, 2)
    ]
    gain = input_gain[None]
    prep_ins = [conv_inner, conv_inner_bias[None], conv_bc, conv_bc_bias, step_bias[None],
                decay_log[None], skip_weight[None], norm_gain[None], weight_step.T]
    prep_outs = [shaped((8, wide)), shaped((8, L)), shaped((L, width + L), BF),
                 shaped((L, d), BF)]
    vecs, hv, mats, wst = launch(
        prep_body,
        [pltpu.with_memory_space_constraint(a, pltpu.HBM) for a in prep_ins],
        [whole(a) for a in prep_ins],
        prep_outs, [whole(o) for o in prep_outs], "prep", vmem=4,
    )
    def stretched(body, name, ins, outs, scratch, reverse, vmem, span=None, old=()):
        begin, length = span or (0, count // per)

        def order(i):
            return count // per - 1 - i - begin if reverse else i + begin

        def spec(kind, shape):
            if kind == ROWS:
                return pl.BlockSpec(
                    (share, shape[1]), lambda i, m: (lax.bitwise_xor(order(i), m[0]), 0)
                )
            if kind == EACH:
                return pl.BlockSpec((per, *shape[1:]), lambda i, m: (order(i), 0, 0))
            return pl.BlockSpec(shape, lambda i, m: (0,) * len(shape))

        kinds = [k for k, _ in ins] + [k for k, _, _ in outs]
        n = len(ins)

        def run(meta, *refs):
            refs = refs[:n] + refs[n + len(old) :]
            step = pl.program_id(0)
            for sub in range(per):
                pos = per - 1 - sub if reverse else sub

                def view(kind, ref, pos=pos):
                    if kind == ROWS:
                        return ref.at[pl.ds(pos * L, L)]
                    return ref.at[pl.ds(pos, 1)] if kind == EACH else ref

                views = [view(k, r) for k, r in zip(kinds, refs)]
                at = Spot(
                    order(step) * per + pos,
                    sub,
                    (sub - 1) % per,
                    step == 0 if sub == 0 else None,
                    step == length - 1 if sub == per - 1 else None,
                )
                body(at, meta, *views, *refs[len(kinds) :])

        return launch(
            run,
            [a for _, a in ins] + list(old),
            [spec(k, a.shape) for k, a in ins] + [pl.BlockSpec(memory_space=pl.ANY)] * len(old),
            [shaped(s, t) for _, s, t in outs],
            [spec(k, s) for k, s, _ in outs],
            name,
            grid=(length,),
            meta=meta,
            scratch=scratch,
            aliases={n + j: j for j in range(len(old))},
            vmem=vmem,
        )

    weights = (gain, weight_zx, weight_bc, wst)
    before = project(meta, [held[f] for f in near], [], *weights, tokens, 0, [])
    space()
    held[half] = hold(arrived, before[3])
    (own_past,) = simple(total_body, past, [shaped((16, d), BF)], "past")
    past = [own_past, swap(own_past, TP, 1)]
    spread_out(held, far)
    before = project(meta, [held[half]], [], *weights, tokens, half, list(before))
    space()
    normed, gate_raw, cat, step_raw, rim, normed_rim = project(
        meta, [held[f] for f in far[1:]], past, *weights, tokens, half + 1, list(before)
    )

    tall = (tokens, L)
    state_shape = (width, L)
    load_shape = (width + 16, L)
    small = (8, L)
    pre, sin, state, load, cum, pfx, decay = stretched(
        states_body,
        "states",
        [(ROWS, cat), (ROWS, step_raw), (ONE, rim), (ONE, vecs), (ONE, hv),
         (ONE, mats)],
        [(ROWS, (tokens, wide), F32), (EACH, (count, *state_shape), BF),
         (ONE, state_shape, F32), (ONE, load_shape, BF), (ROWS, tall, F32),
         (EACH, (count, 8, L), F32), (ONE, small, F32)],
        [pltpu.VMEM((per, L + 8, wide), F32), pltpu.VMEM(state_shape, F32),
         pltpu.VMEM(small, F32)],
        False, 14,
    )

    def link(level, reverse, held, load):
        final = level == levels - 2
        shapes = [load_shape, state_shape, small] + ([] if final else [state_shape, small])
        load, before, through, *more = simple(
            functools.partial(link_body, level, reverse, final), [*held, load],
            [shaped(s, BF if j == 0 else F32) for j, s in enumerate(shapes)], "link", meta,
        )
        return [*more, before, through], load

    thr = decay
    fresh = [jnp.zeros(state_shape, F32), jnp.ones(small, F32)]
    own = [state, decay, *fresh]
    load = swap(load, DP, 1)
    cots = {0: grad_out}
    cots[half] = swap(hold(grad_out), TP, half)
    (y,) = stretched(
        within_body,
        "within",
        [(ROWS, pre), (ROWS, step_raw), (ROWS, cum), (EACH, sin), (ONE, vecs),
         (ONE, hv), (ONE, mats)],
        [(ROWS, (tokens, width), F32)],
        [], False, 14,
    )
    for level in range(levels - 1):
        space()
        own, load = link(level, False, own, load)
        load = swap(load, DP, masks[level + 1])
        if level == levels - 2:
            space()
            late = {half: hold(cots[half])}
            spread_out(late, far)
            spread_out(cots, near)
            cots.update({f: late[f] for f in far[1:]})
            space()
            cot_all, gn = cotangent([cots[f] for f in range(group)], weight_out)
    befores, throughs = own[-2:]
    space()
    mixed, sums, incoming = stretched(
        functools.partial(gate_body, levels - 1),
        "gated",
        [(ROWS, pre), (ROWS, cum), (EACH, pfx), (ROWS, y), (ROWS, gate_raw),
         (ROWS, gn), (ONE, befores), (ONE, throughs), (ONE, load), (ONE, vecs),
         (ONE, mats)],
        [(ROWS, (tokens, width), F32), (EACH, (count, 2, L), F32), (ONE, state_shape, BF)],
        [], False, 14,
    )
    for mask in tmasks[::-1][:-1]:
        got = swap(sums, TP, mask)
        space()
        sums = add(sums, got)
    sums2 = swap(sums, TP, 1)
    space()
    normout, gm, ggr, gs, toward, first_load, sfx, gate_acc = stretched(
        back_gate_body,
        "back_gated",
        [(ROWS, pre), (ROWS, cum), (ROWS, mixed), (ROWS, gate_raw), (ROWS, gn),
         (EACH, sums), (EACH, sums2), (ONE, thr), (ONE, vecs), (ONE, mats)],
        [(ROWS, (tokens, width), BF), (ROWS, (tokens, width), BF),
         (ROWS, (tokens, width), BF), (EACH, (count, *state_shape), BF),
         (ONE, state_shape, F32), (ONE, load_shape, BF), (EACH, (count, 8, L), F32),
         (ONE, (8, width), F32)],
        [pltpu.VMEM(state_shape, F32), pltpu.VMEM(small, F32), pltpu.VMEM((16, width), F32)],
        True, 14,
    )

    kept = SimpleNamespace(within=(), zx=None, wout=None)
    done = set()
    blocks = d // width

    def weights_chain(pairs, finish, need=None):
        yield need, False
        send, keep = wgrads(meta, [pairs()], width, blocks)
        for level in range(levels):
            got = swap(send, DP, masks[level])
            yield None, True
            if level < levels - 1:
                send, keep = halve(meta, 1, level + 1, keep, got)
            else:
                total = add(keep, got)
        for level in range(levels - 1, -1, -1):
            got = swap(total, DP, masks[level])
            if not level:
                finish(total, 1)
            yield None, True
            if level:
                total = join(meta, 1, level, total, got)
        finish(got, 0)

    def out_weights(src, mine):
        kept.wout = columns(meta, src, mine, d, width, kept.wout)

    def gate_weights(src, mine):
        kept.zx = rows_of(meta, src, mine, 0, d, width, kept.zx)

    def inner_weights(src, mine):
        kept.zx = rows_of(meta, src, mine, 1, d, width, kept.zx)

    def links_chain():
        yield None, False
        own, load = [toward, thr, *fresh], first_load
        for level in range(levels):
            got = swap(load, DP, masks[level])
            yield None if level < levels - 1 else "F", True
            if level < levels - 1:
                own, load = link(level, True, own, got)
        befores, throughs = own[-2:]
        ginner, gbc, glog, gst = kept.within
        kept.gcat, kept.gsr, kept.head, kept.extra, kept.conv_acc, kept.head_acc = stretched(
            functools.partial(back_conv_body, levels - 1),
            "back_conv",
            [(ROWS, cat), (ONE, rim), (ROWS, pre), (ROWS, step_raw), (ROWS, cum),
             (EACH, sin), (EACH, pfx), (EACH, sfx), (ROWS, ginner), (ROWS, gbc),
             (ROWS, glog), (ROWS, gst), (ONE, incoming), (ONE, befores), (ONE, throughs),
             (ONE, got), (ONE, vecs), (ONE, hv), (ONE, mats)],
            [(ROWS, (tokens, wide), BF), (ROWS, tall, BF), (ONE, (8, wide), F32),
             (ONE, (16, wide), BF), (ONE, (8, wide), F32), (ONE, small, F32)],
            [pltpu.VMEM((per, L + 8, wide), F32), pltpu.VMEM((40, wide), F32),
             pltpu.VMEM((16, L), F32), pltpu.VMEM(state_shape, F32)],
            True, 16,
        )

    def within_chain():
        for begin in (0, half):
            yield None, False
            kept.within = stretched(
                back_within_body,
                "back_within",
                [(ROWS, pre), (ROWS, step_raw), (ROWS, cum), (EACH, sin), (EACH, pfx),
                 (EACH, gs), (ROWS, gm), (ONE, incoming), (ONE, vecs), (ONE, hv), (ONE, mats)],
                [(ROWS, (tokens, width), F32), (ROWS, (tokens, 2 * L), F32), (ROWS, tall, F32),
                 (ROWS, tall, F32)],
                [], True, 16, (begin, half), kept.within,
            )

    def scattered(frames_in):
        sums_in = []
        for first in (0, half):
            part = dict(enumerate(frames_in[first : first + half]))
            mask = 1
            while mask < half:
                for f in [f for f in part if f & mask]:
                    got = swap(part.pop(f), TP, mask)
                    yield None, True
                    part[f ^ mask] = add(part[f ^ mask], got)
                mask *= 2
            sums_in.append(part[0])
        got = swap(sums_in[1], TP, half)
        yield None, True
        return sums_in[0], got

    def branch_chain():
        yield None, False
        branch = rows_times(outproj_body, group, share, d, [normout], [weight_out], "outproj")
        parts = yield from scattered(branch)
        (kept.layer,) = simple(layer_body, [tokens_in, *parts], [shaped((share, d), BF)], "layer")

    def tokens_chain():
        yield "L", False
        ahead = lax.ppermute(kept.head, DP, [(i + 1, i) for i in range(dps - 1)])
        yield None, True
        gcat = patched(meta, kept.gcat, ahead, vecs, share, group)
        *grads, kept.shared = rows_times(
            dgrad_body, group, share, d, [ggr, gcat, kept.gsr, normed],
            [weight_zx, weight_bc, wst, gain, kept.conv_acc],
            "dgrad", [shaped((16, ROW))], [pltpu.VMEM((8, d), F32)],
        )
        done.add("dgrad")
        parts = yield from scattered(grads)
        (kept.tokens,) = simple(
            tokens_body, [tokens_in, grad_out, *parts, gain], [shaped((share, d))], "tokens",
            None, 12,
        )

    def misc_chain():
        yield "L", False
        send, keep, step_acc = bc_wgrad(
            meta, normed, kept.gcat, kept.gsr, normed_rim, kept.extra, width
        )
        yield "dgrad", False
        shared = kept.shared
        (load,) = simple(lead_body, [send, shared], [shaped((send.shape[0] + 32, ROW), BF)], "lead")
        for level in range(len(tmasks)):
            got = swap(load, TP, tmasks[level])
            yield None, True
            if level < len(tmasks) - 1:
                rows = keep.shape[0] // 2
                load, keep, shared = simple(
                    functools.partial(misc_halve_body, level + 1), [keep, shared, got],
                    [shaped((rows + 32, ROW), BF), shaped((rows, ROW), BF), shaped((16, ROW))],
                    "misc_halve", meta,
                )
        rows = keep.shape[0]
        flat = rows + 8 * (d // ROW)
        (load,) = simple(
            misc_pack_body,
            [keep, shared, got, step_acc, kept.conv_acc, gate_acc, kept.head_acc],
            [shaped((flat + 96, ROW), BF)], "misc_pack",
        )
        for level in range(levels):
            got = swap(load, DP, masks[level])
            yield None, True
            if level < levels - 1:
                (load,) = simple(
                    functools.partial(misc_add_body, flat), [load, got],
                    [shaped(load.shape, BF)], "misc_add",
                )
        outs = [(1, d), (2, 4, L), (2, L), (heads, d), (4, width), (1, width), (1, heads),
                (1, heads), (1, heads), (1, width)]
        total, *kept.small = simple(
            functools.partial(misc_finish_body, rows), [load, got, mats],
            [shaped((rows, ROW), BF)] + [shaped(s) for s in outs], "misc_finish",
        )
        for level in range(len(tmasks) - 1, -1, -1):
            got = swap(total, TP, tmasks[level])
            yield None, True
            if level:
                total = join(meta, 0, level, total, got)
        (kept.bc,) = simple(bc_out_body, [total, got], [shaped((2, d, L))], "bc_weights", meta)

    run_chains(
        {
            "L": links_chain(),
            "W": weights_chain(lambda: (normout, cot_all, 1), out_weights),
            "G": weights_chain(lambda: (normed, ggr, 0), gate_weights),
            "F": within_chain(),
            "B": branch_chain(),
            "T": tokens_chain(),
            "I": weights_chain(
                lambda: (normed, kept.gcat, 0, normed_rim, kept.extra), inner_weights, "L"
            ),
            "M": misc_chain(),
        },
        done,
        ORDER if (dps, group) == (8, 4) else "",
    )

    gain_g, bc_g, bcb_g, step_g, taps_g, bias_g, sb_g, dl_g, sk_g, ng_g = kept.small
    return (
        kept.layer,
        kept.tokens,
        gain_g[0],
        kept.zx,
        kept.bc,
        step_g.T,
        taps_g,
        bias_g[0],
        bc_g,
        bcb_g,
        sb_g[0],
        dl_g[0],
        sk_g[0],
        ng_g[0],
        kept.wout,
    )


def solution(mesh):
    rows = P((DP, TP), None)
    cols = P(None, TP)
    one = P(TP)
    in_specs = (
        rows, rows, P(), P(), P(None, None, TP), P(), cols, cols, one, P(), P(),
        one, one, one, one, P(TP, None),
    )
    out_specs = (
        rows, rows, P(), P(None, None, TP), P(), cols, cols, one, P(), P(),
        one, one, one, one, P(TP, None),
    )
    return jax.shard_map(
        on_device, mesh=mesh, in_specs=in_specs, out_specs=out_specs, check_vma=False
    )
```

```python
import functools
from types import SimpleNamespace
from typing import Any, NamedTuple

import jax
import jax.numpy as jnp
from jax import lax
from jax.experimental import pallas as pl
from jax.experimental.pallas import tpu as pltpu
from jax.sharding import PartitionSpec as P

KERNEL = 4
L = 128
HD = 64
DI = 2048
EPS = 1e-05
F32 = jnp.float32
BF = jnp.bfloat16
MIB = 1 << 20
ROW = 256
DP, TP = "dp", "tensor"
ROWS, EACH, ONE = range(3)


def dot(a, b, ca=1, cb=0):
    return lax.dot_general(a, b, (((ca,), (cb,)), ((), ())), preferred_element_type=F32)


def split(a):
    hi = a.astype(BF)
    return hi, (a - hi.astype(F32)).astype(BF)


def dot_l(a, b, ca=1, cb=0):
    hi, lo = split(a)
    return dot(hi, b, ca, cb) + dot(lo, b, ca, cb)


def dot_r(a, b, ca=1, cb=0):
    hi, lo = split(b)
    return dot(a, hi, ca, cb) + dot(a, lo, ca, cb)


def sigmoid(v):
    return 0.5 * jnp.tanh(0.5 * v) + 0.5


def softplus(v):
    u = jnp.exp(-jnp.abs(v))
    small = u * (1.0 - u * (0.5 - u * (1.0 / 3.0 - u * 0.25)))
    return jnp.maximum(v, 0.0) + jnp.where(u < 0.02, small, jnp.log(1.0 + u))


def per_head(row, heads):
    return jnp.concatenate(
        [jnp.broadcast_to(row[:, h : h + 1], (HD, L)) for h in range(heads)], axis=0
    )


def eights(v):
    return jnp.sum(v.reshape(v.shape[0] // 8, 8, v.shape[1]), axis=0)


def across_lanes(v, width):
    return jnp.concatenate([v] * (width // L), axis=1) if width > L else v


def whole(a):
    return pl.BlockSpec(a.shape, lambda *_: (0,) * a.ndim)


LAST = []

def launch(body, ins, in_specs, outs, out_specs, name, grid=(1,), meta=None, scratch=(),
           aliases=None, vmem=8, flops=0, token=True, tick=False):
    ins, in_specs = list(ins), list(in_specs)
    lead = 0 if meta is None else 1
    at = lead + len(ins)
    given = LAST[-1] if LAST and not any(LAST[-1] is a for a in ins) else None
    if given is not None:
        ins.append(given)
        in_specs.append(pl.BlockSpec(memory_space=pl.ANY))

    outs, out_specs = list(outs), list(out_specs)
    if tick:
        outs.append(shaped((8, L)))
        out_specs.append(whole(outs[-1]))

    def run(*refs):
        refs = refs if given is None else refs[:at] + refs[at + 1 :]
        if tick:
            last = lead + len(ins) - (given is not None) + len(outs) - 1
            refs[last][...] = jnp.zeros((8, L), F32)
            refs = refs[:last] + refs[last + 1 :]
        body(*refs)

    results = pl.pallas_call(
        run,
        grid_spec=pltpu.PrefetchScalarGridSpec(
            num_scalar_prefetch=lead,
            grid=grid,
            in_specs=in_specs,
            out_specs=list(out_specs),
            scratch_shapes=list(scratch),
        ),
        out_shape=list(outs),
        input_output_aliases={lead + k: v for k, v in (aliases or {}).items()},
        compiler_params=pltpu.CompilerParams(vmem_limit_bytes=vmem * MIB),
        cost_estimate=pl.CostEstimate(
            flops=flops,
            bytes_accessed=0,
            transcendentals=0,
        ),
        name=name,
    )(*([] if meta is None else [meta]), *ins)
    if tick:
        *results, LAST[:] = [*results[:-1], results[-1:]]
    elif token:
        LAST[:] = [min(results, key=lambda a: a.size)]
    return results


def space_body(o):
    o[...] = jnp.zeros_like(o)


def space(flops=10 * 10**9):
    o = shaped((8, L))
    launch(space_body, [], [], [o], [whole(o)], "space", vmem=1, flops=flops)


def shaped(shape, dtype=F32):
    return jax.ShapeDtypeStruct(shape, dtype)


def simple(body, ins, outs, name, meta=None, vmem=8, deps=(), tick=False):
    n = len(ins)

    def run(*refs):
        lead = 0 if meta is None else 1
        body(*refs[: lead + n], *refs[lead + n + len(deps) :])

    return launch(
        run, [*ins, *deps],
        [whole(a) for a in ins] + [pl.BlockSpec(memory_space=pl.ANY)] * len(deps),
        outs, [whole(o) for o in outs], name, meta=meta, vmem=vmem, tick=tick,
    )


def unit_rows(x, gain):
    x = x.astype(F32)
    rstd = lax.rsqrt(jnp.mean(x * x, axis=1, keepdims=True) + EPS)
    return (x * rstd * gain).astype(BF)


def proj_body(k, rims, deps, meta, *refs):
    toks, past = refs[:k], refs[k : k + rims]
    gain, wzx, wbc, wst = refs[k + rims : k + rims + 4]
    outs = refs[k + rims + 4 + deps :]
    normed_o, gate_o, cat_o, step_o = outs[:4]
    width = wzx.shape[2]

    def conv_inputs(normed, out):
        out[:, :width] = dot(normed, wzx[1]).astype(BF)
        out[:, width : width + L] = dot(normed, wbc[0]).astype(BF)
        out[:, width + L :] = dot(normed, wbc[1]).astype(BF)

    def one(j):
        normed = unit_rows(toks[j][...], gain[...])
        normed_o[...] = normed
        conv_inputs(normed, cat_o)
        gate_o[...] = dot(normed, wzx[0]).astype(BF)
        step_o[...] = dot(normed, wst[...], 1, 1).astype(BF)
        if rims and j == 0:
            rim = past[0][...].astype(F32)
            for p in past[1:]:
                rim = rim + p[...].astype(F32)
            normed = unit_rows(rim, gain[...])
            outs[5][...] = normed
            conv_inputs(normed, outs[4])

    for j in range(k):
        pl.when(pl.program_id(0) == j)(functools.partial(one, j))


def project(meta, toks, past, gain, wzx, wbc, wst, total, first, before):
    k = len(toks)
    share, d = toks[0].shape
    width = wzx.shape[2]
    wide = width + 2 * L
    cols = (d, width, wide, L)
    ins = [*toks, *past, gain, wzx, wbc, wst]
    specs = [whole(a) for a in ins]
    out_specs = [pl.BlockSpec((share, c), lambda i, m: (i + first, 0)) for c in cols]
    out_shape = [shaped((total, c), BF) for c in cols]
    if past:
        for c in (wide, d):
            out_specs.append(pl.BlockSpec((16, c), lambda i, m: (0, 0)))
            out_shape.append(shaped((16, c), BF))
    aliases = {len(ins) + j: j for j in range(4)} if before else {}
    return launch(
        functools.partial(proj_body, k, len(past), len(before)),
        ins + before,
        specs + [pl.BlockSpec(memory_space=pl.ANY)] * len(before),
        out_shape,
        out_specs,
        "project",
        grid=(k,),
        meta=meta,
        aliases=aliases,
        vmem=16,
        token=False,
    )


def prep_body(taps, tbias, btaps, bbias, sbias, decay, skip, ngain, wst, vecs, hv, mats, wst_o):
    width = taps.shape[1]
    heads = width // HD
    wst_o[...] = jnp.zeros_like(wst_o)
    wst_o[0:heads, :] = wst[...]
    head = lax.broadcasted_iota(jnp.int32, (L, width), 0)
    lane = lax.broadcasted_iota(jnp.int32, (L, width), 1)
    spread = jnp.where(lax.div(lane, HD) == head, 1.0, 0.0).astype(BF)
    mats[:, :width] = spread
    r = lax.broadcasted_iota(jnp.int32, (L, L), 0)
    c = lax.broadcasted_iota(jnp.int32, (L, L), 1)
    mats[:, width:] = jnp.where(r >= c, 1.0, 0.0).astype(BF)
    hv[...] = jnp.zeros_like(hv)
    hv[0:1, :heads] = sbias[...]
    hv[1:2, :heads] = -jnp.exp(decay[...])
    hv[2:3, :heads] = skip[...]
    vecs[...] = jnp.zeros_like(vecs)
    vecs[0:4, :width] = taps[...]
    vecs[4:5, :width] = tbias[...]
    for k in range(2):
        cols = slice(width + k * L, width + k * L + L)
        vecs[0:4, cols] = btaps[k]
        vecs[4:5, cols] = bbias[k : k + 1, :]
    vecs[5:6, :width] = dot_l(hv[...], spread)[2:3, :]
    vecs[6:7, :width] = ngain[...]


def cot_body(k, *refs):
    cots = refs[:k]
    wout, all_o, gn_o = refs[k:]

    def one(cot):
        v = cot[...]
        all_o[...] = v
        gn_o[...] = dot(v, wout[...], 1, 1).astype(BF)

    for j in range(k):
        pl.when(pl.program_id(0) == j)(functools.partial(one, cots[j]))


def cotangent(cots, wout):
    k = len(cots)
    share, d = cots[0].shape
    width = wout.shape[0]
    return launch(
        functools.partial(cot_body, k),
        [*cots, wout],
        [whole(a) for a in (*cots, wout)],
        [shaped((k * share, d), BF), shaped((k * share, width), BF)],
        [pl.BlockSpec((share, c), lambda i: (i, 0)) for c in (d, width)],
        "cotangent",
        grid=(k,),
        vmem=12,
    )


def act_parts(pre, width):
    out = []
    for x0 in range(0, width + 2 * L, L):
        v = pre[:, x0 : x0 + L]
        out.append(v * sigmoid(v))
    return out


def pack(out, state, decay):
    rows = state.shape[0]
    hi, lo = split(jnp.broadcast_to(decay[0:1, :], (16, L)))
    row = lax.broadcasted_iota(jnp.int32, (16, L), 0)
    out[:rows, :] = state.astype(BF)
    tail = jnp.where(row == 0, hi.astype(F32), jnp.where(row == 1, lo.astype(F32), 0.0))
    out[rows:, :] = tail.astype(BF)


def unpack(load):
    v = load[...].astype(F32)
    rows = v.shape[0] - 16
    return v[:rows], v[rows : rows + 1] + v[rows + 1 : rows + 2]


def bit_at(meta, level):
    return jnp.bitwise_and(jnp.right_shift(meta[1], level), 1)


def is_ahead(meta, level, reverse):
    bit = bit_at(meta, level)
    return jnp.where(bit == (0 if reverse else 1), 1.0, 0.0)


def link_body(level, reverse, final, meta, state, decay, before, through, load,
              load_o, before_o, through_o, *more):
    theirs, a = unpack(load)
    heads = theirs.shape[0] // HD
    ahead = is_ahead(meta, level, reverse)
    mine = decay[0:1, :]
    t = through[0:1, :]
    before_o[...] = before[...] + per_head(t * ahead, heads) * theirs
    through_o[...] = jnp.broadcast_to(t * (ahead * a + (1.0 - ahead)), (8, L))
    joined = (
        per_head(mine * ahead + (1.0 - ahead), heads) * theirs
        + per_head(a * (1.0 - ahead) + ahead, heads) * state[...]
    )
    pack(load_o, joined, mine * a)
    if not final:
        state_o, decay_o = more
        state_o[...] = joined
        decay_o[...] = jnp.broadcast_to(mine * a, (8, L))


def final_link(meta, level, reverse, before, through, load):
    theirs, _ = unpack(load)
    t = through[0:1, :] * is_ahead(meta, level, reverse)
    return before[...] + per_head(t, theirs.shape[0] // HD) * theirs


def states_body(
    at, meta, cat, step, rim, vecs, hv, mats,
    pre_o, cb_o, sin_o, end_o, load_o, cum_o, pfx_o, thr_o, buf, state, prod,
):
    width = vecs.shape[1] - 2 * L
    heads = width // HD
    keep = jnp.where(meta[2 + at.c] == 0, 1.0, 0.0)
    before, buf = buf.at[at.other], buf.at[at.sub]

    def follow():
        buf[0:8, :] = before[L : L + 8, :] * keep

    if at.first is None:
        follow()
    else:

        @pl.when(at.first)
        def _():
            buf[0:8, :] = rim[...].astype(F32)[8:16, :] * keep
            state[...] = jnp.zeros_like(state)
            prod[...] = jnp.ones_like(prod)

        pl.when(jnp.logical_not(at.first))(follow)

    buf[8 : 8 + L, :] = cat[...].astype(F32)
    acts = []
    for x0 in range(0, width + 2 * L, L):
        cols = slice(x0, x0 + L)
        v = vecs[4:5, cols] + vecs[3:4, cols] * buf[8 : 8 + L, cols]
        for j in range(1, KERNEL):
            v = v + vecs[3 - j : 4 - j, cols] * buf[8 - j : 8 - j + L, cols]
        pre_o[:, cols] = v
        acts.append(v * sigmoid(v))
    cb_o[...] = acts[-1].astype(BF)
    steps = softplus(step[...].astype(F32) + hv[0:1, :])
    cum = dot_r(mats[:, width:], steps * hv[1:2, :])
    cum_o[...] = cum
    total = cum[L - 1 : L, :]
    weights = dot((jnp.exp(total - cum) * steps).astype(BF), mats[:, :width])
    inner = jnp.concatenate(acts[: width // L], axis=1)
    local = dot((inner * weights).astype(BF), acts[-2].astype(BF), 0, 0)
    entering = state[...] * keep
    sin_o[0] = entering.astype(BF)
    dec = jnp.exp(total)
    leaving = per_head(dec, heads) * entering + local
    state[...] = leaving
    here = prod[...] * keep
    pfx_o[0] = here
    prod[...] = here * dec

    if at.last is not None:

        @pl.when(at.last)
        def _():
            end_o[...] = leaving
            thr_o[...] = here * dec
            pack(load_o, leaving, here * dec)


def within_body(at, meta, pre, step, cum_r, sin, vecs, hv, mats, y_o):
    width = vecs.shape[1] - 2 * L
    heads = width // HD
    acts = act_parts(pre, width)
    bb, cb = acts[-2].astype(BF), acts[-1].astype(BF)
    scores = dot(cb, bb, 1, 1)
    steps = softplus(step[...].astype(F32) + hv[0:1, :])
    cum = cum_r[...]
    cum_t, steps_t = cum.T, steps.T
    lower = lax.broadcasted_iota(jnp.int32, (L, L), 0) >= lax.broadcasted_iota(
        jnp.int32, (L, L), 1
    )
    first = lax.broadcasted_iota(jnp.int32, (L, L), 1) < HD
    grown = dot(jnp.exp(cum).astype(BF), mats[:, :width])
    far = grown * dot(cb, sin[0], 1, 1)
    for pair in range(heads // 2):
        cols = slice(pair * L, pair * L + L)
        x = acts[pair].astype(BF)
        got = []
        for h in (2 * pair, 2 * pair + 1):
            gap = jnp.where(lower, cum[:, h : h + 1] - cum_t[h : h + 1, :], -1e30)
            mix = scores * jnp.exp(gap) * steps_t[h : h + 1, :]
            got.append(dot(mix.astype(BF), x))
        y_o[:, cols] = (
            jnp.where(first, got[0], got[1]) + far[:, cols] + vecs[5:6, cols] * acts[pair]
        )


def gate_body(
    level, at, meta, cb, cum, pfx, y, gate, gn, before, through, load, vecs, mats,
    mixed_o, sums_o, incoming,
):
    width = vecs.shape[1] - 2 * L
    ones = jnp.ones((8, L), BF)

    if at.first is not None:

        @pl.when(at.first)
        def _():
            incoming[...] = final_link(meta, level, False, before, through, load).astype(BF)

    reach = dot((jnp.exp(cum[...]) * pfx[0][0:1, :]).astype(BF), mats[:, :width])
    far = reach * dot(cb[...], incoming[...], 1, 1)
    squares, crosses = [], []
    for x0 in range(0, width, L):
        cols = slice(x0, x0 + L)
        mixed = y[:, cols] + far[:, cols]
        mixed_o[:, cols] = mixed
        g = gate[:, cols].astype(F32)
        gated = mixed * (g * sigmoid(g))
        squares.append(gated * gated)
        crosses.append(gn[:, cols].astype(F32) * vecs[6:7, cols] * gated)
    square = dot_r(ones, functools.reduce(jnp.add, squares), 1, 1)
    cross = dot_r(ones, functools.reduce(jnp.add, crosses), 1, 1)
    sums_o[0, 0:1] = square[0:1]
    sums_o[0, 1:2] = cross[0:1]


def back_gate_body(
    at, meta, pre, cum_r, mixed_r, gate, gn, sums, sums2, thr, vecs, mats,
    normout_o, gm_o, ggr_o, gs_o, toward_o, load_o, sfx_o, acc_o, gstate, prod, acc,
):
    width = vecs.shape[1] - 2 * L
    heads = width // HD
    keep = jnp.where(meta[2 + at.c] == 0, 1.0, 0.0)

    if at.first is not None:

        @pl.when(at.first)
        def _():
            gstate[...] = jnp.zeros_like(gstate)
            prod[...] = jnp.ones_like(prod)
            acc[...] = jnp.zeros_like(acc)

    both = sums[0] + sums2[0]
    square = jnp.broadcast_to(both[0:1, :], (L, L)).T
    cross = jnp.broadcast_to(both[1:2, :], (L, L)).T
    scale = lax.rsqrt(square * (1.0 / DI) + EPS)
    cubed = scale * scale * scale * cross * (1.0 / DI)
    cum = cum_r[...]
    total = cum[L - 1 : L, :]
    grown = dot(jnp.exp(cum).astype(BF), mats[:, :width])
    cv = pre[:, width + L :]
    cb = (cv * sigmoid(cv)).astype(BF)
    moved = []
    for x0 in range(0, width, L):
        cols = slice(x0, x0 + L)
        v = pre[:, cols]
        inner = v * sigmoid(v)
        g = gate[:, cols].astype(F32)
        s = sigmoid(g)
        silu = g * s
        mixed = mixed_r[:, cols]
        gated = mixed * silu
        ng = vecs[6:7, cols]
        gnv = gn[:, cols].astype(F32)
        scaled = gated * scale
        normout_o[:, cols] = (scaled * ng).astype(BF)
        gg = scale * (gnv * ng) - gated * cubed
        gm = gg * silu
        gm_o[:, cols] = gm.astype(BF)
        ggr_o[:, cols] = (gg * mixed * (s + silu * (1.0 - s))).astype(BF)
        acc[0:8, cols] += eights(gnv * scaled)
        acc[8:16, cols] += eights(gm * inner)
        moved.append((gm * grown[:, cols]).astype(BF))
    leaving = gstate[...]
    gs_o[0] = leaving.astype(BF)
    here = prod[...]
    sfx_o[0] = here
    dec = jnp.exp(total)
    entering = per_head(dec, heads) * leaving + dot(jnp.concatenate(moved, axis=1), cb, 0, 0)
    entering = entering * keep
    gstate[...] = entering
    prod[...] = here * dec * keep

    if at.last is not None:

        @pl.when(at.last)
        def _():
            toward_o[...] = entering
            pack(load_o, entering, thr[...])
            row = lax.broadcasted_iota(jnp.int32, (8, width), 0)
            acc_o[...] = jnp.where(
                row == 0,
                jnp.sum(acc[0:8, :], axis=0, keepdims=True),
                jnp.sum(acc[8:16, :], axis=0, keepdims=True),
            )


def head_product(a, b, spread):
    rows = dot(jnp.ones((8, L), BF), (a * b).astype(BF), 1, 1)
    return dot_l(rows, spread, 1, 1)[0:1, :]


def back_within_body(
    at, meta, pre, step, cum_r, sin, pfx, gs, gm_r, incoming, vecs, hv, mats,
    ginner_o, gbc_o, glog_o, gst_o,
):
    width = vecs.shape[1] - 2 * L
    heads = width // HD
    acts = act_parts(pre, width)
    bb, cb = acts[-2].astype(BF), acts[-1].astype(BF)
    scores = dot(cb, bb, 1, 1)
    steps = softplus(step[...].astype(F32) + hv[0:1, :])
    cum = cum_r[...]
    total = cum[L - 1 : L, :]
    cum_t, steps_t = cum.T, steps.T
    row = lax.broadcasted_iota(jnp.int32, (L, L), 0)
    col = lax.broadcasted_iota(jnp.int32, (L, L), 1)
    lower = row >= col
    first = col < HD
    e = jnp.exp(cum)
    wd = jnp.exp(total - cum)
    grown = dot(e.astype(BF), mats[:, :width])
    weights = dot((wd * steps).astype(BF), mats[:, :width])
    gsb = gs[0]
    entering = sin[0].astype(F32) + per_head(pfx[0][0:1, :], heads) * incoming[...].astype(F32)
    eb = entering.astype(BF)
    u = dot(bb, gsb, 1, 1)
    v = dot(cb, eb, 1, 1)
    inner = jnp.concatenate(acts[: width // L], axis=1)
    gm = gm_r[...].astype(F32)
    seen = dot((inner * u).astype(BF), mats[:, :width], 1, 1)
    passed = dot((gm * v).astype(BF), mats[:, :width], 1, 1) * e
    gb = dot((inner * weights).astype(BF), gsb)
    gc = dot((gm * grown).astype(BF), eb)
    through = head_product(gsb.astype(F32), entering, mats[:, :width]) * jnp.exp(total)
    dscores = jnp.zeros((L, L), F32)
    rowsums = jnp.zeros((L, L), F32)
    colsums = jnp.zeros((L, L), F32)
    for pair in range(heads // 2):
        cols = slice(pair * L, pair * L + L)
        xb = acts[pair].astype(BF)
        gmb = gm_r[:, cols]
        got = []
        for h in (2 * pair, 2 * pair + 1):
            mine = first if h % 2 == 0 else jnp.logical_not(first)
            gmh = jnp.where(mine, gm[:, cols], 0.0).astype(BF)
            dm = dot(gmh, xb, 1, 1)
            gap = jnp.where(lower, cum[:, h : h + 1] - cum_t[h : h + 1, :], -1e30)
            decay = jnp.exp(gap)
            st = steps_t[h : h + 1, :]
            t1 = dm * decay
            dscores = dscores + t1 * st
            gp = t1 * scores
            rowsums = jnp.where(col == h, jnp.sum(gp * st, axis=1, keepdims=True), rowsums)
            colsums = jnp.where(row == h, jnp.sum(gp, axis=0, keepdims=True), colsums)
            mix = (scores * decay * st).astype(BF)
            got.append(dot(mix, gmb, 0, 0))
        ginner_o[:, cols] = (
            jnp.where(first, got[0], got[1])
            + weights[:, cols] * u[:, cols]
            + vecs[5:6, cols] * gm[:, cols]
        )
    db = dscores.astype(BF)
    gbc_o[:, :L] = gb + dot(db, cb, 0, 0)
    gbc_o[:, L:] = gc + dot(db, bb)
    direct = colsums.T
    seen = seen * wd
    gst_o[...] = direct + seen
    later = rowsums - direct * steps + passed
    tr = mats[:, width:]
    glog_o[...] = (
        dot_r(tr, later, 0, 0) + dot_r(tr, steps * seen) - steps * seen + through
    )


def crossing(vecs, later):
    row = lax.broadcasted_iota(jnp.int32, (16, later.shape[1]), 0)
    extra = jnp.zeros((16, later.shape[1]), F32)
    for j in range(1, KERNEL):
        for t in range(j):
            part = vecs[3 - j : 4 - j, :] * later[t : t + 1, :]
            extra = extra + jnp.where(row == 16 - j + t, part, 0.0)
    return extra


def back_conv_body(
    level, at, meta, cat, rim, pre, step, cum_r, sin, pfx, sfx, ginner_r, gbc_r, glog_r, gst_r,
    incoming, before, through, load, vecs, hv, mats,
    gcat_o, gsr_o, head_o, extra_o, acc_o, hacc_o, buf, acc, hacc, outgoing,
):
    width = vecs.shape[1] - 2 * L
    heads = width // HD
    keep_next = jnp.where(meta[3 + at.c] == 0, 1.0, 0.0)
    keep = jnp.where(meta[2 + at.c] == 0, 1.0, 0.0)
    later, buf = buf.at[at.other], buf.at[at.sub]

    def follow():
        buf[L : L + 8, :] = later[0:8, :] * keep_next

    if at.first is None:
        follow()
    else:

        @pl.when(at.first)
        def _():
            buf[L : L + 8, :] = jnp.zeros((8, width + 2 * L), F32)
            acc[...] = jnp.zeros_like(acc)
            hacc[...] = jnp.zeros_like(hacc)
            outgoing[...] = final_link(meta, level, True, before, through, load)

        pl.when(jnp.logical_not(at.first))(follow)

    step_in = step[...].astype(F32) + hv[0:1, :]
    steps = softplus(step_in)
    cum = cum_r[...]
    total = cum[L - 1 : L, :]
    wd = jnp.exp(total - cum)
    weights = dot((wd * steps).astype(BF), mats[:, :width])
    far = outgoing[...] * per_head(sfx[0][0:1, :], heads)
    fb = far.astype(BF)
    entering = sin[0].astype(F32) + per_head(pfx[0][0:1, :], heads) * incoming[...].astype(F32)
    through = head_product(far, entering, mats[:, :width]) * jnp.exp(total)
    acts, slopes = [], []
    for x0 in range(0, width + 2 * L, L):
        v = pre[:, x0 : x0 + L]
        s = sigmoid(v)
        a = v * s
        acts.append(a)
        slopes.append(s + a * (1.0 - s))
    bb = acts[-2].astype(BF)
    u = dot(bb, fb, 1, 1)
    inner = jnp.concatenate(acts[: width // L], axis=1)
    seen = dot((inner * u).astype(BF), mats[:, :width], 1, 1) * wd
    gb = dot((inner * weights).astype(BF), fb)
    glog = glog_r[...] + dot_r(mats[:, width:], steps * seen) - steps * seen + through
    gsi = (gst_r[...] + seen + glog * hv[1:2, :]) * sigmoid(step_in)
    gsr_o[...] = gsi.astype(BF)
    hacc[0:8, :] += eights(glog * steps * hv[1:2, :])
    hacc[8:16, :] += eights(gsi)
    for k, x0 in enumerate(range(0, width + 2 * L, L)):
        cols = slice(x0, x0 + L)
        if x0 < width:
            g = ginner_r[:, cols] + weights[:, cols] * u[:, cols]
        elif x0 == width:
            g = gbc_r[:, :L] + gb
        else:
            g = gbc_r[:, L:]
        g = g * slopes[k]
        buf[0:L, cols] = g
        acc[32:40, cols] += eights(g)
        here = cat[:, cols].astype(F32)
        out = vecs[3:4, cols] * g
        acc[24:32, cols] += eights(g * here)
        for j in range(1, KERNEL):
            moved = buf[j : j + L, cols]
            out = out + vecs[3 - j : 4 - j, cols] * moved
            acc[24 - 8 * j : 32 - 8 * j, cols] += eights(moved * here)
        gcat_o[:, cols] = out.astype(BF)
    if at.last is not None:

        @pl.when(at.last)
        def _():
            head_o[...] = buf[0:8, :]
            past = rim[...].astype(F32)[8:16, :] * keep
            now = buf[0:8, :]
            extra_o[...] = crossing(vecs, now * keep).astype(BF)
            row = lax.broadcasted_iota(jnp.int32, now.shape, 0)
            result = jnp.zeros_like(now)
            for k in range(5):
                part = jnp.sum(acc[8 * k : 8 * k + 8, :], axis=0, keepdims=True)
                j = 3 - k
                if 1 <= j <= 3:
                    for t in range(j):
                        part = part + now[t : t + 1, :] * past[8 + t - j : 9 + t - j, :]
                result = jnp.where(row == k, part, result)
            acc_o[...] = result
            hrow = lax.broadcasted_iota(jnp.int32, (8, L), 0)
            hacc_o[...] = jnp.where(
                hrow == 0,
                jnp.sum(hacc[0:8, :], axis=0, keepdims=True),
                jnp.sum(hacc[8:16, :], axis=0, keepdims=True),
            )


def dgrad_body(k, ggr, gcat, gsr, normed, wzx, wbc, wst, gain, conv, *refs):
    outs, shared_o, acc = refs[:k], refs[k], refs[k + 1]
    width, d = wzx.shape[2], gain.shape[1]
    i = pl.program_id(0)

    @pl.when(i == 0)
    def _():
        acc[...] = jnp.zeros_like(acc)

    r = dot(ggr[...], wzx[0], 1, 1)
    r = r + dot(gcat[:, :width], wzx[1], 1, 1)
    r = r + dot(gcat[:, width : width + L], wbc[0], 1, 1)
    r = r + dot(gcat[:, width + L :], wbc[1], 1, 1)
    r = r + dot(gsr[...], wst[...])
    acc[...] += eights(r * normed[...].astype(F32))
    rounded = r.astype(BF)

    def into(out):
        out[...] = rounded

    for j in range(k):
        pl.when(i == j)(functools.partial(into, outs[j]))

    @pl.when(i == k - 1)
    def _():
        shared_o[...] = jnp.zeros_like(shared_o)
        sums = jnp.sum(acc[...], axis=0, keepdims=True) / gain[...]
        for c in range(d // ROW):
            shared_o[c : c + 1, :] = sums[:, c * ROW : (c + 1) * ROW]
        shared_o[d // ROW : d // ROW + 5, :] = conv[0:5, conv.shape[1] - ROW :]


def outproj_body(k, normout, wout, *outs):
    def one(out):
        out[...] = dot(normout[...], wout[...]).astype(BF)

    for j in range(k):
        pl.when(pl.program_id(0) == j)(functools.partial(one, outs[j]))


def rows_times(body, frames_n, share, d, rows, consts, name, more=(), scratch=()):
    k = frames_n
    outs = launch(
        functools.partial(body, k),
        [*rows, *consts],
        [pl.BlockSpec((share, r.shape[1]), lambda i: (k - 1 - i, 0)) for r in rows]
        + [whole(a) for a in consts],
        [shaped((share, d), BF)] * k + list(more),
        [pl.BlockSpec((share, d), lambda i: (0, 0))] * k + [whole(o) for o in more],
        name,
        grid=(k,),
        scratch=scratch,
        vmem=20,
    )
    return [*outs[:k][::-1], *outs[k:]]


def total_body(*refs):
    total = refs[0][...].astype(F32)
    for ref in refs[1:-1]:
        total = total + ref[...].astype(F32)
    refs[-1][...] = total.astype(BF)


def hold_body(x, o):
    o[...] = x[...]


def hold(x, *deps):
    return simple(hold_body, [x], [shaped(x.shape, x.dtype)], "hold", deps=deps)[0]


def add_body(a, b, o):
    o[...] = (a[...].astype(F32) + b[...].astype(F32)).astype(o.dtype)


def add(a, b):
    return simple(add_body, [a, b], [shaped(a.shape, a.dtype)], "add")[0]


def swap(x, axis, mask):
    count = lax.axis_size(axis)
    return lax.ppermute(x, axis, [(i, i ^ mask) for i in range(count)])


def masks_of(axis):
    masks, mask = [], 1
    while mask < lax.axis_size(axis):
        masks.append(mask)
        mask *= 2
    return masks


def halve_body(slot, level, meta, kept, got, send_o, keep_o):
    bit = jnp.bitwise_and(jnp.right_shift(meta[slot], level), 1)
    half = send_o.shape[0]
    for o, b in ((send_o, 1 - bit), (keep_o, bit)):
        rows = pl.ds(pl.multiple_of(b * half, half), half)
        o[...] = (kept[rows, :].astype(F32) + got[rows, :].astype(F32)).astype(BF)


def halve(meta, slot, level, kept, got):
    shape = shaped((kept.shape[0] // 2, kept.shape[1]), BF)
    return simple(
        functools.partial(halve_body, slot, level), [kept, got], [shape, shape], "halve", meta
    )


def join_body(slot, level, meta, own, got, o):
    bit = jnp.bitwise_and(jnp.right_shift(meta[slot], level), 1)
    half = own.shape[0]
    o[pl.ds(pl.multiple_of(bit * half, half), half), :] = own[...]
    o[pl.ds(pl.multiple_of((1 - bit) * half, half), half), :] = got[...]


def join(meta, slot, level, own, got):
    shape = shaped((own.shape[0] * 2, own.shape[1]), BF)
    return simple(functools.partial(join_body, slot, level), [own, got], [shape], "join", meta)[0]


def wgrad_body(blocks, half, tails, meta, *refs):
    ins, (send_o, keep_o) = refs[:-2], refs[-2:]
    bit = bit_at(meta, 0)
    i = pl.program_id(0)
    g = jnp.where(i < half, (1 - bit) * half + i, bit * half + i - half)
    for p, tail in enumerate(tails):
        (a, b), ins = ins[:2], ins[2:]
        ta = tb = None
        if tail:
            (ta, tb), ins = ins[:2], ins[2:]
        inside = jnp.logical_and(g >= p * blocks, g < (p + 1) * blocks)

        def into(o, a=a, b=b, ta=ta, tb=tb):
            v = dot(a[...], b[...], 0, 0)
            if ta is not None:
                v = v + dot(ta[...], tb[...], 0, 0)
            o[...] = v.astype(BF)

        pl.when(jnp.logical_and(inside, i < half))(functools.partial(into, send_o))
        pl.when(jnp.logical_and(inside, i >= half))(functools.partial(into, keep_o))


def wgrads(meta, pairs, width, blocks):
    half = blocks * len(pairs) // 2
    tokens = pairs[0][0].shape[0]

    def cut(i, m):
        bit = jnp.bitwise_and(m[1], 1)
        g = jnp.where(i < half, (1 - bit) * half + i, bit * half + i - half)
        return (0, lax.rem(g, blocks))

    specs, ins = [], []
    for a, b, which, *more in pairs:
        for pair in [(a, b), tuple(more)]:
            for j, v in enumerate(pair):
                ins.append(v)
                specs.append(
                    pl.BlockSpec((v.shape[0], width), cut if j == which else lambda i, m: (0, 0))
                )
    return launch(
        functools.partial(wgrad_body, blocks, half, [len(p) > 3 for p in pairs]),
        ins,
        specs,
        [shaped((half * width, width), BF)] * 2,
        [
            pl.BlockSpec((width, width), lambda i, m: (jnp.minimum(i, half - 1), 0)),
            pl.BlockSpec((width, width), lambda i, m: (jnp.maximum(i - half, 0), 0)),
        ],
        "wgrad",
        grid=(2 * half,),
        meta=meta,
        vmem=20,
    )


def bc_body(meta, normed, gcat, gsr, rim, extra, send_o, keep_o, step_o):
    bit = jnp.bitwise_and(meta[0], 1)
    half = send_o.shape[0]
    for o, b in ((send_o, 1 - bit), (keep_o, bit)):
        cols = pl.ds(pl.multiple_of(b * half, half), half)
        v = dot(normed[:, cols], gcat[...], 0, 0) + dot(rim[:, cols], extra[...], 0, 0)
        o[...] = v.astype(BF)
    step_o[...] = dot(gsr[...], normed[...], 0, 0)[:8]


def bc_wgrad(meta, normed, gcat, gsr, rim, extra, width):
    tokens, d = normed.shape

    def tail(rows):
        return pl.BlockSpec((rows, 2 * L), lambda i, m: (0, width // (2 * L)))

    outs = [shaped((d // 2, 2 * L), BF)] * 2 + [shaped((8, d))]
    return launch(
        bc_body,
        [normed, gcat, gsr, rim, extra],
        [whole(normed), tail(tokens), whole(gsr), whole(rim), tail(16)],
        outs,
        [whole(o) for o in outs],
        "bc_wgrad",
        meta=meta,
        vmem=12,
    )


def columns_body(blocks, width, src, *rest):
    o = rest[-1]
    for k in range(blocks):
        o[:, k * width : (k + 1) * width] = src[k * width : (k + 1) * width, :].astype(F32)


def columns(meta, src, mine, d, width, old):
    half = src.shape[0]
    ins, specs, aliases = [src], [whole(src)], {}
    if old is not None:
        ins.append(old)
        specs.append(pl.BlockSpec(memory_space=pl.ANY))
        aliases = {1: 0}
    return launch(
        lambda meta, *refs: columns_body(half // width, width, *refs), ins, specs,
        [shaped((width, d))],
        [pl.BlockSpec((width, half), lambda i, m: (0, bit_at(m, 0) ^ (1 - mine)))],
        "out_weights", meta=meta, aliases=aliases, vmem=16, token=False,
    )[0]


def rows_body(src, *rest):
    rest[-1][0] = src[...].astype(F32)


def rows_of(meta, src, mine, which, d, width, old):
    half = src.shape[0]
    ins, aliases = [src], {}
    specs = [whole(src)]
    if old is not None:
        ins.append(old)
        specs.append(pl.BlockSpec(memory_space=pl.ANY))
        aliases = {1: 0}
    return launch(
        lambda meta, *refs: rows_body(*refs), ins, specs, [shaped((2, d, width))],
        [pl.BlockSpec((1, half, width), lambda i, m: (which, bit_at(m, 0) ^ (1 - mine), 0))],
        "zx_weights", meta=meta, aliases=aliases, vmem=16, token=False,
    )[0]


def bc_out_body(meta, own, got, o):
    bit = jnp.bitwise_and(meta[0], 1)
    half = own.shape[0]
    for v, b in ((own, bit), (got, 1 - bit)):
        rows = pl.ds(pl.multiple_of(b * half, half), half)
        o[0, rows, :] = v[:, :L].astype(F32)
        o[1, rows, :] = v[:, L:].astype(F32)


def patch_body(meta, gcat, ahead, vecs, o):
    count = meta.shape[0] - 3
    keep = jnp.where(meta[2 + count] == 0, 1.0, 0.0)
    o[...] = (gcat[...].astype(F32) + crossing(vecs, ahead[...] * keep)).astype(BF)


def patched(meta, gcat, ahead, vecs, share, group):
    wide = gcat.shape[1]

    def spot(i, m):
        return ((jnp.bitwise_xor(m[0], group - 1) + 1) * (share // 16) - 1, 0)

    return launch(
        patch_body,
        [gcat, ahead, vecs],
        [pl.BlockSpec((16, wide), spot), whole(ahead), whole(vecs)],
        [shaped(gcat.shape, BF)],
        [pl.BlockSpec((16, wide), spot)],
        "patch",
        meta=meta,
        aliases={0: 0},
        token=False,
    )[0]


def layer_body(tok, a, b, o):
    o[...] = (tok[...].astype(F32) + (a[...].astype(F32) + b[...].astype(F32))).astype(BF)


def tokens_body(tok, cot, a, b, gain, gt_o):
    x = tok[...].astype(F32)
    rstd = lax.rsqrt(jnp.mean(x * x, axis=1, keepdims=True) + EPS)
    unit = x * rstd
    gunit = (a[...].astype(F32) + b[...].astype(F32)) * gain[...]
    gt_o[...] = cot[...].astype(F32) + rstd * (
        gunit - unit * jnp.mean(gunit * unit, axis=1, keepdims=True)
    )


def halves_of(v):
    hi, lo = split(v)
    return jnp.concatenate([hi, lo], axis=0)


def whole_of(v):
    n = v.shape[0] // 2
    v = v.astype(F32)
    return v[:n] + v[n:]


def lead_body(bc, shared, o):
    rows = bc.shape[0]
    o[:rows, :] = bc[...]
    o[rows:, :] = halves_of(shared[...])


def misc_halve_body(level, meta, kept, shared, got, send_o, keep_o, shared_o):
    bit = jnp.bitwise_and(jnp.right_shift(meta[0], level), 1)
    half = keep_o.shape[0]
    total = shared[...] + whole_of(got[2 * half :, :])
    shared_o[...] = total
    for o, b in ((send_o, 1 - bit), (keep_o, bit)):
        rows = pl.ds(pl.multiple_of(b * half, half), half)
        o[0:half, :] = (kept[rows, :].astype(F32) + got[rows, :].astype(F32)).astype(BF)
    send_o[half:, :] = halves_of(total)


def misc_pack_body(kept, shared, got, step, conv, gate, head, o):
    rows = kept.shape[0]
    o[0:rows, :] = (kept[...].astype(F32) + got[0:rows, :].astype(F32)).astype(BF)
    d = step.shape[1]
    at = rows
    for k in range(d // ROW):
        o[at : at + 8, :] = step[:, k * ROW : (k + 1) * ROW].astype(BF)
        at += 8
    total = shared[...] + whole_of(got[rows:, :])
    width = gate.shape[1]
    parts = [total]
    for ref, first, n in ((conv, 0, 5), (gate, 0, 2)):
        for k in range(width // ROW):
            parts.append(ref[first : first + n, k * ROW : (k + 1) * ROW])
    used = 7 * (width // ROW)
    parts.append(jnp.concatenate([head[0:1, :], head[1:2, :]], axis=1))
    parts.append(jnp.zeros((31 - used, ROW), F32))
    o[at:, :] = halves_of(jnp.concatenate(parts, axis=0))


def misc_sum(a, b, plain_rows):
    first = a[0:plain_rows, :].astype(F32) + b[0:plain_rows, :].astype(F32)
    return first, whole_of(a[plain_rows:, :]) + whole_of(b[plain_rows:, :])


def misc_add_body(plain_rows, a, b, o):
    first, rest = misc_sum(a, b, plain_rows)
    o[0:plain_rows, :] = first.astype(BF)
    o[plain_rows:, :] = halves_of(rest)


def misc_finish_body(bc_rows, a, b, mats, bcw_o, gain_o, bc_o, bcb_o, step_o, taps_o, bias_o,
                     sb_o, dl_o, sk_o, ng_o):
    d, width, heads = gain_o.shape[1], taps_o.shape[1], sb_o.shape[1]
    n = d // ROW
    first, rest = misc_sum(a, b, bc_rows + 8 * n)
    bcw_o[...] = first[0:bc_rows].astype(BF)
    for k in range(n):
        cols = slice(k * ROW, (k + 1) * ROW)
        at = bc_rows + 8 * k
        step_o[:, cols] = first[at : at + heads]
        gain_o[:, cols] = rest[k : k + 1]
    for k in range(2):
        v = rest[n : n + 5, k * L : (k + 1) * L]
        bc_o[k] = v[0:4]
        bcb_o[k : k + 1, :] = v[4:5]
    at = 16
    m = width // ROW
    gates = []
    for k in range(m):
        cols = slice(k * ROW, (k + 1) * ROW)
        taps_o[:, cols] = rest[at : at + 4]
        bias_o[:, cols] = rest[at + 4 : at + 5]
        at += 5
    for k in range(m):
        cols = slice(k * ROW, (k + 1) * ROW)
        ng_o[:, cols] = rest[at : at + 1]
        gates.append(jnp.broadcast_to(rest[at + 1 : at + 2], (8, ROW)))
        at += 2
    sk = dot_l(jnp.concatenate(gates, axis=1), mats[:, :width], 1, 1)
    sk_o[...] = sk[0:1, :heads]
    dl_o[...] = rest[at : at + 1, :heads]
    sb_o[...] = rest[at : at + 1, L : L + heads]


class Spot(NamedTuple):
    c: Any
    sub: int
    other: int
    first: Any
    last: Any


ORDER = "WLLFLGFWLGTIWMGTWMIGTMTWMIGMWTIBBMGBIIMWMBGMI"


def run_chains(chains, done, order):
    needs = {name: next(chain) for name, chain in chains.items()}

    def step(name):
        need, waits = needs[name]
        if need is not None and need not in done:
            return False
        if waits:
            space()
        try:
            needs[name] = next(chains[name])
        except StopIteration:
            del needs[name]
            done.add(name)
        return True

    for name in order:
        if not step(name):
            raise ValueError(name)
    while needs:
        for name in list(needs):
            step(name)


def on_device(
    tokens_in,
    grad_out,
    scene_offsets,
    input_gain,
    weight_zx,
    weight_bc,
    weight_step,
    conv_inner,
    conv_inner_bias,
    conv_bc,
    conv_bc_bias,
    step_bias,
    decay_log,
    skip_weight,
    norm_gain,
    weight_out,
):
    share, d = tokens_in.shape
    group = lax.axis_size(TP)
    tokens = share * group
    heads = step_bias.shape[0]
    width = norm_gain.shape[0]
    wide = width + 2 * L
    count = tokens // L
    per = share // L
    half = group // 2
    me = lax.axis_index(TP)
    place = lax.axis_index(DP)

    heads_pos = place * tokens + jnp.arange(count + 1, dtype=jnp.int32) * L
    starts = jnp.any(heads_pos[:, None] == scene_offsets[None, :], axis=1).astype(jnp.int32)
    meta = jnp.concatenate([me[None].astype(jnp.int32), place[None].astype(jnp.int32), starts])
    masks, tmasks = masks_of(DP), masks_of(TP)
    levels = len(masks)

    LAST.clear()
    def spread_out(held, keys):
        mask = half // 2
        while mask:
            for f in [f for f in held if f in keys]:
                held[f ^ mask] = swap(held[f], TP, mask)
            mask //= 2

    near, far = range(half), range(half, group)
    held = {0: tokens_in}
    arrived = swap(tokens_in, TP, half)
    spread_out(held, near)
    dps = lax.axis_size(DP)
    (last_rows,) = launch(
        lambda tok, _, o: hold_body(tok, o), [tokens_in, held[1]],
        [pl.BlockSpec((16, d), lambda i: (share // 16 - 1, 0)), pl.BlockSpec(memory_space=pl.ANY)],
        [shaped((16, d), BF)], [pl.BlockSpec((16, d), lambda i: (0, 0))], "last_rows",
    )
    past = [
        lax.ppermute(
            last_rows,
            (DP, TP),
            [(i * group + group - 1, (i + 1) * group + t) for i in range(dps - 1)],
        )
        for t in range(1, group, 2)
    ]
    gain = input_gain[None]
    prep_ins = [conv_inner, conv_inner_bias[None], conv_bc, conv_bc_bias, step_bias[None],
                decay_log[None], skip_weight[None], norm_gain[None], weight_step.T]
    prep_outs = [shaped((8, wide)), shaped((8, L)), shaped((L, width + L), BF),
                 shaped((L, d), BF)]
    vecs, hv, mats, wst = launch(
        prep_body,
        [pltpu.with_memory_space_constraint(a, pltpu.HBM) for a in prep_ins],
        [whole(a) for a in prep_ins],
        prep_outs, [whole(o) for o in prep_outs], "prep", vmem=4,
    )
    def stretched(body, name, ins, outs, scratch, reverse, vmem, span=None, old=()):
        begin, length = span or (0, count // per)

        def order(i):
            return count // per - 1 - i - begin if reverse else i + begin

        def spec(kind, shape):
            if kind == ROWS:
                return pl.BlockSpec(
                    (share, shape[1]), lambda i, m: (lax.bitwise_xor(order(i), m[0]), 0)
                )
            if kind == EACH:
                return pl.BlockSpec((per, *shape[1:]), lambda i, m: (order(i), 0, 0))
            return pl.BlockSpec(shape, lambda i, m: (0,) * len(shape))

        kinds = [k for k, _ in ins] + [k for k, _, _ in outs]
        n = len(ins)

        def run(meta, *refs):
            refs = refs[:n] + refs[n + len(old) :]
            step = pl.program_id(0)
            for sub in range(per):
                pos = per - 1 - sub if reverse else sub

                def view(kind, ref, pos=pos):
                    if kind == ROWS:
                        return ref.at[pl.ds(pos * L, L)]
                    return ref.at[pl.ds(pos, 1)] if kind == EACH else ref

                views = [view(k, r) for k, r in zip(kinds, refs)]
                at = Spot(
                    order(step) * per + pos,
                    sub,
                    (sub - 1) % per,
                    step == 0 if sub == 0 else None,
                    step == length - 1 if sub == per - 1 else None,
                )
                body(at, meta, *views, *refs[len(kinds) :])

        return launch(
            run,
            [a for _, a in ins] + list(old),
            [spec(k, a.shape) for k, a in ins] + [pl.BlockSpec(memory_space=pl.ANY)] * len(old),
            [shaped(s, t) for _, s, t in outs],
            [spec(k, s) for k, s, _ in outs],
            name,
            grid=(length,),
            meta=meta,
            scratch=scratch,
            aliases={n + j: j for j in range(len(old))},
            vmem=vmem,
        )

    weights = (gain, weight_zx, weight_bc, wst)
    before = project(meta, [held[f] for f in near], [], *weights, tokens, 0, [])
    space()
    held[half] = hold(arrived, before[3])
    (own_past,) = simple(total_body, past, [shaped((16, d), BF)], "past")
    past = [own_past, swap(own_past, TP, 1)]
    spread_out(held, far)
    before = project(meta, [held[half]], [], *weights, tokens, half, list(before))
    space()
    normed, gate_raw, cat, step_raw, rim, normed_rim = project(
        meta, [held[f] for f in far[1:]], past, *weights, tokens, half + 1, list(before)
    )

    tall = (tokens, L)
    state_shape = (width, L)
    load_shape = (width + 16, L)
    small = (8, L)
    pre, cb, sin, state, load, cum, pfx, decay = stretched(
        states_body,
        "states",
        [(ROWS, cat), (ROWS, step_raw), (ONE, rim), (ONE, vecs), (ONE, hv),
         (ONE, mats)],
        [(ROWS, (tokens, wide), F32), (ROWS, tall, BF), (EACH, (count, *state_shape), BF),
         (ONE, state_shape, F32), (ONE, load_shape, BF), (ROWS, tall, F32),
         (EACH, (count, 8, L), F32), (ONE, small, F32)],
        [pltpu.VMEM((per, L + 8, wide), F32), pltpu.VMEM(state_shape, F32),
         pltpu.VMEM(small, F32)],
        False, 14,
    )

    def link(level, reverse, held, load):
        final = level == levels - 2
        shapes = [load_shape, state_shape, small] + ([] if final else [state_shape, small])
        load, before, through, *more = simple(
            functools.partial(link_body, level, reverse, final), [*held, load],
            [shaped(s, BF if j == 0 else F32) for j, s in enumerate(shapes)], "link", meta,
        )
        return [*more, before, through], load

    thr = decay
    fresh = [jnp.zeros(state_shape, F32), jnp.ones(small, F32)]
    own = [state, decay, *fresh]
    load = swap(load, DP, 1)
    cots = {0: grad_out}
    cots[half] = swap(hold(grad_out), TP, half)
    (y,) = stretched(
        within_body,
        "within",
        [(ROWS, pre), (ROWS, step_raw), (ROWS, cum), (EACH, sin), (ONE, vecs),
         (ONE, hv), (ONE, mats)],
        [(ROWS, (tokens, width), F32)],
        [], False, 14,
    )
    for level in range(levels - 1):
        space()
        own, load = link(level, False, own, load)
        load = swap(load, DP, masks[level + 1])
        if level == levels - 2:
            space()
            late = {half: hold(cots[half])}
            spread_out(late, far)
            spread_out(cots, near)
            cots.update({f: late[f] for f in far[1:]})
            space()
            cot_all, gn = cotangent([cots[f] for f in range(group)], weight_out)
    befores, throughs = own[-2:]
    space()
    mixed, sums, incoming = stretched(
        functools.partial(gate_body, levels - 1),
        "gated",
        [(ROWS, cb), (ROWS, cum), (EACH, pfx), (ROWS, y), (ROWS, gate_raw),
         (ROWS, gn), (ONE, befores), (ONE, throughs), (ONE, load), (ONE, vecs),
         (ONE, mats)],
        [(ROWS, (tokens, width), F32), (EACH, (count, 2, L), F32), (ONE, state_shape, BF)],
        [], False, 14,
    )
    for mask in tmasks[::-1][:-1]:
        got = swap(sums, TP, mask)
        space()
        sums = add(sums, got)
    sums2 = swap(sums, TP, 1)
    space()
    normout, gm, ggr, gs, toward, first_load, sfx, gate_acc = stretched(
        back_gate_body,
        "back_gated",
        [(ROWS, pre), (ROWS, cum), (ROWS, mixed), (ROWS, gate_raw), (ROWS, gn),
         (EACH, sums), (EACH, sums2), (ONE, thr), (ONE, vecs), (ONE, mats)],
        [(ROWS, (tokens, width), BF), (ROWS, (tokens, width), BF),
         (ROWS, (tokens, width), BF), (EACH, (count, *state_shape), BF),
         (ONE, state_shape, F32), (ONE, load_shape, BF), (EACH, (count, 8, L), F32),
         (ONE, (8, width), F32)],
        [pltpu.VMEM(state_shape, F32), pltpu.VMEM(small, F32), pltpu.VMEM((16, width), F32)],
        True, 14,
    )

    kept = SimpleNamespace(within=(), zx=None, wout=None)
    done = set()
    blocks = d // width

    def weights_chain(pairs, finish, need=None):
        yield need, False
        send, keep = wgrads(meta, [pairs()], width, blocks)
        for level in range(levels):
            got = swap(send, DP, masks[level])
            yield None, True
            if level < levels - 1:
                send, keep = halve(meta, 1, level + 1, keep, got)
            else:
                total = add(keep, got)
        for level in range(levels - 1, -1, -1):
            got = swap(total, DP, masks[level])
            if not level:
                finish(total, 1)
            yield None, True
            if level:
                total = join(meta, 1, level, total, got)
        finish(got, 0)

    def out_weights(src, mine):
        kept.wout = columns(meta, src, mine, d, width, kept.wout)

    def gate_weights(src, mine):
        kept.zx = rows_of(meta, src, mine, 0, d, width, kept.zx)

    def inner_weights(src, mine):
        kept.zx = rows_of(meta, src, mine, 1, d, width, kept.zx)

    def links_chain():
        yield None, False
        own, load = [toward, thr, *fresh], first_load
        for level in range(levels):
            got = swap(load, DP, masks[level])
            yield None if level < levels - 1 else "F", True
            if level < levels - 1:
                own, load = link(level, True, own, got)
        befores, throughs = own[-2:]
        ginner, gbc, glog, gst = kept.within
        kept.gcat, kept.gsr, kept.head, kept.extra, kept.conv_acc, kept.head_acc = stretched(
            functools.partial(back_conv_body, levels - 1),
            "back_conv",
            [(ROWS, cat), (ONE, rim), (ROWS, pre), (ROWS, step_raw), (ROWS, cum),
             (EACH, sin), (EACH, pfx), (EACH, sfx), (ROWS, ginner), (ROWS, gbc),
             (ROWS, glog), (ROWS, gst), (ONE, incoming), (ONE, befores), (ONE, throughs),
             (ONE, got), (ONE, vecs), (ONE, hv), (ONE, mats)],
            [(ROWS, (tokens, wide), BF), (ROWS, tall, BF), (ONE, (8, wide), F32),
             (ONE, (16, wide), BF), (ONE, (8, wide), F32), (ONE, small, F32)],
            [pltpu.VMEM((per, L + 8, wide), F32), pltpu.VMEM((40, wide), F32),
             pltpu.VMEM((16, L), F32), pltpu.VMEM(state_shape, F32)],
            True, 16,
        )

    def within_chain():
        for begin in (0, half):
            yield None, False
            kept.within = stretched(
                back_within_body,
                "back_within",
                [(ROWS, pre), (ROWS, step_raw), (ROWS, cum), (EACH, sin), (EACH, pfx),
                 (EACH, gs), (ROWS, gm), (ONE, incoming), (ONE, vecs), (ONE, hv), (ONE, mats)],
                [(ROWS, (tokens, width), F32), (ROWS, (tokens, 2 * L), F32), (ROWS, tall, F32),
                 (ROWS, tall, F32)],
                [], True, 16, (begin, half), kept.within,
            )

    def scattered(frames_in):
        sums_in = []
        for first in (0, half):
            part = dict(enumerate(frames_in[first : first + half]))
            mask = 1
            while mask < half:
                for f in [f for f in part if f & mask]:
                    got = swap(part.pop(f), TP, mask)
                    yield None, True
                    part[f ^ mask] = add(part[f ^ mask], got)
                mask *= 2
            sums_in.append(part[0])
        got = swap(sums_in[1], TP, half)
        yield None, True
        return sums_in[0], got

    def branch_chain():
        yield None, False
        branch = rows_times(outproj_body, group, share, d, [normout], [weight_out], "outproj")
        parts = yield from scattered(branch)
        (kept.layer,) = simple(
            layer_body, [tokens_in, *parts], [shaped((share, d), BF)], "layer", tick=True
        )

    def tokens_chain():
        yield "L", False
        ahead = lax.ppermute(kept.head, DP, [(i + 1, i) for i in range(dps - 1)])
        yield None, True
        gcat = patched(meta, kept.gcat, ahead, vecs, share, group)
        *grads, kept.shared = rows_times(
            dgrad_body, group, share, d, [ggr, gcat, kept.gsr, normed],
            [weight_zx, weight_bc, wst, gain, kept.conv_acc],
            "dgrad", [shaped((16, ROW))], [pltpu.VMEM((8, d), F32)],
        )
        done.add("dgrad")
        parts = yield from scattered(grads)
        (kept.tokens,) = simple(
            tokens_body, [tokens_in, grad_out, *parts, gain], [shaped((share, d))], "tokens",
            None, 12, tick=True,
        )

    def misc_chain():
        yield "L", False
        send, keep, step_acc = bc_wgrad(
            meta, normed, kept.gcat, kept.gsr, normed_rim, kept.extra, width
        )
        yield "dgrad", False
        shared = kept.shared
        (load,) = simple(lead_body, [send, shared], [shaped((send.shape[0] + 32, ROW), BF)], "lead")
        for level in range(len(tmasks)):
            got = swap(load, TP, tmasks[level])
            yield None, True
            if level < len(tmasks) - 1:
                rows = keep.shape[0] // 2
                load, keep, shared = simple(
                    functools.partial(misc_halve_body, level + 1), [keep, shared, got],
                    [shaped((rows + 32, ROW), BF), shaped((rows, ROW), BF), shaped((16, ROW))],
                    "misc_halve", meta,
                )
        rows = keep.shape[0]
        flat = rows + 8 * (d // ROW)
        (load,) = simple(
            misc_pack_body,
            [keep, shared, got, step_acc, kept.conv_acc, gate_acc, kept.head_acc],
            [shaped((flat + 96, ROW), BF)], "misc_pack",
        )
        for level in range(levels):
            got = swap(load, DP, masks[level])
            yield None, True
            if level < levels - 1:
                (load,) = simple(
                    functools.partial(misc_add_body, flat), [load, got],
                    [shaped(load.shape, BF)], "misc_add",
                )
        outs = [(1, d), (2, 4, L), (2, L), (heads, d), (4, width), (1, width), (1, heads),
                (1, heads), (1, heads), (1, width)]
        total, *kept.small = simple(
            functools.partial(misc_finish_body, rows), [load, got, mats],
            [shaped((rows, ROW), BF)] + [shaped(s) for s in outs], "misc_finish",
            tick=True,
        )
        for level in range(len(tmasks) - 1, -1, -1):
            got = swap(total, TP, tmasks[level])
            yield None, True
            if level:
                total = join(meta, 0, level, total, got)
        (kept.bc,) = simple(
            bc_out_body, [total, got], [shaped((2, d, L))], "bc_weights", meta, tick=True
        )

    run_chains(
        {
            "L": links_chain(),
            "W": weights_chain(lambda: (normout, cot_all, 1), out_weights),
            "G": weights_chain(lambda: (normed, ggr, 0), gate_weights),
            "F": within_chain(),
            "B": branch_chain(),
            "T": tokens_chain(),
            "I": weights_chain(
                lambda: (normed, kept.gcat, 0, normed_rim, kept.extra), inner_weights, "L"
            ),
            "M": misc_chain(),
        },
        done,
        ORDER if (dps, group) == (8, 4) else "",
    )

    gain_g, bc_g, bcb_g, step_g, taps_g, bias_g, sb_g, dl_g, sk_g, ng_g = kept.small
    return (
        kept.layer,
        kept.tokens,
        gain_g[0],
        kept.zx,
        kept.bc,
        step_g.T,
        taps_g,
        bias_g[0],
        bc_g,
        bcb_g,
        sb_g[0],
        dl_g[0],
        sk_g[0],
        ng_g[0],
        kept.wout,
    )


def solution(mesh):
    rows = P((DP, TP), None)
    cols = P(None, TP)
    one = P(TP)
    in_specs = (
        rows, rows, P(), P(), P(None, None, TP), P(), cols, cols, one, P(), P(),
        one, one, one, one, P(TP, None),
    )
    out_specs = (
        rows, rows, P(), P(None, None, TP), P(), cols, cols, one, P(), P(),
        one, one, one, one, P(TP, None),
    )
    return jax.shard_map(
        on_device, mesh=mesh, in_specs=in_specs, out_specs=out_specs, check_vma=False
    )
```

```python
import functools
from types import SimpleNamespace
from typing import Any, NamedTuple

import jax
import jax.numpy as jnp
from jax import lax
from jax.experimental import pallas as pl
from jax.experimental.pallas import tpu as pltpu
from jax.sharding import PartitionSpec as P

KERNEL = 4
L = 128
HD = 64
DI = 2048
EPS = 1e-05
F32 = jnp.float32
BF = jnp.bfloat16
MIB = 1 << 20
ROW = 256
DP, TP = "dp", "tensor"
ROWS, EACH, ONE = range(3)


def dot(a, b, ca=1, cb=0):
    return lax.dot_general(a, b, (((ca,), (cb,)), ((), ())), preferred_element_type=F32)


def split(a):
    hi = a.astype(BF)
    return hi, (a - hi.astype(F32)).astype(BF)


def dot_l(a, b, ca=1, cb=0):
    hi, lo = split(a)
    return dot(hi, b, ca, cb) + dot(lo, b, ca, cb)


def dot_r(a, b, ca=1, cb=0):
    hi, lo = split(b)
    return dot(a, hi, ca, cb) + dot(a, lo, ca, cb)


def sigmoid(v):
    return 0.5 * jnp.tanh(0.5 * v) + 0.5


def softplus(v):
    u = jnp.exp(-jnp.abs(v))
    small = u * (1.0 - u * (0.5 - u * (1.0 / 3.0 - u * 0.25)))
    return jnp.maximum(v, 0.0) + jnp.where(u < 0.02, small, jnp.log(1.0 + u))


def per_head(row, heads):
    return jnp.concatenate(
        [jnp.broadcast_to(row[:, h : h + 1], (HD, L)) for h in range(heads)], axis=0
    )


def eights(v):
    return jnp.sum(v.reshape(v.shape[0] // 8, 8, v.shape[1]), axis=0)


def across_lanes(v, width):
    return jnp.concatenate([v] * (width // L), axis=1) if width > L else v


def whole(a):
    return pl.BlockSpec(a.shape, lambda *_: (0,) * a.ndim)


LAST = []

def launch(body, ins, in_specs, outs, out_specs, name, grid=(1,), meta=None, scratch=(),
           aliases=None, vmem=8, flops=0, token=True, tick=False):
    ins, in_specs = list(ins), list(in_specs)
    lead = 0 if meta is None else 1
    at = lead + len(ins)
    given = LAST[-1] if LAST and not any(LAST[-1] is a for a in ins) else None
    if given is not None:
        ins.append(given)
        in_specs.append(pl.BlockSpec(memory_space=pl.ANY))

    outs, out_specs = list(outs), list(out_specs)
    if tick:
        outs.append(shaped((8, L)))
        out_specs.append(whole(outs[-1]))

    def run(*refs):
        refs = refs if given is None else refs[:at] + refs[at + 1 :]
        if tick:
            last = lead + len(ins) - (given is not None) + len(outs) - 1
            refs[last][...] = jnp.zeros((8, L), F32)
            refs = refs[:last] + refs[last + 1 :]
        body(*refs)

    results = pl.pallas_call(
        run,
        grid_spec=pltpu.PrefetchScalarGridSpec(
            num_scalar_prefetch=lead,
            grid=grid,
            in_specs=in_specs,
            out_specs=list(out_specs),
            scratch_shapes=list(scratch),
        ),
        out_shape=list(outs),
        input_output_aliases={lead + k: v for k, v in (aliases or {}).items()},
        compiler_params=pltpu.CompilerParams(vmem_limit_bytes=vmem * MIB),
        cost_estimate=pl.CostEstimate(
            flops=flops,
            bytes_accessed=0,
            transcendentals=0,
        ),
        name=name,
    )(*([] if meta is None else [meta]), *ins)
    if tick:
        *results, LAST[:] = [*results[:-1], results[-1:]]
    elif token:
        LAST[:] = [min(results, key=lambda a: a.size)]
    return results


def space_body(o):
    o[...] = jnp.zeros_like(o)


def space(flops=10 * 10**9):
    o = shaped((8, L))
    launch(space_body, [], [], [o], [whole(o)], "space", vmem=1, flops=flops)


def shaped(shape, dtype=F32):
    return jax.ShapeDtypeStruct(shape, dtype)


def simple(body, ins, outs, name, meta=None, vmem=8, deps=(), tick=False):
    n = len(ins)

    def run(*refs):
        lead = 0 if meta is None else 1
        body(*refs[: lead + n], *refs[lead + n + len(deps) :])

    return launch(
        run, [*ins, *deps],
        [whole(a) for a in ins] + [pl.BlockSpec(memory_space=pl.ANY)] * len(deps),
        outs, [whole(o) for o in outs], name, meta=meta, vmem=vmem, tick=tick,
    )


def unit_rows(x, gain):
    x = x.astype(F32)
    rstd = lax.rsqrt(jnp.mean(x * x, axis=1, keepdims=True) + EPS)
    return (x * rstd * gain).astype(BF)


def proj_body(k, rims, deps, meta, *refs):
    toks, past = refs[:k], refs[k : k + rims]
    gain, wzx, wbc, wst = refs[k + rims : k + rims + 4]
    outs = refs[k + rims + 4 + deps :]
    normed_o, gate_o, cat_o, step_o = outs[:4]
    width = wzx.shape[2]

    def conv_inputs(normed, out):
        out[:, :width] = dot(normed, wzx[1]).astype(BF)
        out[:, width : width + L] = dot(normed, wbc[0]).astype(BF)
        out[:, width + L :] = dot(normed, wbc[1]).astype(BF)

    def one(j):
        normed = unit_rows(toks[j][...], gain[...])
        normed_o[...] = normed
        conv_inputs(normed, cat_o)
        gate_o[...] = dot(normed, wzx[0]).astype(BF)
        step_o[...] = dot(normed, wst[...], 1, 1).astype(BF)
        if rims and j == 0:
            rim = past[0][...].astype(F32)
            for p in past[1:]:
                rim = rim + p[...].astype(F32)
            normed = unit_rows(rim, gain[...])
            outs[5][...] = normed
            conv_inputs(normed, outs[4])

    for j in range(k):
        pl.when(pl.program_id(0) == j)(functools.partial(one, j))


def project(meta, toks, past, gain, wzx, wbc, wst, total, first, before):
    k = len(toks)
    share, d = toks[0].shape
    width = wzx.shape[2]
    wide = width + 2 * L
    cols = (d, width, wide, L)
    ins = [*toks, *past, gain, wzx, wbc, wst]
    specs = [whole(a) for a in ins]
    out_specs = [pl.BlockSpec((share, c), lambda i, m: (i + first, 0)) for c in cols]
    out_shape = [shaped((total, c), BF) for c in cols]
    if past:
        for c in (wide, d):
            out_specs.append(pl.BlockSpec((16, c), lambda i, m: (0, 0)))
            out_shape.append(shaped((16, c), BF))
    aliases = {len(ins) + j: j for j in range(4)} if before else {}
    return launch(
        functools.partial(proj_body, k, len(past), len(before)),
        ins + before,
        specs + [pl.BlockSpec(memory_space=pl.ANY)] * len(before),
        out_shape,
        out_specs,
        "project",
        grid=(k,),
        meta=meta,
        aliases=aliases,
        vmem=16,
        token=False,
    )


def prep_body(taps, tbias, btaps, bbias, sbias, decay, skip, ngain, wst, vecs, hv, mats, wst_o):
    width = taps.shape[1]
    heads = width // HD
    wst_o[...] = jnp.zeros_like(wst_o)
    wst_o[0:heads, :] = wst[...]
    head = lax.broadcasted_iota(jnp.int32, (L, width), 0)
    lane = lax.broadcasted_iota(jnp.int32, (L, width), 1)
    spread = jnp.where(lax.div(lane, HD) == head, 1.0, 0.0).astype(BF)
    mats[:, :width] = spread
    r = lax.broadcasted_iota(jnp.int32, (L, L), 0)
    c = lax.broadcasted_iota(jnp.int32, (L, L), 1)
    mats[:, width:] = jnp.where(r >= c, 1.0, 0.0).astype(BF)
    hv[...] = jnp.zeros_like(hv)
    hv[0:1, :heads] = sbias[...]
    hv[1:2, :heads] = -jnp.exp(decay[...])
    hv[2:3, :heads] = skip[...]
    vecs[...] = jnp.zeros_like(vecs)
    vecs[0:4, :width] = taps[...]
    vecs[4:5, :width] = tbias[...]
    for k in range(2):
        cols = slice(width + k * L, width + k * L + L)
        vecs[0:4, cols] = btaps[k]
        vecs[4:5, cols] = bbias[k : k + 1, :]
    vecs[5:6, :width] = dot_l(hv[...], spread)[2:3, :]
    vecs[6:7, :width] = ngain[...]


def cot_body(k, *refs):
    cots = refs[:k]
    wout, all_o, gn_o = refs[k:]

    def one(cot):
        v = cot[...]
        all_o[...] = v
        gn_o[...] = dot(v, wout[...], 1, 1).astype(BF)

    for j in range(k):
        pl.when(pl.program_id(0) == j)(functools.partial(one, cots[j]))


def cotangent(cots, wout):
    k = len(cots)
    share, d = cots[0].shape
    width = wout.shape[0]
    return launch(
        functools.partial(cot_body, k),
        [*cots, wout],
        [whole(a) for a in (*cots, wout)],
        [shaped((k * share, d), BF), shaped((k * share, width), BF)],
        [pl.BlockSpec((share, c), lambda i: (i, 0)) for c in (d, width)],
        "cotangent",
        grid=(k,),
        vmem=12,
    )


def act_parts(pre, width):
    out = []
    for x0 in range(0, width + 2 * L, L):
        v = pre[:, x0 : x0 + L]
        out.append(v * sigmoid(v))
    return out


def pack(out, state, decay):
    rows = state.shape[0]
    hi, lo = split(jnp.broadcast_to(decay[0:1, :], (16, L)))
    row = lax.broadcasted_iota(jnp.int32, (16, L), 0)
    out[:rows, :] = state.astype(BF)
    tail = jnp.where(row == 0, hi.astype(F32), jnp.where(row == 1, lo.astype(F32), 0.0))
    out[rows:, :] = tail.astype(BF)


def unpack(load):
    v = load[...].astype(F32)
    rows = v.shape[0] - 16
    return v[:rows], v[rows : rows + 1] + v[rows + 1 : rows + 2]


def bit_at(meta, level):
    return jnp.bitwise_and(jnp.right_shift(meta[1], level), 1)


def is_ahead(meta, level, reverse):
    bit = bit_at(meta, level)
    return jnp.where(bit == (0 if reverse else 1), 1.0, 0.0)


def link_body(level, reverse, final, meta, state, decay, before, through, load,
              load_o, before_o, through_o, *more):
    theirs, a = unpack(load)
    heads = theirs.shape[0] // HD
    ahead = is_ahead(meta, level, reverse)
    mine = decay[0:1, :]
    t = through[0:1, :]
    before_o[...] = before[...] + per_head(t * ahead, heads) * theirs
    through_o[...] = jnp.broadcast_to(t * (ahead * a + (1.0 - ahead)), (8, L))
    joined = (
        per_head(mine * ahead + (1.0 - ahead), heads) * theirs
        + per_head(a * (1.0 - ahead) + ahead, heads) * state[...]
    )
    pack(load_o, joined, mine * a)
    if not final:
        state_o, decay_o = more
        state_o[...] = joined
        decay_o[...] = jnp.broadcast_to(mine * a, (8, L))


def final_link(meta, level, reverse, before, through, load):
    theirs, _ = unpack(load)
    t = through[0:1, :] * is_ahead(meta, level, reverse)
    return before[...] + per_head(t, theirs.shape[0] // HD) * theirs


def states_body(
    at, meta, cat, step, rim, vecs, hv, mats,
    pre_o, cb_o, sin_o, end_o, load_o, cum_o, pfx_o, thr_o, buf, state, prod,
):
    width = vecs.shape[1] - 2 * L
    heads = width // HD
    keep = jnp.where(meta[2 + at.c] == 0, 1.0, 0.0)
    before, buf = buf.at[at.other], buf.at[at.sub]

    def follow():
        buf[0:8, :] = before[L : L + 8, :] * keep

    if at.first is None:
        follow()
    else:

        @pl.when(at.first)
        def _():
            buf[0:8, :] = rim[...].astype(F32)[8:16, :] * keep
            state[...] = jnp.zeros_like(state)
            prod[...] = jnp.ones_like(prod)

        pl.when(jnp.logical_not(at.first))(follow)

    buf[8 : 8 + L, :] = cat[...].astype(F32)
    acts = []
    for x0 in range(0, width + 2 * L, L):
        cols = slice(x0, x0 + L)
        v = vecs[4:5, cols] + vecs[3:4, cols] * buf[8 : 8 + L, cols]
        for j in range(1, KERNEL):
            v = v + vecs[3 - j : 4 - j, cols] * buf[8 - j : 8 - j + L, cols]
        pre_o[:, cols] = v
        acts.append(v * sigmoid(v))
    cb_o[...] = acts[-1].astype(BF)
    steps = softplus(step[...].astype(F32) + hv[0:1, :])
    cum = dot_r(mats[:, width:], steps * hv[1:2, :])
    cum_o[...] = cum
    total = cum[L - 1 : L, :]
    weights = dot((jnp.exp(total - cum) * steps).astype(BF), mats[:, :width])
    inner = jnp.concatenate(acts[: width // L], axis=1)
    local = dot((inner * weights).astype(BF), acts[-2].astype(BF), 0, 0)
    entering = state[...] * keep
    sin_o[0] = entering.astype(BF)
    dec = jnp.exp(total)
    leaving = per_head(dec, heads) * entering + local
    state[...] = leaving
    here = prod[...] * keep
    pfx_o[0] = here
    prod[...] = here * dec

    if at.last is not None:

        @pl.when(at.last)
        def _():
            end_o[...] = leaving
            thr_o[...] = here * dec
            pack(load_o, leaving, here * dec)


def within_body(at, meta, pre, step, cum_r, sin, vecs, hv, mats, y_o):
    width = vecs.shape[1] - 2 * L
    heads = width // HD
    acts = act_parts(pre, width)
    bb, cb = acts[-2].astype(BF), acts[-1].astype(BF)
    scores = dot(cb, bb, 1, 1)
    steps = softplus(step[...].astype(F32) + hv[0:1, :])
    cum = cum_r[...]
    cum_t, steps_t = cum.T, steps.T
    lower = lax.broadcasted_iota(jnp.int32, (L, L), 0) >= lax.broadcasted_iota(
        jnp.int32, (L, L), 1
    )
    first = lax.broadcasted_iota(jnp.int32, (L, L), 1) < HD
    grown = dot(jnp.exp(cum).astype(BF), mats[:, :width])
    far = grown * dot(cb, sin[0], 1, 1)
    for pair in range(heads // 2):
        cols = slice(pair * L, pair * L + L)
        x = acts[pair].astype(BF)
        got = []
        for h in (2 * pair, 2 * pair + 1):
            gap = jnp.where(lower, cum[:, h : h + 1] - cum_t[h : h + 1, :], -1e30)
            mix = scores * jnp.exp(gap) * steps_t[h : h + 1, :]
            got.append(dot(mix.astype(BF), x))
        y_o[:, cols] = (
            jnp.where(first, got[0], got[1]) + far[:, cols] + vecs[5:6, cols] * acts[pair]
        )


def gate_body(
    level, at, meta, cb, cum, pfx, y, gate, gn, before, through, load, vecs, mats,
    mixed_o, sums_o, incoming,
):
    width = vecs.shape[1] - 2 * L
    ones = jnp.ones((8, L), BF)

    if at.first is not None:

        @pl.when(at.first)
        def _():
            incoming[...] = final_link(meta, level, False, before, through, load).astype(BF)

    reach = dot((jnp.exp(cum[...]) * pfx[0][0:1, :]).astype(BF), mats[:, :width])
    far = reach * dot(cb[...], incoming[...], 1, 1)
    squares, crosses = [], []
    for x0 in range(0, width, L):
        cols = slice(x0, x0 + L)
        mixed = y[:, cols] + far[:, cols]
        mixed_o[:, cols] = mixed
        g = gate[:, cols].astype(F32)
        gated = mixed * (g * sigmoid(g))
        squares.append(gated * gated)
        crosses.append(gn[:, cols].astype(F32) * vecs[6:7, cols] * gated)
    square = dot_r(ones, functools.reduce(jnp.add, squares), 1, 1)
    cross = dot_r(ones, functools.reduce(jnp.add, crosses), 1, 1)
    sums_o[0, 0:1] = square[0:1]
    sums_o[0, 1:2] = cross[0:1]


def back_gate_body(
    at, meta, pre, cum_r, mixed_r, gate, gn, sums, sums2, thr, vecs, mats,
    normout_o, gm_o, ggr_o, gs_o, toward_o, load_o, sfx_o, acc_o, gstate, prod, acc,
):
    width = vecs.shape[1] - 2 * L
    heads = width // HD
    keep = jnp.where(meta[2 + at.c] == 0, 1.0, 0.0)

    if at.first is not None:

        @pl.when(at.first)
        def _():
            gstate[...] = jnp.zeros_like(gstate)
            prod[...] = jnp.ones_like(prod)
            acc[...] = jnp.zeros_like(acc)

    both = sums[0] + sums2[0]
    square = jnp.broadcast_to(both[0:1, :], (L, L)).T
    cross = jnp.broadcast_to(both[1:2, :], (L, L)).T
    scale = lax.rsqrt(square * (1.0 / DI) + EPS)
    cubed = scale * scale * scale * cross * (1.0 / DI)
    cum = cum_r[...]
    total = cum[L - 1 : L, :]
    grown = dot(jnp.exp(cum).astype(BF), mats[:, :width])
    cv = pre[:, width + L :]
    cb = (cv * sigmoid(cv)).astype(BF)
    moved = []
    for x0 in range(0, width, L):
        cols = slice(x0, x0 + L)
        v = pre[:, cols]
        inner = v * sigmoid(v)
        g = gate[:, cols].astype(F32)
        s = sigmoid(g)
        silu = g * s
        mixed = mixed_r[:, cols]
        gated = mixed * silu
        ng = vecs[6:7, cols]
        gnv = gn[:, cols].astype(F32)
        scaled = gated * scale
        normout_o[:, cols] = (scaled * ng).astype(BF)
        gg = scale * (gnv * ng) - gated * cubed
        gm = gg * silu
        gm_o[:, cols] = gm.astype(BF)
        ggr_o[:, cols] = (gg * mixed * (s + silu * (1.0 - s))).astype(BF)
        acc[0:8, cols] += eights(gnv * scaled)
        acc[8:16, cols] += eights(gm * inner)
        moved.append((gm * grown[:, cols]).astype(BF))
    leaving = gstate[...]
    gs_o[0] = leaving.astype(BF)
    here = prod[...]
    sfx_o[0] = here
    dec = jnp.exp(total)
    entering = per_head(dec, heads) * leaving + dot(jnp.concatenate(moved, axis=1), cb, 0, 0)
    entering = entering * keep
    gstate[...] = entering
    prod[...] = here * dec * keep

    if at.last is not None:

        @pl.when(at.last)
        def _():
            toward_o[...] = entering
            pack(load_o, entering, thr[...])
            row = lax.broadcasted_iota(jnp.int32, (8, width), 0)
            acc_o[...] = jnp.where(
                row == 0,
                jnp.sum(acc[0:8, :], axis=0, keepdims=True),
                jnp.sum(acc[8:16, :], axis=0, keepdims=True),
            )


def head_product(a, b, spread):
    rows = dot(jnp.ones((8, L), BF), (a * b).astype(BF), 1, 1)
    return dot_l(rows, spread, 1, 1)[0:1, :]


def back_within_body(
    at, meta, pre, step, cum_r, sin, pfx, gs, gm_r, incoming, vecs, hv, mats,
    ginner_o, gbc_o, glog_o, gst_o,
):
    width = vecs.shape[1] - 2 * L
    heads = width // HD
    acts = act_parts(pre, width)
    bb, cb = acts[-2].astype(BF), acts[-1].astype(BF)
    scores = dot(cb, bb, 1, 1)
    steps = softplus(step[...].astype(F32) + hv[0:1, :])
    cum = cum_r[...]
    total = cum[L - 1 : L, :]
    cum_t, steps_t = cum.T, steps.T
    row = lax.broadcasted_iota(jnp.int32, (L, L), 0)
    col = lax.broadcasted_iota(jnp.int32, (L, L), 1)
    lower = row >= col
    first = col < HD
    e = jnp.exp(cum)
    wd = jnp.exp(total - cum)
    grown = dot(e.astype(BF), mats[:, :width])
    weights = dot((wd * steps).astype(BF), mats[:, :width])
    gsb = gs[0]
    entering = sin[0].astype(F32) + per_head(pfx[0][0:1, :], heads) * incoming[...].astype(F32)
    eb = entering.astype(BF)
    u = dot(bb, gsb, 1, 1)
    v = dot(cb, eb, 1, 1)
    inner = jnp.concatenate(acts[: width // L], axis=1)
    gm = gm_r[...].astype(F32)
    seen = dot((inner * u).astype(BF), mats[:, :width], 1, 1)
    passed = dot((gm * v).astype(BF), mats[:, :width], 1, 1) * e
    gb = dot((inner * weights).astype(BF), gsb)
    gc = dot((gm * grown).astype(BF), eb)
    through = head_product(gsb.astype(F32), entering, mats[:, :width]) * jnp.exp(total)
    dscores = jnp.zeros((L, L), F32)
    rowsums = jnp.zeros((L, L), F32)
    colsums = jnp.zeros((L, L), F32)
    for pair in range(heads // 2):
        cols = slice(pair * L, pair * L + L)
        xb = acts[pair].astype(BF)
        gmb = gm_r[:, cols]
        got = []
        for h in (2 * pair, 2 * pair + 1):
            mine = first if h % 2 == 0 else jnp.logical_not(first)
            gmh = jnp.where(mine, gm[:, cols], 0.0).astype(BF)
            dm = dot(gmh, xb, 1, 1)
            gap = jnp.where(lower, cum[:, h : h + 1] - cum_t[h : h + 1, :], -1e30)
            decay = jnp.exp(gap)
            st = steps_t[h : h + 1, :]
            t1 = dm * decay
            dscores = dscores + t1 * st
            gp = t1 * scores
            rowsums = jnp.where(col == h, jnp.sum(gp * st, axis=1, keepdims=True), rowsums)
            colsums = jnp.where(row == h, jnp.sum(gp, axis=0, keepdims=True), colsums)
            mix = (scores * decay * st).astype(BF)
            got.append(dot(mix, gmb, 0, 0))
        ginner_o[:, cols] = (
            jnp.where(first, got[0], got[1])
            + weights[:, cols] * u[:, cols]
            + vecs[5:6, cols] * gm[:, cols]
        )
    db = dscores.astype(BF)
    gbc_o[:, :L] = gb + dot(db, cb, 0, 0)
    gbc_o[:, L:] = gc + dot(db, bb)
    direct = colsums.T
    seen = seen * wd
    gst_o[...] = direct + seen
    later = rowsums - direct * steps + passed
    tr = mats[:, width:]
    glog_o[...] = (
        dot_r(tr, later, 0, 0) + dot_r(tr, steps * seen) - steps * seen + through
    )


def crossing(vecs, later):
    row = lax.broadcasted_iota(jnp.int32, (16, later.shape[1]), 0)
    extra = jnp.zeros((16, later.shape[1]), F32)
    for j in range(1, KERNEL):
        for t in range(j):
            part = vecs[3 - j : 4 - j, :] * later[t : t + 1, :]
            extra = extra + jnp.where(row == 16 - j + t, part, 0.0)
    return extra


def back_conv_body(
    level, at, meta, cat, rim, pre, step, cum_r, sin, pfx, sfx, ginner_r, gbc_r, glog_r, gst_r,
    incoming, before, through, load, vecs, hv, mats,
    gcat_o, gsr_o, head_o, extra_o, acc_o, hacc_o, buf, acc, hacc, outgoing,
):
    width = vecs.shape[1] - 2 * L
    heads = width // HD
    keep_next = jnp.where(meta[3 + at.c] == 0, 1.0, 0.0)
    keep = jnp.where(meta[2 + at.c] == 0, 1.0, 0.0)
    later, buf = buf.at[at.other], buf.at[at.sub]

    def follow():
        buf[L : L + 8, :] = later[0:8, :] * keep_next

    if at.first is None:
        follow()
    else:

        @pl.when(at.first)
        def _():
            buf[L : L + 8, :] = jnp.zeros((8, width + 2 * L), F32)
            acc[...] = jnp.zeros_like(acc)
            hacc[...] = jnp.zeros_like(hacc)
            outgoing[...] = final_link(meta, level, True, before, through, load)

        pl.when(jnp.logical_not(at.first))(follow)

    step_in = step[...].astype(F32) + hv[0:1, :]
    steps = softplus(step_in)
    cum = cum_r[...]
    total = cum[L - 1 : L, :]
    wd = jnp.exp(total - cum)
    weights = dot((wd * steps).astype(BF), mats[:, :width])
    far = outgoing[...] * per_head(sfx[0][0:1, :], heads)
    fb = far.astype(BF)
    entering = sin[0].astype(F32) + per_head(pfx[0][0:1, :], heads) * incoming[...].astype(F32)
    through = head_product(far, entering, mats[:, :width]) * jnp.exp(total)
    acts, slopes = [], []
    for x0 in range(0, width + 2 * L, L):
        v = pre[:, x0 : x0 + L]
        s = sigmoid(v)
        a = v * s
        acts.append(a)
        slopes.append(s + a * (1.0 - s))
    bb = acts[-2].astype(BF)
    u = dot(bb, fb, 1, 1)
    inner = jnp.concatenate(acts[: width // L], axis=1)
    seen = dot((inner * u).astype(BF), mats[:, :width], 1, 1) * wd
    gb = dot((inner * weights).astype(BF), fb)
    glog = glog_r[...] + dot_r(mats[:, width:], steps * seen) - steps * seen + through
    gsi = (gst_r[...] + seen + glog * hv[1:2, :]) * sigmoid(step_in)
    gsr_o[...] = gsi.astype(BF)
    hacc[0:8, :] += eights(glog * steps * hv[1:2, :])
    hacc[8:16, :] += eights(gsi)
    for k, x0 in enumerate(range(0, width + 2 * L, L)):
        cols = slice(x0, x0 + L)
        if x0 < width:
            g = ginner_r[:, cols] + weights[:, cols] * u[:, cols]
        elif x0 == width:
            g = gbc_r[:, :L] + gb
        else:
            g = gbc_r[:, L:]
        g = g * slopes[k]
        buf[0:L, cols] = g
        acc[32:40, cols] += eights(g)
        here = cat[:, cols].astype(F32)
        out = vecs[3:4, cols] * g
        acc[24:32, cols] += eights(g * here)
        for j in range(1, KERNEL):
            moved = buf[j : j + L, cols]
            out = out + vecs[3 - j : 4 - j, cols] * moved
            acc[24 - 8 * j : 32 - 8 * j, cols] += eights(moved * here)
        gcat_o[:, cols] = out.astype(BF)
    if at.last is not None:

        @pl.when(at.last)
        def _():
            head_o[...] = buf[0:8, :]
            past = rim[...].astype(F32)[8:16, :] * keep
            now = buf[0:8, :]
            extra_o[...] = crossing(vecs, now * keep).astype(BF)
            row = lax.broadcasted_iota(jnp.int32, now.shape, 0)
            result = jnp.zeros_like(now)
            for k in range(5):
                part = jnp.sum(acc[8 * k : 8 * k + 8, :], axis=0, keepdims=True)
                j = 3 - k
                if 1 <= j <= 3:
                    for t in range(j):
                        part = part + now[t : t + 1, :] * past[8 + t - j : 9 + t - j, :]
                result = jnp.where(row == k, part, result)
            acc_o[...] = result
            hrow = lax.broadcasted_iota(jnp.int32, (8, L), 0)
            hacc_o[...] = jnp.where(
                hrow == 0,
                jnp.sum(hacc[0:8, :], axis=0, keepdims=True),
                jnp.sum(hacc[8:16, :], axis=0, keepdims=True),
            )


def dgrad_body(half, ggr, gcat, gsr, normed, wzx, wbc, wst, gain, conv, *refs):
    send_o, keep_o, shared_o, acc = refs
    width, d = wzx.shape[2], gain.shape[1]
    i = pl.program_id(0)

    @pl.when(i == 0)
    def _():
        acc[...] = jnp.zeros_like(acc)

    r = dot(ggr[...], wzx[0], 1, 1)
    r = r + dot(gcat[:, :width], wzx[1], 1, 1)
    r = r + dot(gcat[:, width : width + L], wbc[0], 1, 1)
    r = r + dot(gcat[:, width + L :], wbc[1], 1, 1)
    r = r + dot(gsr[...], wst[...])
    acc[...] += eights(r * normed[...].astype(F32))
    into_two(half, r.astype(BF), send_o, keep_o)

    @pl.when(i == 2 * half - 1)
    def _():
        shared_o[...] = jnp.zeros_like(shared_o)
        sums = jnp.sum(acc[...], axis=0, keepdims=True) / gain[...]
        for c in range(d // ROW):
            shared_o[c : c + 1, :] = sums[:, c * ROW : (c + 1) * ROW]
        shared_o[d // ROW : d // ROW + 5, :] = conv[0:5, conv.shape[1] - ROW :]


def outproj_body(half, normout, wout, send_o, keep_o):
    into_two(half, dot(normout[...], wout[...]).astype(BF), send_o, keep_o)


def exchange_order(count):
    if count == 1:
        return [0]
    inner = exchange_order(count // 2)
    return [2 * f + 1 for f in inner] + [2 * f for f in inner]


def rows_times(body, count, share, d, rows, consts, name, more=(), scratch=()):
    half = count // 2
    frames = [2 * f + odd for odd in (1, 0) for f in reversed(exchange_order(half))]

    def frame(i):
        return sum(jnp.where(i == k, f, 0) for k, f in enumerate(frames))

    return launch(
        functools.partial(body, half),
        [*rows, *consts],
        [pl.BlockSpec((share, r.shape[1]), lambda i: (frame(i), 0)) for r in rows]
        + [whole(a) for a in consts],
        [shaped((half * share, d), BF)] * 2 + list(more),
        [
            pl.BlockSpec((share, d), lambda i: (jnp.minimum(i, half - 1), 0)),
            pl.BlockSpec((share, d), lambda i: (jnp.maximum(i - half, 0), 0)),
            *[whole(o) for o in more],
        ],
        name,
        grid=(count,),
        scratch=scratch,
        vmem=20,
    )


def into_two(half, value, send_o, keep_o):
    i = pl.program_id(0)

    @pl.when(i < half)
    def _():
        send_o[...] = value

    @pl.when(i >= half)
    def _():
        keep_o[...] = value


def part_body(kept, got, keep_o, send_o):
    half = keep_o.shape[0]
    for o, rows in ((keep_o, slice(0, half)), (send_o, slice(half, 2 * half))):
        o[...] = (kept[rows, :].astype(F32) + got[rows, :].astype(F32)).astype(BF)


def total_body(*refs):
    total = refs[0][...].astype(F32)
    for ref in refs[1:-1]:
        total = total + ref[...].astype(F32)
    refs[-1][...] = total.astype(BF)


def hold_body(x, o):
    o[...] = x[...]


def hold(x, *deps):
    return simple(hold_body, [x], [shaped(x.shape, x.dtype)], "hold", deps=deps)[0]


def add_body(a, b, o):
    o[...] = (a[...].astype(F32) + b[...].astype(F32)).astype(o.dtype)


def add(a, b):
    return simple(add_body, [a, b], [shaped(a.shape, a.dtype)], "add")[0]


def swap(x, axis, mask):
    count = lax.axis_size(axis)
    return lax.ppermute(x, axis, [(i, i ^ mask) for i in range(count)])


def masks_of(axis):
    masks, mask = [], 1
    while mask < lax.axis_size(axis):
        masks.append(mask)
        mask *= 2
    return masks


def halve_body(slot, level, meta, kept, got, send_o, keep_o):
    bit = jnp.bitwise_and(jnp.right_shift(meta[slot], level), 1)
    half = send_o.shape[0]
    for o, b in ((send_o, 1 - bit), (keep_o, bit)):
        rows = pl.ds(pl.multiple_of(b * half, half), half)
        o[...] = (kept[rows, :].astype(F32) + got[rows, :].astype(F32)).astype(BF)


def halve(meta, slot, level, kept, got):
    shape = shaped((kept.shape[0] // 2, kept.shape[1]), BF)
    return simple(
        functools.partial(halve_body, slot, level), [kept, got], [shape, shape], "halve", meta
    )


def join_body(slot, level, meta, own, got, o):
    bit = jnp.bitwise_and(jnp.right_shift(meta[slot], level), 1)
    half = own.shape[0]
    o[pl.ds(pl.multiple_of(bit * half, half), half), :] = own[...]
    o[pl.ds(pl.multiple_of((1 - bit) * half, half), half), :] = got[...]


def join(meta, slot, level, own, got):
    shape = shaped((own.shape[0] * 2, own.shape[1]), BF)
    return simple(functools.partial(join_body, slot, level), [own, got], [shape], "join", meta)[0]


def wgrad_body(blocks, half, tails, meta, *refs):
    ins, (send_o, keep_o) = refs[:-2], refs[-2:]
    bit = bit_at(meta, 0)
    i = pl.program_id(0)
    g = jnp.where(i < half, (1 - bit) * half + i, bit * half + i - half)
    for p, tail in enumerate(tails):
        (a, b), ins = ins[:2], ins[2:]
        ta = tb = None
        if tail:
            (ta, tb), ins = ins[:2], ins[2:]
        inside = jnp.logical_and(g >= p * blocks, g < (p + 1) * blocks)

        def into(o, a=a, b=b, ta=ta, tb=tb):
            v = dot(a[...], b[...], 0, 0)
            if ta is not None:
                v = v + dot(ta[...], tb[...], 0, 0)
            o[...] = v.astype(BF)

        pl.when(jnp.logical_and(inside, i < half))(functools.partial(into, send_o))
        pl.when(jnp.logical_and(inside, i >= half))(functools.partial(into, keep_o))


def wgrads(meta, pairs, width, blocks):
    half = blocks * len(pairs) // 2
    tokens = pairs[0][0].shape[0]

    def cut(i, m):
        bit = jnp.bitwise_and(m[1], 1)
        g = jnp.where(i < half, (1 - bit) * half + i, bit * half + i - half)
        return (0, lax.rem(g, blocks))

    specs, ins = [], []
    for a, b, which, *more in pairs:
        for pair in [(a, b), tuple(more)]:
            for j, v in enumerate(pair):
                ins.append(v)
                specs.append(
                    pl.BlockSpec((v.shape[0], width), cut if j == which else lambda i, m: (0, 0))
                )
    return launch(
        functools.partial(wgrad_body, blocks, half, [len(p) > 3 for p in pairs]),
        ins,
        specs,
        [shaped((half * width, width), BF)] * 2,
        [
            pl.BlockSpec((width, width), lambda i, m: (jnp.minimum(i, half - 1), 0)),
            pl.BlockSpec((width, width), lambda i, m: (jnp.maximum(i - half, 0), 0)),
        ],
        "wgrad",
        grid=(2 * half,),
        meta=meta,
        vmem=20,
    )


def bc_body(meta, normed, gcat, gsr, rim, extra, send_o, keep_o, step_o):
    bit = jnp.bitwise_and(meta[0], 1)
    half = send_o.shape[0]
    for o, b in ((send_o, 1 - bit), (keep_o, bit)):
        cols = pl.ds(pl.multiple_of(b * half, half), half)
        v = dot(normed[:, cols], gcat[...], 0, 0) + dot(rim[:, cols], extra[...], 0, 0)
        o[...] = v.astype(BF)
    step_o[...] = dot(gsr[...], normed[...], 0, 0)[:8]


def bc_wgrad(meta, normed, gcat, gsr, rim, extra, width):
    tokens, d = normed.shape

    def tail(rows):
        return pl.BlockSpec((rows, 2 * L), lambda i, m: (0, width // (2 * L)))

    outs = [shaped((d // 2, 2 * L), BF)] * 2 + [shaped((8, d))]
    return launch(
        bc_body,
        [normed, gcat, gsr, rim, extra],
        [whole(normed), tail(tokens), whole(gsr), whole(rim), tail(16)],
        outs,
        [whole(o) for o in outs],
        "bc_wgrad",
        meta=meta,
        vmem=12,
    )


def columns_body(blocks, width, src, *rest):
    o = rest[-1]
    for k in range(blocks):
        o[:, k * width : (k + 1) * width] = src[k * width : (k + 1) * width, :].astype(F32)


def columns(meta, src, mine, d, width, old):
    half = src.shape[0]
    ins, specs, aliases = [src], [whole(src)], {}
    if old is not None:
        ins.append(old)
        specs.append(pl.BlockSpec(memory_space=pl.ANY))
        aliases = {1: 0}
    return launch(
        lambda meta, *refs: columns_body(half // width, width, *refs), ins, specs,
        [shaped((width, d))],
        [pl.BlockSpec((width, half), lambda i, m: (0, bit_at(m, 0) ^ (1 - mine)))],
        "out_weights", meta=meta, aliases=aliases, vmem=16, token=False,
    )[0]


def rows_body(src, *rest):
    rest[-1][0] = src[...].astype(F32)


def rows_of(meta, src, mine, which, d, width, old):
    half = src.shape[0]
    ins, aliases = [src], {}
    specs = [whole(src)]
    if old is not None:
        ins.append(old)
        specs.append(pl.BlockSpec(memory_space=pl.ANY))
        aliases = {1: 0}
    return launch(
        lambda meta, *refs: rows_body(*refs), ins, specs, [shaped((2, d, width))],
        [pl.BlockSpec((1, half, width), lambda i, m: (which, bit_at(m, 0) ^ (1 - mine), 0))],
        "zx_weights", meta=meta, aliases=aliases, vmem=16, token=False,
    )[0]


def bc_out_body(meta, own, got, o):
    bit = jnp.bitwise_and(meta[0], 1)
    half = own.shape[0]
    for v, b in ((own, bit), (got, 1 - bit)):
        rows = pl.ds(pl.multiple_of(b * half, half), half)
        o[0, rows, :] = v[:, :L].astype(F32)
        o[1, rows, :] = v[:, L:].astype(F32)


def patch_body(meta, gcat, ahead, vecs, o):
    count = meta.shape[0] - 3
    keep = jnp.where(meta[2 + count] == 0, 1.0, 0.0)
    o[...] = (gcat[...].astype(F32) + crossing(vecs, ahead[...] * keep)).astype(BF)


def patched(meta, gcat, ahead, vecs, share, group):
    wide = gcat.shape[1]

    def spot(i, m):
        return ((jnp.bitwise_xor(m[0], group - 1) + 1) * (share // 16) - 1, 0)

    return launch(
        patch_body,
        [gcat, ahead, vecs],
        [pl.BlockSpec((16, wide), spot), whole(ahead), whole(vecs)],
        [shaped(gcat.shape, BF)],
        [pl.BlockSpec((16, wide), spot)],
        "patch",
        meta=meta,
        aliases={0: 0},
        token=False,
    )[0]


def layer_body(tok, a, b, o):
    o[...] = (tok[...].astype(F32) + (a[...].astype(F32) + b[...].astype(F32))).astype(BF)


def tokens_body(tok, cot, a, b, gain, gt_o):
    x = tok[...].astype(F32)
    rstd = lax.rsqrt(jnp.mean(x * x, axis=1, keepdims=True) + EPS)
    unit = x * rstd
    gunit = (a[...].astype(F32) + b[...].astype(F32)) * gain[...]
    gt_o[...] = cot[...].astype(F32) + rstd * (
        gunit - unit * jnp.mean(gunit * unit, axis=1, keepdims=True)
    )


def halves_of(v):
    hi, lo = split(v)
    return jnp.concatenate([hi, lo], axis=0)


def whole_of(v):
    n = v.shape[0] // 2
    v = v.astype(F32)
    return v[:n] + v[n:]


def lead_body(bc, shared, o):
    rows = bc.shape[0]
    o[:rows, :] = bc[...]
    o[rows:, :] = halves_of(shared[...])


def misc_halve_body(level, meta, kept, shared, got, send_o, keep_o, shared_o):
    bit = jnp.bitwise_and(jnp.right_shift(meta[0], level), 1)
    half = keep_o.shape[0]
    total = shared[...] + whole_of(got[2 * half :, :])
    shared_o[...] = total
    for o, b in ((send_o, 1 - bit), (keep_o, bit)):
        rows = pl.ds(pl.multiple_of(b * half, half), half)
        o[0:half, :] = (kept[rows, :].astype(F32) + got[rows, :].astype(F32)).astype(BF)
    send_o[half:, :] = halves_of(total)


def misc_pack_body(kept, shared, got, step, conv, gate, head, o):
    rows = kept.shape[0]
    o[0:rows, :] = (kept[...].astype(F32) + got[0:rows, :].astype(F32)).astype(BF)
    d = step.shape[1]
    at = rows
    for k in range(d // ROW):
        o[at : at + 8, :] = step[:, k * ROW : (k + 1) * ROW].astype(BF)
        at += 8
    total = shared[...] + whole_of(got[rows:, :])
    width = gate.shape[1]
    parts = [total]
    for ref, first, n in ((conv, 0, 5), (gate, 0, 2)):
        for k in range(width // ROW):
            parts.append(ref[first : first + n, k * ROW : (k + 1) * ROW])
    used = 7 * (width // ROW)
    parts.append(jnp.concatenate([head[0:1, :], head[1:2, :]], axis=1))
    parts.append(jnp.zeros((31 - used, ROW), F32))
    o[at:, :] = halves_of(jnp.concatenate(parts, axis=0))


def misc_sum(a, b, plain_rows):
    first = a[0:plain_rows, :].astype(F32) + b[0:plain_rows, :].astype(F32)
    return first, whole_of(a[plain_rows:, :]) + whole_of(b[plain_rows:, :])


def misc_add_body(plain_rows, a, b, o):
    first, rest = misc_sum(a, b, plain_rows)
    o[0:plain_rows, :] = first.astype(BF)
    o[plain_rows:, :] = halves_of(rest)


def misc_finish_body(bc_rows, a, b, mats, bcw_o, gain_o, bc_o, bcb_o, step_o, taps_o, bias_o,
                     sb_o, dl_o, sk_o, ng_o):
    d, width, heads = gain_o.shape[1], taps_o.shape[1], sb_o.shape[1]
    n = d // ROW
    first, rest = misc_sum(a, b, bc_rows + 8 * n)
    bcw_o[...] = first[0:bc_rows].astype(BF)
    for k in range(n):
        cols = slice(k * ROW, (k + 1) * ROW)
        at = bc_rows + 8 * k
        step_o[:, cols] = first[at : at + heads]
        gain_o[:, cols] = rest[k : k + 1]
    for k in range(2):
        v = rest[n : n + 5, k * L : (k + 1) * L]
        bc_o[k] = v[0:4]
        bcb_o[k : k + 1, :] = v[4:5]
    at = 16
    m = width // ROW
    gates = []
    for k in range(m):
        cols = slice(k * ROW, (k + 1) * ROW)
        taps_o[:, cols] = rest[at : at + 4]
        bias_o[:, cols] = rest[at + 4 : at + 5]
        at += 5
    for k in range(m):
        cols = slice(k * ROW, (k + 1) * ROW)
        ng_o[:, cols] = rest[at : at + 1]
        gates.append(jnp.broadcast_to(rest[at + 1 : at + 2], (8, ROW)))
        at += 2
    sk = dot_l(jnp.concatenate(gates, axis=1), mats[:, :width], 1, 1)
    sk_o[...] = sk[0:1, :heads]
    dl_o[...] = rest[at : at + 1, :heads]
    sb_o[...] = rest[at : at + 1, L : L + heads]


class Spot(NamedTuple):
    c: Any
    sub: int
    other: int
    first: Any
    last: Any


ORDER = "WLLFLGFWLGTIWMGTWMIGTMWMIGMWTIBMGBIIMWMBGMI"


def run_chains(chains, done, order):
    needs = {name: next(chain) for name, chain in chains.items()}

    def step(name):
        need, waits = needs[name]
        if need is not None and need not in done:
            return False
        if waits:
            space()
        try:
            needs[name] = next(chains[name])
        except StopIteration:
            del needs[name]
            done.add(name)
        return True

    for name in order:
        if not step(name):
            raise ValueError(name)
    while needs:
        for name in list(needs):
            step(name)


def on_device(
    tokens_in,
    grad_out,
    scene_offsets,
    input_gain,
    weight_zx,
    weight_bc,
    weight_step,
    conv_inner,
    conv_inner_bias,
    conv_bc,
    conv_bc_bias,
    step_bias,
    decay_log,
    skip_weight,
    norm_gain,
    weight_out,
):
    share, d = tokens_in.shape
    group = lax.axis_size(TP)
    tokens = share * group
    heads = step_bias.shape[0]
    width = norm_gain.shape[0]
    wide = width + 2 * L
    count = tokens // L
    per = share // L
    half = group // 2
    me = lax.axis_index(TP)
    place = lax.axis_index(DP)

    heads_pos = place * tokens + jnp.arange(count + 1, dtype=jnp.int32) * L
    starts = jnp.any(heads_pos[:, None] == scene_offsets[None, :], axis=1).astype(jnp.int32)
    meta = jnp.concatenate([me[None].astype(jnp.int32), place[None].astype(jnp.int32), starts])
    masks, tmasks = masks_of(DP), masks_of(TP)
    levels = len(masks)

    LAST.clear()
    def spread_out(held, keys):
        mask = half // 2
        while mask:
            for f in [f for f in held if f in keys]:
                held[f ^ mask] = swap(held[f], TP, mask)
            mask //= 2

    near, far = range(half), range(half, group)
    held = {0: tokens_in}
    arrived = swap(tokens_in, TP, half)
    spread_out(held, near)
    dps = lax.axis_size(DP)
    (last_rows,) = launch(
        lambda tok, _, o: hold_body(tok, o), [tokens_in, held[1]],
        [pl.BlockSpec((16, d), lambda i: (share // 16 - 1, 0)), pl.BlockSpec(memory_space=pl.ANY)],
        [shaped((16, d), BF)], [pl.BlockSpec((16, d), lambda i: (0, 0))], "last_rows",
    )
    past = [
        lax.ppermute(
            last_rows,
            (DP, TP),
            [(i * group + group - 1, (i + 1) * group + t) for i in range(dps - 1)],
        )
        for t in range(1, group, 2)
    ]
    gain = input_gain[None]
    prep_ins = [conv_inner, conv_inner_bias[None], conv_bc, conv_bc_bias, step_bias[None],
                decay_log[None], skip_weight[None], norm_gain[None], weight_step.T]
    prep_outs = [shaped((8, wide)), shaped((8, L)), shaped((L, width + L), BF),
                 shaped((L, d), BF)]
    vecs, hv, mats, wst = launch(
        prep_body,
        [pltpu.with_memory_space_constraint(a, pltpu.HBM) for a in prep_ins],
        [whole(a) for a in prep_ins],
        prep_outs, [whole(o) for o in prep_outs], "prep", vmem=4,
    )
    def stretched(body, name, ins, outs, scratch, reverse, vmem, span=None, old=()):
        begin, length = span or (0, count // per)

        def order(i):
            return count // per - 1 - i - begin if reverse else i + begin

        def spec(kind, shape):
            if kind == ROWS:
                return pl.BlockSpec(
                    (share, shape[1]), lambda i, m: (lax.bitwise_xor(order(i), m[0]), 0)
                )
            if kind == EACH:
                return pl.BlockSpec((per, *shape[1:]), lambda i, m: (order(i), 0, 0))
            return pl.BlockSpec(shape, lambda i, m: (0,) * len(shape))

        kinds = [k for k, _ in ins] + [k for k, _, _ in outs]
        n = len(ins)

        def run(meta, *refs):
            refs = refs[:n] + refs[n + len(old) :]
            step = pl.program_id(0)
            for sub in range(per):
                pos = per - 1 - sub if reverse else sub

                def view(kind, ref, pos=pos):
                    if kind == ROWS:
                        return ref.at[pl.ds(pos * L, L)]
                    return ref.at[pl.ds(pos, 1)] if kind == EACH else ref

                views = [view(k, r) for k, r in zip(kinds, refs)]
                at = Spot(
                    order(step) * per + pos,
                    sub,
                    (sub - 1) % per,
                    step == 0 if sub == 0 else None,
                    step == length - 1 if sub == per - 1 else None,
                )
                body(at, meta, *views, *refs[len(kinds) :])

        return launch(
            run,
            [a for _, a in ins] + list(old),
            [spec(k, a.shape) for k, a in ins] + [pl.BlockSpec(memory_space=pl.ANY)] * len(old),
            [shaped(s, t) for _, s, t in outs],
            [spec(k, s) for k, s, _ in outs],
            name,
            grid=(length,),
            meta=meta,
            scratch=scratch,
            aliases={n + j: j for j in range(len(old))},
            vmem=vmem,
        )

    weights = (gain, weight_zx, weight_bc, wst)
    before = project(meta, [held[f] for f in near], [], *weights, tokens, 0, [])
    space()
    held[half] = hold(arrived, before[3])
    (own_past,) = simple(total_body, past, [shaped((16, d), BF)], "past")
    past = [own_past, swap(own_past, TP, 1)]
    spread_out(held, far)
    before = project(meta, [held[half]], [], *weights, tokens, half, list(before))
    space()
    normed, gate_raw, cat, step_raw, rim, normed_rim = project(
        meta, [held[f] for f in far[1:]], past, *weights, tokens, half + 1, list(before)
    )

    tall = (tokens, L)
    state_shape = (width, L)
    load_shape = (width + 16, L)
    small = (8, L)
    pre, cb, sin, state, load, cum, pfx, decay = stretched(
        states_body,
        "states",
        [(ROWS, cat), (ROWS, step_raw), (ONE, rim), (ONE, vecs), (ONE, hv),
         (ONE, mats)],
        [(ROWS, (tokens, wide), F32), (ROWS, tall, BF), (EACH, (count, *state_shape), BF),
         (ONE, state_shape, F32), (ONE, load_shape, BF), (ROWS, tall, F32),
         (EACH, (count, 8, L), F32), (ONE, small, F32)],
        [pltpu.VMEM((per, L + 8, wide), F32), pltpu.VMEM(state_shape, F32),
         pltpu.VMEM(small, F32)],
        False, 14,
    )

    def link(level, reverse, held, load):
        final = level == levels - 2
        shapes = [load_shape, state_shape, small] + ([] if final else [state_shape, small])
        load, before, through, *more = simple(
            functools.partial(link_body, level, reverse, final), [*held, load],
            [shaped(s, BF if j == 0 else F32) for j, s in enumerate(shapes)], "link", meta,
        )
        return [*more, before, through], load

    thr = decay
    fresh = [jnp.zeros(state_shape, F32), jnp.ones(small, F32)]
    own = [state, decay, *fresh]
    load = swap(load, DP, 1)
    cots = {0: grad_out}
    cots[half] = swap(hold(grad_out), TP, half)
    (y,) = stretched(
        within_body,
        "within",
        [(ROWS, pre), (ROWS, step_raw), (ROWS, cum), (EACH, sin), (ONE, vecs),
         (ONE, hv), (ONE, mats)],
        [(ROWS, (tokens, width), F32)],
        [], False, 14,
    )
    for level in range(levels - 1):
        space()
        own, load = link(level, False, own, load)
        load = swap(load, DP, masks[level + 1])
        if level == levels - 2:
            space()
            late = {half: hold(cots[half])}
            spread_out(late, far)
            spread_out(cots, near)
            cots.update({f: late[f] for f in far[1:]})
            space()
            cot_all, gn = cotangent([cots[f] for f in range(group)], weight_out)
    befores, throughs = own[-2:]
    space()
    mixed, sums, incoming = stretched(
        functools.partial(gate_body, levels - 1),
        "gated",
        [(ROWS, cb), (ROWS, cum), (EACH, pfx), (ROWS, y), (ROWS, gate_raw),
         (ROWS, gn), (ONE, befores), (ONE, throughs), (ONE, load), (ONE, vecs),
         (ONE, mats)],
        [(ROWS, (tokens, width), F32), (EACH, (count, 2, L), F32), (ONE, state_shape, BF)],
        [], False, 14,
    )
    for mask in tmasks[::-1][:-1]:
        got = swap(sums, TP, mask)
        space()
        sums = add(sums, got)
    sums2 = swap(sums, TP, 1)
    space()
    normout, gm, ggr, gs, toward, first_load, sfx, gate_acc = stretched(
        back_gate_body,
        "back_gated",
        [(ROWS, pre), (ROWS, cum), (ROWS, mixed), (ROWS, gate_raw), (ROWS, gn),
         (EACH, sums), (EACH, sums2), (ONE, thr), (ONE, vecs), (ONE, mats)],
        [(ROWS, (tokens, width), BF), (ROWS, (tokens, width), BF),
         (ROWS, (tokens, width), BF), (EACH, (count, *state_shape), BF),
         (ONE, state_shape, F32), (ONE, load_shape, BF), (EACH, (count, 8, L), F32),
         (ONE, (8, width), F32)],
        [pltpu.VMEM(state_shape, F32), pltpu.VMEM(small, F32), pltpu.VMEM((16, width), F32)],
        True, 14,
    )

    kept = SimpleNamespace(within=(), zx=None, wout=None)
    done = set()
    blocks = d // width

    def weights_chain(pairs, finish, need=None):
        yield need, False
        send, keep = wgrads(meta, [pairs()], width, blocks)
        for level in range(levels):
            got = swap(send, DP, masks[level])
            yield None, True
            if level < levels - 1:
                send, keep = halve(meta, 1, level + 1, keep, got)
            else:
                total = add(keep, got)
        for level in range(levels - 1, -1, -1):
            got = swap(total, DP, masks[level])
            if not level:
                finish(total, 1)
            yield None, True
            if level:
                total = join(meta, 1, level, total, got)
        finish(got, 0)

    def out_weights(src, mine):
        kept.wout = columns(meta, src, mine, d, width, kept.wout)

    def gate_weights(src, mine):
        kept.zx = rows_of(meta, src, mine, 0, d, width, kept.zx)

    def inner_weights(src, mine):
        kept.zx = rows_of(meta, src, mine, 1, d, width, kept.zx)

    def links_chain():
        yield None, False
        own, load = [toward, thr, *fresh], first_load
        for level in range(levels):
            got = swap(load, DP, masks[level])
            yield None if level < levels - 1 else "F", True
            if level < levels - 1:
                own, load = link(level, True, own, got)
        befores, throughs = own[-2:]
        ginner, gbc, glog, gst = kept.within
        kept.gcat, kept.gsr, kept.head, kept.extra, kept.conv_acc, kept.head_acc = stretched(
            functools.partial(back_conv_body, levels - 1),
            "back_conv",
            [(ROWS, cat), (ONE, rim), (ROWS, pre), (ROWS, step_raw), (ROWS, cum),
             (EACH, sin), (EACH, pfx), (EACH, sfx), (ROWS, ginner), (ROWS, gbc),
             (ROWS, glog), (ROWS, gst), (ONE, incoming), (ONE, befores), (ONE, throughs),
             (ONE, got), (ONE, vecs), (ONE, hv), (ONE, mats)],
            [(ROWS, (tokens, wide), BF), (ROWS, tall, BF), (ONE, (8, wide), F32),
             (ONE, (16, wide), BF), (ONE, (8, wide), F32), (ONE, small, F32)],
            [pltpu.VMEM((per, L + 8, wide), F32), pltpu.VMEM((40, wide), F32),
             pltpu.VMEM((16, L), F32), pltpu.VMEM(state_shape, F32)],
            True, 16,
        )

    def within_chain():
        for begin in (0, half):
            yield None, False
            kept.within = stretched(
                back_within_body,
                "back_within",
                [(ROWS, pre), (ROWS, step_raw), (ROWS, cum), (EACH, sin), (EACH, pfx),
                 (EACH, gs), (ROWS, gm), (ONE, incoming), (ONE, vecs), (ONE, hv), (ONE, mats)],
                [(ROWS, (tokens, width), F32), (ROWS, (tokens, 2 * L), F32), (ROWS, tall, F32),
                 (ROWS, tall, F32)],
                [], True, 16, (begin, half), kept.within,
            )

    def scattered(send, keep):
        for mask in tmasks[:-1]:
            got = swap(send, TP, mask)
            yield None, True
            shape = shaped((keep.shape[0] // 2, d), BF)
            keep, send = simple(part_body, [keep, got], [shape, shape], "part")
        got = swap(send, TP, half)
        yield None, True
        return keep, got

    def branch_chain():
        yield None, False
        branch = rows_times(outproj_body, group, share, d, [normout], [weight_out], "outproj")
        parts = yield from scattered(*branch)
        (kept.layer,) = simple(
            layer_body, [tokens_in, *parts], [shaped((share, d), BF)], "layer", tick=True
        )

    def tokens_chain():
        yield "L", False
        ahead = lax.ppermute(kept.head, DP, [(i + 1, i) for i in range(dps - 1)])
        yield None, True
        gcat = patched(meta, kept.gcat, ahead, vecs, share, group)
        *grads, kept.shared = rows_times(
            dgrad_body, group, share, d, [ggr, gcat, kept.gsr, normed],
            [weight_zx, weight_bc, wst, gain, kept.conv_acc],
            "dgrad", [shaped((16, ROW))], [pltpu.VMEM((8, d), F32)],
        )
        done.add("dgrad")
        parts = yield from scattered(*grads)
        (kept.tokens,) = simple(
            tokens_body, [tokens_in, grad_out, *parts, gain], [shaped((share, d))], "tokens",
            None, 12, tick=True,
        )

    def misc_chain():
        yield "L", False
        send, keep, step_acc = bc_wgrad(
            meta, normed, kept.gcat, kept.gsr, normed_rim, kept.extra, width
        )
        yield "dgrad", False
        shared = kept.shared
        (load,) = simple(lead_body, [send, shared], [shaped((send.shape[0] + 32, ROW), BF)], "lead")
        for level in range(len(tmasks)):
            got = swap(load, TP, tmasks[level])
            yield None, True
            if level < len(tmasks) - 1:
                rows = keep.shape[0] // 2
                load, keep, shared = simple(
                    functools.partial(misc_halve_body, level + 1), [keep, shared, got],
                    [shaped((rows + 32, ROW), BF), shaped((rows, ROW), BF), shaped((16, ROW))],
                    "misc_halve", meta,
                )
        rows = keep.shape[0]
        flat = rows + 8 * (d // ROW)
        (load,) = simple(
            misc_pack_body,
            [keep, shared, got, step_acc, kept.conv_acc, gate_acc, kept.head_acc],
            [shaped((flat + 96, ROW), BF)], "misc_pack",
        )
        for level in range(levels):
            got = swap(load, DP, masks[level])
            yield None, True
            if level < levels - 1:
                (load,) = simple(
                    functools.partial(misc_add_body, flat), [load, got],
                    [shaped(load.shape, BF)], "misc_add",
                )
        outs = [(1, d), (2, 4, L), (2, L), (heads, d), (4, width), (1, width), (1, heads),
                (1, heads), (1, heads), (1, width)]
        total, *kept.small = simple(
            functools.partial(misc_finish_body, rows), [load, got, mats],
            [shaped((rows, ROW), BF)] + [shaped(s) for s in outs], "misc_finish",
            tick=True,
        )
        for level in range(len(tmasks) - 1, -1, -1):
            got = swap(total, TP, tmasks[level])
            yield None, True
            if level:
                total = join(meta, 0, level, total, got)
        (kept.bc,) = simple(
            bc_out_body, [total, got], [shaped((2, d, L))], "bc_weights", meta, tick=True
        )

    run_chains(
        {
            "L": links_chain(),
            "W": weights_chain(lambda: (normout, cot_all, 1), out_weights),
            "G": weights_chain(lambda: (normed, ggr, 0), gate_weights),
            "F": within_chain(),
            "B": branch_chain(),
            "T": tokens_chain(),
            "I": weights_chain(
                lambda: (normed, kept.gcat, 0, normed_rim, kept.extra), inner_weights, "L"
            ),
            "M": misc_chain(),
        },
        done,
        ORDER if (dps, group) == (8, 4) else "",
    )

    gain_g, bc_g, bcb_g, step_g, taps_g, bias_g, sb_g, dl_g, sk_g, ng_g = kept.small
    return (
        kept.layer,
        kept.tokens,
        gain_g[0],
        kept.zx,
        kept.bc,
        step_g.T,
        taps_g,
        bias_g[0],
        bc_g,
        bcb_g,
        sb_g[0],
        dl_g[0],
        sk_g[0],
        ng_g[0],
        kept.wout,
    )


def solution(mesh):
    rows = P((DP, TP), None)
    cols = P(None, TP)
    one = P(TP)
    in_specs = (
        rows, rows, P(), P(), P(None, None, TP), P(), cols, cols, one, P(), P(),
        one, one, one, one, P(TP, None),
    )
    out_specs = (
        rows, rows, P(), P(None, None, TP), P(), cols, cols, one, P(), P(),
        one, one, one, one, P(TP, None),
    )
    return jax.shard_map(
        on_device, mesh=mesh, in_specs=in_specs, out_specs=out_specs, check_vma=False
    )
```
